32 devices in a mesh: dp: 8 (over y, x, core), tensor: 4 (over z).
Axes of the slice: x: 2, y: 2, z: 4, core: 2. Of those that a mesh axis runs over, the one named last changes fastest.
Arguments:
- hidden_in: float32 [4096, 1536], P(('dp', 'tensor')), may hold values from -6 to 6
- text_states: bfloat16 [4096, 4096], P(('dp', 'tensor')), may hold values from -6 to 6
- time_embed: float32 [8, 6, 1536], P('dp'), may hold values from -3 to 3
- positions: int32 [3, 4096], P(None, 'dp'), may hold values from 0 to 34, as said below
- modulation: bfloat16 [6, 1536], P(None, 'dp'), may hold values from -2 to 2
- query_weight: bfloat16 [1536, 1536], P('dp', 'tensor'), may hold values from -0.15625 to 0.15625
- key_weight: bfloat16 [1536, 1536], P('dp', 'tensor'), may hold values from -0.15625 to 0.15625
- value_weight: bfloat16 [1536, 1536], P('dp', 'tensor'), may hold values from -0.15625 to 0.15625
- out_weight: bfloat16 [1536, 1536], P('tensor', 'dp'), may hold values from -1.25 to 1.25
- cross_query: bfloat16 [1536, 1536], P('dp', 'tensor'), may hold values from -0.15625 to 0.15625
- cross_key: bfloat16 [4096, 1536], P('dp', 'tensor'), may hold values from -0.09375 to 0.09375
- cross_value: bfloat16 [4096, 1536], P('dp', 'tensor'), may hold values from -0.09375 to 0.09375
- cross_out: bfloat16 [1536, 1536], P('tensor', 'dp'), may hold values from -1.25 to 1.25
- up_weight: bfloat16 [1536, 8960], P('dp', 'tensor'), may hold values from -0.15625 to 0.15625
- down_weight: bfloat16 [8960, 1536], P('tensor', 'dp'), may hold values from -0.0625 to 0.0625
- qk_gain: bfloat16 [12, 512], P('tensor', 'dp'), may hold values from 0.099609375 to 1.8984375
- norm_gain: bfloat16 [1536], P('dp'), may hold values from 0.099609375 to 1.8984375
- cotangent: float32 [4096, 1536], P(('dp', 'tensor')), may hold values from -6 to 6
Outputs:
- block_out: float32 [4096, 1536], P(('dp', 'tensor'))
- grad_hidden: float32 [4096, 1536], P(('dp', 'tensor'))
- grad_text: float32 [4096, 4096], P(('dp', 'tensor'))
- grad_time: float32 [8, 6, 1536], P('dp')
- grad_modulation: float32 [6, 1536], P(None, 'dp')
- grad_query: float32 [1536, 1536], P('dp', 'tensor')
- grad_key: float32 [1536, 1536], P('dp', 'tensor')
- grad_value: float32 [1536, 1536], P('dp', 'tensor')
- grad_out_weight: float32 [1536, 1536], P('tensor', 'dp')
- grad_cross_query: float32 [1536, 1536], P('dp', 'tensor')
- grad_cross_key: float32 [4096, 1536], P('dp', 'tensor')
- grad_cross_value: float32 [4096, 1536], P('dp', 'tensor')
- grad_cross_out: float32 [1536, 1536], P('tensor', 'dp')
- grad_up: float32 [1536, 8960], P('dp', 'tensor')
- grad_down: float32 [8960, 1536], P('tensor', 'dp')
- grad_qk_gain: float32 [12, 512], P('tensor', 'dp')
- grad_norm_gain: float32 [1536], P('dp')
The draws below stay inside these ranges and needn't reach their ends.
Inputs may be any that keep to these rules, and one draw needn't show every extreme that they name: `positions`: in each of the 8 clips the 512 tokens run over a grid of frames by rows by columns, frames slowest and columns fastest, with 4 or 8 rows and 4 or 8 columns a frame; frame, row and column numbers are shifted by offsets of at most 3, 15 and 15 that are drawn per clip.
All inputs are finite; a program needn't handle non-finite values.
Results may differ from the reference program's by a relative error of at most 0.02.
Values may be sent and summed in bfloat16 or wider, within the bound.
A program may use at most 192 MiB of HBM per device.

```python
import jax
import jax.numpy as jnp
from jax import lax

HEADS = 12
HEAD_DIM = 128
D = 1536
FF = 8960
TEXT_DIM = 4096
TEXT = 512
LEN = 512
CLIPS = 8
TOKENS = 4096


def draw_positions(key, part):
    keys = jax.random.split(key, 5)
    tall = jnp.where(jax.random.randint(keys[0], (CLIPS, 1), 0, 2) == 1, 8, 4)
    broad = jnp.where(jax.random.randint(keys[1], (CLIPS, 1), 0, 2) == 1, 8, 4)
    frame_off = jax.random.randint(keys[4], (CLIPS, 1), 0, 4)
    row_off = jax.random.randint(keys[3], (CLIPS, 1), 0, 16)
    col_off = jax.random.randint(keys[2], (CLIPS, 1), 0, 16)
    tall = tall.at[0, 0].set(4).at[1, 0].set(8)
    broad = broad.at[0, 0].set(4).at[1, 0].set(8)
    frame_off = frame_off.at[0, 0].set(3)
    row_off = row_off.at[0, 0].set(0).at[1, 0].set(15)
    col_off = col_off.at[0, 0].set(0).at[1, 0].set(15)
    order = jnp.arange(LEN, dtype=jnp.int32)[None, :]
    column = order % broad + col_off
    row = order // broad % tall + row_off
    frame = order // (broad * tall) + frame_off
    return jnp.stack([frame, row, column], axis=0).reshape(3, CLIPS * LEN).astype(jnp.int32)


def with_spikes(array, own_key, source, target, parts, factor):
    owner, partner = [(jnp.arange(array.shape[axis_at]) // (array.shape[axis_at] // parts)).reshape([-1 if axis == axis_at else 1 for axis in range(array.ndim)]) for axis_at in (source, target)]
    chosen = jax.random.permutation(own_key, parts)[partner]
    strong = (owner == chosen) | (owner == (partner + parts // 2) % parts)
    return jnp.where(strong, factor * array, array)


def levels(rng, dims, cuts, smallest, high):
    level, own = 1.0, jax.random.fold_in(rng, 6)
    for position, blocks in cuts:
        draws = jnp.exp(jax.random.uniform(jax.random.fold_in(own, position), (blocks,), jnp.float32, smallest / len(cuts), high / len(cuts)))
        level = level * jnp.repeat(draws, dims[position] // blocks).reshape([-1 if axis == position else 1 for axis in range(len(dims))])
    return level


def centred(own_key, shape, scale, bound, cuts=(), held_as=jnp.bfloat16):
    drawn = scale * jax.random.normal(own_key, shape, jnp.float32)
    if cuts:
        drawn = drawn * levels(own_key, shape, cuts, -0.22, 0.18)
    return jnp.clip(drawn, -bound, bound).astype(held_as)


def heavy_noise(rng, shape, scale, reach, shards, heavy, kind=jnp.bfloat16):
    entries = scale * jax.random.normal(rng, shape, jnp.float32)
    if shards:
        entries = entries * levels(rng, shape, shards, -0.22, 0.18)
    return jnp.clip(with_spikes(entries, jax.random.fold_in(rng, 3), *heavy), -reach, reach).astype(kind)


def setup_inputs(seed: int = 0) -> dict:
    streams_of = jax.random.split(jax.random.key(seed), 19)
    hidden_in = heavy_noise(streams_of[0], (TOKENS, D), 1.0, 6.0, ((0, 32),), (0, 1, 32, 2.75), jnp.float32)
    text_states = centred(streams_of[1], (CLIPS * TEXT, TEXT_DIM), 1.0, 6.0, ((0, 32),))
    time_embed = centred(streams_of[2], (CLIPS, 6, D), 0.5, 3.0, ((0, 8),), jnp.float32)
    positions = draw_positions(jax.random.fold_in(streams_of[18], 71), 0)
    modulation = centred(streams_of[4], (6, D), 0.3, 2.0, ((1, 8),))
    query_weight = centred(streams_of[5], (D, D), D ** -0.5, 0.15625, ((0, 8), (1, 4)))
    key_weight = centred(streams_of[6], (D, D), D ** -0.5, 0.15625, ((0, 8), (1, 4)))
    value_weight = centred(streams_of[7], (D, D), D ** -0.5, 0.15625, ((0, 8), (1, 4)))
    out_weight = centred(streams_of[8], (D, D), (max(D // 64, 1)) ** -0.5, 1.25, ((0, 4), (1, 8)))
    cross_query = centred(streams_of[9], (D, D), D ** -0.5, 0.15625, ((0, 8), (1, 4)))
    cross_key = centred(streams_of[10], (TEXT_DIM, D), TEXT_DIM ** -0.5, 0.09375, ((0, 8), (1, 4)))
    cross_value = centred(streams_of[11], (TEXT_DIM, D), TEXT_DIM ** -0.5, 0.09375, ((0, 8), (1, 4)))
    cross_out = centred(streams_of[12], (D, D), (max(D // 64, 1)) ** -0.5, 1.25, ((0, 4), (1, 8)))
    up_weight = centred(streams_of[13], (D, FF), D ** -0.5, 0.15625, ((0, 8), (1, 4)))
    down_weight = centred(streams_of[14], (FF, D), FF ** -0.5, 0.0625, ((0, 4), (1, 8)))
    qk_gain = jnp.clip(1.0 + 0.18 * jax.random.normal(streams_of[15], (HEADS, 4 * HEAD_DIM), jnp.float32), 0.099609375, 1.8984375).astype(jnp.bfloat16)
    norm_gain = jnp.clip(1.0 + 0.18 * jax.random.normal(streams_of[16], (D,), jnp.float32), 0.099609375, 1.8984375).astype(jnp.bfloat16)
    cotangent = heavy_noise(streams_of[17], (TOKENS, D), 1.0, 6.0, ((0, 32),), (0, 1, 32, 2.75), jnp.float32)
    return {"hidden_in": hidden_in, "text_states": text_states, "time_embed": time_embed, "positions": positions, "modulation": modulation, "query_weight": query_weight, "key_weight": key_weight, "value_weight": value_weight, "out_weight": out_weight, "cross_query": cross_query, "cross_key": cross_key, "cross_value": cross_value, "cross_out": cross_out, "up_weight": up_weight, "down_weight": down_weight, "qk_gain": qk_gain, "norm_gain": norm_gain, "cotangent": cotangent}


HIGHEST = lax.Precision.HIGHEST
EPSILON = 1e-06

@jax.custom_vjp
def low(v):
    return lax.optimization_barrier(v.astype(jnp.bfloat16)).astype(jnp.float32)

@jax.custom_vjp
def low_back(v):
    return v

def low_keep(v):
    return (low(v), None)

def low_pass(kept, grad):
    return (grad,)

def back_keep(v):
    return (v, None)

def back_low(kept, grad):
    return (low(grad),)
low.defvjp(low_keep, low_pass)
low_back.defvjp(back_keep, back_low)

def matmul(left, right):
    return jnp.dot(left, right, precision=HIGHEST)

def layer_norm(values):
    center = values - lax.optimization_barrier(jnp.mean(values, axis=-1, keepdims=True))
    spread = lax.optimization_barrier(jnp.mean(center * center, axis=-1, keepdims=True))
    return center * lax.rsqrt(spread + EPSILON)

def modulate(values, shift, scale):
    return layer_norm(values) * (1.0 + scale) + shift

def rms_scale(values, gain):
    return values * lax.rsqrt(lax.optimization_barrier(jnp.mean(values * values, axis=-1, keepdims=True)) + EPSILON) * gain

def gelu_tanh(values):
    return jax.nn.gelu(values, approximate=True)

def rotary_tables(positions, head_width):
    pairs = head_width // 2
    third = pairs // 3
    first = pairs - 2 * third
    freq_frame = jnp.power(10000.0, -jnp.arange(first, dtype=jnp.float32) / first)
    freq_side = jnp.power(10000.0, -jnp.arange(third, dtype=jnp.float32) / third)
    places = positions.astype(jnp.float32)
    angles = jnp.concatenate([places[0][:, None] * freq_frame[None, :], places[1][:, None] * freq_side[None, :], places[2][:, None] * freq_side[None, :]], axis=1)
    return (jnp.cos(angles), jnp.sin(angles))

def rotate(values, cosine, sine):
    shape = values.shape
    paired = values.reshape(shape[0], shape[1], shape[2] // 2, 2)
    real_part = paired[..., 0]
    imag_part = paired[..., 1]
    cos_row = cosine[:, None, :]
    sin_row = sine[:, None, :]
    turned = jnp.stack([real_part * cos_row - imag_part * sin_row, real_part * sin_row + imag_part * cos_row], axis=-1)
    return turned.reshape(shape)

def attend(queries, keys, values):
    rows = queries.shape[0]
    block = min(512, rows)
    scale = HEAD_DIM ** (-0.5)

    def one_block(query_block):
        scores = low_back(jnp.einsum('qhd,khd->hqk', query_block, keys, precision=HIGHEST) * scale)
        top = lax.optimization_barrier(jnp.max(scores, axis=-1, keepdims=True))
        expo = jnp.exp(scores - top)
        probs = expo / lax.optimization_barrier(jnp.sum(expo, axis=-1, keepdims=True))
        return jnp.einsum('hqk,khd->qhd', low(probs), values, precision=HIGHEST)
    blocks = queries.reshape(rows // block, block, queries.shape[1], queries.shape[2])
    result = lax.map(jax.checkpoint(one_block), blocks)
    return result.reshape(queries.shape)

def block_forward(params, hidden, text, time_rows, cosine, sine):
    modulation, query_weight, key_weight, value_weight, out_weight, cross_query, cross_key, cross_value, cross_out, up_weight, down_weight, qk_gain, norm_gain = params
    mixing = modulation + time_rows
    length = hidden.shape[0]
    text_rows = text.shape[0]
    gains = qk_gain.reshape(HEADS, 4, HEAD_DIM)
    gain_parts = [gains[:, index].reshape(D) for index in range(4)]
    self_input = low(modulate(hidden, mixing[0], mixing[1]))
    query_raw = low_back(matmul(self_input, query_weight))
    key_raw = low_back(matmul(self_input, key_weight))
    value_low = low_back(low(matmul(self_input, value_weight)))
    query_rot = low(rotate(rms_scale(query_raw, gain_parts[0]).reshape(length, HEADS, HEAD_DIM), cosine, sine))
    key_rot = low(rotate(rms_scale(key_raw, gain_parts[1]).reshape(length, HEADS, HEAD_DIM), cosine, sine))
    self_heads = attend(query_rot, key_rot, value_low.reshape(length, HEADS, HEAD_DIM))
    self_attended = low_back(low(self_heads.reshape(length, D)))
    self_branch = low_back(matmul(self_attended, out_weight))
    resid_self = hidden + self_branch * mixing[2]
    cross_input = low(layer_norm(resid_self) * norm_gain)
    cross_query_raw = low_back(matmul(cross_input, cross_query))
    cross_key_raw = low_back(matmul(text, cross_key))
    cross_value_low = low_back(low(matmul(text, cross_value)))
    cross_query_norm = low(rms_scale(cross_query_raw, gain_parts[2]).reshape(length, HEADS, HEAD_DIM))
    cross_key_norm = low(rms_scale(cross_key_raw, gain_parts[3]).reshape(text_rows, HEADS, HEAD_DIM))
    cross_heads = attend(cross_query_norm, cross_key_norm, cross_value_low.reshape(text_rows, HEADS, HEAD_DIM))
    cross_attended = low_back(low(cross_heads.reshape(length, D)))
    cross_branch = low_back(matmul(cross_attended, cross_out))
    resid_cross = resid_self + cross_branch
    feed_input = low(modulate(resid_cross, mixing[3], mixing[4]))
    up_raw = low_back(matmul(feed_input, up_weight))
    activated = low(gelu_tanh(up_raw))
    feed_branch = low_back(matmul(activated, down_weight))
    return resid_cross + feed_branch * mixing[5]

def reference(hidden_in, text_states, time_embed, positions, modulation, query_weight, key_weight, value_weight, out_weight, cross_query, cross_key, cross_value, cross_out, up_weight, down_weight, qk_gain, norm_gain, cotangent):
    params = tuple((item.astype(jnp.float32) for item in (modulation, query_weight, key_weight, value_weight, out_weight, cross_query, cross_key, cross_value, cross_out, up_weight, down_weight, qk_gain, norm_gain)))
    hidden_clips = hidden_in.reshape(CLIPS, LEN, D)
    text_clips = text_states.astype(jnp.float32).reshape(CLIPS, TEXT, TEXT_DIM)
    place_clips = positions.reshape(3, CLIPS, LEN).transpose(1, 0, 2)
    grad_clips = cotangent.reshape(CLIPS, LEN, D)

    def one_clip(total, item):
        hidden, text, time_rows, places, grad_rows = item
        cosine, sine = rotary_tables(places, HEAD_DIM)

        def forward(weights, hidden_arg, text_arg, time_arg):
            return block_forward(weights, hidden_arg, text_arg, time_arg, cosine, sine)
        result, pull = jax.vjp(forward, params, hidden, text, time_rows)
        grad_params, grad_hidden, grad_text, grad_time = pull(grad_rows)
        total = jax.tree.map(lambda left, right: left + right, total, grad_params)
        return (total, (result, grad_hidden, grad_text, grad_time))
    zeros = jax.tree.map(jnp.zeros_like, params)
    total, (results, grad_hidden, grad_text, grad_time) = lax.scan(one_clip, zeros, (hidden_clips, text_clips, time_embed, place_clips, grad_clips))
    return (results.reshape(TOKENS, D), grad_hidden.reshape(TOKENS, D), grad_text.reshape(CLIPS * TEXT, TEXT_DIM), grad_time, total[0], total[1], total[2], total[3], total[4], total[5], total[6], total[7], total[8], total[9], total[10], total[11], total[12])
```

```python
import functools

import jax
import jax.numpy as jnp
from jax import lax
from jax.experimental import pallas as pl
from jax.experimental.pallas import tpu as pltpu
from jax.sharding import PartitionSpec as P

MESH = pl.DeviceIdType.MESH
VMEM_BYTES = 60 * 2**20

HEAD_DIM = 128
D = 1536


EPSILON = 1e-06
CONTRACT_LAST = (((1,), (1,)), ((), ()))
CONTRACT_FIRST = (((0,), (0,)), ((), ()))


def layer_norm(values):
    center = values - jnp.mean(values, axis=-1, keepdims=True)
    spread = jnp.mean(center * center, axis=-1, keepdims=True)
    return center * lax.rsqrt(spread + EPSILON)


def modulate(values, shift, scale):
    return layer_norm(values) * (1.0 + scale) + shift


def gained_norm(values, weight):
    return layer_norm(values) * weight


def scaled(values, total, gain):
    return values * lax.rsqrt(total[:, None] / D + EPSILON) * gain


def gelu_tanh(values):
    return jax.nn.gelu(values, approximate=True)


def rotary_tables(positions, head_width):
    pairs = head_width // 2
    third = pairs // 3
    first = pairs - 2 * third
    freq_frame = jnp.power(10000.0, -jnp.arange(first, dtype=jnp.float32) / first)
    freq_side = jnp.power(10000.0, -jnp.arange(third, dtype=jnp.float32) / third)
    places = positions.astype(jnp.float32)
    angles = jnp.concatenate(
        [
            places[0][:, None] * freq_frame[None, :],
            places[1][:, None] * freq_side[None, :],
            places[2][:, None] * freq_side[None, :],
        ],
        axis=1,
    )
    return (jnp.cos(angles), jnp.sin(angles))


def rotate(values, cosine, sine):
    shape = values.shape
    paired = values.reshape(shape[0], shape[1], shape[2] // 2, 2)
    real_part = paired[..., 0]
    imag_part = paired[..., 1]
    cos_row = cosine[:, None, :]
    sin_row = sine[:, None, :]
    turned = jnp.stack(
        [real_part * cos_row - imag_part * sin_row, real_part * sin_row + imag_part * cos_row],
        axis=-1,
    )
    return turned.reshape(shape)


def product_back(grads, weight):
    return lax.dot_general(grads, weight, CONTRACT_LAST, preferred_element_type=jnp.float32)


def weight_grad(inputs, grads):
    return lax.dot_general(inputs, grads, CONTRACT_FIRST, preferred_element_type=jnp.float32)


def attend_forward(queries, keys, values):
    rows, heads, width = queries.shape
    block = min(512, rows)
    scale = width ** (-0.5)

    def one_block(query_block):
        scores = (
            jnp.einsum("qhd,khd->hqk", query_block, keys, preferred_element_type=jnp.float32)
            * scale
        )
        top = jnp.max(scores, axis=-1, keepdims=True)
        expo = jnp.exp(scores - top)
        summed = jnp.sum(expo, axis=-1, keepdims=True)
        probs = expo / summed
        result = jnp.einsum(
            "hqk,khd->qhd", probs.astype(jnp.bfloat16), values, preferred_element_type=jnp.float32
        )
        return (result, top[..., 0] + jnp.log(summed[..., 0]))

    result, logsum = lax.map(one_block, queries.reshape(rows // block, block, heads, width))
    return (result.reshape(rows, heads, width), logsum)


def attend_backward(queries, keys, values, logsum, grad_out):
    rows, heads, width = queries.shape
    block = min(512, rows)
    count = rows // block
    scale = width ** (-0.5)

    def one_block(carry, item):
        key_grad, value_grad = carry
        query_block, grad_block, logsum_block = item
        scores = (
            jnp.einsum("qhd,khd->hqk", query_block, keys, preferred_element_type=jnp.float32)
            * scale
        )
        probs = jnp.exp(scores - logsum_block[..., None])
        prob_grad = jnp.einsum(
            "qhd,khd->hqk", grad_block, values, preferred_element_type=jnp.float32
        )
        inner = jnp.sum(prob_grad * probs, axis=-1, keepdims=True)
        score_grad = (probs * (prob_grad - inner)).astype(jnp.bfloat16)
        query_grad = (
            jnp.einsum("hqk,khd->qhd", score_grad, keys, preferred_element_type=jnp.float32) * scale
        )
        key_grad = (
            key_grad
            + jnp.einsum(
                "hqk,qhd->khd", score_grad, query_block, preferred_element_type=jnp.float32
            )
            * scale
        )
        value_grad = value_grad + jnp.einsum(
            "hqk,qhd->khd",
            probs.astype(jnp.bfloat16),
            grad_block,
            preferred_element_type=jnp.float32,
        )
        return ((key_grad, value_grad), query_grad)

    start_carry = (jnp.zeros(keys.shape, jnp.float32), jnp.zeros(values.shape, jnp.float32))
    items = (
        queries.reshape(count, block, heads, width),
        grad_out.reshape(count, block, heads, width),
        logsum,
    )
    (key_grad, value_grad), query_grad = lax.scan(one_block, start_carry, items)
    return (query_grad.reshape(rows, heads, width), key_grad, value_grad)


def when(cond, run):
    if cond is None:
        run()
    else:
        pl.when(cond)(run)


def flip(index, bit):
    return index + bit - 2 * bit * (index // bit % 2)


def normed(values):
    center = values - jnp.mean(values, axis=-1, keepdims=True)
    inverse = lax.rsqrt(jnp.mean(center * center, axis=-1, keepdims=True) + EPSILON)
    return center * inverse, inverse


def normed_back(unit, inverse, grad):
    mean_grad = jnp.mean(grad, axis=-1, keepdims=True)
    mean_dot = jnp.mean(grad * unit, axis=-1, keepdims=True)
    return (grad - mean_grad - unit * mean_dot) * inverse


class Links:
    def __init__(self, send, recv, local, dp_size, tensor_size):
        self.send, self.recv, self.local = send, recv, local
        self.count = 0
        self.local_count = 0
        self.dp_size, self.size = dp_size, tensor_size
        self.dp = lax.axis_index("dp")
        self.z = lax.axis_index("tensor")

    def slot(self):
        self.count += 1
        return self.count - 1

    def copy(self, source, target, device, slot):
        return pltpu.make_async_remote_copy(
            src_ref=source,
            dst_ref=target,
            send_sem=self.send.at[slot],
            recv_sem=self.recv.at[slot],
            device_id=device,
            device_id_type=MESH,
        )

    def here(self, source, target):
        self.local_count += 1
        return pltpu.make_async_copy(source, target, self.local.at[self.local_count - 1])

    def greet(self, groups):
        barrier = pltpu.get_barrier_semaphore()
        peers = []
        if "line" in groups:
            peers += [
                ((self.dp, self.z - 1), self.z > 0),
                ((self.dp, self.z + 1), self.z < self.size - 1),
            ]
        if "zall" in groups:
            peers += [
                ((self.dp, lax.rem(self.z + k, self.size)), None) for k in range(1, self.size)
            ]
        if "dpall" in groups:
            peers += [
                ((lax.rem(self.dp + k, self.dp_size), self.z), None)
                for k in range(1, self.dp_size)
            ]
        if "bits" in groups:
            bit = 1
            while bit < self.dp_size:
                peers.append(((flip(self.dp, bit), self.z), None))
                bit *= 2
        if "diag" in groups:
            peers.append(((flip(flip(self.dp, 2), 4), self.z), None))
        for device, cond in peers:
            when(
                cond,
                lambda device=device: pl.semaphore_signal(
                    barrier, inc=1, device_id=device, device_id_type=MESH
                ),
            )
        expected = sum(1 for _, cond in peers if cond is None)
        for _, cond in peers:
            if cond is not None:
                expected = expected + cond.astype(jnp.int32)
        pl.semaphore_wait(barrier, expected)


def piece_of(ref, block, rows, start, count):
    return ref.at[pl.ds(pl.multiple_of(block * rows + start, 16), count)]


class LineGather:
    def __init__(self, links, whole, rows, pieces):
        self.links, self.whole, self.rows, self.count = links, whole, rows, rows // pieces
        self.pieces = pieces
        hops = links.size - 1
        self.right = [[links.slot() for _ in range(pieces)] for _ in range(hops)]
        self.left = [[links.slot() for _ in range(pieces)] for _ in range(hops)]

    def block(self, index, piece):
        return piece_of(self.whole, index, self.rows, piece * self.count, self.count)

    def move(self, index, piece, way, slot):
        part = self.block(index, piece)
        return self.links.copy(part, part, (self.links.dp, self.links.z + way), slot)

    def start(self, piece):
        z, last = self.links.z, self.links.size - 1
        when(z < last, lambda: self.move(z, piece, 1, self.right[0][piece]).start())
        when(z > 0, lambda: self.move(z, piece, -1, self.left[0][piece]).start())

    def step(self, hop, piece):
        z, last = self.links.z, self.links.size - 1

        def from_left():
            self.move(z - 1 - hop, piece, -1, self.right[hop][piece]).wait_recv()
            if hop + 1 < last:
                when(
                    z < last,
                    lambda: self.move(z - 1 - hop, piece, 1, self.right[hop + 1][piece]).start(),
                )

        def from_right():
            self.move(z + 1 + hop, piece, 1, self.left[hop][piece]).wait_recv()
            if hop + 1 < last:
                when(
                    z > 0,
                    lambda: self.move(z + 1 + hop, piece, -1, self.left[hop + 1][piece]).start(),
                )

        when(z - 1 - hop >= 0, from_left)
        when(z + 1 + hop <= last, from_right)

    def steps(self, piece):
        for hop in range(self.links.size - 1):
            self.step(hop, piece)

    def finish(self):
        z, last = self.links.z, self.links.size - 1
        for hop in range(last):
            for piece in range(self.pieces):
                when(
                    (z - hop >= 0) & (z < last),
                    lambda: self.move(z - hop, piece, 1, self.right[hop][piece]).wait_send(),
                )
                when(
                    (z + hop <= last) & (z > 0),
                    lambda: self.move(z + hop, piece, -1, self.left[hop][piece]).wait_send(),
                )


class LineReduce:
    def __init__(self, links, partial, land_right, land_left, rows, pieces):
        self.links, self.partial, self.rows, self.count = links, partial, rows, rows // pieces
        self.land = {1: land_right, -1: land_left}
        self.pieces = pieces
        last = links.size - 1
        self.slots = {
            way: [None] + [[links.slot() for _ in range(pieces)] for _ in range(last)]
            for way in (1, -1)
        }

    def landing(self, way, distance, piece):
        return self.land[way].at[distance - 1, pl.ds(piece * self.count, self.count)]

    def part(self, index, piece):
        return piece_of(self.partial, index, self.rows, piece * self.count, self.count)

    def move(self, source, way, distance, piece):
        return self.links.copy(
            source,
            self.landing(way, distance, piece),
            (self.links.dp, self.links.z + way),
            self.slots[way][distance][piece],
        )

    def arrived(self, way, distance, piece):
        self.links.copy(
            self.landing(way, distance, piece),
            self.landing(way, distance, piece),
            (self.links.dp, self.links.z - way),
            self.slots[way][distance][piece],
        ).wait_recv()

    def first(self, piece):
        z, last = self.links.z, self.links.size - 1

        def from_first():
            for distance in range(last, 0, -1):
                self.move(self.part(distance, piece), 1, distance, piece).start()

        def from_last():
            for distance in range(last, 0, -1):
                self.move(self.part(last - distance, piece), -1, distance, piece).start()

        when(z == 0, from_first)
        when(z == last, from_last)

    def clear(self):
        z, last = self.links.z, self.links.size - 1

        def zero(way):
            self.land[way][0] = jnp.zeros(self.land[way].shape[1:], self.land[way].dtype)

        when(z == 0, lambda: zero(1))
        when(z == last, lambda: zero(-1))

    def step(self, piece):
        z, last = self.links.z, self.links.size - 1
        for distance in range(last - 1, 0, -1):
            for way in (1, -1):
                inside = (
                    (z > 0) & (z + distance <= last)
                    if way == 1
                    else (z < last) & (z - distance >= 0)
                )

                def go(way=way, distance=distance):
                    self.arrived(way, distance + 1, piece)
                    held = self.landing(way, distance + 1, piece)
                    own = self.part(z + way * distance, piece)
                    held[...] = (
                        held[...].astype(jnp.float32) + own[...].astype(jnp.float32)
                    ).astype(held.dtype)
                    self.move(held, way, distance, piece).start()

                when(inside, go)

    def total(self, piece):
        z, last = self.links.z, self.links.size - 1
        when(z > 0, lambda: self.arrived(1, 1, piece))
        when(z < last, lambda: self.arrived(-1, 1, piece))
        return (
            self.part(z, piece)[...].astype(jnp.float32)
            + self.landing(1, 1, piece)[...].astype(jnp.float32)
            + self.landing(-1, 1, piece)[...].astype(jnp.float32)
        )

    def finish(self):
        z, last = self.links.z, self.links.size - 1
        for distance in range(1, last + 1):
            for piece in range(self.pieces):
                held = self.landing(1, distance, piece)
                when(
                    z + distance <= last,
                    lambda: self.move(held, 1, distance, piece).wait_send(),
                )
                back = self.landing(-1, distance, piece)
                when(
                    z - distance >= 0,
                    lambda: self.move(back, -1, distance, piece).wait_send(),
                )


class CubeGather:
    def __init__(self, links, shard, whole):
        self.links, self.shard, self.whole = links, shard, whole
        self.rows = shard.shape[0]
        self.slots = [links.slot() for _ in range(8)]
        dp = links.dp
        self.core, self.side, self.over = flip(dp, 1), flip(dp, 2), flip(dp, 4)
        self.far = flip(flip(dp, 2), 4)
        self.sent = []

    def block(self, index, start=0, count=None):
        return piece_of(self.whole, index, self.rows, start, count or self.rows)

    def send(self, source, target, device, slot):
        move = self.links.copy(source, target, (device, self.links.z), self.slots[slot])
        move.start()
        self.sent.append(move)

    def got(self, part, slot):
        self.links.copy(part, part, (self.core, self.links.z), self.slots[slot]).wait_recv()

    def start(self):
        mine = self.block(self.links.dp)
        self.own = self.links.here(self.shard, mine)
        self.own.start()
        self.send(self.shard, mine, self.side, 1)
        self.send(self.shard, mine, self.over, 2)
        self.send(self.shard, mine, self.core, 0)

    def forward(self):
        half = self.rows // 2
        self.got(self.block(self.side), 1)
        part = self.block(self.side, 0, half)
        self.send(part, part, self.over, 3)
        part = self.block(self.side)
        self.send(part, part, self.core, 5)
        self.got(self.block(self.over), 2)
        part = self.block(self.over, half, half)
        self.send(part, part, self.side, 4)
        part = self.block(self.over)
        self.send(part, part, self.core, 6)

    def tail(self):
        half = self.rows // 2
        self.got(self.block(self.far, 0, half), 3)
        self.got(self.block(self.far, half, half), 4)
        part = self.block(self.far)
        self.send(part, part, self.core, 7)

    def finish(self):
        self.got(self.block(self.core), 0)
        self.got(self.block(flip(self.core, 2)), 5)
        self.got(self.block(flip(self.core, 4)), 6)
        self.got(self.block(flip(flip(self.core, 2), 4)), 7)
        for move in self.sent:
            move.wait_send()
        self.own.wait()


class CubeReduce:
    def __init__(self, links, grads, out, own, near, others):
        self.links, self.grads, self.out = links, grads, out
        self.own, self.near, self.others = own, near, others
        self.rows = out.shape[0]
        self.core_slots = [links.slot() for _ in range(4)]
        self.chip_slots = [links.slot() for _ in range(3)]
        self.core = links.dp % 2
        self.chip = links.dp // 2
        self.sent = []

    def block(self, chip, core):
        return piece_of(self.grads, 2 * chip + core, self.rows, 0, self.rows)

    def chips(self):
        return [flip(self.chip, 1), flip(self.chip, 2), flip(flip(self.chip, 1), 2)]

    def start(self):
        links = self.links
        self.copies = []
        for chip in range(4):
            local = links.here(self.block(chip, self.core), self.own.at[chip])
            local.start()
            move = links.copy(
                self.block(chip, 1 - self.core),
                self.near.at[chip],
                (flip(links.dp, 1), links.z),
                self.core_slots[chip],
            )
            move.start()
            self.copies.append((local, move))

    def middle(self):
        links = self.links
        for local, move in self.copies:
            local.wait()
            move.wait_recv()

        def add(step, _):
            rows = pl.ds(pl.multiple_of(step * 16, 16), 16)
            for chip in range(4):
                self.near[chip, rows, :] = (
                    self.near[chip, rows, :].astype(jnp.float32)
                    + self.own[chip, rows, :].astype(jnp.float32)
                ).astype(jnp.bfloat16)
            return 0

        lax.fori_loop(0, self.rows // 16, add, 0)
        for index, chip in enumerate(self.chips()):
            move = links.copy(
                self.near.at[chip],
                self.others.at[index],
                (2 * chip + self.core, links.z),
                self.chip_slots[index],
            )
            move.start()
            self.sent.append(move)

    def finish(self):
        for move in self.sent:
            move.wait_recv()

        def add(step, _):
            rows = pl.ds(pl.multiple_of(step * 16, 16), 16)
            self.out[rows, :] = (
                self.near[self.chip, rows, :].astype(jnp.float32)
                + self.others[0, rows, :].astype(jnp.float32)
                + self.others[1, rows, :].astype(jnp.float32)
                + self.others[2, rows, :].astype(jnp.float32)
            )
            return 0

        lax.fori_loop(0, self.rows // 16, add, 0)
        for move in self.sent:
            move.wait_send()
        for _, move in self.copies:
            move.wait_send()


def cube_scratch(shapes):
    parts = []
    for rows, columns in shapes:
        parts += [
            pltpu.VMEM((4, rows, columns), jnp.bfloat16),
            pltpu.VMEM((4, rows, columns), jnp.bfloat16),
            pltpu.VMEM((3, rows, columns), jnp.bfloat16),
        ]
    return parts


class Plan:
    def __init__(self, mesh):
        self.dp = mesh.shape["dp"]
        self.tensor = mesh.shape["tensor"]
        self.cube = self.dp == 8
        self.calls = 0

    def call(self, name, body, inputs, outputs, scratch, copies):
        self.calls += 1
        spaces = {True: pltpu.VMEM, False: pltpu.HBM}
        count_in, count_out = len(inputs), len(outputs)

        def kernel(*refs):
            ins = refs[:count_in]
            outs = refs[count_in : count_in + count_out]
            rest = refs[count_in + count_out :]
            links = Links(rest[0], rest[1], rest[2], self.dp, self.tensor)
            body(links, ins, outs, rest[3:])

        return pl.pallas_call(
            kernel,
            name=name,
            out_shape=[jax.ShapeDtypeStruct(shape, kind) for shape, kind, _ in outputs],
            in_specs=[pl.BlockSpec(memory_space=spaces[near]) for _, near in inputs],
            out_specs=[pl.BlockSpec(memory_space=spaces[near]) for _, _, near in outputs],
            scratch_shapes=[
                pltpu.SemaphoreType.DMA((copies,)),
                pltpu.SemaphoreType.DMA((copies,)),
                pltpu.SemaphoreType.DMA((64,)),
                *scratch,
            ],
            compiler_params=pltpu.CompilerParams(
                collective_id=self.calls, has_side_effects=True, vmem_limit_bytes=VMEM_BYTES
            ),
        )(*[array for array, _ in inputs])

    def gather_outputs(self, shards):
        return [
            ((self.dp * shard.shape[0], shard.shape[1]), shard.dtype, False) for shard in shards
        ]

    def open(self, hidden, time_rows, small, shards):
        rows, width = hidden.shape
        part = width // self.dp
        gain_part = small.shape[1] - part
        moving = shards if self.cube else []

        def body(links, ins, outs, scratch):
            hidden_ref, time_ref, small_ref = ins[:3]
            table_ref, gain_ref, whole_ref = outs[:3]
            (land,) = scratch
            links.greet({"line", "dpall"})
            gathers = [CubeGather(links, a, b) for a, b in zip(ins[3:], outs[3:])]
            dp, z = links.dp, links.z
            moves = []
            for step in range(1, self.dp):
                target = lax.rem(dp + step, self.dp)
                move = links.copy(small_ref, land.at[dp], (target, z), links.slot())
                move.start()
                moves.append(move)
            for item in gathers:
                item.start()
            land[dp] = small_ref[...]
            unit, _ = normed(hidden_ref[...])
            for move in moves:
                move.wait_recv()
            table = jnp.concatenate([land[k][:, :part] for k in range(self.dp)], axis=1)
            gain_ref[...] = jnp.concatenate([land[k][:, part:] for k in range(self.dp)], axis=1)
            table = table + time_ref[...]
            table_ref[...] = table
            line = LineGather(links, whole_ref, rows, 4)
            first = unit * (1.0 + table[1:2]) + table[0:1]
            whole_ref[pl.ds(pl.multiple_of(z * rows, 16), rows), :] = first.astype(jnp.bfloat16)
            for piece in range(4):
                line.start(piece)
            for piece in range(4):
                line.steps(piece)
                if piece < len(gathers):
                    gathers[piece].forward()
            for item in gathers[4:]:
                item.forward()
            for item in gathers:
                item.tail()
            for item in gathers:
                item.finish()
            line.finish()
            for move in moves:
                move.wait_send()

        results = self.call(
            "open",
            body,
            [(hidden, True), (time_rows, True), (small, True)] + [(s, False) for s in moving],
            [
                ((8, width), jnp.float32, True),
                ((8, gain_part * self.dp), jnp.float32, True),
                ((rows * self.tensor, width), jnp.bfloat16, True),
            ]
            + self.gather_outputs(moving),
            [pltpu.VMEM((self.dp, 8, small.shape[1]), jnp.float32)],
            160,
        )
        return results[:3], self.gathered(results[3:], shards)

    def gathered(self, moved, shards):
        if self.cube:
            return list(moved)
        return [lax.all_gather(shard, "dp", axis=0, tiled=True) for shard in shards]

    def reduced(self, moved, grads):
        if self.cube:
            return list(moved)
        return [
            lax.psum_scatter(grad, "dp", scatter_dimension=0, tiled=True).astype(jnp.float32)
            for grad in grads
        ]

    def between(self, name, partial, near, kinds, post, gather, shards=(), grads=(), extra=None):
        width = partial.shape[1]
        rows = partial.shape[0] // self.tensor
        pieces = 4
        shards, grads = list(shards), list(grads)
        moving = shards if self.cube else []
        summing = grads if self.cube else []
        count_near, count_kinds = len(near), len(kinds)
        lands = 2 if extra is None else 4
        sums = [(g.shape[0] // self.dp, g.shape[1]) for g in summing]

        def body(links, ins, outs, scratch):
            partial_ref = ins[0]
            ins = ins[1:]
            if extra is not None:
                second_ref = ins[0]
                ins = ins[1:]
            near_refs = ins[:count_near]
            shard_refs = ins[count_near : count_near + len(moving)]
            grad_refs = ins[count_near + len(moving) :]
            kind_refs = outs[:count_kinds]
            outs = outs[count_kinds:]
            if gather:
                whole_ref = outs[0]
                outs = outs[1:]
            full_refs = outs[: len(moving)]
            sum_refs = outs[len(moving) :]
            groups = {"line"}
            if moving or summing:
                groups |= {"bits"}
            if summing:
                groups |= {"diag"}
            links.greet(groups)
            reduce = LineReduce(links, partial_ref, scratch[0], scratch[1], rows, pieces)
            later = (
                LineReduce(links, second_ref, scratch[2], scratch[3], rows, pieces)
                if extra is not None
                else None
            )
            line = LineGather(links, whole_ref, rows, pieces) if gather else None
            gathers = [CubeGather(links, a, b) for a, b in zip(shard_refs, full_refs)]
            reduces = [
                CubeReduce(links, g, o, *scratch[lands + 3 * k : lands + 3 * k + 3])
                for k, (g, o) in enumerate(zip(grad_refs, sum_refs))
            ]
            for piece in range(pieces):
                reduce.first(piece)
            for item in reduces:
                item.start()
            for item in gathers:
                item.start()
            reduce.clear()
            if later is not None:
                later.clear()
            for piece in range(pieces):
                reduce.step(piece)
                where = pl.ds(piece * (rows // pieces), rows // pieces)
                result = post(reduce.total(piece), where, near_refs, kind_refs, piece == 0)
                if gather:
                    line.block(links.z, piece)[...] = result
                    line.start(piece)
                    if piece > 0:
                        line.steps(piece - 1)
                if later is not None:
                    later.first(piece)
                if piece == 0:
                    for item in reduces:
                        item.middle()
                if piece == 2:
                    for item in gathers:
                        item.forward()
            if gather:
                line.steps(pieces - 1)
            if later is not None:
                for piece in range(pieces):
                    later.step(piece)
                    where = pl.ds(piece * (rows // pieces), rows // pieces)
                    extra[1](later.total(piece), where, near_refs, kind_refs, piece == 0)
            for item in gathers:
                item.tail()
            for item in gathers:
                item.finish()
            for item in reduces:
                item.finish()
            reduce.finish()
            if later is not None:
                later.finish()
            if gather:
                line.finish()

        inputs = [(partial, True)]
        if extra is not None:
            inputs.append((extra[0], True))
        inputs += [(item, True) for item in near]
        inputs += [(item, False) for item in moving + summing]
        outputs = [(shape, jnp.float32, True) for shape in kinds]
        if gather:
            outputs.append((partial.shape, jnp.bfloat16, True))
        outputs += self.gather_outputs(moving)
        outputs += [(shape, jnp.float32, True) for shape in sums]
        results = self.call(
            name,
            body,
            inputs,
            outputs,
            [pltpu.VMEM((self.tensor - 1, rows, width), jnp.bfloat16) for _ in range(lands)]
            + cube_scratch(sums),
            200,
        )
        kept = count_kinds + (1 if gather else 0)
        full = self.gathered(results[kept : kept + len(moving)], shards)
        summed = self.reduced(results[kept + len(moving) :], grads)
        return results[:kept], full, summed

    def line_sum(self, name, values):
        def body(links, ins, outs, scratch):
            (land,) = scratch
            links.greet({"zall"})
            moves = []
            for step in range(1, self.tensor):
                target = lax.rem(links.z + step, self.tensor)
                move = links.copy(ins[0], land.at[step - 1], (links.dp, target), links.slot())
                move.start()
                moves.append(move)
            total = ins[0][...]
            for step, move in enumerate(moves):
                move.wait_recv()
                total = total + land[step]
            outs[0][...] = total
            for move in moves:
                move.wait_send()

        return self.call(
            name,
            body,
            [(values, True)],
            [(values.shape, jnp.float32, True)],
            [pltpu.VMEM((self.tensor - 1, *values.shape), jnp.float32)],
            8,
        )[0]

    def close(self, time_part, gain_part, grads):
        grads = list(grads)
        summing = grads if self.cube else []
        sums = [(g.shape[0] // self.dp, g.shape[1]) for g in summing]
        bits = [1 << k for k in range(self.dp.bit_length() - 1)]

        def body(links, ins, outs, scratch):
            time_ref, gain_ref = ins[:2]
            total_ref, all_ref, gains_ref = outs[:3]
            land, held, held_gain, come, come_gain = scratch[:5]
            links.greet({"zall", "bits", "diag"} if self.cube else {"zall", "bits"})
            reduces = [
                CubeReduce(links, g, o, *scratch[5 + 3 * k : 8 + 3 * k])
                for k, (g, o) in enumerate(zip(ins[2:], outs[3:]))
            ]
            moves = []
            for step in range(1, self.tensor):
                target = lax.rem(links.z + step, self.tensor)
                move = links.copy(time_ref, land.at[links.z], (links.dp, target), links.slot())
                move.start()
                moves.append(move)
            for item in reduces:
                item.start()
            land[links.z] = time_ref[...]
            held_gain[0] = gain_ref[...]
            for move in moves:
                move.wait_recv()
            total = land[0]
            for index in range(1, self.tensor):
                total = total + land[index]
            total_ref[...] = total
            held[0] = total
            for index, bit in enumerate(bits):
                target = (flip(links.dp, bit), links.z)
                one = links.copy(held.at[index], come.at[index], target, links.slot())
                two = links.copy(held_gain.at[index], come_gain.at[index], target, links.slot())
                one.start()
                two.start()
                if index == 0:
                    for item in reduces:
                        item.middle()
                one.wait_recv()
                two.wait_recv()
                held[index + 1] = held[index] + come[index]
                held_gain[index + 1] = held_gain[index] + come_gain[index]
                moves += [one, two]
            all_ref[...] = held[len(bits)]
            gains_ref[...] = held_gain[len(bits)]
            for item in reduces:
                item.finish()
            for move in moves:
                move.wait_send()

        levels = len(bits)
        results = self.call(
            "close",
            body,
            [(time_part, True), (gain_part, True)] + [(g, False) for g in summing],
            [
                (time_part.shape, jnp.float32, True),
                (time_part.shape, jnp.float32, True),
                (gain_part.shape, jnp.float32, True),
            ]
            + [(shape, jnp.float32, True) for shape in sums],
            [
                pltpu.VMEM((self.tensor, *time_part.shape), jnp.float32),
                pltpu.VMEM((levels + 1, *time_part.shape), jnp.float32),
                pltpu.VMEM((levels + 1, *gain_part.shape), jnp.float32),
                pltpu.VMEM((levels, *time_part.shape), jnp.float32),
                pltpu.VMEM((levels, *gain_part.shape), jnp.float32),
            ]
            + cube_scratch(sums),
            80,
        )
        return results[:3], self.reduced(results[3:], grads)


def summed_back(pairs):
    result = 0.0
    for grads, weight in pairs:
        result = result + product_back(grads, weight)
    return result


def norm_pull(shaping, raw, total, gain, grad):
    _, pull = jax.vjp(shaping, raw, total, gain)
    return pull(grad)


def body(
    plan,
    hidden_in,
    text_states,
    time_embed,
    positions,
    modulation,
    query_weight,
    key_weight,
    value_weight,
    out_weight,
    cross_query,
    cross_key,
    cross_value,
    cross_out,
    up_weight,
    down_weight,
    qk_gain,
    norm_gain,
    cotangent,
):
    plan.calls = 0
    low = jnp.bfloat16
    rows, width = hidden_in.shape
    length = rows * plan.tensor
    heads_here = out_weight.shape[0] // HEAD_DIM
    text_all = lax.all_gather(text_states, "tensor", axis=0, tiled=True)

    part = width // plan.dp
    top = jnp.concatenate([modulation, norm_gain[None], jnp.zeros((1, part), low)], axis=0)
    side = jnp.pad(qk_gain, ((0, 8 - heads_here), (0, 0)))
    small = jnp.concatenate([top, side], axis=1).astype(jnp.float32)
    time_rows = jnp.pad(time_embed[0], ((0, 2), (0, 0)))
    (mixing, gain_rows, self_whole), full = plan.open(
        hidden_in, time_rows, small, [query_weight, key_weight, value_weight, out_weight.T]
    )
    query_full, key_full, value_full, out_full = full
    gains = gain_rows[:heads_here].reshape(heads_here, 4, HEAD_DIM)
    gain_parts = [gains[:, index].reshape(-1) for index in range(4)]
    cosine, sine = rotary_tables(positions, HEAD_DIM)
    feed_grad_whole = lax.all_gather(
        (cotangent * mixing[5]).astype(low), "tensor", axis=0, tiled=True
    )

    query_raw = jnp.dot(self_whole, query_full, preferred_element_type=jnp.float32)
    key_raw = jnp.dot(self_whole, key_full, preferred_element_type=jnp.float32)
    value_low = (
        jnp.dot(self_whole, value_full, preferred_element_type=jnp.float32)
        .astype(low)
        .reshape(length, heads_here, HEAD_DIM)
    )

    def squares(name, first, second):
        sums = jnp.stack([jnp.sum(first * first, axis=-1), jnp.sum(second * second, axis=-1)])
        total = plan.line_sum(name, jnp.pad(sums, ((0, 6), (0, 0))))
        return total[0], total[1]

    def totals(name, first, second):
        total = plan.line_sum(name, jnp.pad(jnp.stack([first, second]), ((0, 6), (0, 0))))
        return total[0], total[1]

    query_total, key_total = squares("squares_self", query_raw, key_raw)

    def self_shape(raw, total, gain):
        return rotate(scaled(raw, total, gain).reshape(length, heads_here, HEAD_DIM), cosine, sine)

    def cross_shape(raw, total, gain):
        return scaled(raw, total, gain).reshape(raw.shape[0], heads_here, HEAD_DIM)

    query_rot = self_shape(query_raw, query_total, gain_parts[0]).astype(low)
    key_rot = self_shape(key_raw, key_total, gain_parts[1]).astype(low)
    self_heads, self_logsum = attend_forward(query_rot, key_rot, value_low)
    self_attended = self_heads.reshape(length, -1).astype(low)
    self_partial = product_back(self_attended, out_full).astype(low)

    def after_self(total, where, near, kinds, first):
        hidden_ref, mixing_ref = near
        branch_ref, resid_ref = kinds
        branch_ref[where, :] = total
        resid = hidden_ref[where, :] + total * mixing_ref[2:3]
        resid_ref[where, :] = resid
        unit, _ = normed(resid)
        return (unit * mixing_ref[6:7]).astype(low)

    (self_branch, resid_self, cross_whole), full, _ = plan.between(
        "after_self",
        self_partial,
        [hidden_in, mixing],
        [(rows, width), (rows, width)],
        after_self,
        True,
        shards=[cross_key, cross_value, cross_query, cross_out.T],
    )
    cross_key_full, cross_value_full, cross_query_full, cross_out_full = full

    text_rows = text_all.shape[0]
    cross_query_raw = jnp.dot(cross_whole, cross_query_full, preferred_element_type=jnp.float32)
    cross_key_raw = jnp.dot(text_all, cross_key_full, preferred_element_type=jnp.float32)
    cross_value_low = (
        jnp.dot(text_all, cross_value_full, preferred_element_type=jnp.float32)
        .astype(low)
        .reshape(text_rows, heads_here, HEAD_DIM)
    )
    cross_query_total, cross_key_total = squares("squares_cross", cross_query_raw, cross_key_raw)
    cross_query_norm = cross_shape(cross_query_raw, cross_query_total, gain_parts[2]).astype(low)
    cross_key_norm = cross_shape(cross_key_raw, cross_key_total, gain_parts[3]).astype(low)
    cross_heads, cross_logsum = attend_forward(cross_query_norm, cross_key_norm, cross_value_low)
    cross_attended = cross_heads.reshape(length, -1).astype(low)
    cross_partial = product_back(cross_attended, cross_out_full).astype(low)

    def after_cross(total, where, near, kinds, first):
        resid_ref, mixing_ref = near
        resid = resid_ref[where, :] + total
        kinds[0][where, :] = resid
        unit, _ = normed(resid)
        return (unit * (1.0 + mixing_ref[4:5]) + mixing_ref[3:4]).astype(low)

    (resid_cross, feed_whole), full, _ = plan.between(
        "after_cross",
        cross_partial,
        [resid_self, mixing],
        [(rows, width)],
        after_cross,
        True,
        shards=[up_weight, down_weight.T],
    )
    up_full, down_full = full

    up_raw = jnp.dot(feed_whole, up_full, preferred_element_type=jnp.float32)
    activated = gelu_tanh(up_raw).astype(low)
    feed_partial = product_back(activated, down_full).astype(low)
    grad_activated = jnp.dot(feed_grad_whole, down_full, preferred_element_type=jnp.float32)
    grad_down = weight_grad(feed_grad_whole, activated).astype(low)
    _, gelu_pull = jax.vjp(gelu_tanh, up_raw)
    grad_up_raw = gelu_pull(grad_activated)[0].astype(low)
    feed_back = product_back(grad_up_raw, up_full).astype(low)

    def add_sum(ref, row, values, first):
        total = jnp.sum(values, axis=0, keepdims=True)
        ref[row : row + 1, :] = total if first else ref[row : row + 1, :] + total

    def before_feed(total, where, near, kinds, first):
        resid_ref, cotangent_ref, mixing_ref = near
        grad_ref, sums_ref, _ = kinds
        unit, inverse = normed(resid_ref[where, :])
        add_sum(sums_ref, 0, total, first)
        add_sum(sums_ref, 1, total * unit, first)
        grad = cotangent_ref[where, :] + normed_back(
            unit, inverse, total * (1.0 + mixing_ref[4:5])
        )
        grad_ref[where, :] = grad
        return grad.astype(low)

    def after_feed(total, where, near, kinds, first):
        resid_ref, cotangent_ref, mixing_ref = near
        _, sums_ref, out_ref = kinds
        out_ref[where, :] = resid_ref[where, :] + total * mixing_ref[5:6]
        add_sum(sums_ref, 2, cotangent_ref[where, :] * total, first)

    (grad_resid_cross, feed_sums, block_out, cross_grad_whole), _, sums = plan.between(
        "before_feed",
        feed_back,
        [resid_cross, cotangent, mixing],
        [(rows, width), (8, width), (rows, width)],
        before_feed,
        True,
        grads=[grad_down],
        extra=(feed_partial, after_feed),
    )
    (sum_down,) = sums

    grad_up = weight_grad(feed_whole, grad_up_raw).astype(low)
    grad_cross_attended = jnp.dot(
        cross_grad_whole, cross_out_full, preferred_element_type=jnp.float32
    ).astype(low)
    grad_cross_out = weight_grad(cross_grad_whole, cross_attended).astype(low)
    grad_cross_query_norm, grad_cross_key_norm, grad_cross_value_heads = attend_backward(
        cross_query_norm,
        cross_key_norm,
        cross_value_low,
        cross_logsum,
        grad_cross_attended.reshape(length, heads_here, HEAD_DIM),
    )
    query_local, query_part, grad_gain_cross_query = norm_pull(
        cross_shape, cross_query_raw, cross_query_total, gain_parts[2], grad_cross_query_norm
    )
    key_local, key_part, grad_gain_cross_key = norm_pull(
        cross_shape, cross_key_raw, cross_key_total, gain_parts[3], grad_cross_key_norm
    )
    query_whole_part, key_whole_part = totals("parts_cross", query_part, key_part)
    grad_cross_query_raw = (query_local + 2.0 * cross_query_raw * query_whole_part[:, None]).astype(
        low
    )
    grad_cross_key_raw = (key_local + 2.0 * cross_key_raw * key_whole_part[:, None]).astype(low)
    grad_cross_value_low = grad_cross_value_heads.reshape(text_rows, -1).astype(low)
    cross_back = product_back(grad_cross_query_raw, cross_query_full).astype(low)

    def before_cross(total, where, near, kinds, first):
        resid_ref, grad_ref, branch_ref, mixing_ref = near
        out_ref, sums_ref = kinds
        unit, inverse = normed(resid_ref[where, :])
        add_sum(sums_ref, 1, total * unit, first)
        grad = grad_ref[where, :] + normed_back(unit, inverse, total * mixing_ref[6:7])
        out_ref[where, :] = grad
        add_sum(sums_ref, 0, grad * branch_ref[where, :], first)
        return (grad * mixing_ref[2:3]).astype(low)

    (grad_resid_self, cross_sums, self_grad_whole), _, sums = plan.between(
        "before_cross",
        cross_back,
        [resid_self, grad_resid_cross, self_branch, mixing],
        [(rows, width), (8, width)],
        before_cross,
        True,
        grads=[grad_up],
    )
    (sum_up,) = sums
    grad_text = lax.psum_scatter(
        summed_back(
            ((grad_cross_key_raw, cross_key_full), (grad_cross_value_low, cross_value_full))
        ).astype(low),
        "tensor",
        scatter_dimension=0,
        tiled=True,
    ).astype(jnp.float32)
    grad_cross_query = weight_grad(cross_whole, grad_cross_query_raw).astype(low)
    grad_cross_key = weight_grad(text_all, grad_cross_key_raw).astype(low)
    grad_cross_value = weight_grad(text_all, grad_cross_value_low).astype(low)

    grad_self_attended = jnp.dot(
        self_grad_whole, out_full, preferred_element_type=jnp.float32
    ).astype(low)
    grad_out = weight_grad(self_grad_whole, self_attended).astype(low)
    grad_query_rot, grad_key_rot, grad_value_heads = attend_backward(
        query_rot,
        key_rot,
        value_low,
        self_logsum,
        grad_self_attended.reshape(length, heads_here, HEAD_DIM),
    )
    query_local, query_part, grad_gain_query = norm_pull(
        self_shape, query_raw, query_total, gain_parts[0], grad_query_rot
    )
    key_local, key_part, grad_gain_key = norm_pull(
        self_shape, key_raw, key_total, gain_parts[1], grad_key_rot
    )
    query_whole_part, key_whole_part = totals("parts_self", query_part, key_part)
    grad_query_raw = (query_local + 2.0 * query_raw * query_whole_part[:, None]).astype(low)
    grad_key_raw = (key_local + 2.0 * key_raw * key_whole_part[:, None]).astype(low)
    grad_value_low = grad_value_heads.reshape(length, -1).astype(low)
    self_back = summed_back(
        ((grad_query_raw, query_full), (grad_key_raw, key_full), (grad_value_low, value_full))
    ).astype(low)

    def before_self(total, where, near, kinds, first):
        hidden_ref, grad_ref, mixing_ref = near
        out_ref, sums_ref = kinds
        unit, inverse = normed(hidden_ref[where, :])
        add_sum(sums_ref, 0, total, first)
        add_sum(sums_ref, 1, total * unit, first)
        out_ref[where, :] = grad_ref[where, :] + normed_back(
            unit, inverse, total * (1.0 + mixing_ref[1:2])
        )

    (grad_hidden, self_sums), _, sums = plan.between(
        "before_self",
        self_back,
        [hidden_in, grad_resid_self, mixing],
        [(rows, width), (8, width)],
        before_self,
        False,
        grads=[grad_cross_key, grad_cross_value, grad_cross_query, grad_cross_out],
    )
    sum_cross_key, sum_cross_value, sum_cross_query, sum_cross_out = sums
    grad_query = weight_grad(self_whole, grad_query_raw).astype(low)
    grad_key = weight_grad(self_whole, grad_key_raw).astype(low)
    grad_value = weight_grad(self_whole, grad_value_low).astype(low)

    time_part = jnp.concatenate(
        [
            self_sums[:2],
            cross_sums[:1],
            feed_sums[:3],
            cross_sums[1:2],
            jnp.zeros((1, width), jnp.float32),
        ],
        axis=0,
    )
    gain_part = jnp.stack(
        [
            item.reshape(heads_here, HEAD_DIM)
            for item in (grad_gain_query, grad_gain_key, grad_gain_cross_query, grad_gain_cross_key)
        ],
        axis=1,
    ).reshape(heads_here, 4 * HEAD_DIM)
    (time_total, all_total, gain_total), sums = plan.close(
        time_part,
        jnp.pad(gain_part, ((0, 8 - heads_here), (0, 0))),
        [grad_query, grad_key, grad_value, grad_out],
    )
    sum_query, sum_key, sum_value, sum_out = sums
    dp = lax.axis_index("dp")
    mine = lax.dynamic_slice_in_dim(all_total, dp * part, part, axis=1)
    gain_width = qk_gain.shape[1]
    gain_mine = lax.dynamic_slice_in_dim(
        gain_total[:heads_here], dp * gain_width, gain_width, axis=1
    )
    return (
        block_out,
        grad_hidden,
        grad_text,
        time_total[None, :6],
        mine[:6],
        sum_query,
        sum_key,
        sum_value,
        sum_out.T,
        sum_cross_query,
        sum_cross_key,
        sum_cross_value,
        sum_cross_out.T,
        sum_up,
        sum_down.T,
        gain_mine,
        mine[6],
    )


def solution(mesh):
    return jax.shard_map(
        functools.partial(body, Plan(mesh)),
        mesh=mesh,
        in_specs=(
            P(("dp", "tensor"), None),
            P(("dp", "tensor"), None),
            P("dp", None, None),
            P(None, "dp"),
            P(None, "dp"),
            P("dp", "tensor"),
            P("dp", "tensor"),
            P("dp", "tensor"),
            P("tensor", "dp"),
            P("dp", "tensor"),
            P("dp", "tensor"),
            P("dp", "tensor"),
            P("tensor", "dp"),
            P("dp", "tensor"),
            P("tensor", "dp"),
            P("tensor", "dp"),
            P("dp"),
            P(("dp", "tensor"), None),
        ),
        out_specs=(
            P(("dp", "tensor"), None),
            P(("dp", "tensor"), None),
            P(("dp", "tensor"), None),
            P("dp", None, None),
            P(None, "dp"),
            P("dp", "tensor"),
            P("dp", "tensor"),
            P("dp", "tensor"),
            P("tensor", "dp"),
            P("dp", "tensor"),
            P("dp", "tensor"),
            P("dp", "tensor"),
            P("tensor", "dp"),
            P("dp", "tensor"),
            P("tensor", "dp"),
            P("tensor", "dp"),
            P("dp"),
        ),
        check_vma=False,
    )
```

```python
import functools

import jax
import jax.numpy as jnp
from jax import lax
from jax.experimental import pallas as pl
from jax.experimental.pallas import tpu as pltpu
from jax.sharding import PartitionSpec as P

MESH = pl.DeviceIdType.MESH
VMEM_BYTES = 60 * 2**20

HEAD_DIM = 128
D = 1536


EPSILON = 1e-06
CONTRACT_LAST = (((1,), (1,)), ((), ()))
CONTRACT_FIRST = (((0,), (0,)), ((), ()))


def rotary_tables(positions, head_width):
    pairs = head_width // 2
    third = pairs // 3
    first = pairs - 2 * third
    freq_frame = jnp.power(10000.0, -jnp.arange(first, dtype=jnp.float32) / first)
    freq_side = jnp.power(10000.0, -jnp.arange(third, dtype=jnp.float32) / third)
    places = positions.astype(jnp.float32)
    angles = jnp.concatenate(
        [
            places[0][:, None] * jnp.repeat(freq_frame, 2)[None, :],
            places[1][:, None] * jnp.repeat(freq_side, 2)[None, :],
            places[2][:, None] * jnp.repeat(freq_side, 2)[None, :],
        ],
        axis=1,
    )
    sign = jnp.where(jnp.arange(head_width) % 2 == 0, -1.0, 1.0)
    return (jnp.cos(angles), jnp.sin(angles) * sign)


def product_back(grads, weight):
    return lax.dot_general(grads, weight, CONTRACT_LAST, preferred_element_type=jnp.float32)


def weight_grad(inputs, grads):
    return lax.dot_general(inputs, grads, CONTRACT_FIRST, preferred_element_type=jnp.float32)


def when(cond, run):
    if cond is None:
        run()
    else:
        pl.when(cond)(run)


def flip(index, bit):
    return index + bit - 2 * bit * (index // bit % 2)


def normed(values):
    center = values - jnp.mean(values, axis=-1, keepdims=True)
    inverse = lax.rsqrt(jnp.mean(center * center, axis=-1, keepdims=True) + EPSILON)
    return center * inverse, inverse


def normed_back(unit, inverse, grad):
    mean_grad = jnp.mean(grad, axis=-1, keepdims=True)
    mean_dot = jnp.mean(grad * unit, axis=-1, keepdims=True)
    return (grad - mean_grad - unit * mean_dot) * inverse


class Links:
    def __init__(self, send, recv, local, dp_size, tensor_size):
        self.send, self.recv, self.local = send, recv, local
        self.count = 0
        self.local_count = 0
        self.dp_size, self.size = dp_size, tensor_size
        self.dp = lax.axis_index("dp")
        self.z = lax.axis_index("tensor")

    def slot(self):
        self.count += 1
        return self.count - 1

    def copy(self, source, target, device, slot):
        return pltpu.make_async_remote_copy(
            src_ref=source,
            dst_ref=target,
            send_sem=self.send.at[slot],
            recv_sem=self.recv.at[slot],
            device_id=device,
            device_id_type=MESH,
        )

    def here(self, source, target):
        self.local_count += 1
        return pltpu.make_async_copy(source, target, self.local.at[self.local_count - 1])

    def greet(self, groups):
        barrier = pltpu.get_barrier_semaphore()
        peers = []
        if "line" in groups and "zall" not in groups:
            peers += [
                ((self.dp, self.z - 1), self.z > 0),
                ((self.dp, self.z + 1), self.z < self.size - 1),
            ]
        if "zall" in groups:
            peers += [
                ((self.dp, lax.rem(self.z + k, self.size)), None) for k in range(1, self.size)
            ]
        if "dpall" in groups:
            peers += [
                ((lax.rem(self.dp + k, self.dp_size), self.z), None)
                for k in range(1, self.dp_size)
            ]
        if "bits" in groups:
            bit = 1
            while bit < self.dp_size:
                peers.append(((flip(self.dp, bit), self.z), None))
                bit *= 2
        if "diag" in groups:
            peers.append(((flip(flip(self.dp, 2), 4), self.z), None))
        for device, cond in peers:
            when(
                cond,
                lambda device=device: pl.semaphore_signal(
                    barrier, inc=1, device_id=device, device_id_type=MESH
                ),
            )
        expected = sum(1 for _, cond in peers if cond is None)
        for _, cond in peers:
            if cond is not None:
                expected = expected + cond.astype(jnp.int32)
        pl.semaphore_wait(barrier, expected)


def piece_of(ref, block, rows, start, count):
    return ref.at[pl.ds(pl.multiple_of(block * rows + start, 16), count)]


class LineGather:
    def __init__(self, links, whole, rows, pieces):
        self.links, self.whole, self.rows, self.count = links, whole, rows, rows // pieces
        self.pieces = pieces
        hops = links.size - 1
        self.right = [[links.slot() for _ in range(pieces)] for _ in range(hops)]
        self.left = [[links.slot() for _ in range(pieces)] for _ in range(hops)]

    def block(self, index, piece):
        return piece_of(self.whole, index, self.rows, piece * self.count, self.count)

    def move(self, index, piece, way, slot):
        part = self.block(index, piece)
        return self.links.copy(part, part, (self.links.dp, self.links.z + way), slot)

    def start(self, piece):
        z, last = self.links.z, self.links.size - 1
        when(z < last, lambda: self.move(z, piece, 1, self.right[0][piece]).start())
        when(z > 0, lambda: self.move(z, piece, -1, self.left[0][piece]).start())

    def step(self, hop, piece):
        z, last = self.links.z, self.links.size - 1

        def from_left():
            self.move(z - 1 - hop, piece, -1, self.right[hop][piece]).wait_recv()
            if hop + 1 < last:
                when(
                    z < last,
                    lambda: self.move(z - 1 - hop, piece, 1, self.right[hop + 1][piece]).start(),
                )

        def from_right():
            self.move(z + 1 + hop, piece, 1, self.left[hop][piece]).wait_recv()
            if hop + 1 < last:
                when(
                    z > 0,
                    lambda: self.move(z + 1 + hop, piece, -1, self.left[hop + 1][piece]).start(),
                )

        when(z - 1 - hop >= 0, from_left)
        when(z + 1 + hop <= last, from_right)

    def steps(self, piece):
        for hop in range(self.links.size - 1):
            self.step(hop, piece)

    def finish(self):
        z, last = self.links.z, self.links.size - 1
        for hop in range(last):
            for piece in range(self.pieces):
                when(
                    (z - hop >= 0) & (z < last),
                    lambda: self.move(z - hop, piece, 1, self.right[hop][piece]).wait_send(),
                )
                when(
                    (z + hop <= last) & (z > 0),
                    lambda: self.move(z + hop, piece, -1, self.left[hop][piece]).wait_send(),
                )


class LineReduce:
    def __init__(self, links, partial, land_right, land_left, rows, pieces):
        self.links, self.partial, self.rows, self.count = links, partial, rows, rows // pieces
        self.land = {1: land_right, -1: land_left}
        self.pieces = pieces
        last = links.size - 1
        self.slots = {
            way: [None] + [[links.slot() for _ in range(pieces)] for _ in range(last)]
            for way in (1, -1)
        }

    def landing(self, way, distance, piece):
        return self.land[way].at[distance - 1, pl.ds(piece * self.count, self.count)]

    def part(self, index, piece):
        return piece_of(self.partial, index, self.rows, piece * self.count, self.count)

    def move(self, source, way, distance, piece):
        return self.links.copy(
            source,
            self.landing(way, distance, piece),
            (self.links.dp, self.links.z + way),
            self.slots[way][distance][piece],
        )

    def arrived(self, way, distance, piece):
        self.links.copy(
            self.landing(way, distance, piece),
            self.landing(way, distance, piece),
            (self.links.dp, self.links.z - way),
            self.slots[way][distance][piece],
        ).wait_recv()

    def first(self, piece):
        z, last = self.links.z, self.links.size - 1

        def from_first():
            for distance in range(last, 0, -1):
                self.move(self.part(distance, piece), 1, distance, piece).start()

        def from_last():
            for distance in range(last, 0, -1):
                self.move(self.part(last - distance, piece), -1, distance, piece).start()

        when(z == 0, from_first)
        when(z == last, from_last)

    def clear(self):
        z, last = self.links.z, self.links.size - 1

        def zero(way):
            self.land[way][0] = jnp.zeros(self.land[way].shape[1:], self.land[way].dtype)

        when(z == 0, lambda: zero(1))
        when(z == last, lambda: zero(-1))

    def step(self, distance, piece):
        z, last = self.links.z, self.links.size - 1
        for way in (1, -1):
            inside = (
                (z > 0) & (z + distance <= last)
                if way == 1
                else (z < last) & (z - distance >= 0)
            )

            def go(way=way):
                self.arrived(way, distance + 1, piece)
                held = self.landing(way, distance + 1, piece)
                own = self.part(z + way * distance, piece)
                held[...] = (
                    held[...].astype(jnp.float32) + own[...].astype(jnp.float32)
                ).astype(held.dtype)
                self.move(held, way, distance, piece).start()

            when(inside, go)

    def total(self, piece):
        z, last = self.links.z, self.links.size - 1
        when(z > 0, lambda: self.arrived(1, 1, piece))
        when(z < last, lambda: self.arrived(-1, 1, piece))
        return (
            self.part(z, piece)[...].astype(jnp.float32)
            + self.landing(1, 1, piece)[...].astype(jnp.float32)
            + self.landing(-1, 1, piece)[...].astype(jnp.float32)
        )

    def finish(self):
        z, last = self.links.z, self.links.size - 1
        for distance in range(1, last + 1):
            for piece in range(self.pieces):
                held = self.landing(1, distance, piece)
                when(
                    z + distance <= last,
                    lambda: self.move(held, 1, distance, piece).wait_send(),
                )
                back = self.landing(-1, distance, piece)
                when(
                    z - distance >= 0,
                    lambda: self.move(back, -1, distance, piece).wait_send(),
                )


def reduce_stages(reduce):
    return [
        functools.partial(reduce.step, distance)
        for distance in range(reduce.links.size - 2, 0, -1)
    ]


def wave(stages, pieces, queue):
    count = pieces + len(stages) - 1
    done = 0
    for step in range(count):
        for index, stage in enumerate(stages):
            if 0 <= step - index < pieces:
                stage(step - index)
        until = len(queue) * (step + 1) // count
        for run in queue[done:until]:
            run()
        done = until


class CubeGather:
    def __init__(self, links, shard, whole):
        self.links, self.shard, self.whole = links, shard, whole
        self.rows = shard.shape[0]
        self.slots = [links.slot() for _ in range(8)]
        dp = links.dp
        self.core, self.side, self.over = flip(dp, 1), flip(dp, 2), flip(dp, 4)
        self.far = flip(flip(dp, 2), 4)
        self.sent = []

    def block(self, index, start=0, count=None):
        return piece_of(self.whole, index, self.rows, start, count or self.rows)

    def send(self, source, target, device, slot):
        move = self.links.copy(source, target, (device, self.links.z), self.slots[slot])
        move.start()
        self.sent.append(move)

    def got(self, part, slot):
        self.links.copy(part, part, (self.core, self.links.z), self.slots[slot]).wait_recv()

    def start(self):
        mine = self.block(self.links.dp)
        self.own = self.links.here(self.shard, mine)
        self.own.start()
        self.send(self.shard, mine, self.side, 1)
        self.send(self.shard, mine, self.over, 2)
        self.send(self.shard, mine, self.core, 0)

    def forward(self):
        half = self.rows // 2
        self.got(self.block(self.side), 1)
        part = self.block(self.side, 0, half)
        self.send(part, part, self.over, 3)
        part = self.block(self.side)
        self.send(part, part, self.core, 5)
        self.got(self.block(self.over), 2)
        part = self.block(self.over, half, half)
        self.send(part, part, self.side, 4)
        part = self.block(self.over)
        self.send(part, part, self.core, 6)

    def tail(self):
        half = self.rows // 2
        self.got(self.block(self.far, 0, half), 3)
        self.got(self.block(self.far, half, half), 4)
        part = self.block(self.far)
        self.send(part, part, self.core, 7)

    def finish(self):
        self.got(self.block(self.core), 0)
        self.got(self.block(flip(self.core, 2)), 5)
        self.got(self.block(flip(self.core, 4)), 6)
        self.got(self.block(flip(flip(self.core, 2), 4)), 7)
        for move in self.sent:
            move.wait_send()
        self.own.wait()


class DirectGather:
    def __init__(self, links, whole, rows):
        self.links, self.whole, self.rows = links, whole, rows
        self.slots = [links.slot() for _ in range(links.size - 1)]

    def start(self, source):
        links = self.links
        mine = piece_of(self.whole, links.z, self.rows, 0, self.rows)
        self.moves = [
            links.copy(source, mine, (links.dp, lax.rem(links.z + step, links.size)), slot)
            for step, slot in enumerate(self.slots, 1)
        ]
        for move in self.moves:
            move.start()

    def finish(self):
        for move in self.moves:
            move.wait_recv()
        for move in self.moves:
            move.wait_send()


class DirectReduce:
    def __init__(self, links, partial, land, rows):
        self.links, self.partial, self.land, self.rows = links, partial, land, rows
        self.slots = [links.slot() for _ in range(links.size - 1)]

    def start(self):
        links = self.links
        self.moves = []
        for step, slot in enumerate(self.slots, 1):
            target = lax.rem(links.z + step, links.size)
            move = links.copy(
                piece_of(self.partial, target, self.rows, 0, self.rows),
                self.land.at[step - 1],
                (links.dp, target),
                slot,
            )
            move.start()
            self.moves.append(move)

    def arrive(self):
        for move in self.moves:
            move.wait_recv()

    def total(self, start, count):
        total = piece_of(self.partial, self.links.z, self.rows, start, count)[...]
        total = total.astype(jnp.float32)
        for index in range(self.links.size - 1):
            total = total + self.land[index, start : start + count, :].astype(jnp.float32)
        return total

    def finish(self):
        for move in self.moves:
            move.wait_send()


class Exchange:
    def __init__(self, links, mine, land, turned):
        self.links, self.mine, self.land, self.turned = links, mine, land, turned
        self.slots = [links.slot() for _ in range(links.size - 1)]

    def start(self, columns):
        links = self.links
        lane = lax.broadcasted_iota(jnp.int32, (columns[0].shape[0], 128), 1)
        flat = jnp.zeros(lane.shape, jnp.float32)
        for index, column in enumerate(columns):
            flat = jnp.where(lane == index, column, flat)
        self.mine[...] = flat.T[:8]
        self.moves = [
            links.copy(
                self.mine,
                self.land.at[step - 1],
                (links.dp, lax.rem(links.z + step, links.size)),
                slot,
            )
            for step, slot in enumerate(self.slots, 1)
        ]
        for move in self.moves:
            move.start()

    def finish(self, shape=lambda total: total):
        total = self.mine[...]
        for step, move in enumerate(self.moves):
            move.wait_recv()
            total = total + self.land[step]
        self.turned[...] = jnp.zeros(self.turned.shape, jnp.float32)
        self.turned[0:8, :] = shape(total)
        for move in self.moves:
            move.wait_send()
        return self.turned[...].T


class CoreSum:
    def __init__(self, links, left, right, product, near):
        self.links, self.left, self.right = links, left, right
        self.product, self.near = product, near
        self.rows = near.shape[1]
        self.slots = [links.slot() for _ in range(4)]
        self.core = links.dp % 2
        self.moves = []

    def multiply(self, chip):
        links, count = self.links, 2 * self.rows
        self.product[chip * count : (chip + 1) * count, :] = weight_grad(
            self.left[:, chip * count : (chip + 1) * count], self.right[...]
        ).astype(jnp.bfloat16)
        move = links.copy(
            piece_of(self.product, 2 * chip + 1 - self.core, self.rows, 0, self.rows),
            self.near.at[chip],
            (flip(links.dp, 1), links.z),
            self.slots[chip],
        )
        move.start()
        self.moves.append(move)

    def add(self):
        for move in self.moves:
            move.wait_recv()

        def one(step, _):
            rows = pl.ds(pl.multiple_of(step * 16, 16), 16)
            for chip in range(4):
                own = pl.ds(
                    pl.multiple_of((2 * chip + self.core) * self.rows + step * 16, 16), 16
                )
                self.near[chip, rows, :] = (
                    self.near[chip, rows, :].astype(jnp.float32)
                    + self.product[own, :].astype(jnp.float32)
                ).astype(jnp.bfloat16)
            return 0

        lax.fori_loop(0, self.rows // 16, one, 0)

    def clear(self):
        for move in self.moves:
            move.wait_send()

    def steps(self):
        return [functools.partial(self.multiply, chip) for chip in range(4)] + [self.add]


class ChipSum:
    def __init__(self, links, near, out, others, own=None):
        self.links, self.near, self.out, self.others, self.own = links, near, out, others, own
        self.slots = [links.slot() for _ in range(3)]
        self.core, self.chip = links.dp % 2, links.dp // 2
        self.rows = out.shape[0]

    def start(self):
        links = self.links
        chips = [flip(self.chip, 1), flip(self.chip, 2), flip(flip(self.chip, 1), 2)]
        self.moves = [
            links.copy(
                self.near.at[chip],
                self.others.at[index],
                (2 * chip + self.core, links.z),
                self.slots[index],
            )
            for index, chip in enumerate(chips)
        ]
        for move in self.moves:
            move.start()
        if self.own is not None:
            self.local = links.here(self.near.at[self.chip], self.own)
            self.local.start()

    def finish(self):
        for move in self.moves:
            move.wait_recv()
        if self.own is not None:
            self.local.wait()

        def one(step, _):
            rows = pl.ds(pl.multiple_of(step * 16, 16), 16)
            mine = self.own[rows, :] if self.own is not None else self.near[self.chip, rows, :]
            total = mine.astype(jnp.float32)
            for index in range(3):
                total = total + self.others[index, rows, :].astype(jnp.float32)
            self.out[rows, :] = total
            return 0

        lax.fori_loop(0, self.rows // 16, one, 0)
        for move in self.moves:
            move.wait_send()


def attend(query, key, value, out, logs, heads, chunk=256):
    scale = HEAD_DIM**-0.5
    for head in range(heads):
        lanes = slice(head * HEAD_DIM, (head + 1) * HEAD_DIM)

        def one(step, _, head=head, lanes=lanes):
            rows = pl.ds(pl.multiple_of(step * chunk, chunk), chunk)
            scores = product_back(query[rows, lanes], key[:, lanes]) * scale
            top = jnp.max(scores, axis=-1, keepdims=True)
            expo = jnp.exp(scores - top)
            summed = jnp.sum(expo, axis=-1, keepdims=True)
            probs = (expo * (1.0 / summed)).astype(jnp.bfloat16)
            out[rows, lanes] = jnp.dot(
                probs, value[:, lanes], preferred_element_type=jnp.float32
            ).astype(jnp.bfloat16)
            logs[rows, head : head + 1] = top + jnp.log(summed)
            return 0

        lax.fori_loop(0, query.shape[0] // chunk, one, 0)


def attend_back(query, key, value, logs, grad, grads, heads, chunk=256):
    scale = HEAD_DIM**-0.5
    grad_query, grad_key, grad_value = grads
    grad_key[...] = jnp.zeros(grad_key.shape, jnp.float32)
    grad_value[...] = jnp.zeros(grad_value.shape, jnp.float32)
    for head in range(heads):
        lanes = slice(head * HEAD_DIM, (head + 1) * HEAD_DIM)

        def one(step, _, head=head, lanes=lanes):
            rows = pl.ds(pl.multiple_of(step * chunk, chunk), chunk)
            scores = product_back(query[rows, lanes], key[:, lanes]) * scale
            probs = jnp.exp(scores - logs[rows, head : head + 1])
            prob_grad = product_back(grad[rows, lanes], value[:, lanes])
            inner = jnp.sum(prob_grad * probs, axis=-1, keepdims=True)
            score_grad = (probs * (prob_grad - inner)).astype(jnp.bfloat16)
            grad_query[rows, lanes] = (
                jnp.dot(score_grad, key[:, lanes], preferred_element_type=jnp.float32) * scale
            )
            grad_key[:, lanes] += weight_grad(score_grad, query[rows, lanes]) * scale
            grad_value[:, lanes] += weight_grad(probs.astype(jnp.bfloat16), grad[rows, lanes])
            return 0

        lax.fori_loop(0, query.shape[0] // chunk, one, 0)


def swapped(values):
    lane = lax.broadcasted_iota(jnp.int32, values.shape, 1)
    width = values.shape[1]
    return jnp.where(lane % 2 == 0, pltpu.roll(values, width - 1, 1), pltpu.roll(values, 1, 1))


def turn(values, cosine, sine, back):
    other = swapped(values) * sine
    return values * cosine - other if back else values * cosine + other


def square_columns(*arrays):
    return [jnp.sum(array * array, axis=-1, keepdims=True) for array in arrays]


def shape_norm(raw, inverse, gain, angles, out, heads, chunk=128):
    for head in range(heads):
        lanes = slice(head * HEAD_DIM, (head + 1) * HEAD_DIM)
        for start in range(0, raw.shape[0], chunk):
            rows = slice(start, start + chunk)
            values = raw[rows, lanes] * inverse[rows] * gain[head]
            if angles is not None:
                values = turn(values, angles[0][rows, :], angles[1][rows, :], False)
            out[rows, lanes] = values.astype(jnp.bfloat16)


def norm_dots(raw, inverse, gain, angles, grad, gain_out, heads, chunk=128):
    columns = []
    for start in range(0, raw.shape[0], chunk):
        rows = slice(start, start + chunk)
        column = jnp.zeros((chunk, 1), jnp.float32)
        for head in range(heads):
            lanes = slice(head * HEAD_DIM, (head + 1) * HEAD_DIM)
            values = grad[rows, lanes]
            if angles is not None:
                values = turn(values, angles[0][rows, :], angles[1][rows, :], True)
                grad[rows, lanes] = values
            part = values * raw[rows, lanes]
            column = column + jnp.sum(part * gain[head], axis=-1, keepdims=True)
            total = jnp.sum(part * inverse[rows], axis=0, keepdims=True)
            where = slice(head, head + 1)
            gain_out[where, :] = total if start == 0 else gain_out[where, :] + total
        columns.append(column)
    return jnp.concatenate(columns, axis=0)


def norm_pull(raw, inverse, gain, dots, grad, out, heads, chunk=128):
    for start in range(0, raw.shape[0], chunk):
        rows = slice(start, start + chunk)
        scale = inverse[rows]
        cut = dots[rows] * scale * scale * scale * (1.0 / D)
        for head in range(heads):
            lanes = slice(head * HEAD_DIM, (head + 1) * HEAD_DIM)
            out[rows, lanes] = (
                grad[rows, lanes] * gain[head] * scale - raw[rows, lanes] * cut
            ).astype(jnp.bfloat16)


def gains_of(gain_ref, kind, heads):
    lanes = slice(kind * HEAD_DIM, (kind + 1) * HEAD_DIM)
    return [gain_ref[head : head + 1, lanes] for head in range(heads)]


def exchange_scratch(length, size):
    return [
        pltpu.VMEM((8, length), jnp.float32),
        pltpu.VMEM((size - 1, 8, length), jnp.float32),
        pltpu.VMEM((128, length), jnp.float32),
    ]


class Plan:
    def __init__(self, mesh):
        self.dp = mesh.shape["dp"]
        self.tensor = mesh.shape["tensor"]
        self.cube = self.dp == 8
        self.calls = 0
        self.pieces = 4

    def call(self, name, body, inputs, outputs, scratch, copies):
        self.calls += 1
        spaces = {True: pltpu.VMEM, False: pltpu.HBM}
        count_in, count_out = len(inputs), len(outputs)

        def kernel(*refs):
            ins = refs[:count_in]
            outs = refs[count_in : count_in + count_out]
            rest = refs[count_in + count_out :]
            links = Links(rest[0], rest[1], rest[2], self.dp, self.tensor)
            body(links, ins, outs, rest[3:])

        return pl.pallas_call(
            kernel,
            name=name,
            out_shape=[jax.ShapeDtypeStruct(shape, kind) for shape, kind, _ in outputs],
            in_specs=[pl.BlockSpec(memory_space=spaces[near]) for _, near in inputs],
            out_specs=[pl.BlockSpec(memory_space=spaces[near]) for _, _, near in outputs],
            scratch_shapes=[
                pltpu.SemaphoreType.DMA((copies,)),
                pltpu.SemaphoreType.DMA((copies,)),
                pltpu.SemaphoreType.DMA((64,)),
                *scratch,
            ],
            compiler_params=pltpu.CompilerParams(
                collective_id=self.calls, has_side_effects=True, vmem_limit_bytes=VMEM_BYTES
            ),
        )(*[array for array, _ in inputs])

    def gather_outputs(self, shards):
        return [
            ((self.dp * shard.shape[0], shard.shape[1]), shard.dtype, False) for shard in shards
        ]

    def open(self, hidden, time_rows, small, shards):
        rows, width = hidden.shape
        part = width // self.dp
        gain_part = small.shape[1] - part
        moving = shards if self.cube else []

        def body(links, ins, outs, scratch):
            hidden_ref, time_ref, small_ref = ins[:3]
            table_ref, gain_ref, whole_ref = outs[:3]
            (land,) = scratch
            links.greet({"line", "dpall"})
            gathers = [CubeGather(links, a, b) for a, b in zip(ins[3:], outs[3:])]
            dp, z = links.dp, links.z
            moves = []
            for step in range(1, self.dp):
                target = lax.rem(dp + step, self.dp)
                move = links.copy(small_ref, land.at[dp], (target, z), links.slot())
                move.start()
                moves.append(move)
            for item in gathers:
                item.start()
            land[dp] = small_ref[...]
            unit, _ = normed(hidden_ref[...])
            for move in moves:
                move.wait_recv()
            table = jnp.concatenate([land[k][:, :part] for k in range(self.dp)], axis=1)
            gain_ref[...] = jnp.concatenate([land[k][:, part:] for k in range(self.dp)], axis=1)
            table = table + time_ref[...]
            table_ref[...] = table
            line = LineGather(links, whole_ref, rows, 4)
            first = unit * (1.0 + table[1:2]) + table[0:1]
            whole_ref[pl.ds(pl.multiple_of(z * rows, 16), rows), :] = first.astype(jnp.bfloat16)
            for piece in range(4):
                line.start(piece)
            for piece in range(4):
                line.steps(piece)
                if piece < len(gathers):
                    gathers[piece].forward()
            for item in gathers[4:]:
                item.forward()
            for item in gathers:
                item.tail()
            for item in gathers:
                item.finish()
            line.finish()
            for move in moves:
                move.wait_send()

        results = self.call(
            "open",
            body,
            [(hidden, True), (time_rows, True), (small, True)] + [(s, False) for s in moving],
            [
                ((8, width), jnp.float32, True),
                ((8, gain_part * self.dp), jnp.float32, True),
                ((rows * self.tensor, width), jnp.bfloat16, True),
            ]
            + self.gather_outputs(moving),
            [pltpu.VMEM((self.dp, 8, small.shape[1]), jnp.float32)],
            160,
        )
        return results[:3], self.gathered(results[3:], shards)

    def gathered(self, moved, shards):
        if self.cube:
            return list(moved)
        return [lax.all_gather(shard, "dp", axis=0, tiled=True) for shard in shards]

    def phase(
        self,
        name,
        near,
        kinds,
        scratch,
        pre,
        post,
        gather,
        shape,
        shards=(),
        lines=(),
        sums=(),
        jobs=(),
        tasks=None,
        begin=None,
        end=None,
        exchange=True,
    ):
        length, width = shape
        rows = length // self.tensor
        pieces = self.pieces
        shards, lines, sums = list(shards), list(lines), list(sums)
        moving = shards if self.cube else []
        adding = sums if self.cube else []
        jobs = list(jobs)
        here = [job for job in jobs if job[4]] if self.cube else []
        count_near, count_kinds, count_scratch = len(near), len(kinds), len(scratch)

        job_scratch, job_outputs = [], []
        products, seats = {}, []
        for left, right, part, columns, now in jobs:
            if not self.cube:
                seats.append(("out", len(job_outputs)))
                job_outputs.append(((self.dp * part, columns), jnp.bfloat16, True))
                continue
            key = (part, columns)
            if key not in products:
                products[key] = len(job_scratch)
                job_scratch.append(pltpu.VMEM((8 * part, columns), jnp.bfloat16))
            if now:
                seats.append((products[key], len(job_scratch), len(job_outputs)))
                job_scratch.append(pltpu.VMEM((4, part, columns), jnp.bfloat16))
                job_scratch.append(pltpu.VMEM((3, part, columns), jnp.bfloat16))
                job_outputs.append(((part, columns), jnp.float32, True))
            else:
                seats.append((products[key], None, len(job_outputs)))
                job_outputs.append(((4, part, columns), jnp.bfloat16, True))
        sum_scratch, sum_outputs = [], []
        for item in adding:
            _, part, columns = item.shape
            sum_scratch.append(pltpu.VMEM((3, part, columns), jnp.bfloat16))
            sum_scratch.append(pltpu.VMEM((part, columns), jnp.bfloat16))
            sum_outputs.append(((part, columns), jnp.float32, True))

        def body(links, ins, outs, rest):
            near_refs, ins = ins[:count_near], ins[count_near:]
            shard_refs, ins = ins[: len(moving)], ins[len(moving) :]
            line_refs, sum_refs = ins[: len(lines)], ins[len(lines) :]
            kind_refs, outs = outs[:count_kinds], outs[count_kinds:]
            if gather:
                whole_ref, outs = outs[0], outs[1:]
            full_refs, outs = outs[: len(moving)], outs[len(moving) :]
            line_outs, outs = outs[: len(lines)], outs[len(lines) :]
            job_refs, added_refs = outs[: len(jobs)], outs[len(jobs) :]
            partial_ref, land_right, land_left = rest[:3]
            user, rest = rest[3 : 3 + count_scratch], rest[3 + count_scratch :]
            job_rest, sum_rest = rest[: len(job_scratch)], rest[len(job_scratch) :]

            groups = {"zall"} if exchange else {"line"}
            if moving or adding or jobs:
                groups |= {"bits"} if self.cube else set()
            if adding or here:
                groups |= {"diag"}
            links.greet(groups)
            gathers = [CubeGather(links, a, b) for a, b in zip(shard_refs, full_refs)]
            straight = [
                DirectGather(links, b, a.shape[0]) for a, b in zip(line_refs, line_outs)
            ]
            old = [
                ChipSum(links, a, b, sum_rest[2 * k], sum_rest[2 * k + 1])
                for k, (a, b) in enumerate(zip(sum_refs, added_refs))
            ]
            for item in gathers + old:
                item.start()
            copies = []
            for item, source in zip(straight, line_refs):
                item.start(source)
                copies.append(
                    links.here(source, piece_of(item.whole, links.z, item.rows, 0, item.rows))
                )
                copies[-1].start()
            state = begin(links, near_refs, kind_refs, user) if begin else None
            pre(links, near_refs, kind_refs, user, partial_ref)

            queue = list(tasks(near_refs, kind_refs, user)) if tasks else []
            fresh, busy, cleared = [], {}, []
            for (left, right, part, columns, now), seat in zip(jobs, seats):
                left_ref, right_ref = left(near_refs, kind_refs, user), right(near_refs, kind_refs, user)
                out = job_refs[seat[-1]]
                if not self.cube:

                    def whole(start, left_ref=left_ref, right_ref=right_ref, out=out):
                        count = out.shape[0] // 4
                        where = slice(start * count, (start + 1) * count)
                        out[where, :] = weight_grad(left_ref[:, where], right_ref[...]).astype(
                            jnp.bfloat16
                        )

                    queue += [functools.partial(whole, start) for start in range(4)]
                    continue
                held = job_rest[seat[1]] if now else out
                item = CoreSum(links, left_ref, right_ref, job_rest[seat[0]], held)
                if seat[0] in busy:
                    queue.append(busy[seat[0]].clear)
                    cleared.append(busy[seat[0]])
                busy[seat[0]] = item
                queue += item.steps()
                if now:
                    chip = ChipSum(links, held, out, job_rest[seat[1] + 1])
                    queue.append(chip.start)
                    fresh.append(chip)
            queue += [item.forward for item in gathers]
            queue += [item.tail for item in gathers]

            reduce = LineReduce(links, partial_ref, land_right, land_left, rows, pieces)
            line = LineGather(links, whole_ref, rows, pieces) if gather else None
            for piece in range(pieces):
                reduce.first(piece)
            reduce.clear()

            def settle(piece):
                where = pl.ds(piece * (rows // pieces), rows // pieces)
                result = post(reduce.total(piece), where, near_refs, kind_refs, piece == 0)
                if gather:
                    line.block(links.z, piece)[...] = result
                    line.start(piece)

            stages = reduce_stages(reduce) + [settle]
            if gather:
                stages += [functools.partial(line.step, hop) for hop in range(links.size - 1)]
            wave(stages, pieces, queue)
            for item in gathers + old + fresh + straight:
                item.finish()
            for item in busy.values():
                item.clear()
            for copy in copies:
                copy.wait()
            if end:
                end(state, links, near_refs, kind_refs, user)
            reduce.finish()
            if gather:
                line.finish()

        inputs = [(item, True) for item in near]
        inputs += [(item, False) for item in moving + lines + adding]
        outputs = [(form, kind, True) for form, kind in kinds]
        if gather:
            outputs.append(((length, width), jnp.bfloat16, True))
        outputs += self.gather_outputs(moving)
        outputs += [
            ((item.shape[0] * self.tensor, item.shape[1]), item.dtype, False) for item in lines
        ]
        outputs += job_outputs + sum_outputs
        results = list(
            self.call(
                name,
                body,
                inputs,
                outputs,
                [
                    pltpu.VMEM((length, width), jnp.bfloat16),
                    pltpu.VMEM((self.tensor - 1, rows, width), jnp.bfloat16),
                    pltpu.VMEM((self.tensor - 1, rows, width), jnp.bfloat16),
                    *scratch,
                    *job_scratch,
                    *sum_scratch,
                ],
                240,
            )
        )
        kept, results = results[:count_kinds], results[count_kinds:]
        whole, results = (results[0], results[1:]) if gather else (None, results)
        full, results = self.gathered(results[: len(moving)], shards), results[len(moving) :]
        lined, results = results[: len(lines)], results[len(lines) :]
        made, added = results[: len(jobs)], results[len(jobs) :]
        if not self.cube:
            made = [
                self.scatter(item) if job[4] else item for item, job in zip(made, jobs)
            ]
            added = [self.scatter(item) for item in sums]
        return kept, whole, full, lined, made, added

    def scatter(self, grad):
        return lax.psum_scatter(grad, "dp", scatter_dimension=0, tiled=True).astype(jnp.float32)

    def close(self, time_part, gain_part):
        bits = [1 << k for k in range(self.dp.bit_length() - 1)]

        def body(links, ins, outs, scratch):
            time_ref, gain_ref = ins[:2]
            total_ref, all_ref, gains_ref = outs[:3]
            land, held, held_gain, come, come_gain = scratch[:5]
            links.greet({"zall", "bits"})
            moves = []
            for step in range(1, self.tensor):
                target = lax.rem(links.z + step, self.tensor)
                move = links.copy(time_ref, land.at[links.z], (links.dp, target), links.slot())
                move.start()
                moves.append(move)
            land[links.z] = time_ref[...]
            held_gain[0] = gain_ref[...]
            for move in moves:
                move.wait_recv()
            total = land[0]
            for index in range(1, self.tensor):
                total = total + land[index]
            total_ref[...] = total
            held[0] = total
            for index, bit in enumerate(bits):
                target = (flip(links.dp, bit), links.z)
                one = links.copy(held.at[index], come.at[index], target, links.slot())
                two = links.copy(held_gain.at[index], come_gain.at[index], target, links.slot())
                one.start()
                two.start()
                one.wait_recv()
                two.wait_recv()
                held[index + 1] = held[index] + come[index]
                held_gain[index + 1] = held_gain[index] + come_gain[index]
                moves += [one, two]
            all_ref[...] = held[len(bits)]
            gains_ref[...] = held_gain[len(bits)]
            for move in moves:
                move.wait_send()

        levels = len(bits)
        results = self.call(
            "close",
            body,
            [(time_part, True), (gain_part, True)],
            [
                (time_part.shape, jnp.float32, True),
                (time_part.shape, jnp.float32, True),
                (gain_part.shape, jnp.float32, True),
            ],
            [
                pltpu.VMEM((self.tensor, *time_part.shape), jnp.float32),
                pltpu.VMEM((levels + 1, *time_part.shape), jnp.float32),
                pltpu.VMEM((levels + 1, *gain_part.shape), jnp.float32),
                pltpu.VMEM((levels, *time_part.shape), jnp.float32),
                pltpu.VMEM((levels, *gain_part.shape), jnp.float32),
            ],
            80,
        )
        return results


def add_sum(ref, row, values, first):
    total = jnp.sum(values, axis=0, keepdims=True)
    ref[row : row + 1, :] = total if first else ref[row : row + 1, :] + total


def tiles(count, size):
    return [(start, min(size, count - start)) for start in range(0, count, size)]


def body(
    plan,
    hidden_in,
    text_states,
    time_embed,
    positions,
    modulation,
    query_weight,
    key_weight,
    value_weight,
    out_weight,
    cross_query,
    cross_key,
    cross_value,
    cross_out,
    up_weight,
    down_weight,
    qk_gain,
    norm_gain,
    cotangent,
):
    plan.calls = 0
    low, full_type = jnp.bfloat16, jnp.float32
    rows, width = hidden_in.shape
    length = rows * plan.tensor
    here = out_weight.shape[0]
    heads = here // HEAD_DIM
    hidden_units = up_weight.shape[1]
    text_rows, text_width = length, text_states.shape[1]
    part = width // plan.dp
    text_part = text_width // plan.dp
    shape = (length, width)

    top = jnp.concatenate([modulation, norm_gain[None], jnp.zeros((1, part), low)], axis=0)
    side = jnp.pad(qk_gain, ((0, 8 - heads), (0, 0)))
    small = jnp.concatenate([top, side], axis=1).astype(full_type)
    time_rows = jnp.pad(time_embed[0], ((0, 2), (0, 0)))
    (mixing, gains, self_whole), full = plan.open(
        hidden_in, time_rows, small, [query_weight, key_weight, value_weight, out_weight.T]
    )
    query_full, key_full, value_full, out_full = full
    cosine, sine = rotary_tables(positions, HEAD_DIM)

    def forward(kinds_of_gain, angles, inputs, weights, gain_ref, kinds, scratch, links, partial):
        query_in, other_in = inputs
        query_w, key_w, value_w, out_w = weights
        query_raw, key_raw, value, query, key, attended, logs, inverse = kinds
        exchange = Exchange(links, *scratch)
        key_raw[...] = jnp.dot(other_in[...], key_w[...], preferred_element_type=full_type)
        query_raw[...] = jnp.dot(query_in[...], query_w[...], preferred_element_type=full_type)
        exchange.start(square_columns(query_raw[...], key_raw[...]))
        value[...] = jnp.dot(
            other_in[...], value_w[...], preferred_element_type=full_type
        ).astype(low)
        inverse[...] = exchange.finish(lambda total: lax.rsqrt(total / D + EPSILON))
        for index, (raw, out) in enumerate(((query_raw, query), (key_raw, key))):
            shape_norm(
                raw,
                inverse[:, index : index + 1],
                gains_of(gain_ref, kinds_of_gain[index], heads),
                angles,
                out,
                heads,
            )
        attend(query, key, value, attended, logs, heads)
        for start, size in tiles(width, 512):
            partial[:, start : start + size] = product_back(
                attended[...], out_w[start : start + size, :]
            ).astype(low)

    kept_kinds = [
        ((length, here), full_type),
        ((length, here), full_type),
        ((length, here), low),
        ((length, here), low),
        ((length, here), low),
        ((length, here), low),
        ((length, HEAD_DIM), full_type),
        ((length, HEAD_DIM), full_type),
    ]

    def self_pre(links, near, kinds, scratch, partial):
        whole, gain_ref, cosine_ref, sine_ref = near[:4]
        forward(
            (0, 1),
            (cosine_ref, sine_ref),
            (whole, whole),
            near[4:8],
            gain_ref,
            kinds[:8],
            scratch,
            links,
            partial,
        )

    def after_self(total, where, near, kinds, first):
        hidden_ref, mixing_ref = near[8:]
        branch_ref, resid_ref = kinds[8:]
        branch_ref[where, :] = total
        resid = hidden_ref[where, :] + total * mixing_ref[2:3]
        resid_ref[where, :] = resid
        unit, _ = normed(resid)
        return (unit * mixing_ref[6:7]).astype(low)

    kept, cross_whole, full, (text_all,), _, _ = plan.phase(
        "self_forward",
        [self_whole, gains, cosine, sine, query_full, key_full, value_full, out_full]
        + [hidden_in, mixing],
        kept_kinds + [((rows, width), full_type)] * 2,
        exchange_scratch(length, plan.tensor),
        self_pre,
        after_self,
        True,
        shape,
        shards=[cross_key, cross_value, cross_query, cross_out.T],
        lines=[text_states],
    )
    self_kept, (self_branch, resid_self) = kept[:8], kept[8:]
    cross_key_full, cross_value_full, cross_query_full, cross_out_full = full

    def cross_begin(links, near, kinds, scratch):
        mixing_ref, cotangent_ref = near[8:]
        whole = kinds[9]
        mine = piece_of(whole, links.z, rows, 0, rows)
        mine[...] = (cotangent_ref[...] * mixing_ref[5:6]).astype(low)
        line = DirectGather(links, whole, rows)
        line.start(mine)
        return line

    def cross_end(line, links, near, kinds, scratch):
        line.finish()

    def cross_pre(links, near, kinds, scratch, partial):
        whole, text, gain_ref = near[:3]
        forward(
            (2, 3), None, (whole, text), near[3:7], gain_ref, kinds[:8], scratch, links, partial
        )

    def after_cross(total, where, near, kinds, first):
        resid_ref, mixing_ref = near[7:9]
        resid = resid_ref[where, :] + total
        kinds[8][where, :] = resid
        unit, _ = normed(resid)
        return (unit * (1.0 + mixing_ref[4:5]) + mixing_ref[3:4]).astype(low)

    kept, feed_whole, full, _, _, _ = plan.phase(
        "cross_forward",
        [cross_whole, text_all, gains]
        + [cross_query_full, cross_key_full, cross_value_full, cross_out_full]
        + [resid_self, mixing, cotangent],
        kept_kinds + [((rows, width), full_type), ((length, width), low)],
        exchange_scratch(length, plan.tensor),
        cross_pre,
        after_cross,
        True,
        shape,
        shards=[up_weight, down_weight.T],
        begin=cross_begin,
        end=cross_end,
    )
    cross_kept, (resid_cross, feed_grad_whole) = kept[:8], kept[8:]
    up_full, down_full = full

    def feed_pre(links, near, kinds, scratch, partial):
        whole, grad_whole, up, down = near[:4]
        activated, grad_raw = scratch
        root = 0.7978845608028654

        def tile(start, size):
            lanes = pl.ds(start, size)
            for first in range(0, length, 256):
                block = slice(first, first + 256)
                raw = jnp.dot(whole[block, :], up[:, lanes], preferred_element_type=full_type)
                grad = jnp.dot(grad_whole[block, :], down[:, lanes], preferred_element_type=full_type)
                square = raw * raw
                bend = jnp.tanh(root * raw * (1.0 + 0.044715 * square))
                half = 0.5 + 0.5 * bend
                activated[block, lanes] = (raw * half).astype(low)
                slope = half + 0.5 * raw * (1.0 - bend * bend) * root * (
                    1.0 + 3.0 * 0.044715 * square
                )
                grad_raw[block, lanes] = (grad * slope).astype(low)

        whole_tiles = hidden_units // 512

        def one(step, _):
            tile(pl.multiple_of(step * 512, 512), 512)
            return 0

        lax.fori_loop(0, whole_tiles, one, 0)
        if hidden_units % 512:
            tile(whole_tiles * 512, hidden_units % 512)
        for start, size in tiles(width, 512):
            partial[:, start : start + size] = product_back(
                grad_raw[...], up[start : start + size, :]
            ).astype(low)

    def feed_tasks(near, kinds, scratch):
        down, activated = near[3], scratch[0]

        def one(start, size):
            kinds[2][:, start : start + size] = product_back(
                activated[...], down[start : start + size, :]
            ).astype(low)

        return [functools.partial(one, start, size) for start, size in tiles(width, 512)]

    def before_feed(total, where, near, kinds, first):
        resid_ref, cotangent_ref, mixing_ref = near[4:]
        grad_ref, sums_ref = kinds[:2]
        unit, inverse = normed(resid_ref[where, :])
        add_sum(sums_ref, 0, total, first)
        add_sum(sums_ref, 1, total * unit, first)
        grad = cotangent_ref[where, :] + normed_back(
            unit, inverse, total * (1.0 + mixing_ref[4:5])
        )
        grad_ref[where, :] = grad
        return grad.astype(low)

    kept, cross_grad_whole, _, _, made, _ = plan.phase(
        "feed",
        [feed_whole, feed_grad_whole, up_full, down_full, resid_cross, cotangent, mixing],
        [((rows, width), full_type), ((8, width), full_type), ((length, width), low)],
        [pltpu.VMEM((length, hidden_units), low), pltpu.VMEM((length, hidden_units), low)],
        feed_pre,
        before_feed,
        True,
        shape,
        jobs=[
            (lambda n, k, s: n[1], lambda n, k, s: s[0], part, hidden_units, True),
            (lambda n, k, s: n[0], lambda n, k, s: s[1], part, hidden_units, False),
        ],
        tasks=feed_tasks,
        exchange=False,
    )
    grad_resid_cross, feed_sums, feed_partial = kept
    sum_down, near_up = made

    def backward(kinds_of_gain, angles, refs, gain_ref, grad_outs, scratch, links, partial):
        (grad_whole, query_w, key_w, value_w, out_w) = refs[:5]
        query_raw, key_raw, value, query, key, attended, logs, inverse = refs[5:]
        gain_query_ref, gain_key_ref, query_out, key_out, value_out = grad_outs
        grad_attended, grad_query, grad_key, grad_value = scratch[3:7]
        exchange = Exchange(links, *scratch[:3])
        grad_attended[...] = jnp.dot(
            grad_whole[...], out_w[...], preferred_element_type=full_type
        ).astype(low)
        attend_back(
            query, key, value, logs, grad_attended, (grad_query, grad_key, grad_value), heads
        )
        sides = (
            (query_raw, inverse[:, 0:1], gains_of(gain_ref, kinds_of_gain[0], heads)),
            (key_raw, inverse[:, 1:2], gains_of(gain_ref, kinds_of_gain[1], heads)),
        )
        exchange.start(
            [
                norm_dots(*sides[0], angles, grad_query, gain_query_ref, heads),
                norm_dots(*sides[1], angles, grad_key, gain_key_ref, heads),
            ]
        )
        value_out[...] = grad_value[...].astype(low)
        dots = exchange.finish()
        norm_pull(*sides[0], dots[:, 0:1], grad_query, query_out, heads)
        norm_pull(*sides[1], dots[:, 1:2], grad_key, key_out, heads)
        pairs = [(query_out, query_w)]
        if angles is not None:
            pairs += [(key_out, key_w), (value_out, value_w)]
        for start, size in tiles(width, 512):
            total = 0.0
            for grads, weight in pairs:
                total = total + product_back(grads[...], weight[start : start + size, :])
            partial[:, start : start + size] = total.astype(low)

    back_scratch = exchange_scratch(length, plan.tensor) + [
        pltpu.VMEM((length, here), low),
        pltpu.VMEM((length, here), full_type),
        pltpu.VMEM((length, here), full_type),
        pltpu.VMEM((length, here), full_type),
        pltpu.VMEM((length, here), low),
        pltpu.VMEM((length, here), low),
        pltpu.VMEM((length, here), low),
    ]

    def cross_back_begin(links, near, kinds, scratch):
        late = DirectReduce(links, near[22], scratch[10], rows)
        late.start()
        return late

    def cross_back_end(late, links, near, kinds, scratch):
        cotangent_ref, mixing_ref, resid_ref = near[19:22]
        late.arrive()
        for start in range(0, rows, 32):
            where = slice(start, start + 32)
            total = late.total(start, 32)
            kinds[2][where, :] = resid_ref[where, :] + total * mixing_ref[5:6]
            add_sum(kinds[1], 2, cotangent_ref[where, :] * total, start == 0)
        late.finish()

    def cross_back_pre(links, near, kinds, scratch, partial):
        backward(
            (2, 3),
            None,
            near[:13],
            near[13],
            (kinds[4], kinds[5], *scratch[7:10]),
            scratch,
            links,
            partial,
        )

    def cross_back_tasks(near, kinds, scratch):
        key_w, value_w = near[2], near[3]

        def one(start, size):
            block = slice(start, start + size)
            kinds[3][:, block] = (
                product_back(scratch[8][...], key_w[block, :])
                + product_back(scratch[9][...], value_w[block, :])
            ).astype(low)

        return [functools.partial(one, start, size) for start, size in tiles(text_width, 1024)]

    def before_cross(total, where, near, kinds, first):
        resid_ref, grad_ref, branch_ref = near[16:19]
        mixing_ref = near[20]
        out_ref, sums_ref = kinds[:2]
        unit, inverse = normed(resid_ref[where, :])
        add_sum(sums_ref, 1, total * unit, first)
        grad = grad_ref[where, :] + normed_back(unit, inverse, total * mixing_ref[6:7])
        out_ref[where, :] = grad
        add_sum(sums_ref, 0, grad * branch_ref[where, :], first)
        return (grad * mixing_ref[2:3]).astype(low)

    kept, self_grad_whole, _, _, made, (sum_up,) = plan.phase(
        "cross_back",
        [cross_grad_whole, cross_query_full, cross_key_full, cross_value_full, cross_out_full]
        + list(cross_kept)
        + [gains, cross_whole, text_all]
        + [resid_self, grad_resid_cross, self_branch, cotangent, mixing, resid_cross]
        + [feed_partial],
        [
            ((rows, width), full_type),
            ((8, width), full_type),
            ((rows, width), full_type),
            ((text_rows, text_width), low),
            ((8, HEAD_DIM), full_type),
            ((8, HEAD_DIM), full_type),
        ],
        back_scratch + [pltpu.VMEM((plan.tensor - 1, rows, width), low)],
        cross_back_pre,
        before_cross,
        True,
        shape,
        sums=[near_up],
        jobs=[
            (lambda n, k, s: n[15], lambda n, k, s: s[8], text_part, here, False),
            (lambda n, k, s: n[15], lambda n, k, s: s[9], text_part, here, False),
            (lambda n, k, s: n[14], lambda n, k, s: s[7], part, here, False),
            (lambda n, k, s: n[0], lambda n, k, s: n[10], part, here, False),
        ],
        tasks=cross_back_tasks,
        begin=cross_back_begin,
        end=cross_back_end,
    )
    grad_resid_self, cross_sums, block_out, text_partial, gain_cross_query, gain_cross_key = kept
    grad_text = lax.psum_scatter(
        text_partial, "tensor", scatter_dimension=0, tiled=True
    ).astype(full_type)

    def self_back_pre(links, near, kinds, scratch, partial):
        backward(
            (0, 1),
            (near[14], near[15]),
            near[:13],
            near[13],
            (kinds[2], kinds[3], *scratch[7:10]),
            scratch,
            links,
            partial,
        )

    def before_self(total, where, near, kinds, first):
        hidden_ref, grad_ref, mixing_ref = near[17:]
        out_ref, sums_ref = kinds[:2]
        unit, inverse = normed(hidden_ref[where, :])
        add_sum(sums_ref, 0, total, first)
        add_sum(sums_ref, 1, total * unit, first)
        out_ref[where, :] = grad_ref[where, :] + normed_back(
            unit, inverse, total * (1.0 + mixing_ref[1:2])
        )

    kept, _, _, _, made, sums = plan.phase(
        "self_back",
        [self_grad_whole, query_full, key_full, value_full, out_full]
        + list(self_kept)
        + [gains, cosine, sine, self_whole, hidden_in, grad_resid_self, mixing],
        [
            ((rows, width), full_type),
            ((8, width), full_type),
            ((8, HEAD_DIM), full_type),
            ((8, HEAD_DIM), full_type),
        ],
        back_scratch,
        self_back_pre,
        before_self,
        False,
        shape,
        sums=made,
        jobs=[
            (lambda n, k, s: n[16], lambda n, k, s: s[7], part, here, True),
            (lambda n, k, s: n[16], lambda n, k, s: s[8], part, here, True),
            (lambda n, k, s: n[16], lambda n, k, s: s[9], part, here, True),
            (lambda n, k, s: n[0], lambda n, k, s: n[10], part, here, True),
        ],
    )
    grad_hidden, self_sums, gain_query, gain_key = kept
    sum_cross_key, sum_cross_value, sum_cross_query, sum_cross_out = sums
    sum_query, sum_key, sum_value, sum_out = made

    time_part = jnp.concatenate(
        [
            self_sums[:2],
            cross_sums[:1],
            feed_sums[:2],
            cross_sums[2:3],
            cross_sums[1:2],
            jnp.zeros((1, width), full_type),
        ],
        axis=0,
    )
    gain_part = jnp.concatenate([gain_query, gain_key, gain_cross_query, gain_cross_key], axis=1)
    time_total, all_total, gain_total = plan.close(time_part, gain_part)
    dp = lax.axis_index("dp")
    mine = lax.dynamic_slice_in_dim(all_total, dp * part, part, axis=1)
    gain_width = qk_gain.shape[1]
    gain_mine = lax.dynamic_slice_in_dim(gain_total[:heads], dp * gain_width, gain_width, axis=1)
    return (
        block_out,
        grad_hidden,
        grad_text,
        time_total[None, :6],
        mine[:6],
        sum_query,
        sum_key,
        sum_value,
        sum_out.T,
        sum_cross_query,
        sum_cross_key,
        sum_cross_value,
        sum_cross_out.T,
        sum_up,
        sum_down.T,
        gain_mine,
        mine[6],
    )


def solution(mesh):
    return jax.shard_map(
        functools.partial(body, Plan(mesh)),
        mesh=mesh,
        in_specs=(
            P(("dp", "tensor"), None),
            P(("dp", "tensor"), None),
            P("dp", None, None),
            P(None, "dp"),
            P(None, "dp"),
            P("dp", "tensor"),
            P("dp", "tensor"),
            P("dp", "tensor"),
            P("tensor", "dp"),
            P("dp", "tensor"),
            P("dp", "tensor"),
            P("dp", "tensor"),
            P("tensor", "dp"),
            P("dp", "tensor"),
            P("tensor", "dp"),
            P("tensor", "dp"),
            P("dp"),
            P(("dp", "tensor"), None),
        ),
        out_specs=(
            P(("dp", "tensor"), None),
            P(("dp", "tensor"), None),
            P(("dp", "tensor"), None),
            P("dp", None, None),
            P(None, "dp"),
            P("dp", "tensor"),
            P("dp", "tensor"),
            P("dp", "tensor"),
            P("tensor", "dp"),
            P("dp", "tensor"),
            P("dp", "tensor"),
            P("dp", "tensor"),
            P("tensor", "dp"),
            P("dp", "tensor"),
            P("tensor", "dp"),
            P("tensor", "dp"),
            P("dp"),
        ),
        check_vma=False,
    )
```

```python
import functools

import jax
import jax.numpy as jnp
from jax import lax
from jax.experimental import pallas as pl
from jax.experimental.pallas import tpu as pltpu
from jax.sharding import PartitionSpec as P

MESH = pl.DeviceIdType.MESH
VMEM_BYTES = 62 * 2**20

HEAD_DIM = 128
D = 1536


EPSILON = 1e-06
CONTRACT_LAST = (((1,), (1,)), ((), ()))
CONTRACT_FIRST = (((0,), (0,)), ((), ()))


def rotary_tables(positions, head_width):
    pairs = head_width // 2
    third = pairs // 3
    first = pairs - 2 * third
    freq_frame = jnp.power(10000.0, -jnp.arange(first, dtype=jnp.float32) / first)
    freq_side = jnp.power(10000.0, -jnp.arange(third, dtype=jnp.float32) / third)
    places = positions.astype(jnp.float32)
    angles = jnp.concatenate(
        [
            places[0][:, None] * jnp.repeat(freq_frame, 2)[None, :],
            places[1][:, None] * jnp.repeat(freq_side, 2)[None, :],
            places[2][:, None] * jnp.repeat(freq_side, 2)[None, :],
        ],
        axis=1,
    )
    sign = jnp.where(jnp.arange(head_width) % 2 == 0, -1.0, 1.0)
    return (jnp.cos(angles), jnp.sin(angles) * sign)


def product_back(grads, weight):
    return lax.dot_general(grads, weight, CONTRACT_LAST, preferred_element_type=jnp.float32)


def weight_grad(inputs, grads):
    return lax.dot_general(inputs, grads, CONTRACT_FIRST, preferred_element_type=jnp.float32)


def when(cond, run):
    if cond is None:
        run()
    else:
        pl.when(cond)(run)


def flip(index, bit):
    return index + bit - 2 * bit * (index // bit % 2)


def normed(values):
    center = values - jnp.mean(values, axis=-1, keepdims=True)
    inverse = lax.rsqrt(jnp.mean(center * center, axis=-1, keepdims=True) + EPSILON)
    return center * inverse, inverse


def normed_back(unit, inverse, grad):
    mean_grad = jnp.mean(grad, axis=-1, keepdims=True)
    mean_dot = jnp.mean(grad * unit, axis=-1, keepdims=True)
    return (grad - mean_grad - unit * mean_dot) * inverse


class Links:
    def __init__(self, send, recv, local, dp_size, tensor_size):
        self.send, self.recv, self.local = send, recv, local
        self.count = 0
        self.local_count = 0
        self.dp_size, self.size = dp_size, tensor_size
        self.dp = lax.axis_index("dp")
        self.z = lax.axis_index("tensor")

    def slot(self):
        self.count += 1
        return self.count - 1

    def copy(self, source, target, device, slot):
        return pltpu.make_async_remote_copy(
            src_ref=source,
            dst_ref=target,
            send_sem=self.send.at[slot],
            recv_sem=self.recv.at[slot],
            device_id=device,
            device_id_type=MESH,
        )

    def here(self, source, target):
        self.local_count += 1
        return pltpu.make_async_copy(source, target, self.local.at[self.local_count - 1])

    def greet(self, groups):
        barrier = pltpu.get_barrier_semaphore()
        peers = []
        if "line" in groups and "zall" not in groups:
            peers += [
                ((self.dp, self.z - 1), self.z > 0),
                ((self.dp, self.z + 1), self.z < self.size - 1),
            ]
        if "zall" in groups:
            peers += [
                ((self.dp, lax.rem(self.z + k, self.size)), None) for k in range(1, self.size)
            ]
        if "dpall" in groups:
            peers += [
                ((lax.rem(self.dp + k, self.dp_size), self.z), None)
                for k in range(1, self.dp_size)
            ]
        if "bits" in groups:
            bit = 1
            while bit < self.dp_size:
                peers.append(((flip(self.dp, bit), self.z), None))
                bit *= 2
        if "diag" in groups:
            peers.append(((flip(flip(self.dp, 2), 4), self.z), None))
        for device, cond in peers:
            when(
                cond,
                lambda device=device: pl.semaphore_signal(
                    barrier, inc=1, device_id=device, device_id_type=MESH
                ),
            )
        expected = sum(1 for _, cond in peers if cond is None)
        for _, cond in peers:
            if cond is not None:
                expected = expected + cond.astype(jnp.int32)
        pl.semaphore_wait(barrier, expected)


def piece_of(ref, block, rows, start, count):
    return ref.at[pl.ds(pl.multiple_of(block * rows + start, 16), count)]


class LineGather:
    def __init__(self, links, whole, rows, pieces):
        self.links, self.whole, self.rows, self.count = links, whole, rows, rows // pieces
        self.pieces = pieces
        hops = links.size - 1
        self.right = [[links.slot() for _ in range(pieces)] for _ in range(hops)]
        self.left = [[links.slot() for _ in range(pieces)] for _ in range(hops)]

    def block(self, index, piece):
        return piece_of(self.whole, index, self.rows, piece * self.count, self.count)

    def move(self, index, piece, way, slot):
        part = self.block(index, piece)
        return self.links.copy(part, part, (self.links.dp, self.links.z + way), slot)

    def start(self, piece):
        z, last = self.links.z, self.links.size - 1
        when(z < last, lambda: self.move(z, piece, 1, self.right[0][piece]).start())
        when(z > 0, lambda: self.move(z, piece, -1, self.left[0][piece]).start())

    def step(self, hop, piece):
        z, last = self.links.z, self.links.size - 1

        def from_left():
            self.move(z - 1 - hop, piece, -1, self.right[hop][piece]).wait_recv()
            if hop + 1 < last:
                when(
                    z < last,
                    lambda: self.move(z - 1 - hop, piece, 1, self.right[hop + 1][piece]).start(),
                )

        def from_right():
            self.move(z + 1 + hop, piece, 1, self.left[hop][piece]).wait_recv()
            if hop + 1 < last:
                when(
                    z > 0,
                    lambda: self.move(z + 1 + hop, piece, -1, self.left[hop + 1][piece]).start(),
                )

        when(z - 1 - hop >= 0, from_left)
        when(z + 1 + hop <= last, from_right)

    def steps(self, piece):
        for hop in range(self.links.size - 1):
            self.step(hop, piece)

    def finish(self):
        z, last = self.links.z, self.links.size - 1
        for hop in range(last):
            for piece in range(self.pieces):
                when(
                    (z - hop >= 0) & (z < last),
                    lambda: self.move(z - hop, piece, 1, self.right[hop][piece]).wait_send(),
                )
                when(
                    (z + hop <= last) & (z > 0),
                    lambda: self.move(z + hop, piece, -1, self.left[hop][piece]).wait_send(),
                )


class LineReduce:
    def __init__(self, links, partial, land_right, land_left, rows, pieces):
        self.links, self.partial, self.rows, self.count = links, partial, rows, rows // pieces
        self.land = {1: land_right, -1: land_left}
        self.pieces = pieces
        last = links.size - 1
        self.slots = {
            way: [None] + [[links.slot() for _ in range(pieces)] for _ in range(last)]
            for way in (1, -1)
        }

    def landing(self, way, distance, piece):
        return self.land[way].at[distance - 1, pl.ds(piece * self.count, self.count)]

    def part(self, index, piece):
        return piece_of(self.partial, index, self.rows, piece * self.count, self.count)

    def move(self, source, way, distance, piece):
        return self.links.copy(
            source,
            self.landing(way, distance, piece),
            (self.links.dp, self.links.z + way),
            self.slots[way][distance][piece],
        )

    def arrived(self, way, distance, piece):
        self.links.copy(
            self.landing(way, distance, piece),
            self.landing(way, distance, piece),
            (self.links.dp, self.links.z - way),
            self.slots[way][distance][piece],
        ).wait_recv()

    def first(self, piece):
        z, last = self.links.z, self.links.size - 1

        def from_first():
            for distance in range(last, 0, -1):
                self.move(self.part(distance, piece), 1, distance, piece).start()

        def from_last():
            for distance in range(last, 0, -1):
                self.move(self.part(last - distance, piece), -1, distance, piece).start()

        when(z == 0, from_first)
        when(z == last, from_last)

    def first_at(self, distance, piece):
        z, last = self.links.z, self.links.size - 1
        when(
            z == 0,
            lambda: self.move(self.part(distance, piece), 1, distance, piece).start(),
        )
        when(
            z == last,
            lambda: self.move(self.part(last - distance, piece), -1, distance, piece).start(),
        )

    def stages(self, piece):
        last = self.links.size - 1

        def one(distance):
            self.first_at(distance, piece)
            if distance < last:
                self.step(distance, piece)

        return [functools.partial(one, distance) for distance in range(last, 0, -1)]

    def clear(self):
        z, last = self.links.z, self.links.size - 1

        def zero(way):
            self.land[way][0] = jnp.zeros(self.land[way].shape[1:], self.land[way].dtype)

        when(z == 0, lambda: zero(1))
        when(z == last, lambda: zero(-1))

    def step(self, distance, piece):
        z, last = self.links.z, self.links.size - 1
        for way in (1, -1):
            inside = (
                (z > 0) & (z + distance <= last)
                if way == 1
                else (z < last) & (z - distance >= 0)
            )

            def go(way=way):
                self.arrived(way, distance + 1, piece)
                held = self.landing(way, distance + 1, piece)
                own = self.part(z + way * distance, piece)
                held[...] = (
                    held[...].astype(jnp.float32) + own[...].astype(jnp.float32)
                ).astype(held.dtype)
                self.move(held, way, distance, piece).start()

            when(inside, go)

    def total(self, piece):
        z, last = self.links.z, self.links.size - 1
        when(z > 0, lambda: self.arrived(1, 1, piece))
        when(z < last, lambda: self.arrived(-1, 1, piece))
        return (
            self.part(z, piece)[...].astype(jnp.float32)
            + self.landing(1, 1, piece)[...].astype(jnp.float32)
            + self.landing(-1, 1, piece)[...].astype(jnp.float32)
        )

    def finish(self):
        z, last = self.links.z, self.links.size - 1
        for distance in range(1, last + 1):
            for piece in range(self.pieces):
                held = self.landing(1, distance, piece)
                when(
                    z + distance <= last,
                    lambda: self.move(held, 1, distance, piece).wait_send(),
                )
                back = self.landing(-1, distance, piece)
                when(
                    z - distance >= 0,
                    lambda: self.move(back, -1, distance, piece).wait_send(),
                )


def reduce_stages(reduce):
    return [
        functools.partial(reduce.step, distance)
        for distance in range(reduce.links.size - 2, 0, -1)
    ]


def wave(stages, pieces, queue):
    count = pieces + len(stages) - 1
    done = 0
    for step in range(count):
        for index, stage in enumerate(stages):
            if 0 <= step - index < pieces:
                stage(step - index)
        until = len(queue) * (step + 1) // count
        for run in queue[done:until]:
            run()
        done = until


class CubeGather:
    def __init__(self, links, shard, whole):
        self.links, self.shard, self.whole = links, shard, whole
        self.rows = shard.shape[0]
        self.slots = [links.slot() for _ in range(8)]
        dp = links.dp
        self.core, self.side, self.over = flip(dp, 1), flip(dp, 2), flip(dp, 4)
        self.far = flip(flip(dp, 2), 4)
        self.sent = []

    def block(self, index, start=0, count=None):
        return piece_of(self.whole, index, self.rows, start, count or self.rows)

    def send(self, source, target, device, slot):
        move = self.links.copy(source, target, (device, self.links.z), self.slots[slot])
        move.start()
        self.sent.append(move)

    def got(self, part, slot):
        self.links.copy(part, part, (self.core, self.links.z), self.slots[slot]).wait_recv()

    def start(self):
        mine = self.block(self.links.dp)
        self.own = self.links.here(self.shard, mine)
        self.own.start()
        self.send(self.shard, mine, self.side, 1)
        self.send(self.shard, mine, self.over, 2)
        self.send(self.shard, mine, self.core, 0)

    def forward(self):
        half = self.rows // 2
        self.got(self.block(self.side), 1)
        part = self.block(self.side, 0, half)
        self.send(part, part, self.over, 3)
        part = self.block(self.side)
        self.send(part, part, self.core, 5)
        self.got(self.block(self.over), 2)
        part = self.block(self.over, half, half)
        self.send(part, part, self.side, 4)
        part = self.block(self.over)
        self.send(part, part, self.core, 6)

    def tail(self):
        half = self.rows // 2
        self.got(self.block(self.far, 0, half), 3)
        self.got(self.block(self.far, half, half), 4)
        part = self.block(self.far)
        self.send(part, part, self.core, 7)

    def finish(self):
        self.got(self.block(self.core), 0)
        self.got(self.block(flip(self.core, 2)), 5)
        self.got(self.block(flip(self.core, 4)), 6)
        self.got(self.block(flip(flip(self.core, 2), 4)), 7)
        for move in self.sent:
            move.wait_send()
        self.own.wait()


class DirectGather:
    def __init__(self, links, whole, rows):
        self.links, self.whole, self.rows = links, whole, rows
        self.slots = [links.slot() for _ in range(links.size - 1)]

    def start(self, source):
        links = self.links
        mine = piece_of(self.whole, links.z, self.rows, 0, self.rows)
        self.moves = [
            links.copy(source, mine, (links.dp, lax.rem(links.z + step, links.size)), slot)
            for step, slot in enumerate(self.slots, 1)
        ]
        for move in self.moves:
            move.start()

    def finish(self):
        for move in self.moves:
            move.wait_recv()
        for move in self.moves:
            move.wait_send()


class Exchange:
    def __init__(self, links, mine, land, turned):
        self.links, self.mine, self.land, self.turned = links, mine, land, turned
        self.slots = [links.slot() for _ in range(links.size - 1)]

    def start(self, columns):
        links = self.links
        lane = lax.broadcasted_iota(jnp.int32, (columns[0].shape[0], 128), 1)
        flat = jnp.zeros(lane.shape, jnp.float32)
        for index, column in enumerate(columns):
            flat = jnp.where(lane == index, column, flat)
        self.mine[...] = flat.T[:8]
        self.moves = [
            links.copy(
                self.mine,
                self.land.at[step - 1],
                (links.dp, lax.rem(links.z + step, links.size)),
                slot,
            )
            for step, slot in enumerate(self.slots, 1)
        ]
        for move in self.moves:
            move.start()

    def finish(self, shape=lambda total: total):
        total = self.mine[...]
        for step, move in enumerate(self.moves):
            move.wait_recv()
            total = total + self.land[step]
        self.turned[...] = jnp.zeros(self.turned.shape, jnp.float32)
        self.turned[0:8, :] = shape(total)
        for move in self.moves:
            move.wait_send()
        return self.turned[...].T


class CoreSum:
    def __init__(self, links, left, right, product, near):
        self.links, self.left, self.right = links, left, right
        self.product, self.near = product, near
        self.rows = near.shape[1]
        self.slots = [links.slot() for _ in range(4)]
        self.core = links.dp % 2
        self.moves = []

    def multiply(self, chip):
        links, count = self.links, 2 * self.rows
        self.product[chip * count : (chip + 1) * count, :] = weight_grad(
            self.left[:, chip * count : (chip + 1) * count], self.right[...]
        ).astype(jnp.bfloat16)
        move = links.copy(
            piece_of(self.product, 2 * chip + 1 - self.core, self.rows, 0, self.rows),
            self.near.at[chip],
            (flip(links.dp, 1), links.z),
            self.slots[chip],
        )
        move.start()
        self.moves.append(move)

    def add(self):
        for move in self.moves:
            move.wait_recv()

        def one(step, _):
            rows = pl.ds(pl.multiple_of(step * 16, 16), 16)
            for chip in range(4):
                own = pl.ds(
                    pl.multiple_of((2 * chip + self.core) * self.rows + step * 16, 16), 16
                )
                self.near[chip, rows, :] = (
                    self.near[chip, rows, :].astype(jnp.float32)
                    + self.product[own, :].astype(jnp.float32)
                ).astype(jnp.bfloat16)
            return 0

        lax.fori_loop(0, self.rows // 16, one, 0)

    def clear(self):
        for move in self.moves:
            move.wait_send()

    def steps(self):
        return [functools.partial(self.multiply, chip) for chip in range(4)] + [self.add]


class ChipSum:
    def __init__(self, links, near, out, others, own=None):
        self.links, self.near, self.out, self.others, self.own = links, near, out, others, own
        self.slots = [links.slot() for _ in range(3)]
        self.core, self.chip = links.dp % 2, links.dp // 2
        self.rows = out.shape[0]

    def start(self):
        links = self.links
        chips = [flip(self.chip, 1), flip(self.chip, 2), flip(flip(self.chip, 1), 2)]
        self.moves = [
            links.copy(
                self.near.at[chip],
                self.others.at[index],
                (2 * chip + self.core, links.z),
                self.slots[index],
            )
            for index, chip in enumerate(chips)
        ]
        for move in self.moves:
            move.start()
        if self.own is not None:
            self.local = links.here(self.near.at[self.chip], self.own)
            self.local.start()

    def finish(self):
        for move in self.moves:
            move.wait_recv()
        if self.own is not None:
            self.local.wait()

        def one(step, _):
            rows = pl.ds(pl.multiple_of(step * 16, 16), 16)
            mine = self.own[rows, :] if self.own is not None else self.near[self.chip, rows, :]
            total = mine.astype(jnp.float32)
            for index in range(3):
                total = total + self.others[index, rows, :].astype(jnp.float32)
            self.out[rows, :] = total
            return 0

        lax.fori_loop(0, self.rows // 16, one, 0)
        for move in self.moves:
            move.wait_send()


def attend(query, key, value, out, logs, heads, chunk=256):
    scale = HEAD_DIM**-0.5
    for head in range(heads):
        lanes = slice(head * HEAD_DIM, (head + 1) * HEAD_DIM)

        def one(step, _, head=head, lanes=lanes):
            rows = pl.ds(pl.multiple_of(step * chunk, chunk), chunk)
            scores = product_back(query[rows, lanes], key[:, lanes]) * scale
            top = jnp.max(scores, axis=-1, keepdims=True)
            expo = jnp.exp(scores - top)
            summed = jnp.sum(expo, axis=-1, keepdims=True)
            probs = (expo * (1.0 / summed)).astype(jnp.bfloat16)
            out[rows, lanes] = jnp.dot(
                probs, value[:, lanes], preferred_element_type=jnp.float32
            ).astype(jnp.bfloat16)
            logs[rows, head : head + 1] = top + jnp.log(summed)
            return 0

        lax.fori_loop(0, query.shape[0] // chunk, one, 0)


def attend_back(query, key, value, logs, grad, grads, heads, chunk=256):
    scale = HEAD_DIM**-0.5
    grad_query, grad_key, grad_value = grads
    grad_key[...] = jnp.zeros(grad_key.shape, jnp.float32)
    grad_value[...] = jnp.zeros(grad_value.shape, jnp.float32)
    for head in range(heads):
        lanes = slice(head * HEAD_DIM, (head + 1) * HEAD_DIM)

        def one(step, _, head=head, lanes=lanes):
            rows = pl.ds(pl.multiple_of(step * chunk, chunk), chunk)
            scores = product_back(query[rows, lanes], key[:, lanes]) * scale
            probs = jnp.exp(scores - logs[rows, head : head + 1])
            prob_grad = product_back(grad[rows, lanes], value[:, lanes])
            inner = jnp.sum(prob_grad * probs, axis=-1, keepdims=True)
            score_grad = (probs * (prob_grad - inner)).astype(jnp.bfloat16)
            grad_query[rows, lanes] = (
                jnp.dot(score_grad, key[:, lanes], preferred_element_type=jnp.float32) * scale
            )
            grad_key[:, lanes] += weight_grad(score_grad, query[rows, lanes]) * scale
            grad_value[:, lanes] += weight_grad(probs.astype(jnp.bfloat16), grad[rows, lanes])
            return 0

        lax.fori_loop(0, query.shape[0] // chunk, one, 0)


def swapped(values):
    lane = lax.broadcasted_iota(jnp.int32, values.shape, 1)
    width = values.shape[1]
    return jnp.where(lane % 2 == 0, pltpu.roll(values, width - 1, 1), pltpu.roll(values, 1, 1))


def turn(values, cosine, sine, back):
    other = swapped(values) * sine
    return values * cosine - other if back else values * cosine + other


def square_columns(*arrays):
    return [jnp.sum(array * array, axis=-1, keepdims=True) for array in arrays]


def shape_norm(raw, inverse, gain, angles, out, heads, chunk=128):
    for head in range(heads):
        lanes = slice(head * HEAD_DIM, (head + 1) * HEAD_DIM)
        for start in range(0, raw.shape[0], chunk):
            rows = slice(start, start + chunk)
            values = raw[rows, lanes] * inverse[rows] * gain[head]
            if angles is not None:
                values = turn(values, angles[0][rows, :], angles[1][rows, :], False)
            out[rows, lanes] = values.astype(jnp.bfloat16)


def norm_dots(raw, inverse, gain, angles, grad, gain_out, heads, chunk=128):
    columns = []
    for start in range(0, raw.shape[0], chunk):
        rows = slice(start, start + chunk)
        column = jnp.zeros((chunk, 1), jnp.float32)
        for head in range(heads):
            lanes = slice(head * HEAD_DIM, (head + 1) * HEAD_DIM)
            values = grad[rows, lanes]
            if angles is not None:
                values = turn(values, angles[0][rows, :], angles[1][rows, :], True)
                grad[rows, lanes] = values
            part = values * raw[rows, lanes]
            column = column + jnp.sum(part * gain[head], axis=-1, keepdims=True)
            total = jnp.sum(part * inverse[rows], axis=0, keepdims=True)
            where = slice(head, head + 1)
            gain_out[where, :] = total if start == 0 else gain_out[where, :] + total
        columns.append(column)
    return jnp.concatenate(columns, axis=0)


def norm_pull(raw, inverse, gain, dots, grad, out, heads, chunk=128):
    for start in range(0, raw.shape[0], chunk):
        rows = slice(start, start + chunk)
        scale = inverse[rows]
        cut = dots[rows] * scale * scale * scale * (1.0 / D)
        for head in range(heads):
            lanes = slice(head * HEAD_DIM, (head + 1) * HEAD_DIM)
            out[rows, lanes] = (
                grad[rows, lanes] * gain[head] * scale - raw[rows, lanes] * cut
            ).astype(jnp.bfloat16)


def gains_of(gain_ref, kind, heads):
    lanes = slice(kind * HEAD_DIM, (kind + 1) * HEAD_DIM)
    return [gain_ref[head : head + 1, lanes] for head in range(heads)]


def exchange_scratch(length, size):
    return [
        pltpu.VMEM((8, length), jnp.float32),
        pltpu.VMEM((size - 1, 8, length), jnp.float32),
        pltpu.VMEM((128, length), jnp.float32),
    ]


class Plan:
    def __init__(self, mesh):
        self.dp = mesh.shape["dp"]
        self.tensor = mesh.shape["tensor"]
        self.cube = self.dp == 8
        self.calls = 0
        self.pieces = 4

    def call(self, name, body, inputs, outputs, scratch, copies):
        self.calls += 1
        spaces = {True: pltpu.VMEM, False: pltpu.HBM}
        count_in, count_out = len(inputs), len(outputs)

        def kernel(*refs):
            ins = refs[:count_in]
            outs = refs[count_in : count_in + count_out]
            rest = refs[count_in + count_out :]
            links = Links(rest[0], rest[1], rest[2], self.dp, self.tensor)
            body(links, ins, outs, rest[3:])

        return pl.pallas_call(
            kernel,
            name=name,
            out_shape=[jax.ShapeDtypeStruct(shape, kind) for shape, kind, _ in outputs],
            in_specs=[pl.BlockSpec(memory_space=spaces[near]) for _, near in inputs],
            out_specs=[pl.BlockSpec(memory_space=spaces[near]) for _, _, near in outputs],
            scratch_shapes=[
                pltpu.SemaphoreType.DMA((copies,)),
                pltpu.SemaphoreType.DMA((copies,)),
                pltpu.SemaphoreType.DMA((64,)),
                *scratch,
            ],
            compiler_params=pltpu.CompilerParams(
                collective_id=self.calls, has_side_effects=True, vmem_limit_bytes=VMEM_BYTES
            ),
        )(*[array for array, _ in inputs])

    def gather_outputs(self, shards):
        return [
            ((self.dp * shard.shape[0], shard.shape[1]), shard.dtype, False) for shard in shards
        ]

    def open(self, hidden, time_rows, small, shards):
        rows, width = hidden.shape
        part = width // self.dp
        gain_part = small.shape[1] - part
        moving = shards if self.cube else []

        def body(links, ins, outs, scratch):
            hidden_ref, time_ref, small_ref = ins[:3]
            table_ref, gain_ref, whole_ref = outs[:3]
            (land,) = scratch
            links.greet({"line", "dpall"})
            gathers = [CubeGather(links, a, b) for a, b in zip(ins[3:], outs[3:])]
            dp, z = links.dp, links.z
            moves = []
            for step in range(1, self.dp):
                target = lax.rem(dp + step, self.dp)
                move = links.copy(small_ref, land.at[dp], (target, z), links.slot())
                move.start()
                moves.append(move)
            for item in gathers:
                item.start()
            land[dp] = small_ref[...]
            unit, _ = normed(hidden_ref[...])
            for move in moves:
                move.wait_recv()
            table = jnp.concatenate([land[k][:, :part] for k in range(self.dp)], axis=1)
            gain_ref[...] = jnp.concatenate([land[k][:, part:] for k in range(self.dp)], axis=1)
            table = table + time_ref[...]
            table_ref[...] = table
            line = LineGather(links, whole_ref, rows, 4)
            first = unit * (1.0 + table[1:2]) + table[0:1]
            whole_ref[pl.ds(pl.multiple_of(z * rows, 16), rows), :] = first.astype(jnp.bfloat16)
            for piece in range(4):
                line.start(piece)
            for piece in range(4):
                line.steps(piece)
                if piece < len(gathers):
                    gathers[piece].forward()
            for item in gathers[4:]:
                item.forward()
            for item in gathers:
                item.tail()
            for item in gathers:
                item.finish()
            line.finish()
            for move in moves:
                move.wait_send()

        results = self.call(
            "open",
            body,
            [(hidden, True), (time_rows, True), (small, True)] + [(s, False) for s in moving],
            [
                ((8, width), jnp.float32, True),
                ((8, gain_part * self.dp), jnp.float32, True),
                ((rows * self.tensor, width), jnp.bfloat16, True),
            ]
            + self.gather_outputs(moving),
            [pltpu.VMEM((self.dp, 8, small.shape[1]), jnp.float32)],
            160,
        )
        return results[:3], self.gathered(results[3:], shards)

    def gathered(self, moved, shards):
        if self.cube:
            return list(moved)
        return [lax.all_gather(shard, "dp", axis=0, tiled=True) for shard in shards]

    def phase(
        self,
        name,
        near,
        kinds,
        scratch,
        pre,
        post,
        gather,
        shape,
        shards=(),
        lines=(),
        sums=(),
        jobs=(),
        tasks=None,
        begin=None,
        end=None,
        exchange=True,
        far=(),
    ):
        length, width = shape
        rows = length // self.tensor
        pieces = self.pieces
        shards, lines, sums, far = list(shards), list(lines), list(sums), list(far)
        moving = shards if self.cube else []
        adding = sums if self.cube else []
        jobs = list(jobs)
        here = [job for job in jobs if job[4]] if self.cube else []
        count_near, count_kinds, count_scratch = len(near), len(kinds), len(scratch)

        job_scratch, job_outputs = [], []
        products, seats = {}, []
        for left, right, part, columns, now in jobs:
            if not self.cube:
                seats.append(("out", len(job_outputs)))
                job_outputs.append(((self.dp * part, columns), jnp.bfloat16, True))
                continue
            key = (part, columns)
            if key not in products:
                products[key] = len(job_scratch)
                job_scratch.append(pltpu.VMEM((8 * part, columns), jnp.bfloat16))
            if now:
                seats.append((products[key], len(job_scratch), len(job_outputs)))
                job_scratch.append(pltpu.VMEM((4, part, columns), jnp.bfloat16))
                job_scratch.append(pltpu.VMEM((3, part, columns), jnp.bfloat16))
                job_outputs.append(((part, columns), jnp.float32, True))
            else:
                seats.append((products[key], len(job_scratch), len(job_outputs)))
                job_scratch.append(pltpu.VMEM((4, part, columns), jnp.bfloat16))
                job_outputs.append(((4, part, columns), jnp.bfloat16, False))
        sum_scratch, sum_outputs = [], []
        for item in adding:
            _, part, columns = item.shape
            sum_scratch.append(pltpu.VMEM((3, part, columns), jnp.bfloat16))
            sum_scratch.append(pltpu.VMEM((part, columns), jnp.bfloat16))
            sum_outputs.append(((part, columns), jnp.float32, True))

        def body(links, ins, outs, rest):
            near_far, ins = ins[:count_near], ins[count_near:]
            shard_refs, ins = ins[: len(moving)], ins[len(moving) :]
            line_refs, ins = ins[: len(lines)], ins[len(lines) :]
            sum_refs, far_refs = ins[: len(adding)], ins[len(adding) :]
            kind_far, outs = outs[:count_kinds], outs[count_kinds:]
            if gather:
                whole_far, outs = outs[0], outs[1:]
            full_refs, outs = outs[: len(moving)], outs[len(moving) :]
            line_outs, outs = outs[: len(lines)], outs[len(lines) :]
            job_refs, added_refs = outs[: len(jobs)], outs[len(jobs) :]
            near_refs, rest = rest[:count_near], rest[count_near:]
            loads = {}
            for index in order:
                copy = links.here(near_far[index], near_refs[index])
                copy.start()
                loads.setdefault(near[index][1], []).append(copy)

            def ready(group):
                for copy in loads.pop(group, []):
                    copy.wait()

            links.ready = ready
            kind_refs, stores = [], []
            for far_ref, (_, _, when_done) in zip(kind_far, kinds):
                if when_done is None:
                    kind_refs.append(far_ref)
                else:
                    kind_refs.append(rest[0])
                    rest = rest[1:]

            def store(source, target):
                stores.append(links.here(source, target))
                stores[-1].start()

            def store_kinds(moment):
                for held, far_ref, (_, _, when_done) in zip(kind_refs, kind_far, kinds):
                    if when_done == moment:
                        store(held, far_ref)

            if gather:
                whole_ref, rest = rest[0], rest[1:]
            partial_ref, land_right, land_left = rest[:3]
            user, rest = rest[3 : 3 + count_scratch], rest[3 + count_scratch :]
            job_rest, sum_rest = rest[: len(job_scratch)], rest[len(job_scratch) :]

            groups = {"zall"} if exchange else {"line"}
            if moving or adding or jobs:
                groups |= {"bits"} if self.cube else set()
            if adding or here:
                groups |= {"diag"}
            links.greet(groups)
            gathers = [CubeGather(links, a, b) for a, b in zip(shard_refs, full_refs)]
            straight = [
                DirectGather(links, b, a.shape[0]) for a, b in zip(line_refs, line_outs)
            ]
            old = [
                ChipSum(links, a, b, sum_rest[2 * k], sum_rest[2 * k + 1])
                for k, (a, b) in enumerate(zip(sum_refs, added_refs))
            ]
            for item in gathers + old:
                item.start()
            copies = []
            for item, source in zip(straight, line_refs):
                item.start(source)
                copies.append(
                    links.here(source, piece_of(item.whole, links.z, item.rows, 0, item.rows))
                )
                copies[-1].start()
            state = begin(links, near_refs, kind_refs, user, far_refs) if begin else (None, [])
            ticks = state[1]
            pre(links, near_refs, kind_refs, user, partial_ref, ticks)
            for run in ticks:
                run()
            store_kinds("pre")
            for group in sorted(loads):
                ready(group)

            queue = list(tasks(links, near_refs, kind_refs, user, far_refs)) if tasks else []
            fresh, busy, cleared = [], {}, []
            for (left, right, part, columns, now), seat in zip(jobs, seats):
                left_ref, right_ref = left(near_refs, kind_refs, user), right(near_refs, kind_refs, user)
                out = job_refs[seat[-1]]
                if not self.cube:

                    def whole(start, left_ref=left_ref, right_ref=right_ref, out=out):
                        count = out.shape[0] // 4
                        where = slice(start * count, (start + 1) * count)
                        out[where, :] = weight_grad(left_ref[:, where], right_ref[...]).astype(
                            jnp.bfloat16
                        )

                    queue += [functools.partial(whole, start) for start in range(4)]
                    continue
                held = job_rest[seat[1]]
                item = CoreSum(links, left_ref, right_ref, job_rest[seat[0]], held)
                if seat[0] in busy:
                    queue.append(busy[seat[0]].clear)
                    cleared.append(busy[seat[0]])
                busy[seat[0]] = item
                queue += item.steps()
                if now:
                    chip = ChipSum(links, held, out, job_rest[seat[1] + 1])
                    queue.append(chip.start)
                    fresh.append(chip)
                else:
                    queue.append(functools.partial(store, held, out))
            queue += [item.forward for item in gathers]
            queue += [item.tail for item in gathers]

            reduce = LineReduce(links, partial_ref, land_right, land_left, rows, pieces)
            line = LineGather(links, whole_ref, rows, pieces) if gather else None
            for piece in range(pieces):
                reduce.first(piece)
            reduce.clear()

            def settle(piece):
                where = pl.ds(piece * (rows // pieces), rows // pieces)
                result = post(reduce.total(piece), where, near_refs, kind_refs, piece == 0)
                if gather:
                    line.block(links.z, piece)[...] = result
                    line.start(piece)

            stages = reduce_stages(reduce) + [settle]
            if gather:
                stages += [functools.partial(line.step, hop) for hop in range(links.size - 1)]
            wave(stages, pieces, queue)
            for item in gathers + old + fresh + straight:
                item.finish()
            for item in busy.values():
                item.clear()
            for copy in copies:
                copy.wait()
            if end:
                end(state[0], links, near_refs, kind_refs, user)
            store_kinds("post")
            if gather:
                store(whole_ref, whole_far)
            reduce.finish()
            if gather:
                line.finish()
            for copy in stores:
                copy.wait()

        order = sorted(range(count_near), key=lambda index: near[index][1])
        inputs = [(item, False) for item, _ in near]
        inputs += [(item, False) for item in moving + lines + adding + far]
        outputs = [(form, kind, False) for form, kind, _ in kinds]
        if gather:
            outputs.append(((length, width), jnp.bfloat16, False))
        outputs += self.gather_outputs(moving)
        outputs += [
            ((item.shape[0] * self.tensor, item.shape[1]), item.dtype, False) for item in lines
        ]
        outputs += job_outputs + sum_outputs
        results = list(
            self.call(
                name,
                body,
                inputs,
                outputs,
                [pltpu.VMEM(item.shape, item.dtype) for item, _ in near]
                + [pltpu.VMEM(form, kind) for form, kind, moment in kinds if moment]
                + ([pltpu.VMEM((length, width), jnp.bfloat16)] if gather else [])
                + [
                    pltpu.VMEM((length, width), jnp.bfloat16),
                    pltpu.VMEM((self.tensor - 1, rows, width), jnp.bfloat16),
                    pltpu.VMEM((self.tensor - 1, rows, width), jnp.bfloat16),
                    *scratch,
                    *job_scratch,
                    *sum_scratch,
                ],
                240,
            )
        )
        kept, results = results[:count_kinds], results[count_kinds:]
        whole, results = (results[0], results[1:]) if gather else (None, results)
        full, results = self.gathered(results[: len(moving)], shards), results[len(moving) :]
        lined, results = results[: len(lines)], results[len(lines) :]
        made, added = results[: len(jobs)], results[len(jobs) :]
        if not self.cube:
            made = [
                self.scatter(item) if job[4] else item for item, job in zip(made, jobs)
            ]
            added = [self.scatter(item) for item in sums]
        return kept, whole, full, lined, made, added

    def scatter(self, grad):
        return lax.psum_scatter(grad, "dp", scatter_dimension=0, tiled=True).astype(jnp.float32)

    def close(self, time_part, gain_part):
        bits = [1 << k for k in range(self.dp.bit_length() - 1)]

        def body(links, ins, outs, scratch):
            time_ref, gain_ref = ins[:2]
            total_ref, all_ref, gains_ref = outs[:3]
            land, held, held_gain, come, come_gain = scratch[:5]
            links.greet({"zall", "bits"})
            moves = []
            for step in range(1, self.tensor):
                target = lax.rem(links.z + step, self.tensor)
                move = links.copy(time_ref, land.at[links.z], (links.dp, target), links.slot())
                move.start()
                moves.append(move)
            land[links.z] = time_ref[...]
            held_gain[0] = gain_ref[...]
            for move in moves:
                move.wait_recv()
            total = land[0]
            for index in range(1, self.tensor):
                total = total + land[index]
            total_ref[...] = total
            held[0] = total
            for index, bit in enumerate(bits):
                target = (flip(links.dp, bit), links.z)
                one = links.copy(held.at[index], come.at[index], target, links.slot())
                two = links.copy(held_gain.at[index], come_gain.at[index], target, links.slot())
                one.start()
                two.start()
                one.wait_recv()
                two.wait_recv()
                held[index + 1] = held[index] + come[index]
                held_gain[index + 1] = held_gain[index] + come_gain[index]
                moves += [one, two]
            all_ref[...] = held[len(bits)]
            gains_ref[...] = held_gain[len(bits)]
            for move in moves:
                move.wait_send()

        levels = len(bits)
        results = self.call(
            "close",
            body,
            [(time_part, True), (gain_part, True)],
            [
                (time_part.shape, jnp.float32, True),
                (time_part.shape, jnp.float32, True),
                (gain_part.shape, jnp.float32, True),
            ],
            [
                pltpu.VMEM((self.tensor, *time_part.shape), jnp.float32),
                pltpu.VMEM((levels + 1, *time_part.shape), jnp.float32),
                pltpu.VMEM((levels + 1, *gain_part.shape), jnp.float32),
                pltpu.VMEM((levels, *time_part.shape), jnp.float32),
                pltpu.VMEM((levels, *gain_part.shape), jnp.float32),
            ],
            80,
        )
        return results


def add_sum(ref, row, values, first):
    total = jnp.sum(values, axis=0, keepdims=True)
    ref[row : row + 1, :] = total if first else ref[row : row + 1, :] + total


def tick(ticks):
    if ticks:
        ticks.pop(0)()


def tiles(count, size):
    return [(start, min(size, count - start)) for start in range(0, count, size)]


def body(
    plan,
    hidden_in,
    text_states,
    time_embed,
    positions,
    modulation,
    query_weight,
    key_weight,
    value_weight,
    out_weight,
    cross_query,
    cross_key,
    cross_value,
    cross_out,
    up_weight,
    down_weight,
    qk_gain,
    norm_gain,
    cotangent,
):
    plan.calls = 0
    low, full_type = jnp.bfloat16, jnp.float32
    rows, width = hidden_in.shape
    length = rows * plan.tensor
    here = out_weight.shape[0]
    heads = here // HEAD_DIM
    hidden_units = up_weight.shape[1]
    text_rows, text_width = length, text_states.shape[1]
    part = width // plan.dp
    text_part = text_width // plan.dp
    shape = (length, width)

    top = jnp.concatenate([modulation, norm_gain[None], jnp.zeros((1, part), low)], axis=0)
    side = jnp.pad(qk_gain, ((0, 8 - heads), (0, 0)))
    small = jnp.concatenate([top, side], axis=1).astype(full_type)
    time_rows = jnp.pad(time_embed[0], ((0, 2), (0, 0)))
    (mixing, gains, self_whole), full = plan.open(
        hidden_in, time_rows, small, [query_weight, key_weight, value_weight, out_weight.T]
    )
    query_full, key_full, value_full, out_full = full
    cosine, sine = rotary_tables(positions, HEAD_DIM)

    def forward(kinds_of_gain, angles, inputs, weights, gain_ref, kinds, scratch, links, partial, ticks):
        query_in, other_in = inputs
        query_w, key_w, value_w, out_w = weights
        query_raw, key_raw, value, query, key, attended, logs, inverse = kinds
        exchange = Exchange(links, *scratch)
        links.ready(0)
        query_raw[...] = jnp.dot(query_in[...], query_w[...], preferred_element_type=full_type)
        links.ready(1)
        key_raw[...] = jnp.dot(other_in[...], key_w[...], preferred_element_type=full_type)
        exchange.start(square_columns(query_raw[...], key_raw[...]))
        links.ready(2)
        value[...] = jnp.dot(
            other_in[...], value_w[...], preferred_element_type=full_type
        ).astype(low)
        inverse[...] = exchange.finish(lambda total: lax.rsqrt(total / D + EPSILON))
        tick(ticks)
        links.ready(3)
        for index, (raw, out) in enumerate(((query_raw, query), (key_raw, key))):
            shape_norm(
                raw,
                inverse[:, index : index + 1],
                gains_of(gain_ref, kinds_of_gain[index], heads),
                angles,
                out,
                heads,
            )
        attend(query, key, value, attended, logs, heads)
        tick(ticks)
        links.ready(4)
        for start, size in tiles(width, 512):
            partial[:, start : start + size] = product_back(
                attended[...], out_w[start : start + size, :]
            ).astype(low)

    kept_kinds = [
        ((length, here), full_type, "pre"),
        ((length, here), full_type, "pre"),
        ((length, here), low, "pre"),
        ((length, here), low, "pre"),
        ((length, here), low, "pre"),
        ((length, here), low, "pre"),
        ((length, HEAD_DIM), full_type, "pre"),
        ((length, HEAD_DIM), full_type, "pre"),
    ]

    def self_pre(links, near, kinds, scratch, partial, ticks):
        whole, gain_ref, cosine_ref, sine_ref = near[:4]
        forward(
            (0, 1),
            (cosine_ref, sine_ref),
            (whole, whole),
            near[4:8],
            gain_ref,
            kinds[:8],
            scratch,
            links,
            partial,
            ticks,
        )

    def after_self(total, where, near, kinds, first):
        hidden_ref, mixing_ref = near[8:]
        branch_ref, resid_ref = kinds[8:]
        branch_ref[where, :] = total
        resid = hidden_ref[where, :] + total * mixing_ref[2:3]
        resid_ref[where, :] = resid
        unit, _ = normed(resid)
        return (unit * mixing_ref[6:7]).astype(low)

    text_after, self_whole = lax.optimization_barrier((text_states, self_whole))
    text_all = lax.all_gather(text_after, "tensor", axis=0, tiled=True)
    kept, cross_whole, full, _, _, _ = plan.phase(
        "self_forward",
        [(self_whole, 0), (gains, 3), (cosine, 3), (sine, 3), (query_full, 0), (key_full, 1)]
        + [(value_full, 2), (out_full, 4), (hidden_in, 5), (mixing, 5)],
        kept_kinds + [((rows, width), full_type, "post")] * 2,
        exchange_scratch(length, plan.tensor),
        self_pre,
        after_self,
        True,
        shape,
        shards=[cross_key, cross_value, cross_query, cross_out.T, up_weight, down_weight.T],
    )
    self_kept, (self_branch, resid_self) = kept[:8], kept[8:]
    cross_key_full, cross_value_full, cross_query_full, cross_out_full = full[:4]
    up_full, down_full = full[4:]

    def cross_begin(links, near, kinds, scratch, far):
        links.ready(-1)
        mixing_ref, cotangent_ref = near[8:]
        whole = kinds[9]
        mine = piece_of(whole, links.z, rows, 0, rows)
        mine[...] = (cotangent_ref[...] * mixing_ref[5:6]).astype(low)
        line = LineGather(links, whole, rows, 1)
        line.start(0)
        return line, [functools.partial(line.step, hop, 0) for hop in range(links.size - 1)]

    def cross_end(line, links, near, kinds, scratch):
        line.finish()

    def cross_pre(links, near, kinds, scratch, partial, ticks):
        whole, text, gain_ref = near[:3]
        forward(
            (2, 3),
            None,
            (whole, text),
            near[3:7],
            gain_ref,
            kinds[:8],
            scratch,
            links,
            partial,
            ticks,
        )

    def after_cross(total, where, near, kinds, first):
        resid_ref, mixing_ref = near[7:9]
        resid = resid_ref[where, :] + total
        kinds[8][where, :] = resid
        unit, _ = normed(resid)
        return (unit * (1.0 + mixing_ref[4:5]) + mixing_ref[3:4]).astype(low)

    kept, feed_whole, _, _, _, _ = plan.phase(
        "cross_forward",
        [(cross_whole, 0), (text_all, 1), (gains, 3), (cross_query_full, 0), (cross_key_full, 1)]
        + [(cross_value_full, 2), (cross_out_full, 4), (resid_self, 5), (mixing, -1)]
        + [(cotangent, -1)],
        kept_kinds + [((rows, width), full_type, "post"), ((length, width), low, "post")],
        exchange_scratch(length, plan.tensor),
        cross_pre,
        after_cross,
        True,
        shape,
        begin=cross_begin,
        end=cross_end,
    )
    cross_kept, (resid_cross, feed_grad_whole) = kept[:8], kept[8:]

    feed_tiles = tiles(hidden_units, 512)

    def feed_begin(links, near, kinds, scratch, far):
        copies = []
        for start, size in feed_tiles:
            lanes = pl.ds(start, size)
            pair = [
                links.here(far[which].at[:, lanes], scratch[2 + which].at[:, lanes])
                for which in range(2)
            ]
            for copy in pair:
                copy.start()
            copies.append(pair)
        return None, copies

    def feed_pre(links, near, kinds, scratch, partial, copies):
        whole, grad_whole = near[:2]
        activated, grad_raw, up, down = scratch
        root = 0.7978845608028654
        links.ready(0)
        for (begin, size), pair in zip(feed_tiles, copies):
            lanes = slice(begin, begin + size)
            for copy in pair:
                copy.wait()

            def one(step, _, lanes=lanes):
                block = pl.ds(pl.multiple_of(step * 256, 256), 256)
                raw = jnp.dot(whole[block, :], up[:, lanes], preferred_element_type=full_type)
                grad = jnp.dot(grad_whole[block, :], down[:, lanes], preferred_element_type=full_type)
                square = raw * raw
                bend = jnp.tanh(root * raw * (1.0 + 0.044715 * square))
                half = 0.5 + 0.5 * bend
                activated[block, lanes] = (raw * half).astype(low)
                slope = half + 0.5 * raw * (1.0 - bend * bend) * root * (
                    1.0 + 3.0 * 0.044715 * square
                )
                grad_raw[block, lanes] = (grad * slope).astype(low)
                return 0

            lax.fori_loop(0, length // 256, one, 0)
        copies.clear()
        for start, size in tiles(width, 512):
            partial[:, start : start + size] = product_back(
                grad_raw[...], up[start : start + size, :]
            ).astype(low)

    def feed_tasks(links, near, kinds, scratch, far):
        activated, down = scratch[0], scratch[3]

        def one(start, size):
            kinds[2][:, start : start + size] = product_back(
                activated[...], down[start : start + size, :]
            ).astype(low)

        return [functools.partial(one, start, size) for start, size in tiles(width, 512)]

    def before_feed(total, where, near, kinds, first):
        resid_ref, cotangent_ref, mixing_ref = near[2:]
        grad_ref, sums_ref = kinds[:2]
        unit, inverse = normed(resid_ref[where, :])
        add_sum(sums_ref, 0, total, first)
        add_sum(sums_ref, 1, total * unit, first)
        grad = cotangent_ref[where, :] + normed_back(
            unit, inverse, total * (1.0 + mixing_ref[4:5])
        )
        grad_ref[where, :] = grad
        return grad.astype(low)

    kept, cross_grad_whole, _, _, made, _ = plan.phase(
        "feed",
        [(feed_whole, 0), (feed_grad_whole, 0), (resid_cross, 1), (cotangent, 1), (mixing, 1)],
        [
            ((rows, width), full_type, "post"),
            ((8, width), full_type, "post"),
            ((length, width), low, "post"),
        ],
        [pltpu.VMEM((length, hidden_units), low)] * 2
        + [pltpu.VMEM((width, hidden_units), low)] * 2,
        feed_pre,
        before_feed,
        True,
        shape,
        jobs=[
            (lambda n, k, s: n[1], lambda n, k, s: s[0], part, hidden_units, False),
            (lambda n, k, s: n[0], lambda n, k, s: s[1], part, hidden_units, False),
        ],
        tasks=feed_tasks,
        begin=feed_begin,
        far=[up_full, down_full],
        exchange=False,
    )
    grad_resid_cross, feed_sums, feed_partial = kept
    near_down, near_up = made

    def backward(kinds_of_gain, angles, refs, gain_ref, grad_outs, scratch, links, partial, ticks):
        (grad_whole, query_w, key_w, value_w, out_w) = refs[:5]
        query_raw, key_raw, value, query, key, attended, logs, inverse = refs[5:]
        gain_query_ref, gain_key_ref, query_out, key_out, value_out = grad_outs
        grad_attended, grad_query, grad_key, grad_value = scratch[3:7]
        exchange = Exchange(links, *scratch[:3])
        links.ready(0)
        grad_attended[...] = jnp.dot(
            grad_whole[...], out_w[...], preferred_element_type=full_type
        ).astype(low)
        links.ready(1)
        attend_back(
            query, key, value, logs, grad_attended, (grad_query, grad_key, grad_value), heads
        )
        tick(ticks)
        links.ready(2)
        sides = (
            (query_raw, inverse[:, 0:1], gains_of(gain_ref, kinds_of_gain[0], heads)),
            (key_raw, inverse[:, 1:2], gains_of(gain_ref, kinds_of_gain[1], heads)),
        )
        exchange.start(
            [
                norm_dots(*sides[0], angles, grad_query, gain_query_ref, heads),
                norm_dots(*sides[1], angles, grad_key, gain_key_ref, heads),
            ]
        )
        value_out[...] = grad_value[...].astype(low)
        dots = exchange.finish()
        tick(ticks)
        norm_pull(*sides[0], dots[:, 0:1], grad_query, query_out, heads)
        norm_pull(*sides[1], dots[:, 1:2], grad_key, key_out, heads)
        links.ready(3)
        pairs = [(query_out, query_w)]
        if angles is not None:
            pairs += [(key_out, key_w), (value_out, value_w)]
        for start, size in tiles(width, 512):
            total = 0.0
            for grads, weight in pairs:
                total = total + product_back(grads[...], weight[start : start + size, :])
            partial[:, start : start + size] = total.astype(low)

    back_scratch = exchange_scratch(length, plan.tensor) + [
        pltpu.VMEM((length, here), low),
        pltpu.VMEM((length, here), full_type),
        pltpu.VMEM((length, here), full_type),
        pltpu.VMEM((length, here), full_type),
        pltpu.VMEM((length, here), low),
        pltpu.VMEM((length, here), low),
        pltpu.VMEM((length, here), low),
    ]

    kept_groups = (2, 2, 1, 1, 1, 4, 1, 2)

    def cross_back_begin(links, near, kinds, scratch, far):
        links.ready(-1)
        late = LineReduce(links, near[20], scratch[10], scratch[11], rows, 1)
        late.clear()
        first, *others = late.stages(0)
        first()
        return late, others

    def cross_back_end(late, links, near, kinds, scratch):
        cotangent_ref, mixing_ref, resid_ref = near[17:20]
        total = late.total(0)
        kinds[2][...] = resid_ref[...] + total * mixing_ref[5:6]
        add_sum(kinds[1], 2, cotangent_ref[...] * total, True)
        late.finish()

    def cross_back_pre(links, near, kinds, scratch, partial, ticks):
        backward(
            (2, 3),
            None,
            (near[0], near[1], None, None, *near[2:11]),
            near[11],
            (kinds[4], kinds[5], *scratch[7:10]),
            scratch,
            links,
            partial,
            ticks,
        )

    def cross_back_tasks(links, near, kinds, scratch, far):
        held, loaded = scratch[12:14]
        size = held.shape[2]
        out_copies, loads = [], {}

        def load(index):
            loads[index] = [
                links.here(weight.at[pl.ds(index * size, size)], loaded.at[index % 2, which])
                for which, weight in enumerate(far)
            ]
            for copy in loads[index]:
                copy.start()

        def one(index):
            if index >= 2:
                out_copies[index - 2].wait()
            for copy in loads[index]:
                copy.wait()
            stage = held.at[index % 2]
            stage[...] = (
                product_back(scratch[8][...], loaded[index % 2, 0])
                + product_back(scratch[9][...], loaded[index % 2, 1])
            ).astype(low)
            if index + 2 < text_width // size:
                load(index + 2)
            copy = links.here(stage, kinds[3].at[:, pl.ds(index * size, size)])
            copy.start()
            out_copies.append(copy)

        def last():
            for copy in out_copies[-2:]:
                copy.wait()

        load(0)
        load(1)
        steps = [functools.partial(one, index) for index in range(text_width // size)]
        return steps + [last]

    def before_cross(total, where, near, kinds, first):
        resid_ref, grad_ref, branch_ref = near[14:17]
        mixing_ref = near[18]
        out_ref, sums_ref = kinds[:2]
        unit, inverse = normed(resid_ref[where, :])
        add_sum(sums_ref, 1, total * unit, first)
        grad = grad_ref[where, :] + normed_back(unit, inverse, total * mixing_ref[6:7])
        out_ref[where, :] = grad
        add_sum(sums_ref, 0, grad * branch_ref[where, :], first)
        return (grad * mixing_ref[2:3]).astype(low)

    kept, self_grad_whole, _, _, made, (sum_down, sum_up) = plan.phase(
        "cross_back",
        [(cross_grad_whole, 0), (cross_query_full, 3), (cross_out_full, 0)]
        + list(zip(cross_kept, kept_groups))
        + [(gains, 2), (cross_whole, 4), (text_all, 4), (resid_self, 4), (grad_resid_cross, 4)]
        + [(self_branch, 4), (cotangent, 4), (mixing, 4), (resid_cross, 4), (feed_partial, -1)],
        [
            ((rows, width), full_type, "post"),
            ((8, width), full_type, "post"),
            ((rows, width), full_type, "post"),
            ((text_rows, text_width), low, None),
            ((8, HEAD_DIM), full_type, "pre"),
            ((8, HEAD_DIM), full_type, "pre"),
        ],
        back_scratch
        + [pltpu.VMEM((plan.tensor - 1, rows, width), low)] * 2
        + [pltpu.VMEM((2, text_rows, 1024), low), pltpu.VMEM((2, 2, 1024, here), low)],
        cross_back_pre,
        before_cross,
        True,
        shape,
        sums=[near_down, near_up],
        jobs=[
            (lambda n, k, s: n[13], lambda n, k, s: s[8], text_part, here, False),
            (lambda n, k, s: n[13], lambda n, k, s: s[9], text_part, here, False),
            (lambda n, k, s: n[12], lambda n, k, s: s[7], part, here, False),
            (lambda n, k, s: n[0], lambda n, k, s: n[8], part, here, False),
        ],
        tasks=cross_back_tasks,
        begin=cross_back_begin,
        end=cross_back_end,
        far=[cross_key_full, cross_value_full],
    )
    grad_resid_self, cross_sums, block_out, text_partial, gain_cross_query, gain_cross_key = kept
    grad_text = lax.psum_scatter(
        text_partial, "tensor", scatter_dimension=0, tiled=True
    ).astype(full_type)

    def self_back_pre(links, near, kinds, scratch, partial, ticks):
        backward(
            (0, 1),
            (near[14], near[15]),
            near[:13],
            near[13],
            (kinds[2], kinds[3], *scratch[7:10]),
            scratch,
            links,
            partial,
            ticks,
        )

    def before_self(total, where, near, kinds, first):
        hidden_ref, grad_ref, mixing_ref = near[17:]
        out_ref, sums_ref = kinds[:2]
        unit, inverse = normed(hidden_ref[where, :])
        add_sum(sums_ref, 0, total, first)
        add_sum(sums_ref, 1, total * unit, first)
        out_ref[where, :] = grad_ref[where, :] + normed_back(
            unit, inverse, total * (1.0 + mixing_ref[1:2])
        )

    kept, _, _, _, made, sums = plan.phase(
        "self_back",
        [(self_grad_whole, 0), (query_full, 3), (key_full, 3), (value_full, 3), (out_full, 0)]
        + list(zip(self_kept, kept_groups))
        + [(gains, 2), (cosine, 2), (sine, 2), (self_whole, 4), (hidden_in, 4)]
        + [(grad_resid_self, 4), (mixing, 4)],
        [
            ((rows, width), full_type, "post"),
            ((8, width), full_type, "post"),
            ((8, HEAD_DIM), full_type, "pre"),
            ((8, HEAD_DIM), full_type, "pre"),
        ],
        back_scratch,
        self_back_pre,
        before_self,
        False,
        shape,
        sums=made,
        jobs=[
            (lambda n, k, s: n[16], lambda n, k, s: s[7], part, here, True),
            (lambda n, k, s: n[16], lambda n, k, s: s[8], part, here, True),
            (lambda n, k, s: n[16], lambda n, k, s: s[9], part, here, True),
            (lambda n, k, s: n[0], lambda n, k, s: n[10], part, here, True),
        ],
    )
    grad_hidden, self_sums, gain_query, gain_key = kept
    sum_cross_key, sum_cross_value, sum_cross_query, sum_cross_out = sums
    sum_query, sum_key, sum_value, sum_out = made

    time_part = jnp.concatenate(
        [
            self_sums[:2],
            cross_sums[:1],
            feed_sums[:2],
            cross_sums[2:3],
            cross_sums[1:2],
            jnp.zeros((1, width), full_type),
        ],
        axis=0,
    )
    gain_part = jnp.concatenate([gain_query, gain_key, gain_cross_query, gain_cross_key], axis=1)
    time_total, all_total, gain_total = plan.close(time_part, gain_part)
    dp = lax.axis_index("dp")
    mine = lax.dynamic_slice_in_dim(all_total, dp * part, part, axis=1)
    gain_width = qk_gain.shape[1]
    gain_mine = lax.dynamic_slice_in_dim(gain_total[:heads], dp * gain_width, gain_width, axis=1)
    return (
        block_out,
        grad_hidden,
        grad_text,
        time_total[None, :6],
        mine[:6],
        sum_query,
        sum_key,
        sum_value,
        sum_out.T,
        sum_cross_query,
        sum_cross_key,
        sum_cross_value,
        sum_cross_out.T,
        sum_up,
        sum_down.T,
        gain_mine,
        mine[6],
    )


def solution(mesh):
    return jax.shard_map(
        functools.partial(body, Plan(mesh)),
        mesh=mesh,
        in_specs=(
            P(("dp", "tensor"), None),
            P(("dp", "tensor"), None),
            P("dp", None, None),
            P(None, "dp"),
            P(None, "dp"),
            P("dp", "tensor"),
            P("dp", "tensor"),
            P("dp", "tensor"),
            P("tensor", "dp"),
            P("dp", "tensor"),
            P("dp", "tensor"),
            P("dp", "tensor"),
            P("tensor", "dp"),
            P("dp", "tensor"),
            P("tensor", "dp"),
            P("tensor", "dp"),
            P("dp"),
            P(("dp", "tensor"), None),
        ),
        out_specs=(
            P(("dp", "tensor"), None),
            P(("dp", "tensor"), None),
            P(("dp", "tensor"), None),
            P("dp", None, None),
            P(None, "dp"),
            P("dp", "tensor"),
            P("dp", "tensor"),
            P("dp", "tensor"),
            P("tensor", "dp"),
            P("dp", "tensor"),
            P("dp", "tensor"),
            P("dp", "tensor"),
            P("tensor", "dp"),
            P("dp", "tensor"),
            P("tensor", "dp"),
            P("tensor", "dp"),
            P("dp"),
        ),
        check_vma=False,
    )
```

```python
import functools

import jax
import jax.numpy as jnp
from jax import lax
from jax.experimental import pallas as pl
from jax.experimental.pallas import tpu as pltpu
from jax.sharding import PartitionSpec as P

MESH = pl.DeviceIdType.MESH
VMEM_BYTES = 62 * 2**20

HEAD_DIM = 128
D = 1536


EPSILON = 1e-06
CONTRACT_LAST = (((1,), (1,)), ((), ()))
CONTRACT_FIRST = (((0,), (0,)), ((), ()))


def rotary_tables(positions, head_width):
    pairs = head_width // 2
    third = pairs // 3
    first = pairs - 2 * third
    freq_frame = jnp.power(10000.0, -jnp.arange(first, dtype=jnp.float32) / first)
    freq_side = jnp.power(10000.0, -jnp.arange(third, dtype=jnp.float32) / third)
    places = positions.astype(jnp.float32)
    angles = jnp.concatenate(
        [
            places[0][:, None] * jnp.repeat(freq_frame, 2)[None, :],
            places[1][:, None] * jnp.repeat(freq_side, 2)[None, :],
            places[2][:, None] * jnp.repeat(freq_side, 2)[None, :],
        ],
        axis=1,
    )
    sign = jnp.where(jnp.arange(head_width) % 2 == 0, -1.0, 1.0)
    return (jnp.cos(angles), jnp.sin(angles) * sign)


def product_back(grads, weight):
    return lax.dot_general(grads, weight, CONTRACT_LAST, preferred_element_type=jnp.float32)


def weight_grad(inputs, grads):
    return lax.dot_general(inputs, grads, CONTRACT_FIRST, preferred_element_type=jnp.float32)


def when(cond, run):
    if cond is None:
        run()
    else:
        pl.when(cond)(run)


def flip(index, bit):
    return index + bit - 2 * bit * (index // bit % 2)


def normed(values):
    center = values - jnp.mean(values, axis=-1, keepdims=True)
    inverse = lax.rsqrt(jnp.mean(center * center, axis=-1, keepdims=True) + EPSILON)
    return center * inverse, inverse


def normed_back(unit, inverse, grad):
    mean_grad = jnp.mean(grad, axis=-1, keepdims=True)
    mean_dot = jnp.mean(grad * unit, axis=-1, keepdims=True)
    return (grad - mean_grad - unit * mean_dot) * inverse


class Links:
    def __init__(self, send, recv, local, dp_size, tensor_size):
        self.send, self.recv, self.local = send, recv, local
        self.count = 0
        self.local_count = 0
        self.dp_size, self.size = dp_size, tensor_size
        self.dp = lax.axis_index("dp")
        self.z = lax.axis_index("tensor")

    def slot(self):
        self.count += 1
        return self.count - 1

    def copy(self, source, target, device, slot):
        return pltpu.make_async_remote_copy(
            src_ref=source,
            dst_ref=target,
            send_sem=self.send.at[slot],
            recv_sem=self.recv.at[slot],
            device_id=device,
            device_id_type=MESH,
        )

    def here(self, source, target):
        self.local_count += 1
        return pltpu.make_async_copy(source, target, self.local.at[self.local_count - 1])

    def greet(self, groups):
        barrier = pltpu.get_barrier_semaphore()
        peers = []
        if "line" in groups and "zall" not in groups:
            peers += [
                ((self.dp, self.z - 1), self.z > 0),
                ((self.dp, self.z + 1), self.z < self.size - 1),
            ]
        if "zall" in groups:
            peers += [
                ((self.dp, lax.rem(self.z + k, self.size)), None) for k in range(1, self.size)
            ]
        if "dpall" in groups:
            peers += [
                ((lax.rem(self.dp + k, self.dp_size), self.z), None)
                for k in range(1, self.dp_size)
            ]
        if "bits" in groups and "dpall" not in groups:
            bit = 1
            while bit < self.dp_size:
                peers.append(((flip(self.dp, bit), self.z), None))
                bit *= 2
        if "diag" in groups and "dpall" not in groups:
            peers.append(((flip(flip(self.dp, 2), 4), self.z), None))
        for device, cond in peers:
            when(
                cond,
                lambda device=device: pl.semaphore_signal(
                    barrier, inc=1, device_id=device, device_id_type=MESH
                ),
            )
        expected = sum(1 for _, cond in peers if cond is None)
        for _, cond in peers:
            if cond is not None:
                expected = expected + cond.astype(jnp.int32)
        pl.semaphore_wait(barrier, expected)


def piece_of(ref, block, rows, start, count):
    return ref.at[pl.ds(pl.multiple_of(block * rows + start, 16), count)]


class LineGather:
    def __init__(self, links, whole, rows, pieces):
        self.links, self.whole, self.rows, self.count = links, whole, rows, rows // pieces
        self.pieces = pieces
        hops = links.size - 1
        self.right = [[links.slot() for _ in range(pieces)] for _ in range(hops)]
        self.left = [[links.slot() for _ in range(pieces)] for _ in range(hops)]

    def block(self, index, piece):
        return piece_of(self.whole, index, self.rows, piece * self.count, self.count)

    def move(self, index, piece, way, slot):
        part = self.block(index, piece)
        return self.links.copy(part, part, (self.links.dp, self.links.z + way), slot)

    def start(self, piece):
        z, last = self.links.z, self.links.size - 1
        when(z < last, lambda: self.move(z, piece, 1, self.right[0][piece]).start())
        when(z > 0, lambda: self.move(z, piece, -1, self.left[0][piece]).start())

    def step(self, hop, piece):
        z, last = self.links.z, self.links.size - 1

        def from_left():
            self.move(z - 1 - hop, piece, -1, self.right[hop][piece]).wait_recv()
            if hop + 1 < last:
                when(
                    z < last,
                    lambda: self.move(z - 1 - hop, piece, 1, self.right[hop + 1][piece]).start(),
                )

        def from_right():
            self.move(z + 1 + hop, piece, 1, self.left[hop][piece]).wait_recv()
            if hop + 1 < last:
                when(
                    z > 0,
                    lambda: self.move(z + 1 + hop, piece, -1, self.left[hop + 1][piece]).start(),
                )

        when(z - 1 - hop >= 0, from_left)
        when(z + 1 + hop <= last, from_right)

    def steps(self, piece):
        for hop in range(self.links.size - 1):
            self.step(hop, piece)

    def finish(self):
        z, last = self.links.z, self.links.size - 1
        for hop in range(last):
            for piece in range(self.pieces):
                when(
                    (z - hop >= 0) & (z < last),
                    lambda: self.move(z - hop, piece, 1, self.right[hop][piece]).wait_send(),
                )
                when(
                    (z + hop <= last) & (z > 0),
                    lambda: self.move(z + hop, piece, -1, self.left[hop][piece]).wait_send(),
                )


class LineReduce:
    def __init__(self, links, partial, land_right, land_left, rows, pieces):
        self.links, self.partial, self.rows, self.count = links, partial, rows, rows // pieces
        self.land = {1: land_right, -1: land_left}
        self.pieces = pieces
        last = links.size - 1
        self.slots = {
            way: [None] + [[links.slot() for _ in range(pieces)] for _ in range(last)]
            for way in (1, -1)
        }

    def landing(self, way, distance, piece):
        return self.land[way].at[distance - 1, pl.ds(piece * self.count, self.count)]

    def part(self, index, piece):
        return piece_of(self.partial, index, self.rows, piece * self.count, self.count)

    def move(self, source, way, distance, piece):
        return self.links.copy(
            source,
            self.landing(way, distance, piece),
            (self.links.dp, self.links.z + way),
            self.slots[way][distance][piece],
        )

    def arrived(self, way, distance, piece):
        self.links.copy(
            self.landing(way, distance, piece),
            self.landing(way, distance, piece),
            (self.links.dp, self.links.z - way),
            self.slots[way][distance][piece],
        ).wait_recv()

    def first(self, piece):
        z, last = self.links.z, self.links.size - 1

        def from_first():
            for distance in range(last, 0, -1):
                self.move(self.part(distance, piece), 1, distance, piece).start()

        def from_last():
            for distance in range(last, 0, -1):
                self.move(self.part(last - distance, piece), -1, distance, piece).start()

        when(z == 0, from_first)
        when(z == last, from_last)

    def first_at(self, distance, piece):
        z, last = self.links.z, self.links.size - 1
        when(
            z == 0,
            lambda: self.move(self.part(distance, piece), 1, distance, piece).start(),
        )
        when(
            z == last,
            lambda: self.move(self.part(last - distance, piece), -1, distance, piece).start(),
        )

    def stages(self, piece):
        last = self.links.size - 1

        def one(distance):
            self.first_at(distance, piece)
            if distance < last:
                self.step(distance, piece)

        return [functools.partial(one, distance) for distance in range(last, 0, -1)]

    def clear(self):
        z, last = self.links.z, self.links.size - 1

        def zero(way):
            self.land[way][0] = jnp.zeros(self.land[way].shape[1:], self.land[way].dtype)

        when(z == 0, lambda: zero(1))
        when(z == last, lambda: zero(-1))

    def step(self, distance, piece):
        z, last = self.links.z, self.links.size - 1
        for way in (1, -1):
            inside = (
                (z > 0) & (z + distance <= last)
                if way == 1
                else (z < last) & (z - distance >= 0)
            )

            def go(way=way):
                self.arrived(way, distance + 1, piece)
                held = self.landing(way, distance + 1, piece)
                own = self.part(z + way * distance, piece)
                held[...] = (
                    held[...].astype(jnp.float32) + own[...].astype(jnp.float32)
                ).astype(held.dtype)
                self.move(held, way, distance, piece).start()

            when(inside, go)

    def total(self, piece):
        z, last = self.links.z, self.links.size - 1
        when(z > 0, lambda: self.arrived(1, 1, piece))
        when(z < last, lambda: self.arrived(-1, 1, piece))
        return (
            self.part(z, piece)[...].astype(jnp.float32)
            + self.landing(1, 1, piece)[...].astype(jnp.float32)
            + self.landing(-1, 1, piece)[...].astype(jnp.float32)
        )

    def finish(self):
        z, last = self.links.z, self.links.size - 1
        for distance in range(1, last + 1):
            for piece in range(self.pieces):
                held = self.landing(1, distance, piece)
                when(
                    z + distance <= last,
                    lambda: self.move(held, 1, distance, piece).wait_send(),
                )
                back = self.landing(-1, distance, piece)
                when(
                    z - distance >= 0,
                    lambda: self.move(back, -1, distance, piece).wait_send(),
                )


def reduce_stages(reduce):
    return [
        functools.partial(reduce.step, distance)
        for distance in range(reduce.links.size - 2, 0, -1)
    ]


def wave(stages, pieces, queue):
    count = pieces + len(stages) - 1
    done = 0
    for step in range(count):
        for index, stage in enumerate(stages):
            if 0 <= step - index < pieces:
                stage(step - index)
        until = len(queue) * (step + 1) // count
        for run in queue[done:until]:
            run()
        done = until


class CubeGather:
    def __init__(self, links, shard, whole):
        self.links, self.shard, self.whole = links, shard, whole
        self.rows = shard.shape[0]
        self.slots = [links.slot() for _ in range(8)]
        dp = links.dp
        self.core, self.side, self.over = flip(dp, 1), flip(dp, 2), flip(dp, 4)
        self.far = flip(flip(dp, 2), 4)
        self.sent = []

    def block(self, index, start=0, count=None):
        return piece_of(self.whole, index, self.rows, start, count or self.rows)

    def send(self, source, target, device, slot):
        move = self.links.copy(source, target, (device, self.links.z), self.slots[slot])
        move.start()
        self.sent.append(move)

    def got(self, part, slot):
        self.links.copy(part, part, (self.core, self.links.z), self.slots[slot]).wait_recv()

    def start(self):
        mine = self.block(self.links.dp)
        self.own = self.links.here(self.shard, mine)
        self.own.start()
        self.send(self.shard, mine, self.side, 1)
        self.send(self.shard, mine, self.over, 2)
        self.send(self.shard, mine, self.core, 0)

    def forward(self):
        half = self.rows // 2
        self.got(self.block(self.side), 1)
        part = self.block(self.side, 0, half)
        self.send(part, part, self.over, 3)
        part = self.block(self.side)
        self.send(part, part, self.core, 5)
        self.got(self.block(self.over), 2)
        part = self.block(self.over, half, half)
        self.send(part, part, self.side, 4)
        part = self.block(self.over)
        self.send(part, part, self.core, 6)

    def tail(self):
        half = self.rows // 2
        self.got(self.block(self.far, 0, half), 3)
        self.got(self.block(self.far, half, half), 4)
        part = self.block(self.far)
        self.send(part, part, self.core, 7)

    def finish(self):
        self.got(self.block(self.core), 0)
        self.got(self.block(flip(self.core, 2)), 5)
        self.got(self.block(flip(self.core, 4)), 6)
        self.got(self.block(flip(flip(self.core, 2), 4)), 7)
        for move in self.sent:
            move.wait_send()
        self.own.wait()


class DirectGather:
    def __init__(self, links, whole, rows):
        self.links, self.whole, self.rows = links, whole, rows
        self.slots = [links.slot() for _ in range(links.size - 1)]

    def start(self, source):
        links = self.links
        mine = piece_of(self.whole, links.z, self.rows, 0, self.rows)
        self.moves = [
            links.copy(source, mine, (links.dp, lax.rem(links.z + step, links.size)), slot)
            for step, slot in enumerate(self.slots, 1)
        ]
        for move in self.moves:
            move.start()

    def finish(self):
        for move in self.moves:
            move.wait_recv()
        for move in self.moves:
            move.wait_send()


class Exchange:
    def __init__(self, links, mine, land, turned):
        self.links, self.mine, self.land, self.turned = links, mine, land, turned
        self.slots = [links.slot() for _ in range(links.size - 1)]

    def start(self, columns):
        links = self.links
        lane = lax.broadcasted_iota(jnp.int32, (columns[0].shape[0], 128), 1)
        flat = jnp.zeros(lane.shape, jnp.float32)
        for index, column in enumerate(columns):
            flat = jnp.where(lane == index, column, flat)
        self.mine[...] = flat.T[:8]
        self.moves = [
            links.copy(
                self.mine,
                self.land.at[step - 1],
                (links.dp, lax.rem(links.z + step, links.size)),
                slot,
            )
            for step, slot in enumerate(self.slots, 1)
        ]
        for move in self.moves:
            move.start()

    def finish(self, shape=lambda total: total):
        total = self.mine[...]
        for step, move in enumerate(self.moves):
            move.wait_recv()
            total = total + self.land[step]
        self.turned[...] = jnp.zeros(self.turned.shape, jnp.float32)
        self.turned[0:8, :] = shape(total)
        for move in self.moves:
            move.wait_send()
        return self.turned[...].T


class CoreSum:
    def __init__(self, links, left, right, product, near):
        self.links, self.left, self.right = links, left, right
        self.product, self.near = product, near
        self.rows = near.shape[1]
        self.slots = [links.slot() for _ in range(4)]
        self.core = links.dp % 2
        self.moves = []

    def multiply(self, chip):
        links, count = self.links, 2 * self.rows
        self.product[chip * count : (chip + 1) * count, :] = weight_grad(
            self.left[:, chip * count : (chip + 1) * count], self.right[...]
        ).astype(jnp.bfloat16)
        move = links.copy(
            piece_of(self.product, 2 * chip + 1 - self.core, self.rows, 0, self.rows),
            self.near.at[chip],
            (flip(links.dp, 1), links.z),
            self.slots[chip],
        )
        move.start()
        self.moves.append(move)

    def add(self):
        for move in self.moves:
            move.wait_recv()

        def one(step, _):
            rows = pl.ds(pl.multiple_of(step * 16, 16), 16)
            for chip in range(4):
                own = pl.ds(
                    pl.multiple_of((2 * chip + self.core) * self.rows + step * 16, 16), 16
                )
                self.near[chip, rows, :] = (
                    self.near[chip, rows, :].astype(jnp.float32)
                    + self.product[own, :].astype(jnp.float32)
                ).astype(jnp.bfloat16)
            return 0

        lax.fori_loop(0, self.rows // 16, one, 0)

    def clear(self):
        for move in self.moves:
            move.wait_send()

    def steps(self):
        return [functools.partial(self.multiply, chip) for chip in range(4)] + [self.add]


class ChipSum:
    def __init__(self, links, near, out, others, own=None):
        self.links, self.near, self.out, self.others, self.own = links, near, out, others, own
        self.slots = [links.slot() for _ in range(3)]
        self.core, self.chip = links.dp % 2, links.dp // 2
        self.rows = out.shape[0]

    def start(self):
        links = self.links
        chips = [flip(self.chip, 1), flip(self.chip, 2), flip(flip(self.chip, 1), 2)]
        self.moves = [
            links.copy(
                self.near.at[chip],
                self.others.at[index],
                (2 * chip + self.core, links.z),
                self.slots[index],
            )
            for index, chip in enumerate(chips)
        ]
        for move in self.moves:
            move.start()
        if self.own is not None:
            self.local = links.here(self.near.at[self.chip], self.own)
            self.local.start()

    def finish(self):
        for move in self.moves:
            move.wait_recv()
        if self.own is not None:
            self.local.wait()

        def one(step, _):
            rows = pl.ds(pl.multiple_of(step * 16, 16), 16)
            mine = self.own[rows, :] if self.own is not None else self.near[self.chip, rows, :]
            total = mine.astype(jnp.float32)
            for index in range(3):
                total = total + self.others[index, rows, :].astype(jnp.float32)
            self.out[rows, :] = total
            return 0

        lax.fori_loop(0, self.rows // 16, one, 0)
        for move in self.moves:
            move.wait_send()


def attend(query, key, value, out, logs, heads, chunk=256):
    scale = HEAD_DIM**-0.5
    for head in range(heads):
        lanes = slice(head * HEAD_DIM, (head + 1) * HEAD_DIM)

        def one(step, _, head=head, lanes=lanes):
            rows = pl.ds(pl.multiple_of(step * chunk, chunk), chunk)
            scores = product_back(query[rows, lanes], key[:, lanes]) * scale
            top = jnp.max(scores, axis=-1, keepdims=True)
            expo = jnp.exp(scores - top)
            summed = jnp.sum(expo, axis=-1, keepdims=True)
            probs = (expo * (1.0 / summed)).astype(jnp.bfloat16)
            out[rows, lanes] = jnp.dot(
                probs, value[:, lanes], preferred_element_type=jnp.float32
            ).astype(jnp.bfloat16)
            logs[rows, head : head + 1] = top + jnp.log(summed)
            return 0

        lax.fori_loop(0, query.shape[0] // chunk, one, 0)


def attend_back(query, key, value, logs, grad, grads, heads, chunk=256):
    scale = HEAD_DIM**-0.5
    grad_query, grad_key, grad_value = grads
    grad_key[...] = jnp.zeros(grad_key.shape, jnp.float32)
    grad_value[...] = jnp.zeros(grad_value.shape, jnp.float32)
    for head in range(heads):
        lanes = slice(head * HEAD_DIM, (head + 1) * HEAD_DIM)

        def one(step, _, head=head, lanes=lanes):
            rows = pl.ds(pl.multiple_of(step * chunk, chunk), chunk)
            scores = product_back(query[rows, lanes], key[:, lanes]) * scale
            probs = jnp.exp(scores - logs[rows, head : head + 1])
            prob_grad = product_back(grad[rows, lanes], value[:, lanes])
            inner = jnp.sum(prob_grad * probs, axis=-1, keepdims=True)
            score_grad = (probs * (prob_grad - inner)).astype(jnp.bfloat16)
            grad_query[rows, lanes] = (
                jnp.dot(score_grad, key[:, lanes], preferred_element_type=jnp.float32) * scale
            )
            grad_key[:, lanes] += weight_grad(score_grad, query[rows, lanes]) * scale
            grad_value[:, lanes] += weight_grad(probs.astype(jnp.bfloat16), grad[rows, lanes])
            return 0

        lax.fori_loop(0, query.shape[0] // chunk, one, 0)


def swapped(values):
    lane = lax.broadcasted_iota(jnp.int32, values.shape, 1)
    width = values.shape[1]
    return jnp.where(lane % 2 == 0, pltpu.roll(values, width - 1, 1), pltpu.roll(values, 1, 1))


def turn(values, cosine, sine, back):
    other = swapped(values) * sine
    return values * cosine - other if back else values * cosine + other


def square_columns(*arrays):
    return [jnp.sum(array * array, axis=-1, keepdims=True) for array in arrays]


def shape_norm(raw, inverse, gain, angles, out, heads, chunk=128):
    for head in range(heads):
        lanes = slice(head * HEAD_DIM, (head + 1) * HEAD_DIM)
        for start in range(0, raw.shape[0], chunk):
            rows = slice(start, start + chunk)
            values = raw[rows, lanes] * inverse[rows] * gain[head]
            if angles is not None:
                values = turn(values, angles[0][rows, :], angles[1][rows, :], False)
            out[rows, lanes] = values.astype(jnp.bfloat16)


def norm_dots(raw, inverse, gain, angles, grad, gain_out, heads, chunk=128):
    columns = []
    for start in range(0, raw.shape[0], chunk):
        rows = slice(start, start + chunk)
        column = jnp.zeros((chunk, 1), jnp.float32)
        for head in range(heads):
            lanes = slice(head * HEAD_DIM, (head + 1) * HEAD_DIM)
            values = grad[rows, lanes]
            if angles is not None:
                values = turn(values, angles[0][rows, :], angles[1][rows, :], True)
                grad[rows, lanes] = values
            part = values * raw[rows, lanes]
            column = column + jnp.sum(part * gain[head], axis=-1, keepdims=True)
            total = jnp.sum(part * inverse[rows], axis=0, keepdims=True)
            where = slice(head, head + 1)
            gain_out[where, :] = total if start == 0 else gain_out[where, :] + total
        columns.append(column)
    return jnp.concatenate(columns, axis=0)


def norm_pull(raw, inverse, gain, dots, grad, out, heads, chunk=128):
    for start in range(0, raw.shape[0], chunk):
        rows = slice(start, start + chunk)
        scale = inverse[rows]
        cut = dots[rows] * scale * scale * scale * (1.0 / D)
        for head in range(heads):
            lanes = slice(head * HEAD_DIM, (head + 1) * HEAD_DIM)
            out[rows, lanes] = (
                grad[rows, lanes] * gain[head] * scale - raw[rows, lanes] * cut
            ).astype(jnp.bfloat16)


def gains_of(gain_ref, kind, heads):
    lanes = slice(kind * HEAD_DIM, (kind + 1) * HEAD_DIM)
    return [gain_ref[head : head + 1, lanes] for head in range(heads)]


def exchange_scratch(length, size):
    return [
        pltpu.VMEM((8, length), jnp.float32),
        pltpu.VMEM((size - 1, 8, length), jnp.float32),
        pltpu.VMEM((128, length), jnp.float32),
    ]


class Plan:
    def __init__(self, mesh):
        self.dp = mesh.shape["dp"]
        self.tensor = mesh.shape["tensor"]
        self.cube = self.dp == 8
        self.calls = 0
        self.pieces = 4

    def call(self, name, body, inputs, outputs, scratch, copies):
        self.calls += 1
        spaces = {True: pltpu.VMEM, False: pltpu.HBM}
        count_in, count_out = len(inputs), len(outputs)

        def kernel(*refs):
            ins = refs[:count_in]
            outs = refs[count_in : count_in + count_out]
            rest = refs[count_in + count_out :]
            links = Links(rest[0], rest[1], rest[2], self.dp, self.tensor)
            body(links, ins, outs, rest[3:])

        return pl.pallas_call(
            kernel,
            name=name,
            out_shape=[jax.ShapeDtypeStruct(shape, kind) for shape, kind, _ in outputs],
            in_specs=[pl.BlockSpec(memory_space=spaces[near]) for _, near in inputs],
            out_specs=[pl.BlockSpec(memory_space=spaces[near]) for _, _, near in outputs],
            scratch_shapes=[
                pltpu.SemaphoreType.DMA((copies,)),
                pltpu.SemaphoreType.DMA((copies,)),
                pltpu.SemaphoreType.DMA((64,)),
                *scratch,
            ],
            compiler_params=pltpu.CompilerParams(
                collective_id=self.calls, has_side_effects=True, vmem_limit_bytes=VMEM_BYTES
            ),
        )(*[array for array, _ in inputs])

    def gather_outputs(self, shards):
        return [
            ((self.dp * shard.shape[0], shard.shape[1]), shard.dtype, False) for shard in shards
        ]

    def open(self, hidden, time_rows, small, shards):
        rows, width = hidden.shape
        part = width // self.dp
        gain_part = small.shape[1] - part
        moving = shards if self.cube else []

        def body(links, ins, outs, scratch):
            hidden_ref, time_ref, small_ref = ins[:3]
            table_ref, gain_ref, whole_ref = outs[:3]
            (land,) = scratch
            links.greet({"line", "dpall"})
            gathers = [CubeGather(links, a, b) for a, b in zip(ins[3:], outs[3:])]
            dp, z = links.dp, links.z
            moves = []
            for step in range(1, self.dp):
                target = lax.rem(dp + step, self.dp)
                move = links.copy(small_ref, land.at[dp], (target, z), links.slot())
                move.start()
                moves.append(move)
            for item in gathers:
                item.start()
            land[dp] = small_ref[...]
            unit, _ = normed(hidden_ref[...])
            for move in moves:
                move.wait_recv()
            table = jnp.concatenate([land[k][:, :part] for k in range(self.dp)], axis=1)
            gain_ref[...] = jnp.concatenate([land[k][:, part:] for k in range(self.dp)], axis=1)
            table = table + time_ref[...]
            table_ref[...] = table
            line = LineGather(links, whole_ref, rows, 4)
            first = unit * (1.0 + table[1:2]) + table[0:1]
            whole_ref[pl.ds(pl.multiple_of(z * rows, 16), rows), :] = first.astype(jnp.bfloat16)
            for piece in range(4):
                line.start(piece)
            for piece in range(4):
                line.steps(piece)
                for item in gathers[2 * piece : 2 * piece + 2]:
                    item.forward()
            for item in gathers:
                item.tail()
            for item in gathers:
                item.finish()
            line.finish()
            for move in moves:
                move.wait_send()

        results = self.call(
            "open",
            body,
            [(hidden, True), (time_rows, True), (small, True)] + [(s, False) for s in moving],
            [
                ((8, width), jnp.float32, True),
                ((8, gain_part * self.dp), jnp.float32, True),
                ((rows * self.tensor, width), jnp.bfloat16, True),
            ]
            + self.gather_outputs(moving),
            [pltpu.VMEM((self.dp, 8, small.shape[1]), jnp.float32)],
            160,
        )
        return results[:3], self.gathered(results[3:], shards)

    def gathered(self, moved, shards):
        if self.cube:
            return list(moved)
        return [lax.all_gather(shard, "dp", axis=0, tiled=True) for shard in shards]

    def phase(
        self,
        name,
        near,
        kinds,
        scratch,
        pre,
        post,
        gather,
        shape,
        shards=(),
        lines=(),
        sums=(),
        jobs=(),
        tasks=None,
        begin=None,
        end=None,
        exchange=True,
        far=(),
        settle_small=None,
    ):
        length, width = shape
        rows = length // self.tensor
        pieces = self.pieces
        near = [(item if isinstance(item, list) else [item], group) for item, group in near]
        shards, lines, sums, far = list(shards), list(lines), list(sums), list(far)
        moving = shards if self.cube else []
        adding = sums if self.cube else []
        jobs = list(jobs)
        here = [job for job in jobs if job[4]] if self.cube else []
        count_near, count_kinds, count_scratch = len(near), len(kinds), len(scratch)

        job_scratch, job_outputs = [], []
        products, seats = {}, []
        for left, right, part, columns, now in jobs:
            if not self.cube:
                seats.append(("out", len(job_outputs)))
                job_outputs.append(((self.dp * part, columns), jnp.bfloat16, True))
                continue
            key = (part, columns)
            if key not in products:
                products[key] = len(job_scratch)
                job_scratch.append(pltpu.VMEM((8 * part, columns), jnp.bfloat16))
            if now:
                seats.append((products[key], len(job_scratch), len(job_outputs)))
                job_scratch.append(pltpu.VMEM((4, part, columns), jnp.bfloat16))
                job_scratch.append(pltpu.VMEM((3, part, columns), jnp.bfloat16))
                job_outputs.append(((part, columns), jnp.float32, True))
            else:
                seats.append((products[key], len(job_scratch), len(job_outputs)))
                job_scratch.append(pltpu.VMEM((4, part, columns), jnp.bfloat16))
                job_outputs.append(((4, part, columns), jnp.bfloat16, False))
        sum_scratch, sum_outputs = [], []
        for item in adding:
            _, part, columns = item.shape
            sum_scratch.append(pltpu.VMEM((3, part, columns), jnp.bfloat16))
            sum_scratch.append(pltpu.VMEM((part, columns), jnp.bfloat16))
            sum_outputs.append(((part, columns), jnp.float32, True))

        def body(links, ins, outs, rest):
            near_far = []
            for item, _ in near:
                near_far.append(ins[: len(item)])
                ins = ins[len(item) :]
            shard_refs, ins = ins[: len(moving)], ins[len(moving) :]
            line_refs, ins = ins[: len(lines)], ins[len(lines) :]
            sum_refs, far_refs = ins[: len(adding)], ins[len(adding) :]
            kind_far, outs = outs[:count_kinds], outs[count_kinds:]
            if gather:
                whole_far, outs = outs[0], outs[1:]
            full_refs, outs = outs[: len(moving)], outs[len(moving) :]
            line_outs, outs = outs[: len(lines)], outs[len(lines) :]
            job_refs, added_refs = outs[: len(jobs)], outs[len(jobs) :]
            near_refs, rest = rest[:count_near], rest[count_near:]
            loads = {}
            for index in order:
                start = 0
                for source in near_far[index]:
                    target = near_refs[index]
                    if len(near_far[index]) > 1:
                        target = target.at[:, pl.ds(start, source.shape[1])]
                        start += source.shape[1]
                    copy = links.here(source, target)
                    copy.start()
                    loads.setdefault(near[index][1], []).append(copy)

            def ready(group):
                for copy in loads.pop(group, []):
                    copy.wait()

            links.ready = ready
            kind_refs, stores = [], []
            for far_ref, (_, _, when_done) in zip(kind_far, kinds):
                if when_done is None:
                    kind_refs.append(far_ref)
                else:
                    kind_refs.append(rest[0])
                    rest = rest[1:]

            def store(source, target):
                stores.append(links.here(source, target))
                stores[-1].start()

            def store_kinds(moment):
                for held, far_ref, (_, _, when_done) in zip(kind_refs, kind_far, kinds):
                    if when_done == moment:
                        store(held, far_ref)

            if gather:
                whole_ref, rest = rest[0], rest[1:]
            partial_ref, land_right, land_left = rest[:3]
            user, rest = rest[3 : 3 + count_scratch], rest[3 + count_scratch :]
            job_rest, sum_rest = rest[: len(job_scratch)], rest[len(job_scratch) :]

            groups = {"zall"} if exchange else {"line"}
            if moving or adding or jobs:
                groups |= {"bits"} if self.cube else set()
            if adding or here:
                groups |= {"diag"}
            if settle_small:
                groups |= {"dpall"}
            links.greet(groups)
            gathers = [CubeGather(links, a, b) for a, b in zip(shard_refs, full_refs)]
            straight = [
                DirectGather(links, b, a.shape[0]) for a, b in zip(line_refs, line_outs)
            ]
            old = [
                ChipSum(links, a, b, sum_rest[2 * k], sum_rest[2 * k + 1])
                for k, (a, b) in enumerate(zip(sum_refs, added_refs))
            ]
            for item in gathers + old:
                item.start()
            copies = []
            for item, source in zip(straight, line_refs):
                item.start(source)
                copies.append(
                    links.here(source, piece_of(item.whole, links.z, item.rows, 0, item.rows))
                )
                copies[-1].start()
            state = begin(links, near_refs, kind_refs, user, far_refs) if begin else (None, [])
            ticks = state[1]
            pre(links, near_refs, kind_refs, user, partial_ref, ticks)
            for run in ticks:
                run()
            store_kinds("pre")
            for group in sorted(loads):
                ready(group)

            queue = list(tasks(links, near_refs, kind_refs, user, far_refs)) if tasks else []
            fresh, busy, cleared = [], {}, []
            for (left, right, part, columns, now), seat in zip(jobs, seats):
                left_ref, right_ref = left(near_refs, kind_refs, user), right(near_refs, kind_refs, user)
                out = job_refs[seat[-1]]
                if not self.cube:

                    def whole(start, left_ref=left_ref, right_ref=right_ref, out=out):
                        count = out.shape[0] // 4
                        where = slice(start * count, (start + 1) * count)
                        out[where, :] = weight_grad(left_ref[:, where], right_ref[...]).astype(
                            jnp.bfloat16
                        )

                    queue += [functools.partial(whole, start) for start in range(4)]
                    continue
                held = job_rest[seat[1]]
                item = CoreSum(links, left_ref, right_ref, job_rest[seat[0]], held)
                if seat[0] in busy:
                    queue.append(busy[seat[0]].clear)
                    cleared.append(busy[seat[0]])
                busy[seat[0]] = item
                queue += item.steps()
                if now:
                    chip = ChipSum(links, held, out, job_rest[seat[1] + 1])
                    queue.append(chip.start)
                    fresh.append(chip)
                else:
                    queue.append(functools.partial(store, held, out))
            queue += [item.forward for item in gathers]
            queue += [item.tail for item in gathers]

            reduce = LineReduce(links, partial_ref, land_right, land_left, rows, pieces)
            line = LineGather(links, whole_ref, rows, pieces) if gather else None
            for piece in range(pieces):
                reduce.first(piece)
            reduce.clear()

            def settle(piece):
                where = pl.ds(piece * (rows // pieces), rows // pieces)
                result = post(reduce.total(piece), where, near_refs, kind_refs, piece == 0)
                if gather:
                    line.block(links.z, piece)[...] = result
                    line.start(piece)

            stages = reduce_stages(reduce) + [settle]
            if gather:
                stages += [functools.partial(line.step, hop) for hop in range(links.size - 1)]
            wave(stages, pieces, queue)
            if settle_small:
                small = settle_small(links, near_refs, kind_refs, user)
            for item in gathers + old + fresh + straight:
                item.finish()
            for item in busy.values():
                item.clear()
            for copy in copies:
                copy.wait()
            if end:
                end(state[0], links, near_refs, kind_refs, user)
            if settle_small:
                small()
            store_kinds("post")
            if gather:
                store(whole_ref, whole_far)
            reduce.finish()
            if gather:
                line.finish()
            for copy in stores:
                copy.wait()

        order = sorted(range(count_near), key=lambda index: near[index][1])
        inputs = [(item, False) for items, _ in near for item in items]
        inputs += [(item, False) for item in moving + lines + adding + far]
        outputs = [(form, kind, False) for form, kind, _ in kinds]
        if gather:
            outputs.append(((length, width), jnp.bfloat16, False))
        outputs += self.gather_outputs(moving)
        outputs += [
            ((item.shape[0] * self.tensor, item.shape[1]), item.dtype, False) for item in lines
        ]
        outputs += job_outputs + sum_outputs
        results = list(
            self.call(
                name,
                body,
                inputs,
                outputs,
                [
                    pltpu.VMEM(
                        (*items[0].shape[:-1], sum(item.shape[-1] for item in items)),
                        items[0].dtype,
                    )
                    for items, _ in near
                ]
                + [pltpu.VMEM(form, kind) for form, kind, moment in kinds if moment]
                + ([pltpu.VMEM((length, width), jnp.bfloat16)] if gather else [])
                + [
                    pltpu.VMEM((length, width), jnp.bfloat16),
                    pltpu.VMEM((self.tensor - 1, rows, width), jnp.bfloat16),
                    pltpu.VMEM((self.tensor - 1, rows, width), jnp.bfloat16),
                    *scratch,
                    *job_scratch,
                    *sum_scratch,
                ],
                240,
            )
        )
        kept, results = results[:count_kinds], results[count_kinds:]
        whole, results = (results[0], results[1:]) if gather else (None, results)
        full, results = self.gathered(results[: len(moving)], shards), results[len(moving) :]
        lined, results = results[: len(lines)], results[len(lines) :]
        made, added = results[: len(jobs)], results[len(jobs) :]
        if not self.cube:
            made = [
                self.scatter(item) if job[4] else item for item, job in zip(made, jobs)
            ]
            added = [self.scatter(item) for item in sums]
        return kept, whole, full, lined, made, added

    def scatter(self, grad):
        return lax.psum_scatter(grad, "dp", scatter_dimension=0, tiled=True).astype(jnp.float32)


def add_sum(ref, row, values, first):
    total = jnp.sum(values, axis=0, keepdims=True)
    ref[row : row + 1, :] = total if first else ref[row : row + 1, :] + total


def tick(ticks):
    if ticks:
        ticks.pop(0)()


def tiles(count, size):
    return [(start, min(size, count - start)) for start in range(0, count, size)]


def body(
    plan,
    hidden_in,
    text_states,
    time_embed,
    positions,
    modulation,
    query_weight,
    key_weight,
    value_weight,
    out_weight,
    cross_query,
    cross_key,
    cross_value,
    cross_out,
    up_weight,
    down_weight,
    qk_gain,
    norm_gain,
    cotangent,
):
    plan.calls = 0
    low, full_type = jnp.bfloat16, jnp.float32
    rows, width = hidden_in.shape
    length = rows * plan.tensor
    here = out_weight.shape[0]
    heads = here // HEAD_DIM
    hidden_units = up_weight.shape[1]
    text_rows, text_width = length, text_states.shape[1]
    part = width // plan.dp
    text_part = text_width // plan.dp
    shape = (length, width)

    top = jnp.concatenate([modulation, norm_gain[None], jnp.zeros((1, part), low)], axis=0)
    side = jnp.pad(qk_gain, ((0, 8 - heads), (0, 0)))
    small = jnp.concatenate([top, side], axis=1).astype(full_type)
    time_rows = jnp.pad(time_embed[0], ((0, 2), (0, 0)))
    (mixing, gains, self_whole), full = plan.open(
        hidden_in, time_rows, small, [query_weight, key_weight, value_weight, out_weight.T]
    )
    query_full, key_full, value_full, out_full = full
    cosine, sine = rotary_tables(positions, HEAD_DIM)

    def forward(kinds_of_gain, angles, inputs, weights, gain_ref, kinds, scratch, links, partial, ticks):
        query_in, other_in = inputs
        query_w, key_w, value_w, out_w = weights
        query_raw, key_raw, value, query, key, attended, logs, inverse = kinds
        exchange = Exchange(links, *scratch)
        links.ready(0)
        query_raw[...] = jnp.dot(query_in[...], query_w[...], preferred_element_type=full_type)
        links.ready(1)
        key_raw[...] = jnp.dot(other_in[...], key_w[...], preferred_element_type=full_type)
        exchange.start(square_columns(query_raw[...], key_raw[...]))
        links.ready(2)
        value[...] = jnp.dot(
            other_in[...], value_w[...], preferred_element_type=full_type
        ).astype(low)
        inverse[...] = exchange.finish(lambda total: lax.rsqrt(total / D + EPSILON))
        tick(ticks)
        links.ready(3)
        for index, (raw, out) in enumerate(((query_raw, query), (key_raw, key))):
            shape_norm(
                raw,
                inverse[:, index : index + 1],
                gains_of(gain_ref, kinds_of_gain[index], heads),
                angles,
                out,
                heads,
            )
        attend(query, key, value, attended, logs, heads)
        tick(ticks)
        links.ready(4)
        for start, size in tiles(width, 512):
            partial[:, start : start + size] = product_back(
                attended[...], out_w[start : start + size, :]
            ).astype(low)

    kept_kinds = [
        ((length, here), full_type, "pre"),
        ((length, here), full_type, "pre"),
        ((length, here), low, "pre"),
        ((length, here), low, "pre"),
        ((length, here), low, "pre"),
        ((length, here), low, "pre"),
        ((length, HEAD_DIM), full_type, "pre"),
        ((length, HEAD_DIM), full_type, "pre"),
    ]

    def self_pre(links, near, kinds, scratch, partial, ticks):
        whole, gain_ref, cosine_ref, sine_ref = near[:4]
        forward(
            (0, 1),
            (cosine_ref, sine_ref),
            (whole, whole),
            near[4:8],
            gain_ref,
            kinds[:8],
            scratch,
            links,
            partial,
            ticks,
        )

    def after_self(total, where, near, kinds, first):
        hidden_ref, mixing_ref = near[8:]
        branch_ref, resid_ref = kinds[8:]
        branch_ref[where, :] = total
        resid = hidden_ref[where, :] + total * mixing_ref[2:3]
        resid_ref[where, :] = resid
        unit, _ = normed(resid)
        return (unit * mixing_ref[6:7]).astype(low)

    text_after, self_whole = lax.optimization_barrier((text_states, self_whole))
    text_all = lax.all_gather(text_after, "tensor", axis=0, tiled=True)
    kept, cross_whole, full, _, _, _ = plan.phase(
        "self_forward",
        [(self_whole, 0), (gains, 3), (cosine, 3), (sine, 3), (query_full, 0), (key_full, 1)]
        + [(value_full, 2), (out_full, 4), (hidden_in, 5), (mixing, 5)],
        kept_kinds + [((rows, width), full_type, "post")] * 2,
        exchange_scratch(length, plan.tensor),
        self_pre,
        after_self,
        True,
        shape,
        shards=[cross_key, cross_value, cross_query, cross_out.T, up_weight, down_weight.T],
    )
    self_kept, (self_branch, resid_self) = kept[:8], kept[8:]
    cross_key_full, cross_value_full, cross_query_full, cross_out_full = full[:4]
    up_full, down_full = full[4:]

    def cross_begin(links, near, kinds, scratch, far):
        links.ready(-1)
        mixing_ref, cotangent_ref = near[8:]
        whole = kinds[9]
        mine = piece_of(whole, links.z, rows, 0, rows)
        mine[...] = (cotangent_ref[...] * mixing_ref[5:6]).astype(low)
        line = LineGather(links, whole, rows, 1)
        line.start(0)
        return line, [functools.partial(line.step, hop, 0) for hop in range(links.size - 1)]

    def cross_end(line, links, near, kinds, scratch):
        line.finish()

    def cross_pre(links, near, kinds, scratch, partial, ticks):
        whole, text, gain_ref = near[:3]
        forward(
            (2, 3),
            None,
            (whole, text),
            near[3:7],
            gain_ref,
            kinds[:8],
            scratch,
            links,
            partial,
            ticks,
        )

    def after_cross(total, where, near, kinds, first):
        resid_ref, mixing_ref = near[7:9]
        resid = resid_ref[where, :] + total
        kinds[8][where, :] = resid
        unit, _ = normed(resid)
        return (unit * (1.0 + mixing_ref[4:5]) + mixing_ref[3:4]).astype(low)

    kept, feed_whole, _, _, _, _ = plan.phase(
        "cross_forward",
        [(cross_whole, 0), (text_all, 1), (gains, 3), (cross_query_full, 0), (cross_key_full, 1)]
        + [(cross_value_full, 2), (cross_out_full, 4), (resid_self, 5), (mixing, -1)]
        + [(cotangent, -1)],
        kept_kinds + [((rows, width), full_type, "post"), ((length, width), low, "post")],
        exchange_scratch(length, plan.tensor),
        cross_pre,
        after_cross,
        True,
        shape,
        begin=cross_begin,
        end=cross_end,
    )
    cross_kept, (resid_cross, feed_grad_whole) = kept[:8], kept[8:]

    feed_tiles = tiles(hidden_units, 512)

    def feed_begin(links, near, kinds, scratch, far):
        copies = []
        for start, size in feed_tiles:
            lanes = pl.ds(start, size)
            pair = [
                links.here(far[which].at[:, lanes], scratch[2 + which].at[:, lanes])
                for which in range(2)
            ]
            for copy in pair:
                copy.start()
            copies.append(pair)
        return None, copies

    def feed_pre(links, near, kinds, scratch, partial, copies):
        whole, grad_whole = near[:2]
        activated, grad_raw, up, down = scratch
        root = 0.7978845608028654
        links.ready(0)
        for (begin, size), pair in zip(feed_tiles, copies):
            lanes = slice(begin, begin + size)
            for copy in pair:
                copy.wait()

            def one(step, _, lanes=lanes):
                block = pl.ds(pl.multiple_of(step * 256, 256), 256)
                raw = jnp.dot(whole[block, :], up[:, lanes], preferred_element_type=full_type)
                grad = jnp.dot(grad_whole[block, :], down[:, lanes], preferred_element_type=full_type)
                square = raw * raw
                bend = jnp.tanh(root * raw * (1.0 + 0.044715 * square))
                half = 0.5 + 0.5 * bend
                activated[block, lanes] = (raw * half).astype(low)
                slope = half + 0.5 * raw * (1.0 - bend * bend) * root * (
                    1.0 + 3.0 * 0.044715 * square
                )
                grad_raw[block, lanes] = (grad * slope).astype(low)
                return 0

            lax.fori_loop(0, length // 256, one, 0)
        copies.clear()
        for start, size in tiles(width, 512):
            partial[:, start : start + size] = product_back(
                grad_raw[...], up[start : start + size, :]
            ).astype(low)

    def feed_tasks(links, near, kinds, scratch, far):
        activated, down = scratch[0], scratch[3]

        def one(start, size):
            kinds[2][:, start : start + size] = product_back(
                activated[...], down[start : start + size, :]
            ).astype(low)

        return [functools.partial(one, start, size) for start, size in tiles(width, 512)]

    def before_feed(total, where, near, kinds, first):
        resid_ref, cotangent_ref, mixing_ref = near[2:]
        grad_ref, sums_ref = kinds[:2]
        unit, inverse = normed(resid_ref[where, :])
        add_sum(sums_ref, 0, total, first)
        add_sum(sums_ref, 1, total * unit, first)
        grad = cotangent_ref[where, :] + normed_back(
            unit, inverse, total * (1.0 + mixing_ref[4:5])
        )
        grad_ref[where, :] = grad
        return grad.astype(low)

    kept, cross_grad_whole, _, _, made, _ = plan.phase(
        "feed",
        [(feed_whole, 0), (feed_grad_whole, 0), (resid_cross, 1), (cotangent, 1), (mixing, 1)],
        [
            ((rows, width), full_type, "post"),
            ((8, width), full_type, "post"),
            ((length, width), low, "post"),
        ],
        [pltpu.VMEM((length, hidden_units), low)] * 2
        + [pltpu.VMEM((width, hidden_units), low)] * 2,
        feed_pre,
        before_feed,
        True,
        shape,
        jobs=[
            (lambda n, k, s: n[1], lambda n, k, s: s[0], part, hidden_units, False),
            (lambda n, k, s: n[0], lambda n, k, s: s[1], part, hidden_units, False),
        ],
        tasks=feed_tasks,
        begin=feed_begin,
        far=[up_full, down_full],
        exchange=False,
    )
    grad_resid_cross, feed_sums, feed_partial = kept
    near_down, near_up = made

    def backward(kinds_of_gain, angles, refs, gain_ref, grad_outs, scratch, links, partial, ticks):
        (grad_whole, query_w, key_w, value_w, out_w) = refs[:5]
        query_raw, key_raw, value, query, key, attended, logs, inverse = refs[5:]
        gain_query_ref, gain_key_ref, query_out, key_out, value_out = grad_outs
        grad_attended, grad_query, grad_key, grad_value = scratch[3:7]
        exchange = Exchange(links, *scratch[:3])
        links.ready(0)
        grad_attended[...] = jnp.dot(
            grad_whole[...], out_w[...], preferred_element_type=full_type
        ).astype(low)
        links.ready(1)
        attend_back(
            query, key, value, logs, grad_attended, (grad_query, grad_key, grad_value), heads
        )
        tick(ticks)
        links.ready(2)
        sides = (
            (query_raw, inverse[:, 0:1], gains_of(gain_ref, kinds_of_gain[0], heads)),
            (key_raw, inverse[:, 1:2], gains_of(gain_ref, kinds_of_gain[1], heads)),
        )
        exchange.start(
            [
                norm_dots(*sides[0], angles, grad_query, gain_query_ref, heads),
                norm_dots(*sides[1], angles, grad_key, gain_key_ref, heads),
            ]
        )
        value_out[...] = grad_value[...].astype(low)
        dots = exchange.finish()
        tick(ticks)
        norm_pull(*sides[0], dots[:, 0:1], grad_query, query_out, heads)
        norm_pull(*sides[1], dots[:, 1:2], grad_key, key_out, heads)
        links.ready(3)
        pairs = [(query_out, query_w)]
        if angles is not None:
            pairs += [(key_out, key_w), (value_out, value_w)]
        for start, size in tiles(width, 512):
            total = 0.0
            for grads, weight in pairs:
                total = total + product_back(grads[...], weight[start : start + size, :])
            partial[:, start : start + size] = total.astype(low)

    back_scratch = exchange_scratch(length, plan.tensor) + [
        pltpu.VMEM((length, here), low),
        pltpu.VMEM((length, here), full_type),
        pltpu.VMEM((length, here), full_type),
        pltpu.VMEM((length, here), full_type),
        pltpu.VMEM((length, here), low),
        pltpu.VMEM((length, here), low),
        pltpu.VMEM((length, here), low),
    ]

    kept_groups = (2, 2, 1, 1, 1, 4, 1, 2)

    def cross_back_begin(links, near, kinds, scratch, far):
        links.ready(-1)
        late = LineReduce(links, near[20], scratch[10], scratch[11], rows, 1)
        late.clear()
        first, *others = late.stages(0)
        first()
        return late, others

    def cross_back_end(late, links, near, kinds, scratch):
        cotangent_ref, mixing_ref, resid_ref = near[17:20]
        total = late.total(0)
        kinds[2][...] = resid_ref[...] + total * mixing_ref[5:6]
        add_sum(kinds[1], 2, cotangent_ref[...] * total, True)
        late.finish()

    def cross_back_pre(links, near, kinds, scratch, partial, ticks):
        backward(
            (2, 3),
            None,
            (near[0], near[1], None, None, *near[2:11]),
            near[11],
            (kinds[4], kinds[5], *scratch[7:10]),
            scratch,
            links,
            partial,
            ticks,
        )

    def cross_back_tasks(links, near, kinds, scratch, far):
        held, loaded = scratch[12:14]
        size = held.shape[2]
        out_copies, loads = [], {}

        def load(index):
            loads[index] = [
                links.here(weight.at[pl.ds(index * size, size)], loaded.at[index % 2, which])
                for which, weight in enumerate(far)
            ]
            for copy in loads[index]:
                copy.start()

        def one(index):
            if index >= 2:
                out_copies[index - 2].wait()
            for copy in loads[index]:
                copy.wait()
            stage = held.at[index % 2]
            stage[...] = (
                product_back(scratch[8][...], loaded[index % 2, 0])
                + product_back(scratch[9][...], loaded[index % 2, 1])
            ).astype(low)
            if index + 2 < text_width // size:
                load(index + 2)
            copy = links.here(stage, kinds[3].at[:, pl.ds(index * size, size)])
            copy.start()
            out_copies.append(copy)

        def last():
            for copy in out_copies[-2:]:
                copy.wait()

        load(0)
        load(1)
        steps = [functools.partial(one, index) for index in range(text_width // size)]
        return steps + [last]

    def before_cross(total, where, near, kinds, first):
        resid_ref, grad_ref, branch_ref = near[14:17]
        mixing_ref = near[18]
        out_ref, sums_ref = kinds[:2]
        unit, inverse = normed(resid_ref[where, :])
        add_sum(sums_ref, 1, total * unit, first)
        grad = grad_ref[where, :] + normed_back(unit, inverse, total * mixing_ref[6:7])
        out_ref[where, :] = grad
        add_sum(sums_ref, 0, grad * branch_ref[where, :], first)
        return (grad * mixing_ref[2:3]).astype(low)

    kept, self_grad_whole, _, _, made, (sum_down, sum_up) = plan.phase(
        "cross_back",
        [(cross_grad_whole, 0), (cross_query_full, 3), (cross_out_full, 0)]
        + list(zip(cross_kept, kept_groups))
        + [(gains, 2), (cross_whole, 4), (text_all, 4), (resid_self, 4), (grad_resid_cross, 4)]
        + [(self_branch, 4), (cotangent, 4), (mixing, 4), (resid_cross, 4), (feed_partial, -1)],
        [
            ((rows, width), full_type, "post"),
            ((8, width), full_type, "post"),
            ((rows, width), full_type, "post"),
            ((text_rows, text_width), low, None),
            ((8, HEAD_DIM), full_type, "pre"),
            ((8, HEAD_DIM), full_type, "pre"),
        ],
        back_scratch
        + [pltpu.VMEM((plan.tensor - 1, rows, width), low)] * 2
        + [pltpu.VMEM((2, text_rows, 1024), low), pltpu.VMEM((2, 2, 1024, here), low)],
        cross_back_pre,
        before_cross,
        True,
        shape,
        sums=[near_down, near_up],
        jobs=[
            (lambda n, k, s: n[13], lambda n, k, s: s[8], text_part, here, False),
            (lambda n, k, s: n[13], lambda n, k, s: s[9], text_part, here, False),
            (lambda n, k, s: n[12], lambda n, k, s: s[7], part, here, False),
            (lambda n, k, s: n[0], lambda n, k, s: n[8], part, here, False),
        ],
        tasks=cross_back_tasks,
        begin=cross_back_begin,
        end=cross_back_end,
        far=[cross_key_full, cross_value_full],
    )
    grad_resid_self, cross_sums, block_out, text_partial, gain_cross_query, gain_cross_key = kept
    grad_text = lax.psum_scatter(
        text_partial, "tensor", scatter_dimension=0, tiled=True
    ).astype(full_type)

    def self_back_pre(links, near, kinds, scratch, partial, ticks):
        backward(
            (0, 1),
            (near[14], near[15]),
            near[:13],
            near[13],
            (kinds[2], kinds[3], *scratch[7:10]),
            scratch,
            links,
            partial,
            ticks,
        )

    def before_self(total, where, near, kinds, first):
        hidden_ref, grad_ref, mixing_ref = near[17:20]
        out_ref, sums_ref = kinds[:2]
        unit, inverse = normed(hidden_ref[where, :])
        add_sum(sums_ref, 0, total, first)
        add_sum(sums_ref, 1, total * unit, first)
        out_ref[where, :] = grad_ref[where, :] + normed_back(
            unit, inverse, total * (1.0 + mixing_ref[1:2])
        )

    gain_width = qk_gain.shape[1]

    def settle_small(links, near, kinds, scratch):
        feed_ref, cross_ref, gain_cross_query_ref, gain_cross_key_ref = near[20:]
        self_ref, gain_query_ref, gain_key_ref, time_ref, slice_ref = kinds[1:]
        mine, line_land, stage, land = scratch[10:]
        z, dp = links.z, links.dp
        mine[...] = jnp.concatenate(
            [
                self_ref[0:2, :],
                cross_ref[0:1, :],
                feed_ref[0:2, :],
                cross_ref[2:3, :],
                cross_ref[1:2, :],
                jnp.zeros((1, width), full_type),
            ],
            axis=0,
        )
        moves = []
        for step in range(1, plan.tensor):
            target = lax.rem(z + step, plan.tensor)
            move = links.copy(mine, line_land.at[z], (dp, target), links.slot())
            move.start()
            moves.append(move)
        line_land[z] = mine[...]
        gain_rows = jnp.concatenate(
            [gain_query_ref[...], gain_key_ref[...]]
            + [gain_cross_query_ref[...], gain_cross_key_ref[...]],
            axis=1,
        )
        for move in moves:
            move.wait_recv()
        total = line_land[0]
        for index in range(1, plan.tensor):
            total = total + line_land[index]
        time_ref[0, :, :] = total[:6]
        for index in range(plan.dp):
            stage[index] = jnp.concatenate(
                [
                    total[:, index * part : (index + 1) * part],
                    gain_rows[:, index * gain_width : (index + 1) * gain_width],
                ],
                axis=1,
            )
        land[dp] = stage[dp]
        others = []
        for step in range(1, plan.dp):
            target = lax.rem(dp + step, plan.dp)
            move = links.copy(stage.at[target], land.at[dp], (target, z), links.slot())
            move.start()
            others.append(move)

        def finish():
            for move in others:
                move.wait_recv()
            summed = land[0]
            for index in range(1, plan.dp):
                summed = summed + land[index]
            slice_ref[...] = summed
            for move in moves + others:
                move.wait_send()

        return finish

    kept, _, _, _, made, sums = plan.phase(
        "self_back",
        [(self_grad_whole, 0), (query_full, 3), (key_full, 3), (value_full, 3), (out_full, 0)]
        + list(zip(self_kept, kept_groups))
        + [(gains, 2), (cosine, 2), (sine, 2), (self_whole, 4), (hidden_in, 4)]
        + [(grad_resid_self, 4), (mixing, 4), (feed_sums, 4), (cross_sums, 4)]
        + [(gain_cross_query, 4), (gain_cross_key, 4)],
        [
            ((rows, width), full_type, "post"),
            ((8, width), full_type, "post"),
            ((8, HEAD_DIM), full_type, "pre"),
            ((8, HEAD_DIM), full_type, "pre"),
            ((1, 6, width), full_type, "post"),
            ((8, part + gain_width), full_type, "post"),
        ],
        back_scratch
        + [
            pltpu.VMEM((8, width), full_type),
            pltpu.VMEM((plan.tensor, 8, width), full_type),
            pltpu.VMEM((plan.dp, 8, part + gain_width), full_type),
            pltpu.VMEM((plan.dp, 8, part + gain_width), full_type),
        ],
        self_back_pre,
        before_self,
        False,
        shape,
        sums=made,
        jobs=[
            (lambda n, k, s: n[16], lambda n, k, s: s[7], part, here, True),
            (lambda n, k, s: n[16], lambda n, k, s: s[8], part, here, True),
            (lambda n, k, s: n[16], lambda n, k, s: s[9], part, here, True),
            (lambda n, k, s: n[0], lambda n, k, s: n[10], part, here, True),
        ],
        settle_small=settle_small,
    )
    grad_hidden, _, _, _, grad_time, mine = kept
    sum_cross_key, sum_cross_value, sum_cross_query, sum_cross_out = sums
    sum_query, sum_key, sum_value, sum_out = made

    return (
        block_out,
        grad_hidden,
        grad_text,
        grad_time,
        mine[:6, :part],
        sum_query,
        sum_key,
        sum_value,
        sum_out.T,
        sum_cross_query,
        sum_cross_key,
        sum_cross_value,
        sum_cross_out.T,
        sum_up,
        sum_down.T,
        mine[:heads, part:],
        mine[6, :part],
    )


def solution(mesh):
    return jax.shard_map(
        functools.partial(body, Plan(mesh)),
        mesh=mesh,
        in_specs=(
            P(("dp", "tensor"), None),
            P(("dp", "tensor"), None),
            P("dp", None, None),
            P(None, "dp"),
            P(None, "dp"),
            P("dp", "tensor"),
            P("dp", "tensor"),
            P("dp", "tensor"),
            P("tensor", "dp"),
            P("dp", "tensor"),
            P("dp", "tensor"),
            P("dp", "tensor"),
            P("tensor", "dp"),
            P("dp", "tensor"),
            P("tensor", "dp"),
            P("tensor", "dp"),
            P("dp"),
            P(("dp", "tensor"), None),
        ),
        out_specs=(
            P(("dp", "tensor"), None),
            P(("dp", "tensor"), None),
            P(("dp", "tensor"), None),
            P("dp", None, None),
            P(None, "dp"),
            P("dp", "tensor"),
            P("dp", "tensor"),
            P("dp", "tensor"),
            P("tensor", "dp"),
            P("dp", "tensor"),
            P("dp", "tensor"),
            P("dp", "tensor"),
            P("tensor", "dp"),
            P("dp", "tensor"),
            P("tensor", "dp"),
            P("tensor", "dp"),
            P("dp"),
        ),
        check_vma=False,
    )
```

```python
import functools

import jax
import jax.numpy as jnp
from jax import lax
from jax.experimental import pallas as pl
from jax.experimental.pallas import tpu as pltpu
from jax.sharding import PartitionSpec as P

MESH = pl.DeviceIdType.MESH
VMEM_BYTES = 62 * 2**20

HEAD_DIM = 128
D = 1536


EPSILON = 1e-06
CONTRACT_LAST = (((1,), (1,)), ((), ()))
CONTRACT_FIRST = (((0,), (0,)), ((), ()))


def rotary_tables(positions, head_width):
    pairs = head_width // 2
    third = pairs // 3
    first = pairs - 2 * third
    freq_frame = jnp.power(10000.0, -jnp.arange(first, dtype=jnp.float32) / first)
    freq_side = jnp.power(10000.0, -jnp.arange(third, dtype=jnp.float32) / third)
    places = positions.astype(jnp.float32)
    angles = jnp.concatenate(
        [
            places[0][:, None] * jnp.repeat(freq_frame, 2)[None, :],
            places[1][:, None] * jnp.repeat(freq_side, 2)[None, :],
            places[2][:, None] * jnp.repeat(freq_side, 2)[None, :],
        ],
        axis=1,
    )
    sign = jnp.where(jnp.arange(head_width) % 2 == 0, -1.0, 1.0)
    return (jnp.cos(angles), jnp.sin(angles) * sign)


def product_back(grads, weight):
    return lax.dot_general(grads, weight, CONTRACT_LAST, preferred_element_type=jnp.float32)


def weight_grad(inputs, grads):
    return lax.dot_general(inputs, grads, CONTRACT_FIRST, preferred_element_type=jnp.float32)


def when(cond, run):
    if cond is None:
        run()
    else:
        pl.when(cond)(run)


def flip(index, bit):
    return index + bit - 2 * bit * (index // bit % 2)


def normed(values):
    center = values - jnp.mean(values, axis=-1, keepdims=True)
    inverse = lax.rsqrt(jnp.mean(center * center, axis=-1, keepdims=True) + EPSILON)
    return center * inverse, inverse


def normed_back(unit, inverse, grad):
    mean_grad = jnp.mean(grad, axis=-1, keepdims=True)
    mean_dot = jnp.mean(grad * unit, axis=-1, keepdims=True)
    return (grad - mean_grad - unit * mean_dot) * inverse


class Links:
    def __init__(self, send, recv, local, dp_size, tensor_size):
        self.send, self.recv, self.local = send, recv, local
        self.count = 0
        self.local_count = 0
        self.dp_size, self.size = dp_size, tensor_size
        self.dp = lax.axis_index("dp")
        self.z = lax.axis_index("tensor")

    def slot(self):
        self.count += 1
        return self.count - 1

    def copy(self, source, target, device, slot):
        return pltpu.make_async_remote_copy(
            src_ref=source,
            dst_ref=target,
            send_sem=self.send.at[slot],
            recv_sem=self.recv.at[slot],
            device_id=device,
            device_id_type=MESH,
        )

    def here(self, source, target):
        self.local_count += 1
        return pltpu.make_async_copy(source, target, self.local.at[self.local_count - 1])

    def greet(self, groups):
        barrier = pltpu.get_barrier_semaphore()
        peers = []
        if "line" in groups and "zall" not in groups:
            peers += [
                ((self.dp, self.z - 1), self.z > 0),
                ((self.dp, self.z + 1), self.z < self.size - 1),
            ]
        if "zall" in groups:
            peers += [
                ((self.dp, lax.rem(self.z + k, self.size)), None) for k in range(1, self.size)
            ]
        if "dpall" in groups:
            peers += [
                ((lax.rem(self.dp + k, self.dp_size), self.z), None)
                for k in range(1, self.dp_size)
            ]
        if "bits" in groups and "dpall" not in groups:
            bit = 1
            while bit < self.dp_size:
                peers.append(((flip(self.dp, bit), self.z), None))
                bit *= 2
        if "diag" in groups and "dpall" not in groups:
            peers.append(((flip(flip(self.dp, 2), 4), self.z), None))
        for device, cond in peers:
            when(
                cond,
                lambda device=device: pl.semaphore_signal(
                    barrier, inc=1, device_id=device, device_id_type=MESH
                ),
            )
        expected = sum(1 for _, cond in peers if cond is None)
        for _, cond in peers:
            if cond is not None:
                expected = expected + cond.astype(jnp.int32)
        pl.semaphore_wait(barrier, expected)


def piece_of(ref, block, rows, start, count):
    return ref.at[pl.ds(pl.multiple_of(block * rows + start, 16), count)]


class LineGather:
    def __init__(self, links, whole, rows, pieces):
        self.links, self.whole, self.rows, self.count = links, whole, rows, rows // pieces
        self.pieces = pieces
        hops = links.size - 1
        self.right = [[links.slot() for _ in range(pieces)] for _ in range(hops)]
        self.left = [[links.slot() for _ in range(pieces)] for _ in range(hops)]

    def block(self, index, piece):
        return piece_of(self.whole, index, self.rows, piece * self.count, self.count)

    def move(self, index, piece, way, slot):
        part = self.block(index, piece)
        return self.links.copy(part, part, (self.links.dp, self.links.z + way), slot)

    def start(self, piece, source=None):
        links = self.links
        z, last = links.z, links.size - 1

        def go(way, slot):
            mine = self.block(z, piece)
            links.copy(mine if source is None else source, mine, (links.dp, z + way), slot).start()

        when(z < last, lambda: go(1, self.right[0][piece]))
        when(z > 0, lambda: go(-1, self.left[0][piece]))

    def step(self, hop, piece):
        z, last = self.links.z, self.links.size - 1

        def from_left():
            self.move(z - 1 - hop, piece, -1, self.right[hop][piece]).wait_recv()
            if hop + 1 < last:
                when(
                    z < last,
                    lambda: self.move(z - 1 - hop, piece, 1, self.right[hop + 1][piece]).start(),
                )

        def from_right():
            self.move(z + 1 + hop, piece, 1, self.left[hop][piece]).wait_recv()
            if hop + 1 < last:
                when(
                    z > 0,
                    lambda: self.move(z + 1 + hop, piece, -1, self.left[hop + 1][piece]).start(),
                )

        when(z - 1 - hop >= 0, from_left)
        when(z + 1 + hop <= last, from_right)

    def steps(self, piece):
        for hop in range(self.links.size - 1):
            self.step(hop, piece)

    def finish(self):
        z, last = self.links.z, self.links.size - 1
        for hop in range(last):
            for piece in range(self.pieces):
                when(
                    (z - hop >= 0) & (z < last),
                    lambda: self.move(z - hop, piece, 1, self.right[hop][piece]).wait_send(),
                )
                when(
                    (z + hop <= last) & (z > 0),
                    lambda: self.move(z + hop, piece, -1, self.left[hop][piece]).wait_send(),
                )


class LineReduce:
    def __init__(self, links, partial, land_right, land_left, rows, pieces):
        self.links, self.partial, self.rows, self.count = links, partial, rows, rows // pieces
        self.land = {1: land_right, -1: land_left}
        self.pieces = pieces
        last = links.size - 1
        self.slots = {
            way: [None] + [[links.slot() for _ in range(pieces)] for _ in range(last)]
            for way in (1, -1)
        }

    def landing(self, way, distance, piece):
        return self.land[way].at[distance - 1, pl.ds(piece * self.count, self.count)]

    def part(self, index, piece):
        return piece_of(self.partial, index, self.rows, piece * self.count, self.count)

    def move(self, source, way, distance, piece):
        return self.links.copy(
            source,
            self.landing(way, distance, piece),
            (self.links.dp, self.links.z + way),
            self.slots[way][distance][piece],
        )

    def arrived(self, way, distance, piece):
        self.links.copy(
            self.landing(way, distance, piece),
            self.landing(way, distance, piece),
            (self.links.dp, self.links.z - way),
            self.slots[way][distance][piece],
        ).wait_recv()

    def first(self, piece):
        z, last = self.links.z, self.links.size - 1

        def from_first():
            for distance in range(last, 0, -1):
                self.move(self.part(distance, piece), 1, distance, piece).start()

        def from_last():
            for distance in range(last, 0, -1):
                self.move(self.part(last - distance, piece), -1, distance, piece).start()

        when(z == 0, from_first)
        when(z == last, from_last)

    def first_at(self, distance, piece):
        z, last = self.links.z, self.links.size - 1
        when(
            z == 0,
            lambda: self.move(self.part(distance, piece), 1, distance, piece).start(),
        )
        when(
            z == last,
            lambda: self.move(self.part(last - distance, piece), -1, distance, piece).start(),
        )

    def stages(self, piece):
        last = self.links.size - 1

        def one(distance):
            self.first_at(distance, piece)
            if distance < last:
                self.step(distance, piece)

        return [functools.partial(one, distance) for distance in range(last, 0, -1)]

    def clear(self):
        z, last = self.links.z, self.links.size - 1

        def zero(way):
            self.land[way][0] = jnp.zeros(self.land[way].shape[1:], self.land[way].dtype)

        when(z == 0, lambda: zero(1))
        when(z == last, lambda: zero(-1))

    def step(self, distance, piece):
        z, last = self.links.z, self.links.size - 1
        for way in (1, -1):
            inside = (
                (z > 0) & (z + distance <= last)
                if way == 1
                else (z < last) & (z - distance >= 0)
            )

            def go(way=way):
                self.arrived(way, distance + 1, piece)
                held = self.landing(way, distance + 1, piece)
                own = self.part(z + way * distance, piece)
                held[...] = (
                    held[...].astype(jnp.float32) + own[...].astype(jnp.float32)
                ).astype(held.dtype)
                self.move(held, way, distance, piece).start()

            when(inside, go)

    def total(self, piece):
        z, last = self.links.z, self.links.size - 1
        when(z > 0, lambda: self.arrived(1, 1, piece))
        when(z < last, lambda: self.arrived(-1, 1, piece))
        return (
            self.part(z, piece)[...].astype(jnp.float32)
            + self.landing(1, 1, piece)[...].astype(jnp.float32)
            + self.landing(-1, 1, piece)[...].astype(jnp.float32)
        )

    def finish(self):
        z, last = self.links.z, self.links.size - 1
        for distance in range(1, last + 1):
            for piece in range(self.pieces):
                held = self.landing(1, distance, piece)
                when(
                    z + distance <= last,
                    lambda: self.move(held, 1, distance, piece).wait_send(),
                )
                back = self.landing(-1, distance, piece)
                when(
                    z - distance >= 0,
                    lambda: self.move(back, -1, distance, piece).wait_send(),
                )


def reduce_stages(reduce):
    return [
        functools.partial(reduce.step, distance)
        for distance in range(reduce.links.size - 2, 0, -1)
    ]


def wave(stages, pieces, queue):
    count = pieces + len(stages) - 1
    done = 0
    for step in range(count):
        for index, stage in enumerate(stages):
            if 0 <= step - index < pieces:
                stage(step - index)
        until = len(queue) * (step + 1) // count
        for run in queue[done:until]:
            run()
        done = until


class CubeGather:
    def __init__(self, links, shard, whole):
        self.links, self.shard, self.whole = links, shard, whole
        self.rows = shard.shape[0]
        self.slots = [links.slot() for _ in range(8)]
        dp = links.dp
        self.core, self.side, self.over = flip(dp, 1), flip(dp, 2), flip(dp, 4)
        self.far = flip(flip(dp, 2), 4)
        self.sent = []

    def block(self, index, start=0, count=None):
        return piece_of(self.whole, index, self.rows, start, count or self.rows)

    def send(self, source, target, device, slot):
        move = self.links.copy(source, target, (device, self.links.z), self.slots[slot])
        move.start()
        self.sent.append(move)

    def got(self, part, slot):
        self.links.copy(part, part, (self.core, self.links.z), self.slots[slot]).wait_recv()

    def start(self):
        mine = self.block(self.links.dp)
        self.own = self.links.here(self.shard, mine)
        self.own.start()
        self.send(self.shard, mine, self.side, 1)
        self.send(self.shard, mine, self.over, 2)
        self.send(self.shard, mine, self.core, 0)

    def forward(self):
        half = self.rows // 2
        self.got(self.block(self.side), 1)
        part = self.block(self.side, 0, half)
        self.send(part, part, self.over, 3)
        part = self.block(self.side)
        self.send(part, part, self.core, 5)
        self.got(self.block(self.over), 2)
        part = self.block(self.over, half, half)
        self.send(part, part, self.side, 4)
        part = self.block(self.over)
        self.send(part, part, self.core, 6)

    def tail(self):
        half = self.rows // 2
        self.got(self.block(self.far, 0, half), 3)
        self.got(self.block(self.far, half, half), 4)
        part = self.block(self.far)
        self.send(part, part, self.core, 7)

    def finish(self):
        self.got(self.block(self.core), 0)
        self.got(self.block(flip(self.core, 2)), 5)
        self.got(self.block(flip(self.core, 4)), 6)
        self.got(self.block(flip(flip(self.core, 2), 4)), 7)
        for move in self.sent:
            move.wait_send()
        self.own.wait()


class Exchange:
    def __init__(self, links, mine, land, turned):
        self.links, self.mine, self.land, self.turned = links, mine, land, turned
        self.slots = [links.slot() for _ in range(links.size - 1)]

    def start(self, columns):
        links = self.links
        lane = lax.broadcasted_iota(jnp.int32, (columns[0].shape[0], 128), 1)
        flat = jnp.zeros(lane.shape, jnp.float32)
        for index, column in enumerate(columns):
            flat = jnp.where(lane == index, column, flat)
        self.mine[...] = flat.T[:8]
        self.moves = [
            links.copy(
                self.mine,
                self.land.at[step - 1],
                (links.dp, lax.rem(links.z + step, links.size)),
                slot,
            )
            for step, slot in enumerate(self.slots, 1)
        ]
        for move in self.moves:
            move.start()

    def finish(self, shape=lambda total: total):
        total = self.mine[...]
        for step, move in enumerate(self.moves):
            move.wait_recv()
            total = total + self.land[step]
        self.turned[...] = jnp.zeros(self.turned.shape, jnp.float32)
        self.turned[0:8, :] = shape(total)
        for move in self.moves:
            move.wait_send()
        return self.turned[...].T


class CoreSum:
    def __init__(self, links, left, right, product, near):
        self.links, self.left, self.right = links, left, right
        self.product, self.near = product, near
        self.rows = near.shape[1]
        self.slots = [links.slot() for _ in range(4)]
        self.core = links.dp % 2
        self.moves = []

    def multiply(self, chip):
        links, count = self.links, 2 * self.rows
        self.product[chip * count : (chip + 1) * count, :] = weight_grad(
            self.left[:, chip * count : (chip + 1) * count], self.right[...]
        ).astype(jnp.bfloat16)
        move = links.copy(
            piece_of(self.product, 2 * chip + 1 - self.core, self.rows, 0, self.rows),
            self.near.at[chip],
            (flip(links.dp, 1), links.z),
            self.slots[chip],
        )
        move.start()
        self.moves.append(move)

    def add(self):
        for move in self.moves:
            move.wait_recv()

        def one(step, _):
            rows = pl.ds(pl.multiple_of(step * 16, 16), 16)
            for chip in range(4):
                own = pl.ds(
                    pl.multiple_of((2 * chip + self.core) * self.rows + step * 16, 16), 16
                )
                self.near[chip, rows, :] = (
                    self.near[chip, rows, :].astype(jnp.float32)
                    + self.product[own, :].astype(jnp.float32)
                ).astype(jnp.bfloat16)
            return 0

        lax.fori_loop(0, self.rows // 16, one, 0)

    def clear(self):
        for move in self.moves:
            move.wait_send()

    def steps(self):
        return [functools.partial(self.multiply, chip) for chip in range(4)] + [self.add]


class ChipSum:
    def __init__(self, links, near, out, others, own=None):
        self.links, self.near, self.out, self.others, self.own = links, near, out, others, own
        self.slots = [links.slot() for _ in range(3)]
        self.core, self.chip = links.dp % 2, links.dp // 2
        self.rows = out.shape[0]

    def start(self):
        links = self.links
        chips = [flip(self.chip, 1), flip(self.chip, 2), flip(flip(self.chip, 1), 2)]
        self.moves = [
            links.copy(
                self.near.at[chip],
                self.others.at[index],
                (2 * chip + self.core, links.z),
                self.slots[index],
            )
            for index, chip in enumerate(chips)
        ]
        for move in self.moves:
            move.start()
        if self.own is not None:
            self.local = links.here(self.near.at[self.chip], self.own)
            self.local.start()

    def finish(self):
        for move in self.moves:
            move.wait_recv()
        if self.own is not None:
            self.local.wait()

        def one(step, _):
            rows = pl.ds(pl.multiple_of(step * 16, 16), 16)
            mine = self.own[rows, :] if self.own is not None else self.near[self.chip, rows, :]
            total = mine.astype(jnp.float32)
            for index in range(3):
                total = total + self.others[index, rows, :].astype(jnp.float32)
            self.out[rows, :] = total
            return 0

        lax.fori_loop(0, self.rows // 16, one, 0)
        for move in self.moves:
            move.wait_send()


def attend(query, key, value, out, logs, heads, chunk=256):
    scale = HEAD_DIM**-0.5
    for head in range(heads):
        lanes = slice(head * HEAD_DIM, (head + 1) * HEAD_DIM)

        def one(step, _, head=head, lanes=lanes):
            rows = pl.ds(pl.multiple_of(step * chunk, chunk), chunk)
            scores = product_back(query[rows, lanes], key[:, lanes]) * scale
            top = jnp.max(scores, axis=-1, keepdims=True)
            expo = jnp.exp(scores - top)
            summed = jnp.sum(expo, axis=-1, keepdims=True)
            probs = (expo * (1.0 / summed)).astype(jnp.bfloat16)
            out[rows, lanes] = jnp.dot(
                probs, value[:, lanes], preferred_element_type=jnp.float32
            ).astype(jnp.bfloat16)
            logs[rows, head : head + 1] = top + jnp.log(summed)
            return 0

        lax.fori_loop(0, query.shape[0] // chunk, one, 0)


def attend_back(query, key, value, logs, grad, grads, heads, chunk=256):
    scale = HEAD_DIM**-0.5
    grad_query, grad_key, grad_value = grads
    grad_key[...] = jnp.zeros(grad_key.shape, jnp.float32)
    grad_value[...] = jnp.zeros(grad_value.shape, jnp.float32)
    for head in range(heads):
        lanes = slice(head * HEAD_DIM, (head + 1) * HEAD_DIM)

        def one(step, _, head=head, lanes=lanes):
            rows = pl.ds(pl.multiple_of(step * chunk, chunk), chunk)
            scores = product_back(query[rows, lanes], key[:, lanes]) * scale
            probs = jnp.exp(scores - logs[rows, head : head + 1])
            prob_grad = product_back(grad[rows, lanes], value[:, lanes])
            inner = jnp.sum(prob_grad * probs, axis=-1, keepdims=True)
            score_grad = (probs * (prob_grad - inner)).astype(jnp.bfloat16)
            grad_query[rows, lanes] = (
                jnp.dot(score_grad, key[:, lanes], preferred_element_type=jnp.float32) * scale
            )
            grad_key[:, lanes] += weight_grad(score_grad, query[rows, lanes]) * scale
            grad_value[:, lanes] += weight_grad(probs.astype(jnp.bfloat16), grad[rows, lanes])
            return 0

        lax.fori_loop(0, query.shape[0] // chunk, one, 0)


def swapped(values):
    lane = lax.broadcasted_iota(jnp.int32, values.shape, 1)
    width = values.shape[1]
    return jnp.where(lane % 2 == 0, pltpu.roll(values, width - 1, 1), pltpu.roll(values, 1, 1))


def turn(values, cosine, sine, back):
    other = swapped(values) * sine
    return values * cosine - other if back else values * cosine + other


def square_columns(*arrays):
    return [jnp.sum(array * array, axis=-1, keepdims=True) for array in arrays]


def shape_norm(raw, inverse, gain, angles, out, heads, chunk=128):
    for head in range(heads):
        lanes = slice(head * HEAD_DIM, (head + 1) * HEAD_DIM)
        for start in range(0, raw.shape[0], chunk):
            rows = slice(start, start + chunk)
            values = raw[rows, lanes] * inverse[rows] * gain[head]
            if angles is not None:
                values = turn(values, angles[0][rows, :], angles[1][rows, :], False)
            out[rows, lanes] = values.astype(jnp.bfloat16)


def norm_dots(raw, inverse, gain, angles, grad, gain_out, heads, chunk=128):
    columns = []
    for start in range(0, raw.shape[0], chunk):
        rows = slice(start, start + chunk)
        column = jnp.zeros((chunk, 1), jnp.float32)
        for head in range(heads):
            lanes = slice(head * HEAD_DIM, (head + 1) * HEAD_DIM)
            values = grad[rows, lanes]
            if angles is not None:
                values = turn(values, angles[0][rows, :], angles[1][rows, :], True)
                grad[rows, lanes] = values
            part = values * raw[rows, lanes]
            column = column + jnp.sum(part * gain[head], axis=-1, keepdims=True)
            total = jnp.sum(part * inverse[rows], axis=0, keepdims=True)
            where = slice(head, head + 1)
            gain_out[where, :] = total if start == 0 else gain_out[where, :] + total
        columns.append(column)
    return jnp.concatenate(columns, axis=0)


def norm_pull(raw, inverse, gain, dots, grad, out, heads, chunk=128):
    for start in range(0, raw.shape[0], chunk):
        rows = slice(start, start + chunk)
        scale = inverse[rows]
        cut = dots[rows] * scale * scale * scale * (1.0 / D)
        for head in range(heads):
            lanes = slice(head * HEAD_DIM, (head + 1) * HEAD_DIM)
            out[rows, lanes] = (
                grad[rows, lanes] * gain[head] * scale - raw[rows, lanes] * cut
            ).astype(jnp.bfloat16)


def gains_of(gain_ref, kind, heads):
    lanes = slice(kind * HEAD_DIM, (kind + 1) * HEAD_DIM)
    return [gain_ref[head : head + 1, lanes] for head in range(heads)]


def exchange_scratch(length, size):
    return [
        pltpu.VMEM((8, length), jnp.float32),
        pltpu.VMEM((size - 1, 8, length), jnp.float32),
        pltpu.VMEM((128, length), jnp.float32),
    ]


class Plan:
    def __init__(self, mesh):
        self.dp = mesh.shape["dp"]
        self.tensor = mesh.shape["tensor"]
        self.cube = self.dp == 8
        self.calls = 0
        self.pieces = 4
        self.chunk = 1024
        self.counts = (1, 2, 3)

    def call(self, name, body, inputs, outputs, scratch, copies):
        self.calls += 1
        spaces = {True: pltpu.VMEM, False: pltpu.HBM}
        count_in, count_out = len(inputs), len(outputs)

        def kernel(*refs):
            ins = refs[:count_in]
            outs = refs[count_in : count_in + count_out]
            rest = refs[count_in + count_out :]
            links = Links(rest[0], rest[1], rest[2], self.dp, self.tensor)
            body(links, ins, outs, rest[3:])

        return pl.pallas_call(
            kernel,
            name=name,
            out_shape=[jax.ShapeDtypeStruct(shape, kind) for shape, kind, _ in outputs],
            in_specs=[pl.BlockSpec(memory_space=spaces[near]) for _, near in inputs],
            out_specs=[pl.BlockSpec(memory_space=spaces[near]) for _, _, near in outputs],
            scratch_shapes=[
                pltpu.SemaphoreType.DMA((copies,)),
                pltpu.SemaphoreType.DMA((copies,)),
                pltpu.SemaphoreType.DMA((64,)),
                *scratch,
            ],
            compiler_params=pltpu.CompilerParams(
                collective_id=self.calls, has_side_effects=True, vmem_limit_bytes=VMEM_BYTES
            ),
        )(*[array for array, _ in inputs])

    def gather_outputs(self, shards):
        return [
            ((self.dp * shard.shape[0], shard.shape[1]), shard.dtype, False) for shard in shards
        ]

    def open(self, hidden, time_rows, small, shards):
        rows, width = hidden.shape
        part = width // self.dp
        gain_part = small.shape[1] - part
        moving = shards if self.cube else []

        def body(links, ins, outs, scratch):
            hidden_ref, time_ref, small_ref = ins[:3]
            table_ref, gain_ref, whole_ref = outs[:3]
            (land,) = scratch
            links.greet({"line", "dpall"})
            gathers = [CubeGather(links, a, b) for a, b in zip(ins[3:], outs[3:])]
            dp, z = links.dp, links.z
            moves = []
            for step in range(1, self.dp):
                target = lax.rem(dp + step, self.dp)
                move = links.copy(small_ref, land.at[dp], (target, z), links.slot())
                move.start()
                moves.append(move)
            for item in gathers:
                item.start()
            land[dp] = small_ref[...]
            unit, _ = normed(hidden_ref[...])
            for move in moves:
                move.wait_recv()
            table = jnp.concatenate([land[k][:, :part] for k in range(self.dp)], axis=1)
            gain_ref[...] = jnp.concatenate([land[k][:, part:] for k in range(self.dp)], axis=1)
            table = table + time_ref[...]
            table_ref[...] = table
            line = LineGather(links, whole_ref, rows, 4)
            first = unit * (1.0 + table[1:2]) + table[0:1]
            whole_ref[pl.ds(pl.multiple_of(z * rows, 16), rows), :] = first.astype(jnp.bfloat16)
            for piece in range(4):
                line.start(piece)
            for piece in range(4):
                line.steps(piece)
                for item in gathers[2 * piece : 2 * piece + 2]:
                    item.forward()
            for item in gathers:
                item.tail()
            for item in gathers:
                item.finish()
            line.finish()
            for move in moves:
                move.wait_send()

        results = self.call(
            "open",
            body,
            [(hidden, True), (time_rows, True), (small, True)] + [(s, False) for s in moving],
            [
                ((8, width), jnp.float32, True),
                ((8, gain_part * self.dp), jnp.float32, True),
                ((rows * self.tensor, width), jnp.bfloat16, True),
            ]
            + self.gather_outputs(moving),
            [pltpu.VMEM((self.dp, 8, small.shape[1]), jnp.float32)],
            160,
        )
        return results[:3], self.gathered(results[3:], shards)

    def gathered(self, moved, shards):
        if self.cube:
            return list(moved)
        return [lax.all_gather(shard, "dp", axis=0, tiled=True) for shard in shards]

    def phase(
        self,
        name,
        near,
        kinds,
        scratch,
        pre,
        post,
        gather,
        shape,
        shards=(),
        lines=(),
        sums=(),
        jobs=(),
        tasks=None,
        begin=None,
        end=None,
        exchange=True,
        far=(),
        settle_small=None,
    ):
        length, width = shape
        rows = length // self.tensor
        pieces = self.pieces
        near = [(item if isinstance(item, list) else [item], group) for item, group in near]
        shards, lines, sums, far = list(shards), list(lines), list(sums), list(far)
        moving = shards if self.cube else []
        adding = sums if self.cube else []
        jobs = list(jobs)
        here = [job for job in jobs if job[4]] if self.cube else []
        count_near, count_kinds, count_scratch = len(near), len(kinds), len(scratch)

        job_scratch, job_outputs = [], []
        products, seats = {}, []
        for left, right, part, columns, now in jobs:
            if not self.cube:
                seats.append(("out", len(job_outputs)))
                job_outputs.append(((self.dp * part, columns), jnp.bfloat16, True))
                continue
            key = (part, columns)
            if key not in products:
                products[key] = len(job_scratch)
                job_scratch.append(pltpu.VMEM((8 * part, columns), jnp.bfloat16))
            if now:
                seats.append((products[key], len(job_scratch), len(job_outputs)))
                job_scratch.append(pltpu.VMEM((4, part, columns), jnp.bfloat16))
                job_scratch.append(pltpu.VMEM((3, part, columns), jnp.bfloat16))
                job_outputs.append(((part, columns), jnp.float32, True))
            else:
                seats.append((products[key], len(job_scratch), len(job_outputs)))
                job_scratch.append(pltpu.VMEM((4, part, columns), jnp.bfloat16))
                job_outputs.append(((4, part, columns), jnp.bfloat16, False))
        sum_scratch, sum_outputs = [], []
        for item in adding:
            _, part, columns = item.shape
            sum_scratch.append(pltpu.VMEM((3, part, columns), jnp.bfloat16))
            sum_scratch.append(pltpu.VMEM((part, columns), jnp.bfloat16))
            sum_outputs.append(((part, columns), jnp.float32, True))

        def body(links, ins, outs, rest):
            near_far = []
            for item, _ in near:
                near_far.append(ins[: len(item)])
                ins = ins[len(item) :]
            shard_refs, ins = ins[: len(moving)], ins[len(moving) :]
            line_refs, ins = ins[: len(lines)], ins[len(lines) :]
            sum_refs, far_refs = ins[: len(adding)], ins[len(adding) :]
            kind_far, outs = outs[:count_kinds], outs[count_kinds:]
            if gather:
                whole_far, outs = outs[0], outs[1:]
            full_refs, outs = outs[: len(moving)], outs[len(moving) :]
            line_outs, outs = outs[: len(lines)], outs[len(lines) :]
            job_refs, added_refs = outs[: len(jobs)], outs[len(jobs) :]
            near_refs, rest = rest[:count_near], rest[count_near:]
            loads = {}
            for index in order:
                start = 0
                for source in near_far[index]:
                    target = near_refs[index]
                    if len(near_far[index]) > 1:
                        target = target.at[:, pl.ds(start, source.shape[1])]
                        start += source.shape[1]
                    copy = links.here(source, target)
                    copy.start()
                    loads.setdefault(near[index][1], []).append(copy)

            def ready(group):
                for copy in loads.pop(group, []):
                    copy.wait()

            links.ready = ready
            kind_refs, stores = [], []
            for far_ref, (_, _, when_done) in zip(kind_far, kinds):
                if when_done is None:
                    kind_refs.append(far_ref)
                else:
                    kind_refs.append(rest[0])
                    rest = rest[1:]

            def store(source, target):
                stores.append(links.here(source, target))
                stores[-1].start()

            def store_kinds(moment):
                for held, far_ref, (_, _, when_done) in zip(kind_refs, kind_far, kinds):
                    if when_done == moment:
                        store(held, far_ref)

            if gather:
                whole_ref, rest = rest[0], rest[1:]
            partial_ref, land_right, land_left = rest[:3]
            user, rest = rest[3 : 3 + count_scratch], rest[3 + count_scratch :]
            job_rest, sum_rest = rest[: len(job_scratch)], rest[len(job_scratch) :]

            groups = {"zall"} if exchange else {"line"}
            if moving or adding or jobs:
                groups |= {"bits"} if self.cube else set()
            if adding or here:
                groups |= {"diag"}
            if settle_small:
                groups |= {"dpall"}
            links.greet(groups)
            gathers = [CubeGather(links, a, b) for a, b in zip(shard_refs, full_refs)]
            chunked, line_steps = [], []
            for source, target in zip(line_refs, line_outs):
                size = self.chunk
                parts = []
                for start in range(0, source.shape[1], size):
                    lanes = pl.ds(start, size)
                    item = LineGather(links, target.at[:, lanes], source.shape[0], 1)
                    parts.append(
                        [functools.partial(item.start, 0, source.at[:, lanes])]
                        + [functools.partial(item.step, hop, 0) for hop in range(links.size - 1)]
                    )
                    chunked.append(item)
                for turn_at in range(len(parts) + links.size - 1):
                    for index, steps in enumerate(parts):
                        if 0 <= turn_at - index < links.size:
                            line_steps.append(steps[turn_at - index])
            old = [
                ChipSum(links, a, b, sum_rest[2 * k], sum_rest[2 * k + 1])
                for k, (a, b) in enumerate(zip(sum_refs, added_refs))
            ]
            for item in gathers + old:
                item.start()
            copies = []
            for source, target in zip(line_refs, line_outs):
                copies.append(
                    links.here(
                        source, piece_of(target, links.z, source.shape[0], 0, source.shape[0])
                    )
                )
                copies[-1].start()

            def line_some(count):
                for _ in range(min(count, len(line_steps))):
                    line_steps.pop(0)()

            if line_steps:
                line_some(self.counts[0])
            state = begin(links, near_refs, kind_refs, user, far_refs) if begin else (None, [])
            ticks = state[1]
            if line_steps:
                ticks = [functools.partial(line_some, count) for count in self.counts[1:]]
            pre(links, near_refs, kind_refs, user, partial_ref, ticks)
            for run in ticks:
                run()
            store_kinds("pre")
            for group in sorted(loads):
                ready(group)

            queue = list(tasks(links, near_refs, kind_refs, user, far_refs)) if tasks else []
            fresh, busy, cleared = [], {}, []
            for (left, right, part, columns, now), seat in zip(jobs, seats):
                left_ref, right_ref = left(near_refs, kind_refs, user), right(near_refs, kind_refs, user)
                out = job_refs[seat[-1]]
                if not self.cube:

                    def whole(start, left_ref=left_ref, right_ref=right_ref, out=out):
                        count = out.shape[0] // 4
                        where = slice(start * count, (start + 1) * count)
                        out[where, :] = weight_grad(left_ref[:, where], right_ref[...]).astype(
                            jnp.bfloat16
                        )

                    queue += [functools.partial(whole, start) for start in range(4)]
                    continue
                held = job_rest[seat[1]]
                item = CoreSum(links, left_ref, right_ref, job_rest[seat[0]], held)
                if seat[0] in busy:
                    queue.append(busy[seat[0]].clear)
                    cleared.append(busy[seat[0]])
                busy[seat[0]] = item
                queue += item.steps()
                if now:
                    chip = ChipSum(links, held, out, job_rest[seat[1] + 1])
                    queue.append(chip.start)
                    fresh.append(chip)
                else:
                    queue.append(functools.partial(store, held, out))
            queue += [item.forward for item in gathers]
            queue += [item.tail for item in gathers]
            if line_steps:
                plain, queue = queue, []
                total = len(line_steps)
                for index, run in enumerate(line_steps):
                    queue.append(run)
                    queue += plain[len(plain) * index // total : len(plain) * (index + 1) // total]

            reduce = LineReduce(links, partial_ref, land_right, land_left, rows, pieces)
            line = LineGather(links, whole_ref, rows, pieces) if gather else None
            for piece in range(pieces):
                reduce.first(piece)
            reduce.clear()

            def settle(piece):
                where = pl.ds(piece * (rows // pieces), rows // pieces)
                result = post(reduce.total(piece), where, near_refs, kind_refs, piece == 0)
                if gather:
                    line.block(links.z, piece)[...] = result
                    line.start(piece)

            stages = reduce_stages(reduce) + [settle]
            if gather:
                stages += [functools.partial(line.step, hop) for hop in range(links.size - 1)]
            wave(stages, pieces, queue)
            if settle_small:
                small = settle_small(links, near_refs, kind_refs, user)
            for item in gathers + old + fresh + chunked:
                item.finish()
            for item in busy.values():
                item.clear()
            for copy in copies:
                copy.wait()
            if end:
                end(state[0], links, near_refs, kind_refs, user)
            if settle_small:
                small()
            store_kinds("post")
            if gather:
                store(whole_ref, whole_far)
            reduce.finish()
            if gather:
                line.finish()
            for copy in stores:
                copy.wait()

        order = sorted(range(count_near), key=lambda index: near[index][1])
        inputs = [(item, False) for items, _ in near for item in items]
        inputs += [(item, False) for item in moving + lines + adding + far]
        outputs = [(form, kind, False) for form, kind, _ in kinds]
        if gather:
            outputs.append(((length, width), jnp.bfloat16, False))
        outputs += self.gather_outputs(moving)
        outputs += [
            ((item.shape[0] * self.tensor, item.shape[1]), item.dtype, False) for item in lines
        ]
        outputs += job_outputs + sum_outputs
        results = list(
            self.call(
                name,
                body,
                inputs,
                outputs,
                [
                    pltpu.VMEM(
                        (*items[0].shape[:-1], sum(item.shape[-1] for item in items)),
                        items[0].dtype,
                    )
                    for items, _ in near
                ]
                + [pltpu.VMEM(form, kind) for form, kind, moment in kinds if moment]
                + ([pltpu.VMEM((length, width), jnp.bfloat16)] if gather else [])
                + [
                    pltpu.VMEM((length, width), jnp.bfloat16),
                    pltpu.VMEM((self.tensor - 1, rows, width), jnp.bfloat16),
                    pltpu.VMEM((self.tensor - 1, rows, width), jnp.bfloat16),
                    *scratch,
                    *job_scratch,
                    *sum_scratch,
                ],
                240,
            )
        )
        kept, results = results[:count_kinds], results[count_kinds:]
        whole, results = (results[0], results[1:]) if gather else (None, results)
        full, results = self.gathered(results[: len(moving)], shards), results[len(moving) :]
        lined, results = results[: len(lines)], results[len(lines) :]
        made, added = results[: len(jobs)], results[len(jobs) :]
        if not self.cube:
            made = [
                self.scatter(item) if job[4] else item for item, job in zip(made, jobs)
            ]
            added = [self.scatter(item) for item in sums]
        return kept, whole, full, lined, made, added

    def scatter(self, grad):
        return lax.psum_scatter(grad, "dp", scatter_dimension=0, tiled=True).astype(jnp.float32)


def add_sum(ref, row, values, first):
    total = jnp.sum(values, axis=0, keepdims=True)
    ref[row : row + 1, :] = total if first else ref[row : row + 1, :] + total


def tick(ticks):
    if ticks:
        ticks.pop(0)()


def tiles(count, size):
    return [(start, min(size, count - start)) for start in range(0, count, size)]


def body(
    plan,
    hidden_in,
    text_states,
    time_embed,
    positions,
    modulation,
    query_weight,
    key_weight,
    value_weight,
    out_weight,
    cross_query,
    cross_key,
    cross_value,
    cross_out,
    up_weight,
    down_weight,
    qk_gain,
    norm_gain,
    cotangent,
):
    plan.calls = 0
    low, full_type = jnp.bfloat16, jnp.float32
    rows, width = hidden_in.shape
    length = rows * plan.tensor
    here = out_weight.shape[0]
    heads = here // HEAD_DIM
    hidden_units = up_weight.shape[1]
    text_rows, text_width = length, text_states.shape[1]
    part = width // plan.dp
    text_part = text_width // plan.dp
    shape = (length, width)

    top = jnp.concatenate([modulation, norm_gain[None], jnp.zeros((1, part), low)], axis=0)
    side = jnp.pad(qk_gain, ((0, 8 - heads), (0, 0)))
    small = jnp.concatenate([top, side], axis=1).astype(full_type)
    time_rows = jnp.pad(time_embed[0], ((0, 2), (0, 0)))
    (mixing, gains, self_whole), full = plan.open(
        hidden_in, time_rows, small, [query_weight, key_weight, value_weight, out_weight.T]
    )
    query_full, key_full, value_full, out_full = full
    cosine, sine = rotary_tables(positions, HEAD_DIM)

    def forward(kinds_of_gain, angles, inputs, weights, gain_ref, kinds, scratch, links, partial, ticks):
        query_in, other_in = inputs
        query_w, key_w, value_w, out_w = weights
        query_raw, key_raw, value, query, key, attended, logs, inverse = kinds
        exchange = Exchange(links, *scratch)
        links.ready(0)
        query_raw[...] = jnp.dot(query_in[...], query_w[...], preferred_element_type=full_type)
        links.ready(1)
        key_raw[...] = jnp.dot(other_in[...], key_w[...], preferred_element_type=full_type)
        exchange.start(square_columns(query_raw[...], key_raw[...]))
        links.ready(2)
        value[...] = jnp.dot(
            other_in[...], value_w[...], preferred_element_type=full_type
        ).astype(low)
        inverse[...] = exchange.finish(lambda total: lax.rsqrt(total / D + EPSILON))
        tick(ticks)
        links.ready(3)
        for index, (raw, out) in enumerate(((query_raw, query), (key_raw, key))):
            shape_norm(
                raw,
                inverse[:, index : index + 1],
                gains_of(gain_ref, kinds_of_gain[index], heads),
                angles,
                out,
                heads,
            )
        attend(query, key, value, attended, logs, heads)
        tick(ticks)
        links.ready(4)
        for start, size in tiles(width, 512):
            partial[:, start : start + size] = product_back(
                attended[...], out_w[start : start + size, :]
            ).astype(low)

    kept_kinds = [
        ((length, here), full_type, "pre"),
        ((length, here), full_type, "pre"),
        ((length, here), low, "pre"),
        ((length, here), low, "pre"),
        ((length, here), low, "pre"),
        ((length, here), low, "pre"),
        ((length, HEAD_DIM), full_type, "pre"),
        ((length, HEAD_DIM), full_type, "pre"),
    ]

    def self_pre(links, near, kinds, scratch, partial, ticks):
        whole, gain_ref, cosine_ref, sine_ref = near[:4]
        forward(
            (0, 1),
            (cosine_ref, sine_ref),
            (whole, whole),
            near[4:8],
            gain_ref,
            kinds[:8],
            scratch,
            links,
            partial,
            ticks,
        )

    def after_self(total, where, near, kinds, first):
        hidden_ref, mixing_ref = near[8:]
        branch_ref, resid_ref = kinds[8:]
        branch_ref[where, :] = total
        resid = hidden_ref[where, :] + total * mixing_ref[2:3]
        resid_ref[where, :] = resid
        unit, _ = normed(resid)
        return (unit * mixing_ref[6:7]).astype(low)

    kept, cross_whole, full, (text_all,), _, _ = plan.phase(
        "self_forward",
        [(self_whole, 0), (gains, 3), (cosine, 3), (sine, 3), (query_full, 0), (key_full, 1)]
        + [(value_full, 2), (out_full, 4), (hidden_in, 5), (mixing, 5)],
        kept_kinds + [((rows, width), full_type, "post")] * 2,
        exchange_scratch(length, plan.tensor),
        self_pre,
        after_self,
        True,
        shape,
        shards=[cross_key, cross_value, cross_query, cross_out.T],
        lines=[text_states],
    )
    self_kept, (self_branch, resid_self) = kept[:8], kept[8:]
    cross_key_full, cross_value_full, cross_query_full, cross_out_full = full[:4]

    def cross_begin(links, near, kinds, scratch, far):
        links.ready(-1)
        mixing_ref, cotangent_ref = near[8:]
        whole = kinds[9]
        mine = piece_of(whole, links.z, rows, 0, rows)
        mine[...] = (cotangent_ref[...] * mixing_ref[5:6]).astype(low)
        line = LineGather(links, whole, rows, 1)
        line.start(0)
        return line, [functools.partial(line.step, hop, 0) for hop in range(links.size - 1)]

    def cross_end(line, links, near, kinds, scratch):
        line.finish()

    def cross_pre(links, near, kinds, scratch, partial, ticks):
        whole, text, gain_ref = near[:3]
        forward(
            (2, 3),
            None,
            (whole, text),
            near[3:7],
            gain_ref,
            kinds[:8],
            scratch,
            links,
            partial,
            ticks,
        )

    def after_cross(total, where, near, kinds, first):
        resid_ref, mixing_ref = near[7:9]
        resid = resid_ref[where, :] + total
        kinds[8][where, :] = resid
        unit, _ = normed(resid)
        return (unit * (1.0 + mixing_ref[4:5]) + mixing_ref[3:4]).astype(low)

    kept, feed_whole, (up_full, down_full), _, _, _ = plan.phase(
        "cross_forward",
        [(cross_whole, 0), (text_all, 1), (gains, 3), (cross_query_full, 0), (cross_key_full, 1)]
        + [(cross_value_full, 2), (cross_out_full, 4), (resid_self, 5), (mixing, -1)]
        + [(cotangent, -1)],
        kept_kinds + [((rows, width), full_type, "post"), ((length, width), low, "post")],
        exchange_scratch(length, plan.tensor),
        cross_pre,
        after_cross,
        True,
        shape,
        shards=[up_weight, down_weight.T],
        begin=cross_begin,
        end=cross_end,
    )
    cross_kept, (resid_cross, feed_grad_whole) = kept[:8], kept[8:]

    feed_tiles = tiles(hidden_units, 512)

    def feed_begin(links, near, kinds, scratch, far):
        copies = []
        for start, size in feed_tiles:
            lanes = pl.ds(start, size)
            pair = [
                links.here(far[which].at[:, lanes], scratch[2 + which].at[:, lanes])
                for which in range(2)
            ]
            for copy in pair:
                copy.start()
            copies.append(pair)
        return None, copies

    def feed_pre(links, near, kinds, scratch, partial, copies):
        whole, grad_whole = near[:2]
        activated, grad_raw, up, down = scratch
        root = 0.7978845608028654
        links.ready(0)
        for (begin, size), pair in zip(feed_tiles, copies):
            lanes = slice(begin, begin + size)
            for copy in pair:
                copy.wait()

            def one(step, _, lanes=lanes):
                block = pl.ds(pl.multiple_of(step * 256, 256), 256)
                raw = jnp.dot(whole[block, :], up[:, lanes], preferred_element_type=full_type)
                grad = jnp.dot(grad_whole[block, :], down[:, lanes], preferred_element_type=full_type)
                square = raw * raw
                bend = jnp.tanh(root * raw * (1.0 + 0.044715 * square))
                half = 0.5 + 0.5 * bend
                activated[block, lanes] = (raw * half).astype(low)
                slope = half + 0.5 * raw * (1.0 - bend * bend) * root * (
                    1.0 + 3.0 * 0.044715 * square
                )
                grad_raw[block, lanes] = (grad * slope).astype(low)
                return 0

            lax.fori_loop(0, length // 256, one, 0)
        copies.clear()
        for start, size in tiles(width, 512):
            partial[:, start : start + size] = product_back(
                grad_raw[...], up[start : start + size, :]
            ).astype(low)

    def feed_tasks(links, near, kinds, scratch, far):
        activated, down = scratch[0], scratch[3]

        def one(start, size):
            kinds[2][:, start : start + size] = product_back(
                activated[...], down[start : start + size, :]
            ).astype(low)

        return [functools.partial(one, start, size) for start, size in tiles(width, 512)]

    def before_feed(total, where, near, kinds, first):
        resid_ref, cotangent_ref, mixing_ref = near[2:]
        grad_ref, sums_ref = kinds[:2]
        unit, inverse = normed(resid_ref[where, :])
        add_sum(sums_ref, 0, total, first)
        add_sum(sums_ref, 1, total * unit, first)
        grad = cotangent_ref[where, :] + normed_back(
            unit, inverse, total * (1.0 + mixing_ref[4:5])
        )
        grad_ref[where, :] = grad
        return grad.astype(low)

    kept, cross_grad_whole, _, _, made, _ = plan.phase(
        "feed",
        [(feed_whole, 0), (feed_grad_whole, 0), (resid_cross, 1), (cotangent, 1), (mixing, 1)],
        [
            ((rows, width), full_type, "post"),
            ((8, width), full_type, "post"),
            ((length, width), low, "post"),
        ],
        [pltpu.VMEM((length, hidden_units), low)] * 2
        + [pltpu.VMEM((width, hidden_units), low)] * 2,
        feed_pre,
        before_feed,
        True,
        shape,
        jobs=[
            (lambda n, k, s: n[1], lambda n, k, s: s[0], part, hidden_units, False),
            (lambda n, k, s: n[0], lambda n, k, s: s[1], part, hidden_units, False),
        ],
        tasks=feed_tasks,
        begin=feed_begin,
        far=[up_full, down_full],
        exchange=False,
    )
    grad_resid_cross, feed_sums, feed_partial = kept
    near_down, near_up = made

    def backward(kinds_of_gain, angles, refs, gain_ref, grad_outs, scratch, links, partial, ticks):
        (grad_whole, query_w, key_w, value_w, out_w) = refs[:5]
        query_raw, key_raw, value, query, key, attended, logs, inverse = refs[5:]
        gain_query_ref, gain_key_ref, query_out, key_out, value_out = grad_outs
        grad_attended, grad_query, grad_key, grad_value = scratch[3:7]
        exchange = Exchange(links, *scratch[:3])
        links.ready(0)
        grad_attended[...] = jnp.dot(
            grad_whole[...], out_w[...], preferred_element_type=full_type
        ).astype(low)
        links.ready(1)
        attend_back(
            query, key, value, logs, grad_attended, (grad_query, grad_key, grad_value), heads
        )
        tick(ticks)
        links.ready(2)
        sides = (
            (query_raw, inverse[:, 0:1], gains_of(gain_ref, kinds_of_gain[0], heads)),
            (key_raw, inverse[:, 1:2], gains_of(gain_ref, kinds_of_gain[1], heads)),
        )
        exchange.start(
            [
                norm_dots(*sides[0], angles, grad_query, gain_query_ref, heads),
                norm_dots(*sides[1], angles, grad_key, gain_key_ref, heads),
            ]
        )
        value_out[...] = grad_value[...].astype(low)
        dots = exchange.finish()
        tick(ticks)
        norm_pull(*sides[0], dots[:, 0:1], grad_query, query_out, heads)
        norm_pull(*sides[1], dots[:, 1:2], grad_key, key_out, heads)
        links.ready(3)
        pairs = [(query_out, query_w)]
        if angles is not None:
            pairs += [(key_out, key_w), (value_out, value_w)]
        for start, size in tiles(width, 512):
            total = 0.0
            for grads, weight in pairs:
                total = total + product_back(grads[...], weight[start : start + size, :])
            partial[:, start : start + size] = total.astype(low)

    back_scratch = exchange_scratch(length, plan.tensor) + [
        pltpu.VMEM((length, here), low),
        pltpu.VMEM((length, here), full_type),
        pltpu.VMEM((length, here), full_type),
        pltpu.VMEM((length, here), full_type),
        pltpu.VMEM((length, here), low),
        pltpu.VMEM((length, here), low),
        pltpu.VMEM((length, here), low),
    ]

    kept_groups = (2, 2, 1, 1, 1, 4, 1, 2)

    def cross_back_begin(links, near, kinds, scratch, far):
        links.ready(-1)
        late = LineReduce(links, near[20], scratch[10], scratch[11], rows, 1)
        late.clear()
        first, *others = late.stages(0)
        first()
        return late, others

    def cross_back_end(late, links, near, kinds, scratch):
        cotangent_ref, mixing_ref, resid_ref = near[17:20]
        total = late.total(0)
        kinds[2][...] = resid_ref[...] + total * mixing_ref[5:6]
        add_sum(kinds[1], 2, cotangent_ref[...] * total, True)
        late.finish()

    def cross_back_pre(links, near, kinds, scratch, partial, ticks):
        backward(
            (2, 3),
            None,
            (near[0], near[1], None, None, *near[2:11]),
            near[11],
            (kinds[4], kinds[5], *scratch[7:10]),
            scratch,
            links,
            partial,
            ticks,
        )

    def cross_back_tasks(links, near, kinds, scratch, far):
        held, loaded = scratch[12:14]
        size = held.shape[2]
        out_copies, loads = [], {}

        def load(index):
            loads[index] = [
                links.here(weight.at[pl.ds(index * size, size)], loaded.at[index % 2, which])
                for which, weight in enumerate(far)
            ]
            for copy in loads[index]:
                copy.start()

        def one(index):
            if index >= 2:
                out_copies[index - 2].wait()
            for copy in loads[index]:
                copy.wait()
            stage = held.at[index % 2]
            stage[...] = (
                product_back(scratch[8][...], loaded[index % 2, 0])
                + product_back(scratch[9][...], loaded[index % 2, 1])
            ).astype(low)
            if index + 2 < text_width // size:
                load(index + 2)
            copy = links.here(stage, kinds[3].at[:, pl.ds(index * size, size)])
            copy.start()
            out_copies.append(copy)

        def last():
            for copy in out_copies[-2:]:
                copy.wait()

        load(0)
        load(1)
        steps = [functools.partial(one, index) for index in range(text_width // size)]
        return steps + [last]

    def before_cross(total, where, near, kinds, first):
        resid_ref, grad_ref, branch_ref = near[14:17]
        mixing_ref = near[18]
        out_ref, sums_ref = kinds[:2]
        unit, inverse = normed(resid_ref[where, :])
        add_sum(sums_ref, 1, total * unit, first)
        grad = grad_ref[where, :] + normed_back(unit, inverse, total * mixing_ref[6:7])
        out_ref[where, :] = grad
        add_sum(sums_ref, 0, grad * branch_ref[where, :], first)
        return (grad * mixing_ref[2:3]).astype(low)

    kept, self_grad_whole, _, _, made, (sum_down, sum_up) = plan.phase(
        "cross_back",
        [(cross_grad_whole, 0), (cross_query_full, 3), (cross_out_full, 0)]
        + list(zip(cross_kept, kept_groups))
        + [(gains, 2), (cross_whole, 4), (text_all, 4), (resid_self, 4), (grad_resid_cross, 4)]
        + [(self_branch, 4), (cotangent, 4), (mixing, 4), (resid_cross, 4), (feed_partial, -1)],
        [
            ((rows, width), full_type, "post"),
            ((8, width), full_type, "post"),
            ((rows, width), full_type, "post"),
            ((text_rows, text_width), low, None),
            ((8, HEAD_DIM), full_type, "pre"),
            ((8, HEAD_DIM), full_type, "pre"),
        ],
        back_scratch
        + [pltpu.VMEM((plan.tensor - 1, rows, width), low)] * 2
        + [pltpu.VMEM((2, text_rows, 1024), low), pltpu.VMEM((2, 2, 1024, here), low)],
        cross_back_pre,
        before_cross,
        True,
        shape,
        sums=[near_down, near_up],
        jobs=[
            (lambda n, k, s: n[13], lambda n, k, s: s[8], text_part, here, False),
            (lambda n, k, s: n[13], lambda n, k, s: s[9], text_part, here, False),
            (lambda n, k, s: n[12], lambda n, k, s: s[7], part, here, False),
            (lambda n, k, s: n[0], lambda n, k, s: n[8], part, here, False),
        ],
        tasks=cross_back_tasks,
        begin=cross_back_begin,
        end=cross_back_end,
        far=[cross_key_full, cross_value_full],
    )
    grad_resid_self, cross_sums, block_out, text_partial, gain_cross_query, gain_cross_key = kept
    grad_text = lax.psum_scatter(
        text_partial, "tensor", scatter_dimension=0, tiled=True
    ).astype(full_type)

    def self_back_pre(links, near, kinds, scratch, partial, ticks):
        backward(
            (0, 1),
            (near[14], near[15]),
            near[:13],
            near[13],
            (kinds[2], kinds[3], *scratch[7:10]),
            scratch,
            links,
            partial,
            ticks,
        )

    def before_self(total, where, near, kinds, first):
        hidden_ref, grad_ref, mixing_ref = near[17:20]
        out_ref, sums_ref = kinds[:2]
        unit, inverse = normed(hidden_ref[where, :])
        add_sum(sums_ref, 0, total, first)
        add_sum(sums_ref, 1, total * unit, first)
        out_ref[where, :] = grad_ref[where, :] + normed_back(
            unit, inverse, total * (1.0 + mixing_ref[1:2])
        )

    gain_width = qk_gain.shape[1]

    def settle_small(links, near, kinds, scratch):
        feed_ref, cross_ref, gain_cross_query_ref, gain_cross_key_ref = near[20:]
        self_ref, gain_query_ref, gain_key_ref, time_ref, slice_ref = kinds[1:]
        mine, line_land, stage, land = scratch[10:]
        z, dp = links.z, links.dp
        mine[...] = jnp.concatenate(
            [
                self_ref[0:2, :],
                cross_ref[0:1, :],
                feed_ref[0:2, :],
                cross_ref[2:3, :],
                cross_ref[1:2, :],
                jnp.zeros((1, width), full_type),
            ],
            axis=0,
        )
        moves = []
        for step in range(1, plan.tensor):
            target = lax.rem(z + step, plan.tensor)
            move = links.copy(mine, line_land.at[z], (dp, target), links.slot())
            move.start()
            moves.append(move)
        line_land[z] = mine[...]
        gain_rows = jnp.concatenate(
            [gain_query_ref[...], gain_key_ref[...]]
            + [gain_cross_query_ref[...], gain_cross_key_ref[...]],
            axis=1,
        )
        for move in moves:
            move.wait_recv()
        total = line_land[0]
        for index in range(1, plan.tensor):
            total = total + line_land[index]
        time_ref[0, :, :] = total[:6]
        for index in range(plan.dp):
            stage[index] = jnp.concatenate(
                [
                    total[:, index * part : (index + 1) * part],
                    gain_rows[:, index * gain_width : (index + 1) * gain_width],
                ],
                axis=1,
            )
        land[dp] = stage[dp]
        others = []
        for step in range(1, plan.dp):
            target = lax.rem(dp + step, plan.dp)
            move = links.copy(stage.at[target], land.at[dp], (target, z), links.slot())
            move.start()
            others.append(move)

        def finish():
            for move in others:
                move.wait_recv()
            summed = land[0]
            for index in range(1, plan.dp):
                summed = summed + land[index]
            slice_ref[...] = summed
            for move in moves + others:
                move.wait_send()

        return finish

    kept, _, _, _, made, sums = plan.phase(
        "self_back",
        [(self_grad_whole, 0), (query_full, 3), (key_full, 3), (value_full, 3), (out_full, 0)]
        + list(zip(self_kept, kept_groups))
        + [(gains, 2), (cosine, 2), (sine, 2), (self_whole, 4), (hidden_in, 4)]
        + [(grad_resid_self, 4), (mixing, 4), (feed_sums, 4), (cross_sums, 4)]
        + [(gain_cross_query, 4), (gain_cross_key, 4)],
        [
            ((rows, width), full_type, "post"),
            ((8, width), full_type, "post"),
            ((8, HEAD_DIM), full_type, "pre"),
            ((8, HEAD_DIM), full_type, "pre"),
            ((1, 6, width), full_type, "post"),
            ((8, part + gain_width), full_type, "post"),
        ],
        back_scratch
        + [
            pltpu.VMEM((8, width), full_type),
            pltpu.VMEM((plan.tensor, 8, width), full_type),
            pltpu.VMEM((plan.dp, 8, part + gain_width), full_type),
            pltpu.VMEM((plan.dp, 8, part + gain_width), full_type),
        ],
        self_back_pre,
        before_self,
        False,
        shape,
        sums=made,
        jobs=[
            (lambda n, k, s: n[16], lambda n, k, s: s[7], part, here, True),
            (lambda n, k, s: n[16], lambda n, k, s: s[8], part, here, True),
            (lambda n, k, s: n[16], lambda n, k, s: s[9], part, here, True),
            (lambda n, k, s: n[0], lambda n, k, s: n[10], part, here, True),
        ],
        settle_small=settle_small,
    )
    grad_hidden, _, _, _, grad_time, mine = kept
    sum_cross_key, sum_cross_value, sum_cross_query, sum_cross_out = sums
    sum_query, sum_key, sum_value, sum_out = made

    return (
        block_out,
        grad_hidden,
        grad_text,
        grad_time,
        mine[:6, :part],
        sum_query,
        sum_key,
        sum_value,
        sum_out.T,
        sum_cross_query,
        sum_cross_key,
        sum_cross_value,
        sum_cross_out.T,
        sum_up,
        sum_down.T,
        mine[:heads, part:],
        mine[6, :part],
    )


def solution(mesh):
    return jax.shard_map(
        functools.partial(body, Plan(mesh)),
        mesh=mesh,
        in_specs=(
            P(("dp", "tensor"), None),
            P(("dp", "tensor"), None),
            P("dp", None, None),
            P(None, "dp"),
            P(None, "dp"),
            P("dp", "tensor"),
            P("dp", "tensor"),
            P("dp", "tensor"),
            P("tensor", "dp"),
            P("dp", "tensor"),
            P("dp", "tensor"),
            P("dp", "tensor"),
            P("tensor", "dp"),
            P("dp", "tensor"),
            P("tensor", "dp"),
            P("tensor", "dp"),
            P("dp"),
            P(("dp", "tensor"), None),
        ),
        out_specs=(
            P(("dp", "tensor"), None),
            P(("dp", "tensor"), None),
            P(("dp", "tensor"), None),
            P("dp", None, None),
            P(None, "dp"),
            P("dp", "tensor"),
            P("dp", "tensor"),
            P("dp", "tensor"),
            P("tensor", "dp"),
            P("dp", "tensor"),
            P("dp", "tensor"),
            P("dp", "tensor"),
            P("tensor", "dp"),
            P("dp", "tensor"),
            P("tensor", "dp"),
            P("tensor", "dp"),
            P("dp"),
        ),
        check_vma=False,
    )
```

```python
import functools

import jax
import jax.numpy as jnp
from jax import lax
from jax.experimental import pallas as pl
from jax.experimental.pallas import tpu as pltpu
from jax.sharding import PartitionSpec as P

MESH = pl.DeviceIdType.MESH
VMEM_BYTES = 62 * 2**20

HEAD_DIM = 128
D = 1536


EPSILON = 1e-06
CONTRACT_LAST = (((1,), (1,)), ((), ()))
CONTRACT_FIRST = (((0,), (0,)), ((), ()))


def rotary_tables(positions, head_width):
    pairs = head_width // 2
    third = pairs // 3
    first = pairs - 2 * third
    freq_frame = jnp.power(10000.0, -jnp.arange(first, dtype=jnp.float32) / first)
    freq_side = jnp.power(10000.0, -jnp.arange(third, dtype=jnp.float32) / third)
    places = positions.astype(jnp.float32)
    angles = jnp.concatenate(
        [
            places[0][:, None] * jnp.repeat(freq_frame, 2)[None, :],
            places[1][:, None] * jnp.repeat(freq_side, 2)[None, :],
            places[2][:, None] * jnp.repeat(freq_side, 2)[None, :],
        ],
        axis=1,
    )
    sign = jnp.where(jnp.arange(head_width) % 2 == 0, -1.0, 1.0)
    return (jnp.cos(angles), jnp.sin(angles) * sign)


def product_back(grads, weight):
    return lax.dot_general(grads, weight, CONTRACT_LAST, preferred_element_type=jnp.float32)


def weight_grad(inputs, grads):
    return lax.dot_general(inputs, grads, CONTRACT_FIRST, preferred_element_type=jnp.float32)


def when(cond, run):
    if cond is None:
        run()
    else:
        pl.when(cond)(run)


def flip(index, bit):
    return index + bit - 2 * bit * (index // bit % 2)


def normed(values):
    center = values - jnp.mean(values, axis=-1, keepdims=True)
    inverse = lax.rsqrt(jnp.mean(center * center, axis=-1, keepdims=True) + EPSILON)
    return center * inverse, inverse


def normed_back(unit, inverse, grad):
    mean_grad = jnp.mean(grad, axis=-1, keepdims=True)
    mean_dot = jnp.mean(grad * unit, axis=-1, keepdims=True)
    return (grad - mean_grad - unit * mean_dot) * inverse


class Links:
    def __init__(self, send, recv, local, dp_size, tensor_size):
        self.send, self.recv, self.local = send, recv, local
        self.count = 0
        self.local_count = 0
        self.dp_size, self.size = dp_size, tensor_size
        self.dp = lax.axis_index("dp")
        self.z = lax.axis_index("tensor")

    def slot(self):
        self.count += 1
        return self.count - 1

    def copy(self, source, target, device, slot):
        return pltpu.make_async_remote_copy(
            src_ref=source,
            dst_ref=target,
            send_sem=self.send.at[slot],
            recv_sem=self.recv.at[slot],
            device_id=device,
            device_id_type=MESH,
        )

    def here(self, source, target):
        self.local_count += 1
        return pltpu.make_async_copy(source, target, self.local.at[self.local_count - 1])

    def greet(self, groups):
        barrier = pltpu.get_barrier_semaphore()
        peers = []
        if "line" in groups and "zall" not in groups:
            peers += [
                ((self.dp, self.z - 1), self.z > 0),
                ((self.dp, self.z + 1), self.z < self.size - 1),
            ]
        if "zall" in groups:
            peers += [
                ((self.dp, lax.rem(self.z + k, self.size)), None) for k in range(1, self.size)
            ]
        if "dpall" in groups:
            peers += [
                ((lax.rem(self.dp + k, self.dp_size), self.z), None)
                for k in range(1, self.dp_size)
            ]
        if "bits" in groups and "dpall" not in groups:
            bit = 1
            while bit < self.dp_size:
                peers.append(((flip(self.dp, bit), self.z), None))
                bit *= 2
        if "diag" in groups and "dpall" not in groups:
            peers.append(((flip(flip(self.dp, 2), 4), self.z), None))
        for device, cond in peers:
            when(
                cond,
                lambda device=device: pl.semaphore_signal(
                    barrier, inc=1, device_id=device, device_id_type=MESH
                ),
            )
        expected = sum(1 for _, cond in peers if cond is None)
        for _, cond in peers:
            if cond is not None:
                expected = expected + cond.astype(jnp.int32)
        pl.semaphore_wait(barrier, expected)


def piece_of(ref, block, rows, start, count):
    return ref.at[pl.ds(pl.multiple_of(block * rows + start, 16), count)]


class LineGather:
    def __init__(self, links, whole, rows, pieces):
        self.links, self.whole, self.rows, self.count = links, whole, rows, rows // pieces
        self.pieces = pieces
        hops = links.size - 1
        self.right = [[links.slot() for _ in range(pieces)] for _ in range(hops)]
        self.left = [[links.slot() for _ in range(pieces)] for _ in range(hops)]

    def block(self, index, piece):
        return piece_of(self.whole, index, self.rows, piece * self.count, self.count)

    def move(self, index, piece, way, slot):
        part = self.block(index, piece)
        return self.links.copy(part, part, (self.links.dp, self.links.z + way), slot)

    def start(self, piece, source=None):
        links = self.links
        z, last = links.z, links.size - 1

        def go(way, slot):
            mine = self.block(z, piece)
            links.copy(mine if source is None else source, mine, (links.dp, z + way), slot).start()

        when(z < last, lambda: go(1, self.right[0][piece]))
        when(z > 0, lambda: go(-1, self.left[0][piece]))

    def step(self, hop, piece):
        z, last = self.links.z, self.links.size - 1

        def from_left():
            self.move(z - 1 - hop, piece, -1, self.right[hop][piece]).wait_recv()
            if hop + 1 < last:
                when(
                    z < last,
                    lambda: self.move(z - 1 - hop, piece, 1, self.right[hop + 1][piece]).start(),
                )

        def from_right():
            self.move(z + 1 + hop, piece, 1, self.left[hop][piece]).wait_recv()
            if hop + 1 < last:
                when(
                    z > 0,
                    lambda: self.move(z + 1 + hop, piece, -1, self.left[hop + 1][piece]).start(),
                )

        when(z - 1 - hop >= 0, from_left)
        when(z + 1 + hop <= last, from_right)

    def steps(self, piece):
        for hop in range(self.links.size - 1):
            self.step(hop, piece)

    def finish(self):
        z, last = self.links.z, self.links.size - 1
        for hop in range(last):
            for piece in range(self.pieces):
                when(
                    (z - hop >= 0) & (z < last),
                    lambda: self.move(z - hop, piece, 1, self.right[hop][piece]).wait_send(),
                )
                when(
                    (z + hop <= last) & (z > 0),
                    lambda: self.move(z + hop, piece, -1, self.left[hop][piece]).wait_send(),
                )


class LineReduce:
    def __init__(self, links, partial, land_right, land_left, rows, pieces):
        self.links, self.partial, self.rows, self.count = links, partial, rows, rows // pieces
        self.land = {1: land_right, -1: land_left}
        self.pieces = pieces
        last = links.size - 1
        self.slots = {
            way: [None] + [[links.slot() for _ in range(pieces)] for _ in range(last)]
            for way in (1, -1)
        }

    def landing(self, way, distance, piece):
        return self.land[way].at[distance - 1, pl.ds(piece * self.count, self.count)]

    def part(self, index, piece):
        return piece_of(self.partial, index, self.rows, piece * self.count, self.count)

    def move(self, source, way, distance, piece):
        return self.links.copy(
            source,
            self.landing(way, distance, piece),
            (self.links.dp, self.links.z + way),
            self.slots[way][distance][piece],
        )

    def arrived(self, way, distance, piece):
        self.links.copy(
            self.landing(way, distance, piece),
            self.landing(way, distance, piece),
            (self.links.dp, self.links.z - way),
            self.slots[way][distance][piece],
        ).wait_recv()

    def first(self, piece):
        z, last = self.links.z, self.links.size - 1

        def from_first():
            for distance in range(last, 0, -1):
                self.move(self.part(distance, piece), 1, distance, piece).start()

        def from_last():
            for distance in range(last, 0, -1):
                self.move(self.part(last - distance, piece), -1, distance, piece).start()

        when(z == 0, from_first)
        when(z == last, from_last)

    def first_at(self, distance, piece):
        z, last = self.links.z, self.links.size - 1
        when(
            z == 0,
            lambda: self.move(self.part(distance, piece), 1, distance, piece).start(),
        )
        when(
            z == last,
            lambda: self.move(self.part(last - distance, piece), -1, distance, piece).start(),
        )

    def stages(self, piece):
        last = self.links.size - 1

        def one(distance):
            self.first_at(distance, piece)
            if distance < last:
                self.step(distance, piece)

        return [functools.partial(one, distance) for distance in range(last, 0, -1)]

    def clear(self):
        z, last = self.links.z, self.links.size - 1

        def zero(way):
            self.land[way][0] = jnp.zeros(self.land[way].shape[1:], self.land[way].dtype)

        when(z == 0, lambda: zero(1))
        when(z == last, lambda: zero(-1))

    def step(self, distance, piece):
        z, last = self.links.z, self.links.size - 1
        for way in (1, -1):
            inside = (
                (z > 0) & (z + distance <= last)
                if way == 1
                else (z < last) & (z - distance >= 0)
            )

            def go(way=way):
                self.arrived(way, distance + 1, piece)
                held = self.landing(way, distance + 1, piece)
                own = self.part(z + way * distance, piece)
                held[...] = (
                    held[...].astype(jnp.float32) + own[...].astype(jnp.float32)
                ).astype(held.dtype)
                self.move(held, way, distance, piece).start()

            when(inside, go)

    def total(self, piece):
        z, last = self.links.z, self.links.size - 1
        when(z > 0, lambda: self.arrived(1, 1, piece))
        when(z < last, lambda: self.arrived(-1, 1, piece))
        return (
            self.part(z, piece)[...].astype(jnp.float32)
            + self.landing(1, 1, piece)[...].astype(jnp.float32)
            + self.landing(-1, 1, piece)[...].astype(jnp.float32)
        )

    def finish(self):
        z, last = self.links.z, self.links.size - 1
        for distance in range(1, last + 1):
            for piece in range(self.pieces):
                held = self.landing(1, distance, piece)
                when(
                    z + distance <= last,
                    lambda: self.move(held, 1, distance, piece).wait_send(),
                )
                back = self.landing(-1, distance, piece)
                when(
                    z - distance >= 0,
                    lambda: self.move(back, -1, distance, piece).wait_send(),
                )


def reduce_stages(reduce):
    return [
        functools.partial(reduce.step, distance)
        for distance in range(reduce.links.size - 2, 0, -1)
    ]


def wave(stages, pieces, queue):
    count = pieces + len(stages) - 1
    done = 0
    for step in range(count):
        for index, stage in enumerate(stages):
            if 0 <= step - index < pieces:
                stage(step - index)
        until = min(len(queue), len(queue) * (step + 1) * 2 // (count * 1))
        for run in queue[done:until]:
            run()
        done = until


class CubeGather:
    def __init__(self, links, shard, whole):
        self.links, self.shard, self.whole = links, shard, whole
        self.rows = shard.shape[0]
        self.slots = [links.slot() for _ in range(8)]
        dp = links.dp
        self.core, self.side, self.over = flip(dp, 1), flip(dp, 2), flip(dp, 4)
        self.far = flip(flip(dp, 2), 4)
        self.sent = []

    def block(self, index, start=0, count=None):
        return piece_of(self.whole, index, self.rows, start, count or self.rows)

    def send(self, source, target, device, slot):
        move = self.links.copy(source, target, (device, self.links.z), self.slots[slot])
        move.start()
        self.sent.append(move)

    def got(self, part, slot):
        self.links.copy(part, part, (self.core, self.links.z), self.slots[slot]).wait_recv()

    def start(self):
        mine = self.block(self.links.dp)
        self.own = self.links.here(self.shard, mine)
        self.own.start()
        self.send(self.shard, mine, self.side, 1)
        self.send(self.shard, mine, self.over, 2)
        self.send(self.shard, mine, self.core, 0)

    def forward(self):
        half = self.rows // 2
        self.got(self.block(self.side), 1)
        part = self.block(self.side, 0, half)
        self.send(part, part, self.over, 3)
        part = self.block(self.side)
        self.send(part, part, self.core, 5)
        self.got(self.block(self.over), 2)
        part = self.block(self.over, half, half)
        self.send(part, part, self.side, 4)
        part = self.block(self.over)
        self.send(part, part, self.core, 6)

    def tail(self):
        half = self.rows // 2
        self.got(self.block(self.far, 0, half), 3)
        self.got(self.block(self.far, half, half), 4)
        part = self.block(self.far)
        self.send(part, part, self.core, 7)

    def finish(self):
        self.got(self.block(self.core), 0)
        self.got(self.block(flip(self.core, 2)), 5)
        self.got(self.block(flip(self.core, 4)), 6)
        self.got(self.block(flip(flip(self.core, 2), 4)), 7)
        for move in self.sent:
            move.wait_send()
        self.own.wait()


class Exchange:
    def __init__(self, links, mine, land, turned):
        self.links, self.mine, self.land, self.turned = links, mine, land, turned
        self.slots = [links.slot() for _ in range(links.size - 1)]

    def start(self, columns):
        links = self.links
        lane = lax.broadcasted_iota(jnp.int32, (columns[0].shape[0], 128), 1)
        flat = jnp.zeros(lane.shape, jnp.float32)
        for index, column in enumerate(columns):
            flat = jnp.where(lane == index, column, flat)
        self.mine[...] = flat.T[:8]
        self.moves = [
            links.copy(
                self.mine,
                self.land.at[step - 1],
                (links.dp, lax.rem(links.z + step, links.size)),
                slot,
            )
            for step, slot in enumerate(self.slots, 1)
        ]
        for move in self.moves:
            move.start()

    def finish(self, shape=lambda total: total):
        total = self.mine[...]
        for step, move in enumerate(self.moves):
            move.wait_recv()
            total = total + self.land[step]
        self.turned[...] = jnp.zeros(self.turned.shape, jnp.float32)
        self.turned[0:8, :] = shape(total)
        for move in self.moves:
            move.wait_send()
        return self.turned[...].T


class CoreSum:
    def __init__(self, links, left, right, product, near):
        self.links, self.left, self.right = links, left, right
        self.product, self.near = product, near
        self.rows = near.shape[1]
        self.slots = [links.slot() for _ in range(4)]
        self.core = links.dp % 2
        self.moves = []

    def multiply(self, chip):
        links, count = self.links, 2 * self.rows
        self.product[chip * count : (chip + 1) * count, :] = weight_grad(
            self.left[:, chip * count : (chip + 1) * count], self.right[...]
        ).astype(jnp.bfloat16)
        move = links.copy(
            piece_of(self.product, 2 * chip + 1 - self.core, self.rows, 0, self.rows),
            self.near.at[chip],
            (flip(links.dp, 1), links.z),
            self.slots[chip],
        )
        move.start()
        self.moves.append(move)

    def add(self):
        for move in self.moves:
            move.wait_recv()

        def one(step, _):
            rows = pl.ds(pl.multiple_of(step * 16, 16), 16)
            for chip in range(4):
                own = pl.ds(
                    pl.multiple_of((2 * chip + self.core) * self.rows + step * 16, 16), 16
                )
                self.near[chip, rows, :] = (
                    self.near[chip, rows, :].astype(jnp.float32)
                    + self.product[own, :].astype(jnp.float32)
                ).astype(jnp.bfloat16)
            return 0

        lax.fori_loop(0, self.rows // 16, one, 0)

    def clear(self):
        for move in self.moves:
            move.wait_send()

    def steps(self):
        return [functools.partial(self.multiply, chip) for chip in range(4)] + [self.add]


class ChipSum:
    def __init__(self, links, near, out, others, own=None):
        self.links, self.near, self.out, self.others, self.own = links, near, out, others, own
        self.slots = [links.slot() for _ in range(3)]
        self.core, self.chip = links.dp % 2, links.dp // 2
        self.rows = out.shape[0]

    def start(self):
        links = self.links
        chips = [flip(self.chip, 1), flip(self.chip, 2), flip(flip(self.chip, 1), 2)]
        self.moves = [
            links.copy(
                self.near.at[chip],
                self.others.at[index],
                (2 * chip + self.core, links.z),
                self.slots[index],
            )
            for index, chip in enumerate(chips)
        ]
        for move in self.moves:
            move.start()
        if self.own is not None:
            self.local = links.here(self.near.at[self.chip], self.own)
            self.local.start()

    def finish(self):
        for move in self.moves:
            move.wait_recv()
        if self.own is not None:
            self.local.wait()

        def one(step, _):
            rows = pl.ds(pl.multiple_of(step * 16, 16), 16)
            mine = self.own[rows, :] if self.own is not None else self.near[self.chip, rows, :]
            total = mine.astype(jnp.float32)
            for index in range(3):
                total = total + self.others[index, rows, :].astype(jnp.float32)
            self.out[rows, :] = total
            return 0

        lax.fori_loop(0, self.rows // 16, one, 0)
        for move in self.moves:
            move.wait_send()


def attend(query, key, value, out, logs, heads, chunk=256):
    scale = HEAD_DIM**-0.5
    for head in range(heads):
        lanes = slice(head * HEAD_DIM, (head + 1) * HEAD_DIM)

        def one(step, _, head=head, lanes=lanes):
            rows = pl.ds(pl.multiple_of(step * chunk, chunk), chunk)
            scores = product_back(query[rows, lanes], key[:, lanes]) * scale
            top = jnp.max(scores, axis=-1, keepdims=True)
            expo = jnp.exp(scores - top)
            summed = jnp.sum(expo, axis=-1, keepdims=True)
            probs = (expo * (1.0 / summed)).astype(jnp.bfloat16)
            out[rows, lanes] = jnp.dot(
                probs, value[:, lanes], preferred_element_type=jnp.float32
            ).astype(jnp.bfloat16)
            logs[rows, head : head + 1] = top + jnp.log(summed)
            return 0

        lax.fori_loop(0, query.shape[0] // chunk, one, 0)


def attend_back(query, key, value, logs, grad, grads, heads, chunk=256):
    scale = HEAD_DIM**-0.5
    grad_query, grad_key, grad_value = grads
    grad_key[...] = jnp.zeros(grad_key.shape, jnp.float32)
    grad_value[...] = jnp.zeros(grad_value.shape, jnp.float32)
    for head in range(heads):
        lanes = slice(head * HEAD_DIM, (head + 1) * HEAD_DIM)

        def one(step, _, head=head, lanes=lanes):
            rows = pl.ds(pl.multiple_of(step * chunk, chunk), chunk)
            scores = product_back(query[rows, lanes], key[:, lanes]) * scale
            probs = jnp.exp(scores - logs[rows, head : head + 1])
            prob_grad = product_back(grad[rows, lanes], value[:, lanes])
            inner = jnp.sum(prob_grad * probs, axis=-1, keepdims=True)
            score_grad = (probs * (prob_grad - inner)).astype(jnp.bfloat16)
            grad_query[rows, lanes] = (
                jnp.dot(score_grad, key[:, lanes], preferred_element_type=jnp.float32) * scale
            )
            grad_key[:, lanes] += weight_grad(score_grad, query[rows, lanes]) * scale
            grad_value[:, lanes] += weight_grad(probs.astype(jnp.bfloat16), grad[rows, lanes])
            return 0

        lax.fori_loop(0, query.shape[0] // chunk, one, 0)


def swapped(values):
    lane = lax.broadcasted_iota(jnp.int32, values.shape, 1)
    width = values.shape[1]
    return jnp.where(lane % 2 == 0, pltpu.roll(values, width - 1, 1), pltpu.roll(values, 1, 1))


def turn(values, cosine, sine, back):
    other = swapped(values) * sine
    return values * cosine - other if back else values * cosine + other


def square_columns(*arrays):
    return [jnp.sum(array * array, axis=-1, keepdims=True) for array in arrays]


def shape_norm(raw, inverse, gain, angles, out, heads, chunk=128):
    for head in range(heads):
        lanes = slice(head * HEAD_DIM, (head + 1) * HEAD_DIM)
        for start in range(0, raw.shape[0], chunk):
            rows = slice(start, start + chunk)
            values = raw[rows, lanes] * inverse[rows] * gain[head]
            if angles is not None:
                values = turn(values, angles[0][rows, :], angles[1][rows, :], False)
            out[rows, lanes] = values.astype(jnp.bfloat16)


def norm_dots(raw, inverse, gain, angles, grad, gain_out, heads, chunk=128):
    columns = []
    for start in range(0, raw.shape[0], chunk):
        rows = slice(start, start + chunk)
        column = jnp.zeros((chunk, 1), jnp.float32)
        for head in range(heads):
            lanes = slice(head * HEAD_DIM, (head + 1) * HEAD_DIM)
            values = grad[rows, lanes]
            if angles is not None:
                values = turn(values, angles[0][rows, :], angles[1][rows, :], True)
                grad[rows, lanes] = values
            part = values * raw[rows, lanes]
            column = column + jnp.sum(part * gain[head], axis=-1, keepdims=True)
            total = jnp.sum(part * inverse[rows], axis=0, keepdims=True)
            where = slice(head, head + 1)
            gain_out[where, :] = total if start == 0 else gain_out[where, :] + total
        columns.append(column)
    return jnp.concatenate(columns, axis=0)


def norm_pull(raw, inverse, gain, dots, grad, out, heads, chunk=128):
    for start in range(0, raw.shape[0], chunk):
        rows = slice(start, start + chunk)
        scale = inverse[rows]
        cut = dots[rows] * scale * scale * scale * (1.0 / D)
        for head in range(heads):
            lanes = slice(head * HEAD_DIM, (head + 1) * HEAD_DIM)
            out[rows, lanes] = (
                grad[rows, lanes] * gain[head] * scale - raw[rows, lanes] * cut
            ).astype(jnp.bfloat16)


def gains_of(gain_ref, kind, heads):
    lanes = slice(kind * HEAD_DIM, (kind + 1) * HEAD_DIM)
    return [gain_ref[head : head + 1, lanes] for head in range(heads)]


def exchange_scratch(length, size):
    return [
        pltpu.VMEM((8, length), jnp.float32),
        pltpu.VMEM((size - 1, 8, length), jnp.float32),
        pltpu.VMEM((128, length), jnp.float32),
    ]


class Plan:
    def __init__(self, mesh):
        self.dp = mesh.shape["dp"]
        self.tensor = mesh.shape["tensor"]
        self.cube = self.dp == 8
        self.calls = 0
        self.pieces = 4
        self.chunk = 1024
        self.counts = (1, 2, 3)

    def call(self, name, body, inputs, outputs, scratch, copies):
        self.calls += 1
        spaces = {True: pltpu.VMEM, False: pltpu.HBM}
        count_in, count_out = len(inputs), len(outputs)

        def kernel(*refs):
            ins = refs[:count_in]
            outs = refs[count_in : count_in + count_out]
            rest = refs[count_in + count_out :]
            links = Links(rest[0], rest[1], rest[2], self.dp, self.tensor)
            body(links, ins, outs, rest[3:])

        return pl.pallas_call(
            kernel,
            name=name,
            out_shape=[jax.ShapeDtypeStruct(shape, kind) for shape, kind, _ in outputs],
            in_specs=[pl.BlockSpec(memory_space=spaces[near]) for _, near in inputs],
            out_specs=[pl.BlockSpec(memory_space=spaces[near]) for _, _, near in outputs],
            scratch_shapes=[
                pltpu.SemaphoreType.DMA((copies,)),
                pltpu.SemaphoreType.DMA((copies,)),
                pltpu.SemaphoreType.DMA((64,)),
                *scratch,
            ],
            compiler_params=pltpu.CompilerParams(
                collective_id=self.calls, has_side_effects=True, vmem_limit_bytes=VMEM_BYTES
            ),
        )(*[array for array, _ in inputs])

    def gather_outputs(self, shards):
        return [
            ((self.dp * shard.shape[0], shard.shape[1]), shard.dtype, False) for shard in shards
        ]

    def open(self, hidden, time_rows, small, shards):
        rows, width = hidden.shape
        part = width // self.dp
        gain_part = small.shape[1] - part
        moving = shards if self.cube else []

        def body(links, ins, outs, scratch):
            hidden_ref, time_ref, small_ref = ins[:3]
            table_ref, gain_ref, whole_ref = outs[:3]
            (land,) = scratch
            links.greet({"line", "dpall"})
            gathers = [CubeGather(links, a, b) for a, b in zip(ins[3:], outs[3:])]
            dp, z = links.dp, links.z
            moves = []
            for step in range(1, self.dp):
                target = lax.rem(dp + step, self.dp)
                move = links.copy(small_ref, land.at[dp], (target, z), links.slot())
                move.start()
                moves.append(move)
            for item in gathers:
                item.start()
            land[dp] = small_ref[...]
            unit, _ = normed(hidden_ref[...])
            for move in moves:
                move.wait_recv()
            table = jnp.concatenate([land[k][:, :part] for k in range(self.dp)], axis=1)
            gain_ref[...] = jnp.concatenate([land[k][:, part:] for k in range(self.dp)], axis=1)
            table = table + time_ref[...]
            table_ref[...] = table
            line = LineGather(links, whole_ref, rows, 4)
            first = unit * (1.0 + table[1:2]) + table[0:1]
            whole_ref[pl.ds(pl.multiple_of(z * rows, 16), rows), :] = first.astype(jnp.bfloat16)
            for piece in range(4):
                line.start(piece)
            for piece in range(4):
                line.steps(piece)
                for item in gathers[2 * piece : 2 * piece + 2]:
                    item.forward()
            for item in gathers:
                item.tail()
            for item in gathers:
                item.finish()
            line.finish()
            for move in moves:
                move.wait_send()

        results = self.call(
            "open",
            body,
            [(hidden, True), (time_rows, True), (small, True)] + [(s, False) for s in moving],
            [
                ((8, width), jnp.float32, True),
                ((8, gain_part * self.dp), jnp.float32, True),
                ((rows * self.tensor, width), jnp.bfloat16, True),
            ]
            + self.gather_outputs(moving),
            [pltpu.VMEM((self.dp, 8, small.shape[1]), jnp.float32)],
            160,
        )
        return results[:3], self.gathered(results[3:], shards)

    def gathered(self, moved, shards):
        if self.cube:
            return list(moved)
        return [lax.all_gather(shard, "dp", axis=0, tiled=True) for shard in shards]

    def phase(
        self,
        name,
        near,
        kinds,
        scratch,
        pre,
        post,
        gather,
        shape,
        shards=(),
        lines=(),
        sums=(),
        jobs=(),
        tasks=None,
        begin=None,
        end=None,
        exchange=True,
        far=(),
        settle_small=None,
    ):
        length, width = shape
        rows = length // self.tensor
        pieces = self.pieces
        near = [(item if isinstance(item, list) else [item], group) for item, group in near]
        shards, lines, sums, far = list(shards), list(lines), list(sums), list(far)
        moving = shards if self.cube else []
        adding = sums if self.cube else []
        jobs = list(jobs)
        here = [job for job in jobs if job[4]] if self.cube else []
        count_near, count_kinds, count_scratch = len(near), len(kinds), len(scratch)

        job_scratch, job_outputs = [], []
        products, seats = {}, []
        for left, right, part, columns, now in jobs:
            if not self.cube:
                seats.append(("out", len(job_outputs)))
                job_outputs.append(((self.dp * part, columns), jnp.bfloat16, True))
                continue
            key = (part, columns)
            if key not in products:
                products[key] = len(job_scratch)
                job_scratch.append(pltpu.VMEM((8 * part, columns), jnp.bfloat16))
            if now:
                seats.append((products[key], len(job_scratch), len(job_outputs)))
                job_scratch.append(pltpu.VMEM((4, part, columns), jnp.bfloat16))
                job_scratch.append(pltpu.VMEM((3, part, columns), jnp.bfloat16))
                job_outputs.append(((part, columns), jnp.float32, True))
            else:
                seats.append((products[key], len(job_scratch), len(job_outputs)))
                job_scratch.append(pltpu.VMEM((4, part, columns), jnp.bfloat16))
                job_outputs.append(((4, part, columns), jnp.bfloat16, False))
        sum_scratch, sum_outputs = [], []
        for item in adding:
            _, part, columns = item.shape
            sum_scratch.append(pltpu.VMEM((3, part, columns), jnp.bfloat16))
            sum_scratch.append(pltpu.VMEM((part, columns), jnp.bfloat16))
            sum_outputs.append(((part, columns), jnp.float32, True))

        def body(links, ins, outs, rest):
            near_far = []
            for item, _ in near:
                near_far.append(ins[: len(item)])
                ins = ins[len(item) :]
            shard_refs, ins = ins[: len(moving)], ins[len(moving) :]
            line_refs, ins = ins[: len(lines)], ins[len(lines) :]
            sum_refs, far_refs = ins[: len(adding)], ins[len(adding) :]
            kind_far, outs = outs[:count_kinds], outs[count_kinds:]
            if gather:
                whole_far, outs = outs[0], outs[1:]
            full_refs, outs = outs[: len(moving)], outs[len(moving) :]
            line_outs, outs = outs[: len(lines)], outs[len(lines) :]
            job_refs, added_refs = outs[: len(jobs)], outs[len(jobs) :]
            near_refs, rest = rest[:count_near], rest[count_near:]
            loads = {}
            for index in order:
                start = 0
                for source in near_far[index]:
                    target = near_refs[index]
                    if len(near_far[index]) > 1:
                        target = target.at[:, pl.ds(start, source.shape[1])]
                        start += source.shape[1]
                    copy = links.here(source, target)
                    copy.start()
                    loads.setdefault(near[index][1], []).append(copy)

            def ready(group):
                for copy in loads.pop(group, []):
                    copy.wait()

            links.ready = ready
            kind_refs, stores = [], []
            for far_ref, (_, _, when_done) in zip(kind_far, kinds):
                if when_done is None:
                    kind_refs.append(far_ref)
                else:
                    kind_refs.append(rest[0])
                    rest = rest[1:]

            def store(source, target):
                stores.append(links.here(source, target))
                stores[-1].start()

            def store_kinds(moment):
                for held, far_ref, (_, _, when_done) in zip(kind_refs, kind_far, kinds):
                    if when_done == moment:
                        store(held, far_ref)

            if gather:
                whole_ref, rest = rest[0], rest[1:]
            partial_ref, land_right, land_left = rest[:3]
            user, rest = rest[3 : 3 + count_scratch], rest[3 + count_scratch :]
            job_rest, sum_rest = rest[: len(job_scratch)], rest[len(job_scratch) :]

            groups = {"zall"} if exchange else {"line"}
            if moving or adding or jobs:
                groups |= {"bits"} if self.cube else set()
            if adding or here:
                groups |= {"diag"}
            if settle_small:
                groups |= {"dpall"}
            links.greet(groups)
            gathers = [CubeGather(links, a, b) for a, b in zip(shard_refs, full_refs)]
            chunked, line_steps = [], []
            for source, target in zip(line_refs, line_outs):
                size = self.chunk
                parts = []
                for start in range(0, source.shape[1], size):
                    lanes = pl.ds(start, size)
                    item = LineGather(links, target.at[:, lanes], source.shape[0], 1)
                    parts.append(
                        [functools.partial(item.start, 0, source.at[:, lanes])]
                        + [functools.partial(item.step, hop, 0) for hop in range(links.size - 1)]
                    )
                    chunked.append(item)
                for turn_at in range(len(parts) + links.size - 1):
                    for index, steps in enumerate(parts):
                        if 0 <= turn_at - index < links.size:
                            line_steps.append(steps[turn_at - index])
            old = [
                ChipSum(links, a, b, sum_rest[2 * k], sum_rest[2 * k + 1])
                for k, (a, b) in enumerate(zip(sum_refs, added_refs))
            ]
            for item in gathers + old:
                item.start()
            copies = []
            for source, target in zip(line_refs, line_outs):
                copies.append(
                    links.here(
                        source, piece_of(target, links.z, source.shape[0], 0, source.shape[0])
                    )
                )
                copies[-1].start()

            def line_some(count):
                for _ in range(min(count, len(line_steps))):
                    line_steps.pop(0)()

            if line_steps:
                line_some(self.counts[0])
            state = begin(links, near_refs, kind_refs, user, far_refs) if begin else (None, [])
            ticks = state[1]
            if line_steps:
                ticks = [functools.partial(line_some, count) for count in self.counts[1:]]
            pre(links, near_refs, kind_refs, user, partial_ref, ticks)
            store_kinds("pre")
            for group in sorted(loads):
                ready(group)

            queue = list(ticks)
            queue += tasks(links, near_refs, kind_refs, user, far_refs) if tasks else []
            fresh, busy, cleared = [], {}, []
            for (left, right, part, columns, now), seat in zip(jobs, seats):
                left_ref, right_ref = left(near_refs, kind_refs, user), right(near_refs, kind_refs, user)
                out = job_refs[seat[-1]]
                if not self.cube:

                    def whole(start, left_ref=left_ref, right_ref=right_ref, out=out):
                        count = out.shape[0] // 4
                        where = slice(start * count, (start + 1) * count)
                        out[where, :] = weight_grad(left_ref[:, where], right_ref[...]).astype(
                            jnp.bfloat16
                        )

                    queue += [functools.partial(whole, start) for start in range(4)]
                    continue
                held = job_rest[seat[1]]
                item = CoreSum(links, left_ref, right_ref, job_rest[seat[0]], held)
                if seat[0] in busy:
                    queue.append(busy[seat[0]].clear)
                    cleared.append(busy[seat[0]])
                busy[seat[0]] = item
                queue += item.steps()
                if now:
                    chip = ChipSum(links, held, out, job_rest[seat[1] + 1])
                    queue.append(chip.start)
                    fresh.append(chip)
                else:
                    queue.append(functools.partial(store, held, out))
            queue += [item.forward for item in gathers]
            queue += [item.tail for item in gathers]
            if line_steps:
                plain, queue = queue, []
                total = len(line_steps)
                for index, run in enumerate(line_steps):
                    queue.append(run)
                    queue += plain[len(plain) * index // total : len(plain) * (index + 1) // total]

            reduce = LineReduce(links, partial_ref, land_right, land_left, rows, pieces)
            line = LineGather(links, whole_ref, rows, pieces) if gather else None
            for piece in range(pieces):
                reduce.first(piece)
            reduce.clear()

            def settle(piece):
                where = pl.ds(piece * (rows // pieces), rows // pieces)
                result = post(reduce.total(piece), where, near_refs, kind_refs, piece == 0)
                if gather:
                    line.block(links.z, piece)[...] = result
                    line.start(piece)

            stages = reduce_stages(reduce) + [settle]
            if gather:
                stages += [functools.partial(line.step, hop) for hop in range(links.size - 1)]
            wave(stages, pieces, queue)
            if settle_small:
                small = settle_small(links, near_refs, kind_refs, user)
            for item in gathers + old + fresh + chunked:
                item.finish()
            for item in busy.values():
                item.clear()
            for copy in copies:
                copy.wait()
            if end:
                end(state[0], links, near_refs, kind_refs, user)
            if settle_small:
                small()
            store_kinds("post")
            if gather:
                store(whole_ref, whole_far)
            reduce.finish()
            if gather:
                line.finish()
            for copy in stores:
                copy.wait()

        order = sorted(range(count_near), key=lambda index: near[index][1])
        inputs = [(item, False) for items, _ in near for item in items]
        inputs += [(item, False) for item in moving + lines + adding + far]
        outputs = [(form, kind, False) for form, kind, _ in kinds]
        if gather:
            outputs.append(((length, width), jnp.bfloat16, False))
        outputs += self.gather_outputs(moving)
        outputs += [
            ((item.shape[0] * self.tensor, item.shape[1]), item.dtype, False) for item in lines
        ]
        outputs += job_outputs + sum_outputs
        results = list(
            self.call(
                name,
                body,
                inputs,
                outputs,
                [
                    pltpu.VMEM(
                        (*items[0].shape[:-1], sum(item.shape[-1] for item in items)),
                        items[0].dtype,
                    )
                    for items, _ in near
                ]
                + [pltpu.VMEM(form, kind) for form, kind, moment in kinds if moment]
                + ([pltpu.VMEM((length, width), jnp.bfloat16)] if gather else [])
                + [
                    pltpu.VMEM((length, width), jnp.bfloat16),
                    pltpu.VMEM((self.tensor - 1, rows, width), jnp.bfloat16),
                    pltpu.VMEM((self.tensor - 1, rows, width), jnp.bfloat16),
                    *scratch,
                    *job_scratch,
                    *sum_scratch,
                ],
                240,
            )
        )
        kept, results = results[:count_kinds], results[count_kinds:]
        whole, results = (results[0], results[1:]) if gather else (None, results)
        full, results = self.gathered(results[: len(moving)], shards), results[len(moving) :]
        lined, results = results[: len(lines)], results[len(lines) :]
        made, added = results[: len(jobs)], results[len(jobs) :]
        if not self.cube:
            made = [
                self.scatter(item) if job[4] else item for item, job in zip(made, jobs)
            ]
            added = [self.scatter(item) for item in sums]
        return kept, whole, full, lined, made, added

    def scatter(self, grad):
        return lax.psum_scatter(grad, "dp", scatter_dimension=0, tiled=True).astype(jnp.float32)


def add_sum(ref, row, values, first):
    total = jnp.sum(values, axis=0, keepdims=True)
    ref[row : row + 1, :] = total if first else ref[row : row + 1, :] + total


def tick(ticks):
    if ticks:
        ticks.pop(0)()


def tiles(count, size):
    return [(start, min(size, count - start)) for start in range(0, count, size)]


def body(
    plan,
    hidden_in,
    text_states,
    time_embed,
    positions,
    modulation,
    query_weight,
    key_weight,
    value_weight,
    out_weight,
    cross_query,
    cross_key,
    cross_value,
    cross_out,
    up_weight,
    down_weight,
    qk_gain,
    norm_gain,
    cotangent,
):
    plan.calls = 0
    low, full_type = jnp.bfloat16, jnp.float32
    rows, width = hidden_in.shape
    length = rows * plan.tensor
    here = out_weight.shape[0]
    heads = here // HEAD_DIM
    hidden_units = up_weight.shape[1]
    text_rows, text_width = length, text_states.shape[1]
    part = width // plan.dp
    text_part = text_width // plan.dp
    shape = (length, width)

    top = jnp.concatenate([modulation, norm_gain[None], jnp.zeros((1, part), low)], axis=0)
    side = jnp.pad(qk_gain, ((0, 8 - heads), (0, 0)))
    small = jnp.concatenate([top, side], axis=1).astype(full_type)
    time_rows = jnp.pad(time_embed[0], ((0, 2), (0, 0)))
    (mixing, gains, self_whole), full = plan.open(
        hidden_in, time_rows, small, [query_weight, key_weight, value_weight, out_weight.T]
    )
    query_full, key_full, value_full, out_full = full
    cosine, sine = rotary_tables(positions, HEAD_DIM)

    def forward(kinds_of_gain, angles, inputs, weights, gain_ref, kinds, scratch, links, partial, ticks):
        query_in, other_in = inputs
        query_w, key_w, value_w, out_w = weights
        query_raw, key_raw, value, query, key, attended, logs, inverse = kinds
        exchange = Exchange(links, *scratch)
        links.ready(0)
        query_raw[...] = jnp.dot(query_in[...], query_w[...], preferred_element_type=full_type)
        links.ready(1)
        key_raw[...] = jnp.dot(other_in[...], key_w[...], preferred_element_type=full_type)
        exchange.start(square_columns(query_raw[...], key_raw[...]))
        links.ready(2)
        value[...] = jnp.dot(
            other_in[...], value_w[...], preferred_element_type=full_type
        ).astype(low)
        inverse[...] = exchange.finish(lambda total: lax.rsqrt(total / D + EPSILON))
        tick(ticks)
        links.ready(3)
        for index, (raw, out) in enumerate(((query_raw, query), (key_raw, key))):
            shape_norm(
                raw,
                inverse[:, index : index + 1],
                gains_of(gain_ref, kinds_of_gain[index], heads),
                angles,
                out,
                heads,
            )
        attend(query, key, value, attended, logs, heads)
        tick(ticks)
        links.ready(4)
        for start, size in tiles(width, 512):
            partial[:, start : start + size] = product_back(
                attended[...], out_w[start : start + size, :]
            ).astype(low)

    kept_kinds = [
        ((length, here), full_type, "pre"),
        ((length, here), full_type, "pre"),
        ((length, here), low, "pre"),
        ((length, here), low, "pre"),
        ((length, here), low, "pre"),
        ((length, here), low, "pre"),
        ((length, HEAD_DIM), full_type, "pre"),
        ((length, HEAD_DIM), full_type, "pre"),
    ]

    def self_pre(links, near, kinds, scratch, partial, ticks):
        whole, gain_ref, cosine_ref, sine_ref = near[:4]
        forward(
            (0, 1),
            (cosine_ref, sine_ref),
            (whole, whole),
            near[4:8],
            gain_ref,
            kinds[:8],
            scratch,
            links,
            partial,
            ticks,
        )

    def after_self(total, where, near, kinds, first):
        hidden_ref, mixing_ref = near[8:]
        branch_ref, resid_ref = kinds[8:]
        branch_ref[where, :] = total
        resid = hidden_ref[where, :] + total * mixing_ref[2:3]
        resid_ref[where, :] = resid
        unit, _ = normed(resid)
        return (unit * mixing_ref[6:7]).astype(low)

    kept, cross_whole, full, (text_all,), _, _ = plan.phase(
        "self_forward",
        [(self_whole, 0), (gains, 3), (cosine, 3), (sine, 3), (query_full, 0), (key_full, 1)]
        + [(value_full, 2), (out_full, 4), (hidden_in, 5), (mixing, 5)],
        kept_kinds + [((rows, width), full_type, "post")] * 2,
        exchange_scratch(length, plan.tensor),
        self_pre,
        after_self,
        True,
        shape,
        shards=[cross_key, cross_value, cross_query, cross_out.T],
        lines=[text_states],
    )
    self_kept, (self_branch, resid_self) = kept[:8], kept[8:]
    cross_key_full, cross_value_full, cross_query_full, cross_out_full = full[:4]

    def cross_begin(links, near, kinds, scratch, far):
        links.ready(-1)
        mixing_ref, cotangent_ref = near[8:]
        whole = kinds[9]
        mine = piece_of(whole, links.z, rows, 0, rows)
        mine[...] = (cotangent_ref[...] * mixing_ref[5:6]).astype(low)
        line = LineGather(links, whole, rows, 1)
        line.start(0)
        return line, [functools.partial(line.step, hop, 0) for hop in range(links.size - 1)]

    def cross_end(line, links, near, kinds, scratch):
        line.finish()

    def cross_pre(links, near, kinds, scratch, partial, ticks):
        whole, text, gain_ref = near[:3]
        forward(
            (2, 3),
            None,
            (whole, text),
            near[3:7],
            gain_ref,
            kinds[:8],
            scratch,
            links,
            partial,
            ticks,
        )

    def after_cross(total, where, near, kinds, first):
        resid_ref, mixing_ref = near[7:9]
        resid = resid_ref[where, :] + total
        kinds[8][where, :] = resid
        unit, _ = normed(resid)
        return (unit * (1.0 + mixing_ref[4:5]) + mixing_ref[3:4]).astype(low)

    kept, feed_whole, (up_full, down_full), _, _, _ = plan.phase(
        "cross_forward",
        [(cross_whole, 0), (text_all, 1), (gains, 3), (cross_query_full, 0), (cross_key_full, 1)]
        + [(cross_value_full, 2), (cross_out_full, 4), (resid_self, 5), (mixing, -1)]
        + [(cotangent, -1)],
        kept_kinds + [((rows, width), full_type, "post"), ((length, width), low, "post")],
        exchange_scratch(length, plan.tensor),
        cross_pre,
        after_cross,
        True,
        shape,
        shards=[up_weight, down_weight.T],
        begin=cross_begin,
        end=cross_end,
    )
    cross_kept, (resid_cross, feed_grad_whole) = kept[:8], kept[8:]

    feed_tiles = tiles(hidden_units, 512)

    def feed_begin(links, near, kinds, scratch, far):
        copies = []
        for start, size in feed_tiles:
            lanes = pl.ds(start, size)
            pair = [
                links.here(far[which].at[:, lanes], scratch[2 + which].at[:, lanes])
                for which in range(2)
            ]
            for copy in pair:
                copy.start()
            copies.append(pair)
        return None, copies

    def feed_pre(links, near, kinds, scratch, partial, copies):
        whole, grad_whole = near[:2]
        activated, grad_raw, up, down = scratch
        root = 0.7978845608028654
        links.ready(0)
        for (begin, size), pair in zip(feed_tiles, copies):
            lanes = slice(begin, begin + size)
            for copy in pair:
                copy.wait()

            def one(step, _, lanes=lanes):
                block = pl.ds(pl.multiple_of(step * 256, 256), 256)
                raw = jnp.dot(whole[block, :], up[:, lanes], preferred_element_type=full_type)
                grad = jnp.dot(grad_whole[block, :], down[:, lanes], preferred_element_type=full_type)
                square = raw * raw
                bend = jnp.tanh(root * raw * (1.0 + 0.044715 * square))
                half = 0.5 + 0.5 * bend
                activated[block, lanes] = (raw * half).astype(low)
                slope = half + 0.5 * raw * (1.0 - bend * bend) * root * (
                    1.0 + 3.0 * 0.044715 * square
                )
                grad_raw[block, lanes] = (grad * slope).astype(low)
                return 0

            lax.fori_loop(0, length // 256, one, 0)
        copies.clear()
        for start, size in tiles(width, 512):
            partial[:, start : start + size] = product_back(
                grad_raw[...], up[start : start + size, :]
            ).astype(low)

    def feed_tasks(links, near, kinds, scratch, far):
        activated, down = scratch[0], scratch[3]

        def one(start, size):
            kinds[2][:, start : start + size] = product_back(
                activated[...], down[start : start + size, :]
            ).astype(low)

        return [functools.partial(one, start, size) for start, size in tiles(width, 512)]

    def before_feed(total, where, near, kinds, first):
        resid_ref, cotangent_ref, mixing_ref = near[2:]
        grad_ref, sums_ref = kinds[:2]
        unit, inverse = normed(resid_ref[where, :])
        add_sum(sums_ref, 0, total, first)
        add_sum(sums_ref, 1, total * unit, first)
        grad = cotangent_ref[where, :] + normed_back(
            unit, inverse, total * (1.0 + mixing_ref[4:5])
        )
        grad_ref[where, :] = grad
        return grad.astype(low)

    kept, cross_grad_whole, _, _, made, _ = plan.phase(
        "feed",
        [(feed_whole, 0), (feed_grad_whole, 0), (resid_cross, 1), (cotangent, 1), (mixing, 1)],
        [
            ((rows, width), full_type, "post"),
            ((8, width), full_type, "post"),
            ((length, width), low, "post"),
        ],
        [pltpu.VMEM((length, hidden_units), low)] * 2
        + [pltpu.VMEM((width, hidden_units), low)] * 2,
        feed_pre,
        before_feed,
        True,
        shape,
        jobs=[
            (lambda n, k, s: n[1], lambda n, k, s: s[0], part, hidden_units, False),
            (lambda n, k, s: n[0], lambda n, k, s: s[1], part, hidden_units, False),
        ],
        tasks=feed_tasks,
        begin=feed_begin,
        far=[up_full, down_full],
        exchange=False,
    )
    grad_resid_cross, feed_sums, feed_partial = kept
    near_down, near_up = made

    def backward(kinds_of_gain, angles, refs, gain_ref, grad_outs, scratch, links, partial, ticks):
        (grad_whole, query_w, key_w, value_w, out_w) = refs[:5]
        query_raw, key_raw, value, query, key, attended, logs, inverse = refs[5:]
        gain_query_ref, gain_key_ref, query_out, key_out, value_out = grad_outs
        grad_attended, grad_query, grad_key, grad_value = scratch[3:7]
        exchange = Exchange(links, *scratch[:3])
        links.ready(0)
        grad_attended[...] = jnp.dot(
            grad_whole[...], out_w[...], preferred_element_type=full_type
        ).astype(low)
        links.ready(1)
        attend_back(
            query, key, value, logs, grad_attended, (grad_query, grad_key, grad_value), heads
        )
        tick(ticks)
        links.ready(2)
        sides = (
            (query_raw, inverse[:, 0:1], gains_of(gain_ref, kinds_of_gain[0], heads)),
            (key_raw, inverse[:, 1:2], gains_of(gain_ref, kinds_of_gain[1], heads)),
        )
        exchange.start(
            [
                norm_dots(*sides[0], angles, grad_query, gain_query_ref, heads),
                norm_dots(*sides[1], angles, grad_key, gain_key_ref, heads),
            ]
        )
        value_out[...] = grad_value[...].astype(low)
        dots = exchange.finish()
        tick(ticks)
        norm_pull(*sides[0], dots[:, 0:1], grad_query, query_out, heads)
        norm_pull(*sides[1], dots[:, 1:2], grad_key, key_out, heads)
        links.ready(3)
        pairs = [(query_out, query_w)]
        if angles is not None:
            pairs += [(key_out, key_w), (value_out, value_w)]
        for start, size in tiles(width, 512):
            total = 0.0
            for grads, weight in pairs:
                total = total + product_back(grads[...], weight[start : start + size, :])
            partial[:, start : start + size] = total.astype(low)

    back_scratch = exchange_scratch(length, plan.tensor) + [
        pltpu.VMEM((length, here), low),
        pltpu.VMEM((length, here), full_type),
        pltpu.VMEM((length, here), full_type),
        pltpu.VMEM((length, here), full_type),
        pltpu.VMEM((length, here), low),
        pltpu.VMEM((length, here), low),
        pltpu.VMEM((length, here), low),
    ]

    kept_groups = (2, 2, 1, 1, 1, 4, 1, 2)

    def cross_back_begin(links, near, kinds, scratch, far):
        links.ready(-1)
        late = LineReduce(links, near[20], scratch[10], scratch[11], rows, 1)
        late.clear()
        first, *others = late.stages(0)
        first()
        return late, others

    def cross_back_end(late, links, near, kinds, scratch):
        cotangent_ref, mixing_ref, resid_ref = near[17:20]
        total = late.total(0)
        kinds[2][...] = resid_ref[...] + total * mixing_ref[5:6]
        add_sum(kinds[1], 2, cotangent_ref[...] * total, True)
        late.finish()

    def cross_back_pre(links, near, kinds, scratch, partial, ticks):
        backward(
            (2, 3),
            None,
            (near[0], near[1], None, None, *near[2:11]),
            near[11],
            (kinds[4], kinds[5], *scratch[7:10]),
            scratch,
            links,
            partial,
            ticks,
        )

    def cross_back_tasks(links, near, kinds, scratch, far):
        held, loaded = scratch[12:14]
        size = held.shape[2]
        out_copies, loads = [], {}

        def load(index):
            loads[index] = [
                links.here(weight.at[pl.ds(index * size, size)], loaded.at[index % 2, which])
                for which, weight in enumerate(far)
            ]
            for copy in loads[index]:
                copy.start()

        def one(index):
            if index >= 2:
                out_copies[index - 2].wait()
            for copy in loads[index]:
                copy.wait()
            stage = held.at[index % 2]
            stage[...] = (
                product_back(scratch[8][...], loaded[index % 2, 0])
                + product_back(scratch[9][...], loaded[index % 2, 1])
            ).astype(low)
            if index + 2 < text_width // size:
                load(index + 2)
            copy = links.here(stage, kinds[3].at[:, pl.ds(index * size, size)])
            copy.start()
            out_copies.append(copy)

        def last():
            for copy in out_copies[-2:]:
                copy.wait()

        load(0)
        load(1)
        steps = [functools.partial(one, index) for index in range(text_width // size)]
        return steps + [last]

    def before_cross(total, where, near, kinds, first):
        resid_ref, grad_ref, branch_ref = near[14:17]
        mixing_ref = near[18]
        out_ref, sums_ref = kinds[:2]
        unit, inverse = normed(resid_ref[where, :])
        add_sum(sums_ref, 1, total * unit, first)
        grad = grad_ref[where, :] + normed_back(unit, inverse, total * mixing_ref[6:7])
        out_ref[where, :] = grad
        add_sum(sums_ref, 0, grad * branch_ref[where, :], first)
        return (grad * mixing_ref[2:3]).astype(low)

    kept, self_grad_whole, _, _, made, (sum_down, sum_up) = plan.phase(
        "cross_back",
        [(cross_grad_whole, 0), (cross_query_full, 3), (cross_out_full, 0)]
        + list(zip(cross_kept, kept_groups))
        + [(gains, 2), (cross_whole, 4), (text_all, 4), (resid_self, 4), (grad_resid_cross, 4)]
        + [(self_branch, 4), (cotangent, 4), (mixing, 4), (resid_cross, 4), (feed_partial, -1)],
        [
            ((rows, width), full_type, "post"),
            ((8, width), full_type, "post"),
            ((rows, width), full_type, "post"),
            ((text_rows, text_width), low, None),
            ((8, HEAD_DIM), full_type, "pre"),
            ((8, HEAD_DIM), full_type, "pre"),
        ],
        back_scratch
        + [pltpu.VMEM((plan.tensor - 1, rows, width), low)] * 2
        + [pltpu.VMEM((2, text_rows, 1024), low), pltpu.VMEM((2, 2, 1024, here), low)],
        cross_back_pre,
        before_cross,
        True,
        shape,
        sums=[near_down, near_up],
        jobs=[
            (lambda n, k, s: n[13], lambda n, k, s: s[8], text_part, here, False),
            (lambda n, k, s: n[13], lambda n, k, s: s[9], text_part, here, False),
            (lambda n, k, s: n[12], lambda n, k, s: s[7], part, here, False),
            (lambda n, k, s: n[0], lambda n, k, s: n[8], part, here, False),
        ],
        tasks=cross_back_tasks,
        begin=cross_back_begin,
        end=cross_back_end,
        far=[cross_key_full, cross_value_full],
    )
    grad_resid_self, cross_sums, block_out, text_partial, gain_cross_query, gain_cross_key = kept
    grad_text = lax.psum_scatter(
        text_partial, "tensor", scatter_dimension=0, tiled=True
    ).astype(full_type)

    def self_back_pre(links, near, kinds, scratch, partial, ticks):
        backward(
            (0, 1),
            (near[14], near[15]),
            near[:13],
            near[13],
            (kinds[2], kinds[3], *scratch[7:10]),
            scratch,
            links,
            partial,
            ticks,
        )

    def before_self(total, where, near, kinds, first):
        hidden_ref, grad_ref, mixing_ref = near[17:20]
        out_ref, sums_ref = kinds[:2]
        unit, inverse = normed(hidden_ref[where, :])
        add_sum(sums_ref, 0, total, first)
        add_sum(sums_ref, 1, total * unit, first)
        out_ref[where, :] = grad_ref[where, :] + normed_back(
            unit, inverse, total * (1.0 + mixing_ref[1:2])
        )

    gain_width = qk_gain.shape[1]

    def settle_small(links, near, kinds, scratch):
        feed_ref, cross_ref, gain_cross_query_ref, gain_cross_key_ref = near[20:]
        self_ref, gain_query_ref, gain_key_ref, time_ref, slice_ref = kinds[1:]
        mine, line_land, stage, land = scratch[10:]
        z, dp = links.z, links.dp
        mine[...] = jnp.concatenate(
            [
                self_ref[0:2, :],
                cross_ref[0:1, :],
                feed_ref[0:2, :],
                cross_ref[2:3, :],
                cross_ref[1:2, :],
                jnp.zeros((1, width), full_type),
            ],
            axis=0,
        )
        moves = []
        for step in range(1, plan.tensor):
            target = lax.rem(z + step, plan.tensor)
            move = links.copy(mine, line_land.at[z], (dp, target), links.slot())
            move.start()
            moves.append(move)
        line_land[z] = mine[...]
        gain_rows = jnp.concatenate(
            [gain_query_ref[...], gain_key_ref[...]]
            + [gain_cross_query_ref[...], gain_cross_key_ref[...]],
            axis=1,
        )
        for move in moves:
            move.wait_recv()
        total = line_land[0]
        for index in range(1, plan.tensor):
            total = total + line_land[index]
        time_ref[0, :, :] = total[:6]
        for index in range(plan.dp):
            stage[index] = jnp.concatenate(
                [
                    total[:, index * part : (index + 1) * part],
                    gain_rows[:, index * gain_width : (index + 1) * gain_width],
                ],
                axis=1,
            )
        land[dp] = stage[dp]
        others = []
        for step in range(1, plan.dp):
            target = lax.rem(dp + step, plan.dp)
            move = links.copy(stage.at[target], land.at[dp], (target, z), links.slot())
            move.start()
            others.append(move)

        def finish():
            for move in others:
                move.wait_recv()
            summed = land[0]
            for index in range(1, plan.dp):
                summed = summed + land[index]
            slice_ref[...] = summed
            for move in moves + others:
                move.wait_send()

        return finish

    kept, _, _, _, made, sums = plan.phase(
        "self_back",
        [(self_grad_whole, 0), (query_full, 3), (key_full, 3), (value_full, 3), (out_full, 0)]
        + list(zip(self_kept, kept_groups))
        + [(gains, 2), (cosine, 2), (sine, 2), (self_whole, 4), (hidden_in, 4)]
        + [(grad_resid_self, 4), (mixing, 4), (feed_sums, 4), (cross_sums, 4)]
        + [(gain_cross_query, 4), (gain_cross_key, 4)],
        [
            ((rows, width), full_type, "post"),
            ((8, width), full_type, "post"),
            ((8, HEAD_DIM), full_type, "pre"),
            ((8, HEAD_DIM), full_type, "pre"),
            ((1, 6, width), full_type, "post"),
            ((8, part + gain_width), full_type, "post"),
        ],
        back_scratch
        + [
            pltpu.VMEM((8, width), full_type),
            pltpu.VMEM((plan.tensor, 8, width), full_type),
            pltpu.VMEM((plan.dp, 8, part + gain_width), full_type),
            pltpu.VMEM((plan.dp, 8, part + gain_width), full_type),
        ],
        self_back_pre,
        before_self,
        False,
        shape,
        sums=made,
        jobs=[
            (lambda n, k, s: n[16], lambda n, k, s: s[7], part, here, True),
            (lambda n, k, s: n[16], lambda n, k, s: s[8], part, here, True),
            (lambda n, k, s: n[16], lambda n, k, s: s[9], part, here, True),
            (lambda n, k, s: n[0], lambda n, k, s: n[10], part, here, True),
        ],
        settle_small=settle_small,
    )
    grad_hidden, _, _, _, grad_time, mine = kept
    sum_cross_key, sum_cross_value, sum_cross_query, sum_cross_out = sums
    sum_query, sum_key, sum_value, sum_out = made

    return (
        block_out,
        grad_hidden,
        grad_text,
        grad_time,
        mine[:6, :part],
        sum_query,
        sum_key,
        sum_value,
        sum_out.T,
        sum_cross_query,
        sum_cross_key,
        sum_cross_value,
        sum_cross_out.T,
        sum_up,
        sum_down.T,
        mine[:heads, part:],
        mine[6, :part],
    )


def solution(mesh):
    return jax.shard_map(
        functools.partial(body, Plan(mesh)),
        mesh=mesh,
        in_specs=(
            P(("dp", "tensor"), None),
            P(("dp", "tensor"), None),
            P("dp", None, None),
            P(None, "dp"),
            P(None, "dp"),
            P("dp", "tensor"),
            P("dp", "tensor"),
            P("dp", "tensor"),
            P("tensor", "dp"),
            P("dp", "tensor"),
            P("dp", "tensor"),
            P("dp", "tensor"),
            P("tensor", "dp"),
            P("dp", "tensor"),
            P("tensor", "dp"),
            P("tensor", "dp"),
            P("dp"),
            P(("dp", "tensor"), None),
        ),
        out_specs=(
            P(("dp", "tensor"), None),
            P(("dp", "tensor"), None),
            P(("dp", "tensor"), None),
            P("dp", None, None),
            P(None, "dp"),
            P("dp", "tensor"),
            P("dp", "tensor"),
            P("dp", "tensor"),
            P("tensor", "dp"),
            P("dp", "tensor"),
            P("dp", "tensor"),
            P("dp", "tensor"),
            P("tensor", "dp"),
            P("dp", "tensor"),
            P("tensor", "dp"),
            P("tensor", "dp"),
            P("dp"),
        ),
        check_vma=False,
    )
```

```python
import functools

import jax
import jax.numpy as jnp
from jax import lax
from jax.experimental import pallas as pl
from jax.experimental.pallas import tpu as pltpu
from jax.sharding import PartitionSpec as P

MESH = pl.DeviceIdType.MESH
VMEM_BYTES = 62 * 2**20

HEAD_DIM = 128
D = 1536


EPSILON = 1e-06
CONTRACT_LAST = (((1,), (1,)), ((), ()))
CONTRACT_FIRST = (((0,), (0,)), ((), ()))


def rotary_tables(positions, head_width):
    pairs = head_width // 2
    third = pairs // 3
    first = pairs - 2 * third
    freq_frame = jnp.power(10000.0, -jnp.arange(first, dtype=jnp.float32) / first)
    freq_side = jnp.power(10000.0, -jnp.arange(third, dtype=jnp.float32) / third)
    places = positions.astype(jnp.float32)
    angles = jnp.concatenate(
        [
            places[0][:, None] * jnp.repeat(freq_frame, 2)[None, :],
            places[1][:, None] * jnp.repeat(freq_side, 2)[None, :],
            places[2][:, None] * jnp.repeat(freq_side, 2)[None, :],
        ],
        axis=1,
    )
    sign = jnp.where(jnp.arange(head_width) % 2 == 0, -1.0, 1.0)
    return (jnp.cos(angles), jnp.sin(angles) * sign)


def product_back(grads, weight):
    return lax.dot_general(grads, weight, CONTRACT_LAST, preferred_element_type=jnp.float32)


def weight_grad(inputs, grads):
    return lax.dot_general(inputs, grads, CONTRACT_FIRST, preferred_element_type=jnp.float32)


def when(cond, run):
    if cond is None:
        run()
    else:
        pl.when(cond)(run)


def flip(index, bit):
    return index + bit - 2 * bit * (index // bit % 2)


def normed(values):
    center = values - jnp.mean(values, axis=-1, keepdims=True)
    inverse = lax.rsqrt(jnp.mean(center * center, axis=-1, keepdims=True) + EPSILON)
    return center * inverse, inverse


def normed_back(unit, inverse, grad):
    mean_grad = jnp.mean(grad, axis=-1, keepdims=True)
    mean_dot = jnp.mean(grad * unit, axis=-1, keepdims=True)
    return (grad - mean_grad - unit * mean_dot) * inverse


class Links:
    def __init__(self, send, recv, local, dp_size, tensor_size):
        self.send, self.recv, self.local = send, recv, local
        self.count = 0
        self.local_count = 0
        self.dp_size, self.size = dp_size, tensor_size
        self.dp = lax.axis_index("dp")
        self.z = lax.axis_index("tensor")

    def slot(self):
        self.count += 1
        return self.count - 1

    def copy(self, source, target, device, slot):
        return pltpu.make_async_remote_copy(
            src_ref=source,
            dst_ref=target,
            send_sem=self.send.at[slot],
            recv_sem=self.recv.at[slot],
            device_id=device,
            device_id_type=MESH,
        )

    def here(self, source, target):
        self.local_count += 1
        return pltpu.make_async_copy(source, target, self.local.at[self.local_count - 1])

    def greet(self, groups):
        barrier = pltpu.get_barrier_semaphore()
        peers = []
        if "line" in groups and "zall" not in groups:
            peers += [
                ((self.dp, self.z - 1), self.z > 0),
                ((self.dp, self.z + 1), self.z < self.size - 1),
            ]
        if "zall" in groups:
            peers += [
                ((self.dp, lax.rem(self.z + k, self.size)), None) for k in range(1, self.size)
            ]
        if "dpall" in groups:
            peers += [
                ((lax.rem(self.dp + k, self.dp_size), self.z), None)
                for k in range(1, self.dp_size)
            ]
        if "bits" in groups and "dpall" not in groups:
            bit = 1
            while bit < self.dp_size:
                peers.append(((flip(self.dp, bit), self.z), None))
                bit *= 2
        if "diag" in groups and "dpall" not in groups:
            peers.append(((flip(flip(self.dp, 2), 4), self.z), None))
        for device, cond in peers:
            when(
                cond,
                lambda device=device: pl.semaphore_signal(
                    barrier, inc=1, device_id=device, device_id_type=MESH
                ),
            )
        expected = sum(1 for _, cond in peers if cond is None)
        for _, cond in peers:
            if cond is not None:
                expected = expected + cond.astype(jnp.int32)
        pl.semaphore_wait(barrier, expected)


def piece_of(ref, block, rows, start, count):
    return ref.at[pl.ds(pl.multiple_of(block * rows + start, 16), count)]


class LineGather:
    def __init__(self, links, whole, rows, pieces):
        self.links, self.whole, self.rows, self.count = links, whole, rows, rows // pieces
        self.pieces = pieces
        hops = links.size - 1
        self.right = [[links.slot() for _ in range(pieces)] for _ in range(hops)]
        self.left = [[links.slot() for _ in range(pieces)] for _ in range(hops)]

    def block(self, index, piece):
        return piece_of(self.whole, index, self.rows, piece * self.count, self.count)

    def move(self, index, piece, way, slot):
        part = self.block(index, piece)
        return self.links.copy(part, part, (self.links.dp, self.links.z + way), slot)

    def start(self, piece, source=None):
        links = self.links
        z, last = links.z, links.size - 1

        def go(way, slot):
            mine = self.block(z, piece)
            links.copy(mine if source is None else source, mine, (links.dp, z + way), slot).start()

        when(z < last, lambda: go(1, self.right[0][piece]))
        when(z > 0, lambda: go(-1, self.left[0][piece]))

    def step(self, hop, piece):
        z, last = self.links.z, self.links.size - 1

        def from_left():
            self.move(z - 1 - hop, piece, -1, self.right[hop][piece]).wait_recv()
            if hop + 1 < last:
                when(
                    z < last,
                    lambda: self.move(z - 1 - hop, piece, 1, self.right[hop + 1][piece]).start(),
                )

        def from_right():
            self.move(z + 1 + hop, piece, 1, self.left[hop][piece]).wait_recv()
            if hop + 1 < last:
                when(
                    z > 0,
                    lambda: self.move(z + 1 + hop, piece, -1, self.left[hop + 1][piece]).start(),
                )

        when(z - 1 - hop >= 0, from_left)
        when(z + 1 + hop <= last, from_right)

    def steps(self, piece):
        for hop in range(self.links.size - 1):
            self.step(hop, piece)

    def finish(self):
        z, last = self.links.z, self.links.size - 1
        for hop in range(last):
            for piece in range(self.pieces):
                when(
                    (z - hop >= 0) & (z < last),
                    lambda: self.move(z - hop, piece, 1, self.right[hop][piece]).wait_send(),
                )
                when(
                    (z + hop <= last) & (z > 0),
                    lambda: self.move(z + hop, piece, -1, self.left[hop][piece]).wait_send(),
                )


class LineReduce:
    def __init__(self, links, partial, land_right, land_left, rows, pieces):
        self.links, self.partial, self.rows, self.count = links, partial, rows, rows // pieces
        self.land = {1: land_right, -1: land_left}
        self.pieces = pieces
        last = links.size - 1
        self.slots = {
            way: [None] + [[links.slot() for _ in range(pieces)] for _ in range(last)]
            for way in (1, -1)
        }

    def landing(self, way, distance, piece):
        return self.land[way].at[distance - 1, pl.ds(piece * self.count, self.count)]

    def part(self, index, piece):
        return piece_of(self.partial, index, self.rows, piece * self.count, self.count)

    def move(self, source, way, distance, piece):
        return self.links.copy(
            source,
            self.landing(way, distance, piece),
            (self.links.dp, self.links.z + way),
            self.slots[way][distance][piece],
        )

    def arrived(self, way, distance, piece):
        self.links.copy(
            self.landing(way, distance, piece),
            self.landing(way, distance, piece),
            (self.links.dp, self.links.z - way),
            self.slots[way][distance][piece],
        ).wait_recv()

    def first(self, piece):
        z, last = self.links.z, self.links.size - 1

        def from_first():
            for distance in range(last, 0, -1):
                self.move(self.part(distance, piece), 1, distance, piece).start()

        def from_last():
            for distance in range(last, 0, -1):
                self.move(self.part(last - distance, piece), -1, distance, piece).start()

        when(z == 0, from_first)
        when(z == last, from_last)

    def first_at(self, distance, piece):
        z, last = self.links.z, self.links.size - 1
        when(
            z == 0,
            lambda: self.move(self.part(distance, piece), 1, distance, piece).start(),
        )
        when(
            z == last,
            lambda: self.move(self.part(last - distance, piece), -1, distance, piece).start(),
        )

    def stages(self, piece):
        last = self.links.size - 1

        def one(distance):
            self.first_at(distance, piece)
            if distance < last:
                self.step(distance, piece)

        return [functools.partial(one, distance) for distance in range(last, 0, -1)]

    def clear(self):
        z, last = self.links.z, self.links.size - 1

        def zero(way):
            self.land[way][0] = jnp.zeros(self.land[way].shape[1:], self.land[way].dtype)

        when(z == 0, lambda: zero(1))
        when(z == last, lambda: zero(-1))

    def step(self, distance, piece):
        z, last = self.links.z, self.links.size - 1
        for way in (1, -1):
            inside = (
                (z > 0) & (z + distance <= last)
                if way == 1
                else (z < last) & (z - distance >= 0)
            )

            def go(way=way):
                self.arrived(way, distance + 1, piece)
                held = self.landing(way, distance + 1, piece)
                own = self.part(z + way * distance, piece)
                held[...] = (
                    held[...].astype(jnp.float32) + own[...].astype(jnp.float32)
                ).astype(held.dtype)
                self.move(held, way, distance, piece).start()

            when(inside, go)

    def total(self, piece):
        z, last = self.links.z, self.links.size - 1
        when(z > 0, lambda: self.arrived(1, 1, piece))
        when(z < last, lambda: self.arrived(-1, 1, piece))
        return (
            self.part(z, piece)[...].astype(jnp.float32)
            + self.landing(1, 1, piece)[...].astype(jnp.float32)
            + self.landing(-1, 1, piece)[...].astype(jnp.float32)
        )

    def finish(self):
        z, last = self.links.z, self.links.size - 1
        for distance in range(1, last + 1):
            for piece in range(self.pieces):
                held = self.landing(1, distance, piece)
                when(
                    z + distance <= last,
                    lambda: self.move(held, 1, distance, piece).wait_send(),
                )
                back = self.landing(-1, distance, piece)
                when(
                    z - distance >= 0,
                    lambda: self.move(back, -1, distance, piece).wait_send(),
                )


def reduce_stages(reduce):
    return [
        functools.partial(reduce.step, distance)
        for distance in range(reduce.links.size - 2, 0, -1)
    ]


def wave(stages, pieces, queue, rate=4):
    count = pieces + len(stages) - 1
    done = 0
    for step in range(count):
        for index, stage in enumerate(stages):
            if 0 <= step - index < pieces:
                stage(step - index)
        until = min(len(queue), len(queue) * (step + 1) * rate // (2 * count))
        for run in queue[done:until]:
            run()
        done = until


class CubeGather:
    def __init__(self, links, shard, whole):
        self.links, self.shard, self.whole = links, shard, whole
        self.rows = shard.shape[0]
        self.slots = [links.slot() for _ in range(8)]
        dp = links.dp
        self.core, self.side, self.over = flip(dp, 1), flip(dp, 2), flip(dp, 4)
        self.far = flip(flip(dp, 2), 4)
        self.sent = []

    def block(self, index, start=0, count=None):
        return piece_of(self.whole, index, self.rows, start, count or self.rows)

    def send(self, source, target, device, slot):
        move = self.links.copy(source, target, (device, self.links.z), self.slots[slot])
        move.start()
        self.sent.append(move)

    def got(self, part, slot):
        self.links.copy(part, part, (self.core, self.links.z), self.slots[slot]).wait_recv()

    def start(self):
        mine = self.block(self.links.dp)
        self.own = self.links.here(self.shard, mine)
        self.own.start()
        self.send(self.shard, mine, self.side, 1)
        self.send(self.shard, mine, self.over, 2)
        self.send(self.shard, mine, self.core, 0)

    def forward(self):
        half = self.rows // 2
        self.got(self.block(self.side), 1)
        part = self.block(self.side, 0, half)
        self.send(part, part, self.over, 3)
        part = self.block(self.side)
        self.send(part, part, self.core, 5)
        self.got(self.block(self.over), 2)
        part = self.block(self.over, half, half)
        self.send(part, part, self.side, 4)
        part = self.block(self.over)
        self.send(part, part, self.core, 6)

    def tail(self):
        half = self.rows // 2
        self.got(self.block(self.far, 0, half), 3)
        self.got(self.block(self.far, half, half), 4)
        part = self.block(self.far)
        self.send(part, part, self.core, 7)

    def finish(self):
        self.got(self.block(self.core), 0)
        self.got(self.block(flip(self.core, 2)), 5)
        self.got(self.block(flip(self.core, 4)), 6)
        self.got(self.block(flip(flip(self.core, 2), 4)), 7)
        for move in self.sent:
            move.wait_send()
        self.own.wait()


class Exchange:
    def __init__(self, links, mine, land, turned):
        self.links, self.mine, self.land, self.turned = links, mine, land, turned
        self.slots = [links.slot() for _ in range(links.size - 1)]

    def start(self, columns):
        links = self.links
        lane = lax.broadcasted_iota(jnp.int32, (columns[0].shape[0], 128), 1)
        flat = jnp.zeros(lane.shape, jnp.float32)
        for index, column in enumerate(columns):
            flat = jnp.where(lane == index, column, flat)
        self.mine[...] = flat.T[:8]
        self.moves = [
            links.copy(
                self.mine,
                self.land.at[step - 1],
                (links.dp, lax.rem(links.z + step, links.size)),
                slot,
            )
            for step, slot in enumerate(self.slots, 1)
        ]
        for move in self.moves:
            move.start()

    def finish(self, shape=lambda total: total):
        total = self.mine[...]
        for step, move in enumerate(self.moves):
            move.wait_recv()
            total = total + self.land[step]
        self.turned[...] = jnp.zeros(self.turned.shape, jnp.float32)
        self.turned[0:8, :] = shape(total)
        for move in self.moves:
            move.wait_send()
        return self.turned[...].T


class CoreSum:
    def __init__(self, links, left, right, product, near):
        self.links, self.left, self.right = links, left, right
        self.product, self.near = product, near
        self.rows = near.shape[1]
        self.slots = [links.slot() for _ in range(4)]
        self.core = links.dp % 2
        self.moves = []

    def multiply(self, chip):
        links, count = self.links, 2 * self.rows
        self.product[chip * count : (chip + 1) * count, :] = weight_grad(
            self.left[:, chip * count : (chip + 1) * count], self.right[...]
        ).astype(jnp.bfloat16)
        move = links.copy(
            piece_of(self.product, 2 * chip + 1 - self.core, self.rows, 0, self.rows),
            self.near.at[chip],
            (flip(links.dp, 1), links.z),
            self.slots[chip],
        )
        move.start()
        self.moves.append(move)

    def add(self):
        for move in self.moves:
            move.wait_recv()

        def one(step, _):
            rows = pl.ds(pl.multiple_of(step * 16, 16), 16)
            for chip in range(4):
                own = pl.ds(
                    pl.multiple_of((2 * chip + self.core) * self.rows + step * 16, 16), 16
                )
                self.near[chip, rows, :] = (
                    self.near[chip, rows, :].astype(jnp.float32)
                    + self.product[own, :].astype(jnp.float32)
                ).astype(jnp.bfloat16)
            return 0

        lax.fori_loop(0, self.rows // 16, one, 0)

    def clear(self):
        for move in self.moves:
            move.wait_send()

    def steps(self):
        return [functools.partial(self.multiply, chip) for chip in range(4)] + [self.add]


class ChipSum:
    def __init__(self, links, near, out, others, own=None):
        self.links, self.near, self.out, self.others, self.own = links, near, out, others, own
        self.slots = [links.slot() for _ in range(3)]
        self.core, self.chip = links.dp % 2, links.dp // 2
        self.rows = out.shape[0]

    def start(self):
        links = self.links
        chips = [flip(self.chip, 1), flip(self.chip, 2), flip(flip(self.chip, 1), 2)]
        self.moves = [
            links.copy(
                self.near.at[chip],
                self.others.at[index],
                (2 * chip + self.core, links.z),
                self.slots[index],
            )
            for index, chip in enumerate(chips)
        ]
        for move in self.moves:
            move.start()
        if self.own is not None:
            self.local = links.here(self.near.at[self.chip], self.own)
            self.local.start()

    def finish(self):
        for move in self.moves:
            move.wait_recv()
        if self.own is not None:
            self.local.wait()

        def one(step, _):
            rows = pl.ds(pl.multiple_of(step * 16, 16), 16)
            mine = self.own[rows, :] if self.own is not None else self.near[self.chip, rows, :]
            total = mine.astype(jnp.float32)
            for index in range(3):
                total = total + self.others[index, rows, :].astype(jnp.float32)
            self.out[rows, :] = total
            return 0

        lax.fori_loop(0, self.rows // 16, one, 0)
        for move in self.moves:
            move.wait_send()


def attend(query, key, value, out, logs, heads, chunk=256):
    scale = HEAD_DIM**-0.5
    for head in range(heads):
        lanes = slice(head * HEAD_DIM, (head + 1) * HEAD_DIM)

        def one(step, _, head=head, lanes=lanes):
            rows = pl.ds(pl.multiple_of(step * chunk, chunk), chunk)
            scores = product_back(query[rows, lanes], key[:, lanes]) * scale
            top = jnp.max(scores, axis=-1, keepdims=True)
            expo = jnp.exp(scores - top)
            summed = jnp.sum(expo, axis=-1, keepdims=True)
            probs = (expo * (1.0 / summed)).astype(jnp.bfloat16)
            out[rows, lanes] = jnp.dot(
                probs, value[:, lanes], preferred_element_type=jnp.float32
            ).astype(jnp.bfloat16)
            logs[rows, head : head + 1] = top + jnp.log(summed)
            return 0

        lax.fori_loop(0, query.shape[0] // chunk, one, 0)


def attend_back(query, key, value, logs, grad, grads, heads, chunk=256):
    scale = HEAD_DIM**-0.5
    grad_query, grad_key, grad_value = grads
    grad_key[...] = jnp.zeros(grad_key.shape, jnp.float32)
    grad_value[...] = jnp.zeros(grad_value.shape, jnp.float32)
    for head in range(heads):
        lanes = slice(head * HEAD_DIM, (head + 1) * HEAD_DIM)

        def one(step, _, head=head, lanes=lanes):
            rows = pl.ds(pl.multiple_of(step * chunk, chunk), chunk)
            scores = product_back(query[rows, lanes], key[:, lanes]) * scale
            probs = jnp.exp(scores - logs[rows, head : head + 1])
            prob_grad = product_back(grad[rows, lanes], value[:, lanes])
            inner = jnp.sum(prob_grad * probs, axis=-1, keepdims=True)
            score_grad = (probs * (prob_grad - inner)).astype(jnp.bfloat16)
            grad_query[rows, lanes] = (
                jnp.dot(score_grad, key[:, lanes], preferred_element_type=jnp.float32) * scale
            )
            grad_key[:, lanes] += weight_grad(score_grad, query[rows, lanes]) * scale
            grad_value[:, lanes] += weight_grad(probs.astype(jnp.bfloat16), grad[rows, lanes])
            return 0

        lax.fori_loop(0, query.shape[0] // chunk, one, 0)


def swapped(values):
    lane = lax.broadcasted_iota(jnp.int32, values.shape, 1)
    width = values.shape[1]
    return jnp.where(lane % 2 == 0, pltpu.roll(values, width - 1, 1), pltpu.roll(values, 1, 1))


def turn(values, cosine, sine, back):
    other = swapped(values) * sine
    return values * cosine - other if back else values * cosine + other


def square_columns(*arrays):
    return [jnp.sum(array * array, axis=-1, keepdims=True) for array in arrays]


def shape_norm(raw, inverse, gain, angles, out, heads, chunk=128):
    for head in range(heads):
        lanes = slice(head * HEAD_DIM, (head + 1) * HEAD_DIM)
        for start in range(0, raw.shape[0], chunk):
            rows = slice(start, start + chunk)
            values = raw[rows, lanes] * inverse[rows] * gain[head]
            if angles is not None:
                values = turn(values, angles[0][rows, :], angles[1][rows, :], False)
            out[rows, lanes] = values.astype(jnp.bfloat16)


def norm_dots(raw, inverse, gain, angles, grad, gain_out, heads, chunk=128):
    columns = []
    for start in range(0, raw.shape[0], chunk):
        rows = slice(start, start + chunk)
        column = jnp.zeros((chunk, 1), jnp.float32)
        for head in range(heads):
            lanes = slice(head * HEAD_DIM, (head + 1) * HEAD_DIM)
            values = grad[rows, lanes]
            if angles is not None:
                values = turn(values, angles[0][rows, :], angles[1][rows, :], True)
                grad[rows, lanes] = values
            part = values * raw[rows, lanes]
            column = column + jnp.sum(part * gain[head], axis=-1, keepdims=True)
            total = jnp.sum(part * inverse[rows], axis=0, keepdims=True)
            where = slice(head, head + 1)
            gain_out[where, :] = total if start == 0 else gain_out[where, :] + total
        columns.append(column)
    return jnp.concatenate(columns, axis=0)


def norm_pull(raw, inverse, gain, dots, grad, out, heads, chunk=128):
    for start in range(0, raw.shape[0], chunk):
        rows = slice(start, start + chunk)
        scale = inverse[rows]
        cut = dots[rows] * scale * scale * scale * (1.0 / D)
        for head in range(heads):
            lanes = slice(head * HEAD_DIM, (head + 1) * HEAD_DIM)
            out[rows, lanes] = (
                grad[rows, lanes] * gain[head] * scale - raw[rows, lanes] * cut
            ).astype(jnp.bfloat16)


def gains_of(gain_ref, kind, heads):
    lanes = slice(kind * HEAD_DIM, (kind + 1) * HEAD_DIM)
    return [gain_ref[head : head + 1, lanes] for head in range(heads)]


def exchange_scratch(length, size):
    return [
        pltpu.VMEM((8, length), jnp.float32),
        pltpu.VMEM((size - 1, 8, length), jnp.float32),
        pltpu.VMEM((128, length), jnp.float32),
    ]


class Plan:
    def __init__(self, mesh):
        self.dp = mesh.shape["dp"]
        self.tensor = mesh.shape["tensor"]
        self.cube = self.dp == 8
        self.calls = 0
        self.pieces = 4
        self.chunk = 1024
        self.counts = (1, 2, 3)

    def call(self, name, body, inputs, outputs, scratch, copies):
        self.calls += 1
        spaces = {True: pltpu.VMEM, False: pltpu.HBM}
        count_in, count_out = len(inputs), len(outputs)

        def kernel(*refs):
            ins = refs[:count_in]
            outs = refs[count_in : count_in + count_out]
            rest = refs[count_in + count_out :]
            links = Links(rest[0], rest[1], rest[2], self.dp, self.tensor)
            body(links, ins, outs, rest[3:])

        return pl.pallas_call(
            kernel,
            name=name,
            out_shape=[jax.ShapeDtypeStruct(shape, kind) for shape, kind, _ in outputs],
            in_specs=[pl.BlockSpec(memory_space=spaces[near]) for _, near in inputs],
            out_specs=[pl.BlockSpec(memory_space=spaces[near]) for _, _, near in outputs],
            scratch_shapes=[
                pltpu.SemaphoreType.DMA((copies,)),
                pltpu.SemaphoreType.DMA((copies,)),
                pltpu.SemaphoreType.DMA((64,)),
                *scratch,
            ],
            compiler_params=pltpu.CompilerParams(
                collective_id=self.calls, has_side_effects=True, vmem_limit_bytes=VMEM_BYTES
            ),
        )(*[array for array, _ in inputs])

    def gather_outputs(self, shards):
        return [
            ((self.dp * shard.shape[0], shard.shape[1]), shard.dtype, False) for shard in shards
        ]

    def open(self, hidden, time_rows, small, shards):
        rows, width = hidden.shape
        part = width // self.dp
        gain_part = small.shape[1] - part
        moving = shards if self.cube else []

        def body(links, ins, outs, scratch):
            hidden_ref, time_ref, small_ref = ins[:3]
            table_ref, gain_ref, whole_ref = outs[:3]
            (land,) = scratch
            links.greet({"line", "dpall"})
            gathers = [CubeGather(links, a, b) for a, b in zip(ins[3:], outs[3:])]
            dp, z = links.dp, links.z
            moves = []
            for step in range(1, self.dp):
                target = lax.rem(dp + step, self.dp)
                move = links.copy(small_ref, land.at[dp], (target, z), links.slot())
                move.start()
                moves.append(move)
            for item in gathers:
                item.start()
            land[dp] = small_ref[...]
            unit, _ = normed(hidden_ref[...])
            for move in moves:
                move.wait_recv()
            table = jnp.concatenate([land[k][:, :part] for k in range(self.dp)], axis=1)
            gain_ref[...] = jnp.concatenate([land[k][:, part:] for k in range(self.dp)], axis=1)
            table = table + time_ref[...]
            table_ref[...] = table
            line = LineGather(links, whole_ref, rows, 4)
            first = unit * (1.0 + table[1:2]) + table[0:1]
            whole_ref[pl.ds(pl.multiple_of(z * rows, 16), rows), :] = first.astype(jnp.bfloat16)
            for piece in range(4):
                line.start(piece)
            for piece in range(4):
                line.steps(piece)
                for item in gathers[2 * piece : 2 * piece + 2]:
                    item.forward()
            for item in gathers:
                item.tail()
            for item in gathers:
                item.finish()
            line.finish()
            for move in moves:
                move.wait_send()

        results = self.call(
            "open",
            body,
            [(hidden, True), (time_rows, True), (small, True)] + [(s, False) for s in moving],
            [
                ((8, width), jnp.float32, True),
                ((8, gain_part * self.dp), jnp.float32, True),
                ((rows * self.tensor, width), jnp.bfloat16, True),
            ]
            + self.gather_outputs(moving),
            [pltpu.VMEM((self.dp, 8, small.shape[1]), jnp.float32)],
            160,
        )
        return results[:3], self.gathered(results[3:], shards)

    def gathered(self, moved, shards):
        if self.cube:
            return list(moved)
        return [lax.all_gather(shard, "dp", axis=0, tiled=True) for shard in shards]

    def phase(
        self,
        name,
        near,
        kinds,
        scratch,
        pre,
        post,
        gather,
        shape,
        shards=(),
        lines=(),
        sums=(),
        jobs=(),
        tasks=None,
        begin=None,
        end=None,
        exchange=True,
        far=(),
        settle_small=None,
    ):
        length, width = shape
        rows = length // self.tensor
        pieces = self.pieces
        near = [(item if isinstance(item, list) else [item], group) for item, group in near]
        shards, lines, sums, far = list(shards), list(lines), list(sums), list(far)
        moving = shards if self.cube else []
        adding = sums if self.cube else []
        jobs = list(jobs)
        here = [job for job in jobs if job[4]] if self.cube else []
        count_near, count_kinds, count_scratch = len(near), len(kinds), len(scratch)

        job_scratch, job_outputs = [], []
        products, seats = {}, []
        for left, right, part, columns, now in jobs:
            if not self.cube:
                seats.append(("out", len(job_outputs)))
                job_outputs.append(((self.dp * part, columns), jnp.bfloat16, True))
                continue
            key = (part, columns)
            if key not in products:
                products[key] = len(job_scratch)
                job_scratch.append(pltpu.VMEM((8 * part, columns), jnp.bfloat16))
            if now:
                seats.append((products[key], len(job_scratch), len(job_outputs)))
                job_scratch.append(pltpu.VMEM((4, part, columns), jnp.bfloat16))
                job_scratch.append(pltpu.VMEM((3, part, columns), jnp.bfloat16))
                job_outputs.append(((part, columns), jnp.float32, True))
            else:
                seats.append((products[key], len(job_scratch), len(job_outputs)))
                job_scratch.append(pltpu.VMEM((4, part, columns), jnp.bfloat16))
                job_outputs.append(((4, part, columns), jnp.bfloat16, False))
        sum_scratch, sum_outputs = [], []
        for item in adding:
            _, part, columns = item.shape
            sum_scratch.append(pltpu.VMEM((3, part, columns), jnp.bfloat16))
            sum_scratch.append(pltpu.VMEM((part, columns), jnp.bfloat16))
            sum_outputs.append(((part, columns), jnp.float32, True))

        def body(links, ins, outs, rest):
            near_far = []
            for item, _ in near:
                near_far.append(ins[: len(item)])
                ins = ins[len(item) :]
            shard_refs, ins = ins[: len(moving)], ins[len(moving) :]
            line_refs, ins = ins[: len(lines)], ins[len(lines) :]
            sum_refs, far_refs = ins[: len(adding)], ins[len(adding) :]
            kind_far, outs = outs[:count_kinds], outs[count_kinds:]
            if gather:
                whole_far, outs = outs[0], outs[1:]
            full_refs, outs = outs[: len(moving)], outs[len(moving) :]
            line_outs, outs = outs[: len(lines)], outs[len(lines) :]
            job_refs, added_refs = outs[: len(jobs)], outs[len(jobs) :]
            near_refs, rest = rest[:count_near], rest[count_near:]
            loads = {}
            for index in order:
                start = 0
                for source in near_far[index]:
                    target = near_refs[index]
                    if len(near_far[index]) > 1:
                        target = target.at[:, pl.ds(start, source.shape[1])]
                        start += source.shape[1]
                    copy = links.here(source, target)
                    copy.start()
                    loads.setdefault(near[index][1], []).append(copy)

            def ready(group):
                for copy in loads.pop(group, []):
                    copy.wait()

            links.ready = ready
            kind_refs, stores = [], []
            for far_ref, (_, _, when_done) in zip(kind_far, kinds):
                if when_done is None:
                    kind_refs.append(far_ref)
                else:
                    kind_refs.append(rest[0])
                    rest = rest[1:]

            def store(source, target):
                stores.append(links.here(source, target))
                stores[-1].start()

            def store_kinds(moment):
                for held, far_ref, (_, _, when_done) in zip(kind_refs, kind_far, kinds):
                    if when_done == moment:
                        store(held, far_ref)

            if gather:
                whole_ref, rest = rest[0], rest[1:]
            partial_ref, land_right, land_left = rest[:3]
            user, rest = rest[3 : 3 + count_scratch], rest[3 + count_scratch :]
            job_rest, sum_rest = rest[: len(job_scratch)], rest[len(job_scratch) :]

            groups = {"zall"} if exchange else {"line"}
            if moving or adding or jobs:
                groups |= {"bits"} if self.cube else set()
            if adding or here:
                groups |= {"diag"}
            if settle_small:
                groups |= {"dpall"}
            links.greet(groups)
            gathers = [CubeGather(links, a, b) for a, b in zip(shard_refs, full_refs)]
            chunked, line_steps = [], []
            for source, target in zip(line_refs, line_outs):
                size = self.chunk
                parts = []
                for start in range(0, source.shape[1], size):
                    lanes = pl.ds(start, size)
                    item = LineGather(links, target.at[:, lanes], source.shape[0], 1)
                    parts.append(
                        [functools.partial(item.start, 0, source.at[:, lanes])]
                        + [functools.partial(item.step, hop, 0) for hop in range(links.size - 1)]
                    )
                    chunked.append(item)
                for turn_at in range(len(parts) + links.size - 1):
                    for index, steps in enumerate(parts):
                        if 0 <= turn_at - index < links.size:
                            line_steps.append(steps[turn_at - index])
            old = [
                ChipSum(links, a, b, sum_rest[2 * k], sum_rest[2 * k + 1])
                for k, (a, b) in enumerate(zip(sum_refs, added_refs))
            ]
            for item in gathers + old:
                item.start()
            copies = []
            for source, target in zip(line_refs, line_outs):
                copies.append(
                    links.here(
                        source, piece_of(target, links.z, source.shape[0], 0, source.shape[0])
                    )
                )
                copies[-1].start()

            def line_some(count):
                for _ in range(min(count, len(line_steps))):
                    line_steps.pop(0)()

            if line_steps:
                line_some(self.counts[0])
            state = begin(links, near_refs, kind_refs, user, far_refs) if begin else (None, [])
            ticks = state[1]
            if line_steps:
                ticks = [functools.partial(line_some, count) for count in self.counts[1:]]
            pre(links, near_refs, kind_refs, user, partial_ref, ticks)
            store_kinds("pre")
            for group in sorted(loads):
                ready(group)

            queue = list(ticks)
            queue += tasks(links, near_refs, kind_refs, user, far_refs) if tasks else []
            fresh, busy, cleared = [], {}, []
            for (left, right, part, columns, now), seat in zip(jobs, seats):
                left_ref, right_ref = left(near_refs, kind_refs, user), right(near_refs, kind_refs, user)
                out = job_refs[seat[-1]]
                if not self.cube:

                    def whole(start, left_ref=left_ref, right_ref=right_ref, out=out):
                        count = out.shape[0] // 4
                        where = slice(start * count, (start + 1) * count)
                        out[where, :] = weight_grad(left_ref[:, where], right_ref[...]).astype(
                            jnp.bfloat16
                        )

                    queue += [functools.partial(whole, start) for start in range(4)]
                    continue
                held = job_rest[seat[1]]
                item = CoreSum(links, left_ref, right_ref, job_rest[seat[0]], held)
                if seat[0] in busy:
                    queue.append(busy[seat[0]].clear)
                    cleared.append(busy[seat[0]])
                busy[seat[0]] = item
                queue += item.steps()
                if now:
                    chip = ChipSum(links, held, out, job_rest[seat[1] + 1])
                    queue.append(chip.start)
                    fresh.append(chip)
                else:
                    queue.append(functools.partial(store, held, out))
            queue += [item.forward for item in gathers]
            queue += [item.tail for item in gathers]
            if line_steps:
                plain, queue = queue, []
                total = len(line_steps)
                for index, run in enumerate(line_steps):
                    queue.append(run)
                    queue += plain[len(plain) * index // total : len(plain) * (index + 1) // total]

            reduce = LineReduce(links, partial_ref, land_right, land_left, rows, pieces)
            line = LineGather(links, whole_ref, rows, pieces) if gather else None
            for piece in range(pieces):
                reduce.first(piece)
            reduce.clear()

            def settle(piece):
                where = pl.ds(piece * (rows // pieces), rows // pieces)
                result = post(reduce.total(piece), where, near_refs, kind_refs, piece == 0)
                if gather:
                    line.block(links.z, piece)[...] = result
                    line.start(piece)

            stages = reduce_stages(reduce) + [settle]
            if gather:
                stages += [functools.partial(line.step, hop) for hop in range(links.size - 1)]
            wave(stages, pieces, queue, 3 if moving else 4)
            if settle_small:
                small = settle_small(links, near_refs, kind_refs, user)
            for item in gathers + old + fresh + chunked:
                item.finish()
            for item in busy.values():
                item.clear()
            for copy in copies:
                copy.wait()
            if end:
                end(state[0], links, near_refs, kind_refs, user)
            if settle_small:
                small()
            store_kinds("post")
            if gather:
                store(whole_ref, whole_far)
            reduce.finish()
            if gather:
                line.finish()
            for copy in stores:
                copy.wait()

        order = sorted(range(count_near), key=lambda index: near[index][1])
        inputs = [(item, False) for items, _ in near for item in items]
        inputs += [(item, False) for item in moving + lines + adding + far]
        outputs = [(form, kind, False) for form, kind, _ in kinds]
        if gather:
            outputs.append(((length, width), jnp.bfloat16, False))
        outputs += self.gather_outputs(moving)
        outputs += [
            ((item.shape[0] * self.tensor, item.shape[1]), item.dtype, False) for item in lines
        ]
        outputs += job_outputs + sum_outputs
        results = list(
            self.call(
                name,
                body,
                inputs,
                outputs,
                [
                    pltpu.VMEM(
                        (*items[0].shape[:-1], sum(item.shape[-1] for item in items)),
                        items[0].dtype,
                    )
                    for items, _ in near
                ]
                + [pltpu.VMEM(form, kind) for form, kind, moment in kinds if moment]
                + ([pltpu.VMEM((length, width), jnp.bfloat16)] if gather else [])
                + [
                    pltpu.VMEM((length, width), jnp.bfloat16),
                    pltpu.VMEM((self.tensor - 1, rows, width), jnp.bfloat16),
                    pltpu.VMEM((self.tensor - 1, rows, width), jnp.bfloat16),
                    *scratch,
                    *job_scratch,
                    *sum_scratch,
                ],
                240,
            )
        )
        kept, results = results[:count_kinds], results[count_kinds:]
        whole, results = (results[0], results[1:]) if gather else (None, results)
        full, results = self.gathered(results[: len(moving)], shards), results[len(moving) :]
        lined, results = results[: len(lines)], results[len(lines) :]
        made, added = results[: len(jobs)], results[len(jobs) :]
        if not self.cube:
            made = [
                self.scatter(item) if job[4] else item for item, job in zip(made, jobs)
            ]
            added = [self.scatter(item) for item in sums]
        return kept, whole, full, lined, made, added

    def scatter(self, grad):
        return lax.psum_scatter(grad, "dp", scatter_dimension=0, tiled=True).astype(jnp.float32)


def add_sum(ref, row, values, first):
    total = jnp.sum(values, axis=0, keepdims=True)
    ref[row : row + 1, :] = total if first else ref[row : row + 1, :] + total


def tick(ticks):
    if ticks:
        ticks.pop(0)()


def tiles(count, size):
    return [(start, min(size, count - start)) for start in range(0, count, size)]


def body(
    plan,
    hidden_in,
    text_states,
    time_embed,
    positions,
    modulation,
    query_weight,
    key_weight,
    value_weight,
    out_weight,
    cross_query,
    cross_key,
    cross_value,
    cross_out,
    up_weight,
    down_weight,
    qk_gain,
    norm_gain,
    cotangent,
):
    plan.calls = 0
    low, full_type = jnp.bfloat16, jnp.float32
    rows, width = hidden_in.shape
    length = rows * plan.tensor
    here = out_weight.shape[0]
    heads = here // HEAD_DIM
    hidden_units = up_weight.shape[1]
    text_rows, text_width = length, text_states.shape[1]
    part = width // plan.dp
    text_part = text_width // plan.dp
    shape = (length, width)

    top = jnp.concatenate([modulation, norm_gain[None], jnp.zeros((1, part), low)], axis=0)
    side = jnp.pad(qk_gain, ((0, 8 - heads), (0, 0)))
    small = jnp.concatenate([top, side], axis=1).astype(full_type)
    time_rows = jnp.pad(time_embed[0], ((0, 2), (0, 0)))
    (mixing, gains, self_whole), full = plan.open(
        hidden_in, time_rows, small, [query_weight, key_weight, value_weight, out_weight.T]
    )
    query_full, key_full, value_full, out_full = full
    cosine, sine = rotary_tables(positions, HEAD_DIM)

    def forward(kinds_of_gain, angles, inputs, weights, gain_ref, kinds, scratch, links, partial, ticks):
        query_in, other_in = inputs
        query_w, key_w, value_w, out_w = weights
        query_raw, key_raw, value, query, key, attended, logs, inverse = kinds
        exchange = Exchange(links, *scratch)
        links.ready(0)
        query_raw[...] = jnp.dot(query_in[...], query_w[...], preferred_element_type=full_type)
        links.ready(1)
        key_raw[...] = jnp.dot(other_in[...], key_w[...], preferred_element_type=full_type)
        exchange.start(square_columns(query_raw[...], key_raw[...]))
        links.ready(2)
        value[...] = jnp.dot(
            other_in[...], value_w[...], preferred_element_type=full_type
        ).astype(low)
        inverse[...] = exchange.finish(lambda total: lax.rsqrt(total / D + EPSILON))
        tick(ticks)
        links.ready(3)
        for index, (raw, out) in enumerate(((query_raw, query), (key_raw, key))):
            shape_norm(
                raw,
                inverse[:, index : index + 1],
                gains_of(gain_ref, kinds_of_gain[index], heads),
                angles,
                out,
                heads,
            )
        attend(query, key, value, attended, logs, heads)
        tick(ticks)
        links.ready(4)
        for start, size in tiles(width, 512):
            partial[:, start : start + size] = product_back(
                attended[...], out_w[start : start + size, :]
            ).astype(low)

    kept_kinds = [
        ((length, here), full_type, "pre"),
        ((length, here), full_type, "pre"),
        ((length, here), low, "pre"),
        ((length, here), low, "pre"),
        ((length, here), low, "pre"),
        ((length, here), low, "pre"),
        ((length, HEAD_DIM), full_type, "pre"),
        ((length, HEAD_DIM), full_type, "pre"),
    ]

    def self_pre(links, near, kinds, scratch, partial, ticks):
        whole, gain_ref, cosine_ref, sine_ref = near[:4]
        forward(
            (0, 1),
            (cosine_ref, sine_ref),
            (whole, whole),
            near[4:8],
            gain_ref,
            kinds[:8],
            scratch,
            links,
            partial,
            ticks,
        )

    def after_self(total, where, near, kinds, first):
        hidden_ref, mixing_ref = near[8:]
        branch_ref, resid_ref = kinds[8:]
        branch_ref[where, :] = total
        resid = hidden_ref[where, :] + total * mixing_ref[2:3]
        resid_ref[where, :] = resid
        unit, _ = normed(resid)
        return (unit * mixing_ref[6:7]).astype(low)

    kept, cross_whole, full, (text_all,), _, _ = plan.phase(
        "self_forward",
        [(self_whole, 0), (gains, 3), (cosine, 3), (sine, 3), (query_full, 0), (key_full, 1)]
        + [(value_full, 2), (out_full, 4), (hidden_in, 5), (mixing, 5)],
        kept_kinds + [((rows, width), full_type, "post")] * 2,
        exchange_scratch(length, plan.tensor),
        self_pre,
        after_self,
        True,
        shape,
        shards=[cross_key, cross_value, cross_query, cross_out.T],
        lines=[text_states],
    )
    self_kept, (self_branch, resid_self) = kept[:8], kept[8:]
    cross_key_full, cross_value_full, cross_query_full, cross_out_full = full[:4]

    def cross_begin(links, near, kinds, scratch, far):
        links.ready(-1)
        mixing_ref, cotangent_ref = near[8:]
        whole = kinds[9]
        mine = piece_of(whole, links.z, rows, 0, rows)
        mine[...] = (cotangent_ref[...] * mixing_ref[5:6]).astype(low)
        line = LineGather(links, whole, rows, 1)
        line.start(0)
        return line, [functools.partial(line.step, hop, 0) for hop in range(links.size - 1)]

    def cross_end(line, links, near, kinds, scratch):
        line.finish()

    def cross_pre(links, near, kinds, scratch, partial, ticks):
        whole, text, gain_ref = near[:3]
        forward(
            (2, 3),
            None,
            (whole, text),
            near[3:7],
            gain_ref,
            kinds[:8],
            scratch,
            links,
            partial,
            ticks,
        )

    def after_cross(total, where, near, kinds, first):
        resid_ref, mixing_ref = near[7:9]
        resid = resid_ref[where, :] + total
        kinds[8][where, :] = resid
        unit, _ = normed(resid)
        return (unit * (1.0 + mixing_ref[4:5]) + mixing_ref[3:4]).astype(low)

    kept, feed_whole, (up_full, down_full), _, _, _ = plan.phase(
        "cross_forward",
        [(cross_whole, 0), (text_all, 1), (gains, 3), (cross_query_full, 0), (cross_key_full, 1)]
        + [(cross_value_full, 2), (cross_out_full, 4), (resid_self, 5), (mixing, -1)]
        + [(cotangent, -1)],
        kept_kinds + [((rows, width), full_type, "post"), ((length, width), low, "post")],
        exchange_scratch(length, plan.tensor),
        cross_pre,
        after_cross,
        True,
        shape,
        shards=[up_weight, down_weight.T],
        begin=cross_begin,
        end=cross_end,
    )
    cross_kept, (resid_cross, feed_grad_whole) = kept[:8], kept[8:]

    feed_tiles = tiles(hidden_units, 512)

    def feed_begin(links, near, kinds, scratch, far):
        copies = []
        for start, size in feed_tiles:
            lanes = pl.ds(start, size)
            pair = [
                links.here(far[which].at[:, lanes], scratch[2 + which].at[:, lanes])
                for which in range(2)
            ]
            for copy in pair:
                copy.start()
            copies.append(pair)
        return None, copies

    def feed_pre(links, near, kinds, scratch, partial, copies):
        whole, grad_whole = near[:2]
        activated, grad_raw, up, down = scratch
        root = 0.7978845608028654
        links.ready(0)
        for (begin, size), pair in zip(feed_tiles, copies):
            lanes = slice(begin, begin + size)
            for copy in pair:
                copy.wait()

            def one(step, _, lanes=lanes):
                block = pl.ds(pl.multiple_of(step * 256, 256), 256)
                raw = jnp.dot(whole[block, :], up[:, lanes], preferred_element_type=full_type)
                grad = jnp.dot(grad_whole[block, :], down[:, lanes], preferred_element_type=full_type)
                square = raw * raw
                bend = jnp.tanh(root * raw * (1.0 + 0.044715 * square))
                half = 0.5 + 0.5 * bend
                activated[block, lanes] = (raw * half).astype(low)
                slope = half + 0.5 * raw * (1.0 - bend * bend) * root * (
                    1.0 + 3.0 * 0.044715 * square
                )
                grad_raw[block, lanes] = (grad * slope).astype(low)
                return 0

            lax.fori_loop(0, length // 256, one, 0)
        copies.clear()
        for start, size in tiles(width, 512):
            partial[:, start : start + size] = product_back(
                grad_raw[...], up[start : start + size, :]
            ).astype(low)

    def feed_tasks(links, near, kinds, scratch, far):
        activated, down = scratch[0], scratch[3]

        def one(start, size):
            kinds[2][:, start : start + size] = product_back(
                activated[...], down[start : start + size, :]
            ).astype(low)

        return [functools.partial(one, start, size) for start, size in tiles(width, 512)]

    def before_feed(total, where, near, kinds, first):
        resid_ref, cotangent_ref, mixing_ref = near[2:]
        grad_ref, sums_ref = kinds[:2]
        unit, inverse = normed(resid_ref[where, :])
        add_sum(sums_ref, 0, total, first)
        add_sum(sums_ref, 1, total * unit, first)
        grad = cotangent_ref[where, :] + normed_back(
            unit, inverse, total * (1.0 + mixing_ref[4:5])
        )
        grad_ref[where, :] = grad
        return grad.astype(low)

    kept, cross_grad_whole, _, _, made, _ = plan.phase(
        "feed",
        [(feed_whole, 0), (feed_grad_whole, 0), (resid_cross, 1), (cotangent, 1), (mixing, 1)],
        [
            ((rows, width), full_type, "post"),
            ((8, width), full_type, "post"),
            ((length, width), low, "post"),
        ],
        [pltpu.VMEM((length, hidden_units), low)] * 2
        + [pltpu.VMEM((width, hidden_units), low)] * 2,
        feed_pre,
        before_feed,
        True,
        shape,
        jobs=[
            (lambda n, k, s: n[1], lambda n, k, s: s[0], part, hidden_units, False),
            (lambda n, k, s: n[0], lambda n, k, s: s[1], part, hidden_units, False),
        ],
        tasks=feed_tasks,
        begin=feed_begin,
        far=[up_full, down_full],
        exchange=False,
    )
    grad_resid_cross, feed_sums, feed_partial = kept
    near_down, near_up = made

    def backward(kinds_of_gain, angles, refs, gain_ref, grad_outs, scratch, links, partial, ticks):
        (grad_whole, query_w, key_w, value_w, out_w) = refs[:5]
        query_raw, key_raw, value, query, key, attended, logs, inverse = refs[5:]
        gain_query_ref, gain_key_ref, query_out, key_out, value_out = grad_outs
        grad_attended, grad_query, grad_key, grad_value = scratch[3:7]
        exchange = Exchange(links, *scratch[:3])
        links.ready(0)
        grad_attended[...] = jnp.dot(
            grad_whole[...], out_w[...], preferred_element_type=full_type
        ).astype(low)
        links.ready(1)
        attend_back(
            query, key, value, logs, grad_attended, (grad_query, grad_key, grad_value), heads
        )
        tick(ticks)
        links.ready(2)
        sides = (
            (query_raw, inverse[:, 0:1], gains_of(gain_ref, kinds_of_gain[0], heads)),
            (key_raw, inverse[:, 1:2], gains_of(gain_ref, kinds_of_gain[1], heads)),
        )
        exchange.start(
            [
                norm_dots(*sides[0], angles, grad_query, gain_query_ref, heads),
                norm_dots(*sides[1], angles, grad_key, gain_key_ref, heads),
            ]
        )
        value_out[...] = grad_value[...].astype(low)
        dots = exchange.finish()
        tick(ticks)
        norm_pull(*sides[0], dots[:, 0:1], grad_query, query_out, heads)
        norm_pull(*sides[1], dots[:, 1:2], grad_key, key_out, heads)
        links.ready(3)
        pairs = [(query_out, query_w)]
        if angles is not None:
            pairs += [(key_out, key_w), (value_out, value_w)]
        for start, size in tiles(width, 512):
            total = 0.0
            for grads, weight in pairs:
                total = total + product_back(grads[...], weight[start : start + size, :])
            partial[:, start : start + size] = total.astype(low)

    back_scratch = exchange_scratch(length, plan.tensor) + [
        pltpu.VMEM((length, here), low),
        pltpu.VMEM((length, here), full_type),
        pltpu.VMEM((length, here), full_type),
        pltpu.VMEM((length, here), full_type),
        pltpu.VMEM((length, here), low),
        pltpu.VMEM((length, here), low),
        pltpu.VMEM((length, here), low),
    ]

    kept_groups = (2, 2, 1, 1, 1, 4, 1, 2)

    def cross_back_begin(links, near, kinds, scratch, far):
        links.ready(-1)
        late = LineReduce(links, near[20], scratch[10], scratch[11], rows, 1)
        late.clear()
        first, *others = late.stages(0)
        first()
        return late, others

    def cross_back_end(late, links, near, kinds, scratch):
        cotangent_ref, mixing_ref, resid_ref = near[17:20]
        total = late.total(0)
        kinds[2][...] = resid_ref[...] + total * mixing_ref[5:6]
        add_sum(kinds[1], 2, cotangent_ref[...] * total, True)
        late.finish()

    def cross_back_pre(links, near, kinds, scratch, partial, ticks):
        backward(
            (2, 3),
            None,
            (near[0], near[1], None, None, *near[2:11]),
            near[11],
            (kinds[4], kinds[5], *scratch[7:10]),
            scratch,
            links,
            partial,
            ticks,
        )

    def cross_back_tasks(links, near, kinds, scratch, far):
        held, loaded = scratch[12:14]
        size = held.shape[2]
        out_copies, loads = [], {}

        def load(index):
            loads[index] = [
                links.here(weight.at[pl.ds(index * size, size)], loaded.at[index % 2, which])
                for which, weight in enumerate(far)
            ]
            for copy in loads[index]:
                copy.start()

        def one(index):
            if index >= 2:
                out_copies[index - 2].wait()
            for copy in loads[index]:
                copy.wait()
            stage = held.at[index % 2]
            stage[...] = (
                product_back(scratch[8][...], loaded[index % 2, 0])
                + product_back(scratch[9][...], loaded[index % 2, 1])
            ).astype(low)
            if index + 2 < text_width // size:
                load(index + 2)
            copy = links.here(stage, kinds[3].at[:, pl.ds(index * size, size)])
            copy.start()
            out_copies.append(copy)

        def last():
            for copy in out_copies[-2:]:
                copy.wait()

        load(0)
        load(1)
        steps = [functools.partial(one, index) for index in range(text_width // size)]
        return steps + [last]

    def before_cross(total, where, near, kinds, first):
        resid_ref, grad_ref, branch_ref = near[14:17]
        mixing_ref = near[18]
        out_ref, sums_ref = kinds[:2]
        unit, inverse = normed(resid_ref[where, :])
        add_sum(sums_ref, 1, total * unit, first)
        grad = grad_ref[where, :] + normed_back(unit, inverse, total * mixing_ref[6:7])
        out_ref[where, :] = grad
        add_sum(sums_ref, 0, grad * branch_ref[where, :], first)
        return (grad * mixing_ref[2:3]).astype(low)

    kept, self_grad_whole, _, _, made, (sum_down, sum_up) = plan.phase(
        "cross_back",
        [(cross_grad_whole, 0), (cross_query_full, 3), (cross_out_full, 0)]
        + list(zip(cross_kept, kept_groups))
        + [(gains, 2), (cross_whole, 4), (text_all, 4), (resid_self, 4), (grad_resid_cross, 4)]
        + [(self_branch, 4), (cotangent, 4), (mixing, 4), (resid_cross, 4), (feed_partial, -1)],
        [
            ((rows, width), full_type, "post"),
            ((8, width), full_type, "post"),
            ((rows, width), full_type, "post"),
            ((text_rows, text_width), low, None),
            ((8, HEAD_DIM), full_type, "pre"),
            ((8, HEAD_DIM), full_type, "pre"),
        ],
        back_scratch
        + [pltpu.VMEM((plan.tensor - 1, rows, width), low)] * 2
        + [pltpu.VMEM((2, text_rows, 1024), low), pltpu.VMEM((2, 2, 1024, here), low)],
        cross_back_pre,
        before_cross,
        True,
        shape,
        sums=[near_down, near_up],
        jobs=[
            (lambda n, k, s: n[13], lambda n, k, s: s[8], text_part, here, False),
            (lambda n, k, s: n[13], lambda n, k, s: s[9], text_part, here, False),
            (lambda n, k, s: n[12], lambda n, k, s: s[7], part, here, False),
            (lambda n, k, s: n[0], lambda n, k, s: n[8], part, here, False),
        ],
        tasks=cross_back_tasks,
        begin=cross_back_begin,
        end=cross_back_end,
        far=[cross_key_full, cross_value_full],
    )
    grad_resid_self, cross_sums, block_out, text_partial, gain_cross_query, gain_cross_key = kept
    grad_text = lax.psum_scatter(
        text_partial, "tensor", scatter_dimension=0, tiled=True
    ).astype(full_type)

    def self_back_pre(links, near, kinds, scratch, partial, ticks):
        backward(
            (0, 1),
            (near[14], near[15]),
            near[:13],
            near[13],
            (kinds[2], kinds[3], *scratch[7:10]),
            scratch,
            links,
            partial,
            ticks,
        )

    def before_self(total, where, near, kinds, first):
        hidden_ref, grad_ref, mixing_ref = near[17:20]
        out_ref, sums_ref = kinds[:2]
        unit, inverse = normed(hidden_ref[where, :])
        add_sum(sums_ref, 0, total, first)
        add_sum(sums_ref, 1, total * unit, first)
        out_ref[where, :] = grad_ref[where, :] + normed_back(
            unit, inverse, total * (1.0 + mixing_ref[1:2])
        )

    gain_width = qk_gain.shape[1]

    def settle_small(links, near, kinds, scratch):
        feed_ref, cross_ref, gain_cross_query_ref, gain_cross_key_ref = near[20:]
        self_ref, gain_query_ref, gain_key_ref, time_ref, slice_ref = kinds[1:]
        mine, line_land, stage, land = scratch[10:]
        z, dp = links.z, links.dp
        mine[...] = jnp.concatenate(
            [
                self_ref[0:2, :],
                cross_ref[0:1, :],
                feed_ref[0:2, :],
                cross_ref[2:3, :],
                cross_ref[1:2, :],
                jnp.zeros((1, width), full_type),
            ],
            axis=0,
        )
        moves = []
        for step in range(1, plan.tensor):
            target = lax.rem(z + step, plan.tensor)
            move = links.copy(mine, line_land.at[z], (dp, target), links.slot())
            move.start()
            moves.append(move)
        line_land[z] = mine[...]
        gain_rows = jnp.concatenate(
            [gain_query_ref[...], gain_key_ref[...]]
            + [gain_cross_query_ref[...], gain_cross_key_ref[...]],
            axis=1,
        )
        for move in moves:
            move.wait_recv()
        total = line_land[0]
        for index in range(1, plan.tensor):
            total = total + line_land[index]
        time_ref[0, :, :] = total[:6]
        for index in range(plan.dp):
            stage[index] = jnp.concatenate(
                [
                    total[:, index * part : (index + 1) * part],
                    gain_rows[:, index * gain_width : (index + 1) * gain_width],
                ],
                axis=1,
            )
        land[dp] = stage[dp]
        others = []
        for step in range(1, plan.dp):
            target = lax.rem(dp + step, plan.dp)
            move = links.copy(stage.at[target], land.at[dp], (target, z), links.slot())
            move.start()
            others.append(move)

        def finish():
            for move in others:
                move.wait_recv()
            summed = land[0]
            for index in range(1, plan.dp):
                summed = summed + land[index]
            slice_ref[...] = summed
            for move in moves + others:
                move.wait_send()

        return finish

    kept, _, _, _, made, sums = plan.phase(
        "self_back",
        [(self_grad_whole, 0), (query_full, 3), (key_full, 3), (value_full, 3), (out_full, 0)]
        + list(zip(self_kept, kept_groups))
        + [(gains, 2), (cosine, 2), (sine, 2), (self_whole, 4), (hidden_in, 4)]
        + [(grad_resid_self, 4), (mixing, 4), (feed_sums, 4), (cross_sums, 4)]
        + [(gain_cross_query, 4), (gain_cross_key, 4)],
        [
            ((rows, width), full_type, "post"),
            ((8, width), full_type, "post"),
            ((8, HEAD_DIM), full_type, "pre"),
            ((8, HEAD_DIM), full_type, "pre"),
            ((1, 6, width), full_type, "post"),
            ((8, part + gain_width), full_type, "post"),
        ],
        back_scratch
        + [
            pltpu.VMEM((8, width), full_type),
            pltpu.VMEM((plan.tensor, 8, width), full_type),
            pltpu.VMEM((plan.dp, 8, part + gain_width), full_type),
            pltpu.VMEM((plan.dp, 8, part + gain_width), full_type),
        ],
        self_back_pre,
        before_self,
        False,
        shape,
        sums=made,
        jobs=[
            (lambda n, k, s: n[16], lambda n, k, s: s[7], part, here, True),
            (lambda n, k, s: n[16], lambda n, k, s: s[8], part, here, True),
            (lambda n, k, s: n[16], lambda n, k, s: s[9], part, here, True),
            (lambda n, k, s: n[0], lambda n, k, s: n[10], part, here, True),
        ],
        settle_small=settle_small,
    )
    grad_hidden, _, _, _, grad_time, mine = kept
    sum_cross_key, sum_cross_value, sum_cross_query, sum_cross_out = sums
    sum_query, sum_key, sum_value, sum_out = made

    return (
        block_out,
        grad_hidden,
        grad_text,
        grad_time,
        mine[:6, :part],
        sum_query,
        sum_key,
        sum_value,
        sum_out.T,
        sum_cross_query,
        sum_cross_key,
        sum_cross_value,
        sum_cross_out.T,
        sum_up,
        sum_down.T,
        mine[:heads, part:],
        mine[6, :part],
    )


def solution(mesh):
    return jax.shard_map(
        functools.partial(body, Plan(mesh)),
        mesh=mesh,
        in_specs=(
            P(("dp", "tensor"), None),
            P(("dp", "tensor"), None),
            P("dp", None, None),
            P(None, "dp"),
            P(None, "dp"),
            P("dp", "tensor"),
            P("dp", "tensor"),
            P("dp", "tensor"),
            P("tensor", "dp"),
            P("dp", "tensor"),
            P("dp", "tensor"),
            P("dp", "tensor"),
            P("tensor", "dp"),
            P("dp", "tensor"),
            P("tensor", "dp"),
            P("tensor", "dp"),
            P("dp"),
            P(("dp", "tensor"), None),
        ),
        out_specs=(
            P(("dp", "tensor"), None),
            P(("dp", "tensor"), None),
            P(("dp", "tensor"), None),
            P("dp", None, None),
            P(None, "dp"),
            P("dp", "tensor"),
            P("dp", "tensor"),
            P("dp", "tensor"),
            P("tensor", "dp"),
            P("dp", "tensor"),
            P("dp", "tensor"),
            P("dp", "tensor"),
            P("tensor", "dp"),
            P("dp", "tensor"),
            P("tensor", "dp"),
            P("tensor", "dp"),
            P("dp"),
        ),
        check_vma=False,
    )
```
